128 devices in a mesh: dp: 32 (over x, z, y_hi), tensor: 4 (over y_lo, core).
Axes of the slice: x: 4, y: 4 (y_hi: 2, y_lo: 2; y = y_hi * 2 + y_lo), z: 4, core: 2. Of those that a mesh axis runs over, the one named last changes fastest.
Arguments:
- tokens: bfloat16 [32768, 1024], P(('dp', 'tensor')), may hold values from -6 to 6
- norm_in: bfloat16 [1024], replicated, may hold values from 0.099609375 to 1.8984375
- w_query: bfloat16 [1024, 2048], P(None, 'tensor'), may hold values from -0.1875 to 0.1875
- key_matrix: bfloat16 [1024, 1024], P(None, 'tensor'), may hold values from -0.1875 to 0.1875
- value_matrix: bfloat16 [1024, 1024], P(None, 'tensor'), may hold values from -0.1875 to 0.1875
- query_gain: bfloat16 [128], replicated, may hold values from 0.099609375 to 1.8984375
- key_gain: bfloat16 [128], replicated, may hold values from 0.099609375 to 1.8984375
- w_out: bfloat16 [2048, 1024], P('tensor'), may hold values from -2 to 2
- norm_mid: bfloat16 [1024], replicated, may hold values from 0.099609375 to 1.8984375
- w_gate: bfloat16 [1024, 3072], P(None, 'tensor'), may hold values from -0.1875 to 0.1875
- w_up: bfloat16 [1024, 3072], P(None, 'tensor'), may hold values from -0.1875 to 0.1875
- w_down: bfloat16 [3072, 1024], P('tensor'), may hold values from -0.21875 to 0.21875
- cotangent: bfloat16 [32768, 1024], P(('dp', 'tensor')), may hold values from -6 to 6
Outputs:
- result: bfloat16 [32768, 1024], P(('dp', 'tensor'))
- grad_tokens: bfloat16 [32768, 1024], P(('dp', 'tensor'))
- grad_norm_in: float32 [1024], replicated
- grad_query: float32 [1024, 2048], P('dp', 'tensor')
- grad_key: float32 [1024, 1024], P('dp', 'tensor')
- grad_value: float32 [1024, 1024], P('dp', 'tensor')
- grad_query_gain: float32 [128], replicated
- grad_key_gain: float32 [128], replicated
- grad_out: float32 [2048, 1024], P('tensor', 'dp')
- grad_norm_mid: float32 [1024], replicated
- grad_gate: float32 [1024, 3072], P('dp', 'tensor')
- grad_up: float32 [1024, 3072], P('dp', 'tensor')
- grad_down: float32 [3072, 1024], P('tensor', 'dp')
The draws below stay inside these ranges and needn't reach their ends.
All inputs are finite; a program needn't handle non-finite values.
Results may differ from the reference program's by a relative error of at most 0.028.
Values may be sent and summed in bfloat16 or wider, within the bound.
A program may use at most 128 MiB of HBM per device.

```python
import jax
import jax.numpy as jnp
from jax import lax

MODEL_WIDTH = 1024
QUERY_HEADS = 16
KEY_VALUE_HEADS = 8
HEAD_SIZE = 128
FF = 3072
SEQUENCE_TOKENS = 1024
TOKENS = 32768


def level_of(stream_key, dims, cuts, least, high):
    factor_of, own = 1.0, jax.random.fold_in(stream_key, 6)
    for dim, parts in cuts:
        steps = jnp.exp(jax.random.uniform(jax.random.fold_in(own, dim), (parts,), jnp.float32, least / len(cuts), high / len(cuts)))
        factor_of = factor_of * jnp.repeat(steps, dims[dim] // parts).reshape([-1 if axis == dim else 1 for axis in range(len(dims))])
    return factor_of


def noise(key, extent, deviation, limit, cuts=(), kind=jnp.bfloat16):
    result = deviation * jax.random.normal(key, extent, jnp.float32)
    if cuts:
        result = result * level_of(key, extent, cuts, -0.22, 0.18)
    return jnp.clip(result, -limit, limit).astype(kind)


def setup_inputs(seed: int = 0) -> dict:
    key_list = jax.random.split(jax.random.key(seed), 14)
    return {
        "tokens": noise(key_list[0], (TOKENS, MODEL_WIDTH), 1.0, 6.0, ((0, 128),)),
        "norm_in": jnp.clip(1.0 + 0.18 * jax.random.normal(key_list[1], (MODEL_WIDTH,), jnp.float32), 0.099609375, 1.8984375).astype(jnp.bfloat16),
        "w_query": noise(key_list[2], (MODEL_WIDTH, QUERY_HEADS * HEAD_SIZE), MODEL_WIDTH ** -0.5, 0.1875, ((1, 4),)),
        "key_matrix": noise(key_list[3], (MODEL_WIDTH, KEY_VALUE_HEADS * HEAD_SIZE), MODEL_WIDTH ** -0.5, 0.1875, ((1, 4),)),
        "value_matrix": noise(key_list[4], (MODEL_WIDTH, KEY_VALUE_HEADS * HEAD_SIZE), MODEL_WIDTH ** -0.5, 0.1875, ((1, 4),)),
        "query_gain": jnp.clip(1.0 + 0.18 * jax.random.normal(key_list[5], (HEAD_SIZE,), jnp.float32), 0.099609375, 1.8984375).astype(jnp.bfloat16),
        "key_gain": jnp.clip(1.0 + 0.18 * jax.random.normal(key_list[6], (HEAD_SIZE,), jnp.float32), 0.099609375, 1.8984375).astype(jnp.bfloat16),
        "w_out": noise(key_list[7], (QUERY_HEADS * HEAD_SIZE, MODEL_WIDTH), (QUERY_HEADS * HEAD_SIZE // 256) ** -0.5, 2.0, ((0, 4),)),
        "norm_mid": jnp.clip(1.0 + 0.18 * jax.random.normal(key_list[8], (MODEL_WIDTH,), jnp.float32), 0.099609375, 1.8984375).astype(jnp.bfloat16),
        "w_gate": noise(key_list[9], (MODEL_WIDTH, FF), MODEL_WIDTH ** -0.5, 0.1875, ((1, 4),)),
        "w_up": noise(key_list[10], (MODEL_WIDTH, FF), MODEL_WIDTH ** -0.5, 0.1875, ((1, 4),)),
        "w_down": noise(key_list[11], (FF, MODEL_WIDTH), (FF // 4) ** -0.5, 0.21875, ((0, 4),)),
        "cotangent": noise(key_list[12], (TOKENS, MODEL_WIDTH), 1.0, 6.0, ((0, 128),)),
    }


@jax.custom_vjp
def reduced_precision(v):
    return lax.optimization_barrier(v.astype(jnp.bfloat16)).astype(jnp.float32)

@jax.custom_vjp
def reduced_precision_backward(v):
    return v

def low_keep(v):
    return (reduced_precision(v), None)

def low_pass(kept, grad):
    return (grad,)

def back_keep(v):
    return (v, None)

def back_low(kept, grad):
    return (reduced_precision(grad),)
reduced_precision.defvjp(low_keep, low_pass)
reduced_precision_backward.defvjp(back_keep, back_low)
epsilon = 1e-06
highest = lax.Precision.HIGHEST

def matrix_product(left, right):
    return jnp.dot(left, right, precision=highest)

def rms_scale(values):
    return lax.rsqrt(lax.optimization_barrier(jnp.mean(values * values, axis=-1, keepdims=True)) + epsilon)

def rotary_tables():
    position = jnp.arange(SEQUENCE_TOKENS, dtype=jnp.float32)
    inverse = jnp.power(jnp.float32(1000000.0), -jnp.arange(HEAD_SIZE // 2, dtype=jnp.float32) * 2.0 / HEAD_SIZE)
    angles = position[:, None] * inverse[None, :]
    return (jnp.cos(angles)[:, None, :], jnp.sin(angles)[:, None, :])

def rotate(values, cosine_table, sine_table):
    half_size = values.shape[-1] // 2
    first_half = values[..., :half_size]
    second = values[..., half_size:]
    return jnp.concatenate([first_half * cosine_table - second * sine_table, second * cosine_table + first_half * sine_table], axis=-1)

def attend_block(query_block, block_start, split_key_heads, split_value_heads):
    scores = jnp.einsum('qhd,khd->hqk', query_block, split_key_heads, precision=highest) * HEAD_SIZE ** (-0.5)
    scores = reduced_precision_backward(scores)
    query_pos = block_start + jnp.arange(query_block.shape[0], dtype=jnp.int32)
    key_pos = jnp.arange(SEQUENCE_TOKENS, dtype=jnp.int32)
    allowed = key_pos[None, :] <= query_pos[:, None]
    scores = jnp.where(allowed[None], scores, -jnp.inf)
    probabilities = reduced_precision(jax.nn.softmax(scores, axis=-1))
    return jnp.einsum('hqk,khd->qhd', probabilities, split_value_heads, precision=highest)

def block_forward(tokens, norm_in, w_query, key_matrix, value_matrix, query_gain, key_gain, w_out, norm_mid, w_gate, w_up, w_down):
    cosine_table, sine_table = rotary_tables()
    normalized_rows = reduced_precision(tokens * rms_scale(tokens) * norm_in)
    queries = reduced_precision_backward(matrix_product(normalized_rows, w_query)).reshape(SEQUENCE_TOKENS, QUERY_HEADS, HEAD_SIZE)
    split_key_heads = reduced_precision_backward(matrix_product(normalized_rows, key_matrix)).reshape(SEQUENCE_TOKENS, KEY_VALUE_HEADS, HEAD_SIZE)
    split_value_heads = reduced_precision(reduced_precision_backward(matrix_product(normalized_rows, value_matrix))).reshape(SEQUENCE_TOKENS, KEY_VALUE_HEADS, HEAD_SIZE)
    queries = reduced_precision(rotate(queries * rms_scale(queries) * query_gain, cosine_table, sine_table))
    split_key_heads = reduced_precision(rotate(split_key_heads * rms_scale(split_key_heads) * key_gain, cosine_table, sine_table))
    heads_per_group = QUERY_HEADS // KEY_VALUE_HEADS
    split_key_heads = jnp.repeat(split_key_heads, heads_per_group, axis=1)
    split_value_heads = jnp.repeat(split_value_heads, heads_per_group, axis=1)
    block_size = min(512, SEQUENCE_TOKENS)
    blocks = SEQUENCE_TOKENS // block_size
    attend = jax.checkpoint(attend_block)
    starts = jnp.arange(blocks, dtype=jnp.int32) * block_size
    attended = lax.map(lambda packed: attend(packed[0], packed[1], split_key_heads, split_value_heads), (queries.reshape(blocks, block_size, QUERY_HEADS, HEAD_SIZE), starts))
    attended = reduced_precision(reduced_precision_backward(attended.reshape(SEQUENCE_TOKENS, QUERY_HEADS * HEAD_SIZE)))
    hidden_state = tokens + reduced_precision_backward(matrix_product(attended, w_out))
    normed_mid = reduced_precision(hidden_state * rms_scale(hidden_state) * norm_mid)
    gate_proj = reduced_precision_backward(matrix_product(normed_mid, w_gate))
    up_proj = reduced_precision_backward(matrix_product(normed_mid, w_up))
    activated = reduced_precision(jax.nn.silu(gate_proj) * up_proj)
    return hidden_state + reduced_precision_backward(matrix_product(activated, w_down))

def reference(tokens, norm_in, w_query, key_matrix, value_matrix, query_gain, key_gain, w_out, norm_mid, w_gate, w_up, w_down, cotangent):
    weights = tuple((weight.astype(jnp.float32) for weight in (norm_in, w_query, key_matrix, value_matrix, query_gain, key_gain, w_out, norm_mid, w_gate, w_up, w_down)))
    sequences = tokens.astype(jnp.float32).reshape(-1, SEQUENCE_TOKENS, MODEL_WIDTH)
    seq_cots = cotangent.astype(jnp.float32).reshape(-1, SEQUENCE_TOKENS, MODEL_WIDTH)

    def one_sequence(totals, seq_item):
        seq_in, seq_cot = seq_item
        output, pullback = jax.vjp(block_forward, seq_in, *weights)
        gradients = pullback(seq_cot)
        totals = tuple((running + fresh for running, fresh in zip(totals, gradients[1:])))
        return (totals, (output.astype(jnp.bfloat16), gradients[0].astype(jnp.bfloat16)))
    zero_init = tuple((jnp.zeros_like(weight) for weight in weights))
    totals, (outputs, input_grads) = lax.scan(one_sequence, zero_init, (sequences, seq_cots))
    return (outputs.reshape(-1, MODEL_WIDTH), input_grads.reshape(-1, MODEL_WIDTH), totals[0], totals[1], totals[2], totals[3], totals[4], totals[5], totals[6], totals[7], totals[8], totals[9], totals[10])
```

```python
import functools

import jax
import jax.numpy as jnp
from jax import lax
from jax.experimental import pallas as pl
from jax.experimental.pallas import tpu as pltpu
from jax.sharding import PartitionSpec as P

HEAD_SIZE = 128
SEQUENCE_TOKENS = 1024
GROUP = 4
CHUNKS = 4
VMEM_SPACE = pl.BlockSpec(memory_space=pltpu.VMEM)
FLIP, MIRROR = 1, 3


def partner(index, pairing):
    if pairing == FLIP:
        return index + 1 - 2 * lax.rem(index, 2)
    return 3 - index


def across(index):
    return lax.rem(index + 2, 4)


def send(source, target, send_sem, recv_sem, where):
    return pltpu.make_async_remote_copy(
        src_ref=source,
        dst_ref=target,
        send_sem=send_sem,
        recv_sem=recv_sem,
        device_id=where,
        device_id_type=pl.DeviceIdType.MESH,
    )


def greet(others):
    barrier = pltpu.get_barrier_semaphore()
    for where in others:
        pl.semaphore_signal(barrier, inc=1, device_id=where, device_id_type=pl.DeviceIdType.MESH)
    pl.semaphore_wait(barrier, len(others))


def gather_kernel(shard, whole, own_sem, send_sems, recv_sems):
    me = lax.axis_index("tensor")
    sibling, far = {"tensor": partner(me, FLIP)}, {"tensor": across(me)}
    rows = shard.shape[0] // CHUNKS
    greet([sibling, far])
    copies = []
    for chunk in range(CHUNKS):
        part = pl.ds(chunk * rows, rows)
        copies.append(
            send(shard.at[part], whole.at[me, part], send_sems.at[0, chunk], recv_sems.at[0, chunk], far)
        )
    for copy in copies:
        copy.start()
    near = send(shard, whole.at[me], send_sems.at[1, 0], recv_sems.at[1, 0], sibling)
    near.start()
    own = pltpu.make_async_copy(shard, whole.at[me], own_sem)
    own.start()
    passed = []
    there = across(me)
    for chunk in range(CHUNKS):
        part = pl.ds(chunk * rows, rows)
        copies[chunk].wait_recv()
        onward = send(
            whole.at[there, part],
            whole.at[there, part],
            send_sems.at[2, chunk],
            recv_sems.at[2, chunk],
            sibling,
        )
        onward.start()
        passed.append(onward)
    own.wait()
    near.wait()
    for copy in copies:
        copy.wait_send()
    for copy in passed:
        copy.wait()


def group_gather(shard):
    rows, width = shard.shape
    return pl.pallas_call(
        gather_kernel,
        out_shape=jax.ShapeDtypeStruct((GROUP, rows, width), shard.dtype),
        in_specs=[VMEM_SPACE],
        out_specs=VMEM_SPACE,
        scratch_shapes=[
            pltpu.SemaphoreType.DMA,
            pltpu.SemaphoreType.DMA((3, CHUNKS)),
            pltpu.SemaphoreType.DMA((3, CHUNKS)),
        ],
        compiler_params=pltpu.CompilerParams(
            collective_id=0, has_side_effects=True, vmem_limit_bytes=32 << 20
        ),
    )(shard).reshape(GROUP * rows, width)


def scatter_kernel(partial, total, near, summed, arrived, send_sems, recv_sems):
    me = lax.axis_index("tensor")
    sibling, far = {"tensor": partner(me, FLIP)}, {"tensor": across(me)}
    rows = total.shape[0] // CHUNKS
    greet([sibling, far])
    copies = [[], [], []]
    for slot, block in ((0, partner(me, MIRROR)), (1, partner(me, FLIP))):
        for chunk in range(CHUNKS):
            part = pl.ds(chunk * rows, rows)
            copies[slot].append(
                send(
                    partial.at[block, part],
                    near.at[slot, part],
                    send_sems.at[slot, chunk],
                    recv_sems.at[slot, chunk],
                    sibling,
                )
            )
            copies[slot][chunk].start()
    there = across(me)
    for chunk in range(CHUNKS):
        part = pl.ds(chunk * rows, rows)
        copies[0][chunk].wait_recv()
        summed[part] = (
            partial[there, part].astype(jnp.float32) + near[0, part].astype(jnp.float32)
        ).astype(jnp.bfloat16)
        onward = send(
            summed.at[part], arrived.at[part], send_sems.at[2, chunk], recv_sems.at[2, chunk], far
        )
        onward.start()
        copies[2].append(onward)
    for chunk in range(CHUNKS):
        part = pl.ds(chunk * rows, rows)
        copies[1][chunk].wait_recv()
        copies[2][chunk].wait_recv()
        total[part] = (
            partial[me, part].astype(jnp.float32)
            + near[1, part].astype(jnp.float32)
            + arrived[part].astype(jnp.float32)
        )
    for group in copies:
        for copy in group:
            copy.wait_send()


def group_scatter(partial):
    rows, width = partial.shape[0] // GROUP, partial.shape[1]
    return pl.pallas_call(
        scatter_kernel,
        out_shape=jax.ShapeDtypeStruct((rows, width), jnp.float32),
        in_specs=[VMEM_SPACE],
        out_specs=VMEM_SPACE,
        scratch_shapes=[
            pltpu.VMEM((2, rows, width), jnp.bfloat16),
            pltpu.VMEM((rows, width), jnp.bfloat16),
            pltpu.VMEM((rows, width), jnp.bfloat16),
            pltpu.SemaphoreType.DMA((3, CHUNKS)),
            pltpu.SemaphoreType.DMA((3, CHUNKS)),
        ],
        compiler_params=pltpu.CompilerParams(
            collective_id=1, has_side_effects=True, vmem_limit_bytes=32 << 20
        ),
    )(partial.reshape(GROUP, rows, width))


class Stream:
    def __init__(self, order, grad, out, scratch, sems, place, where):
        self.first, self.orders = order[0], order[1:]
        self.grad, self.out = grad, out
        self.early, self.mid, self.late, self.held, self.low, self.pair, self.last = scratch
        self.send_sems, self.recv_sems = sems
        self.place, self.where = place, where
        self.pending = []

    def axis(self, stage):
        return self.first if stage == 0 else ("z" if self.first == "x" else "x")

    def block(self, stage, index):
        if stage == 1:
            return self.held.at[index]
        return self.grad.at[index] if self.first == "x" else self.grad.at[:, index]

    def launch(self, source, target, slot, where):
        copy = send(source, target, self.send_sems.at[slot], self.recv_sems.at[slot], where)
        copy.start()
        self.pending.append(copy)
        return copy

    def halve(self, stage):
        axis, here = self.axis(stage), self.place[self.axis(stage)]
        other = partner(here, self.orders[stage])
        box = self.early if stage == 0 else self.late
        self.copies = [
            self.launch(
                self.block(stage, index), box.at[slot], 4 * stage + slot, self.where(axis, other)
            )
            for slot, index in ((1, across(here)), (0, other))
        ]

    def quarter(self, stage):
        axis, here = self.axis(stage), self.place[self.axis(stage)]
        other = partner(here, FLIP + MIRROR - self.orders[stage])
        box, mid = (self.early, self.mid) if stage == 0 else (self.late, self.low)
        self.copies[0].wait_recv()
        mine = self.block(stage, other)

        def add(row, _):
            mid[0, row] = (
                mine[row].astype(jnp.float32) + box[1, row].astype(jnp.float32)
            ).astype(jnp.bfloat16)
            return _

        lax.fori_loop(0, mid.shape[1], add, 0)
        self.copies.append(
            self.launch(mid.at[0], mid.at[1], 4 * stage + 2, self.where(axis, other))
        )

    def settle(self, stage):
        here = self.place[self.axis(stage)]
        self.copies[1].wait_recv()
        self.copies[2].wait_recv()
        box, mid = (self.early, self.mid) if stage == 0 else (self.late, self.low)
        mine = self.block(stage, here)
        if stage == 0:

            def add(row, _):
                self.held[row] = (
                    mine[row].astype(jnp.float32)
                    + box[0, row].astype(jnp.float32)
                    + mid[1, row].astype(jnp.float32)
                ).astype(jnp.bfloat16)
                return _

            lax.fori_loop(0, mid.shape[1], add, 0)
            return
        keep = self.place["y"]
        give = 1 - keep
        self.pair[0] = (
            mine[give].astype(jnp.float32)
            + box[0, give].astype(jnp.float32)
            + mid[1, give].astype(jnp.float32)
        ).astype(jnp.bfloat16)
        self.copies.append(
            self.launch(self.pair.at[0], self.pair.at[1], 3, self.where("y", give))
        )
        self.last[...] = (
            mine[keep].astype(jnp.float32)
            + box[0, keep].astype(jnp.float32)
            + mid[1, keep].astype(jnp.float32)
        )

    def finish(self):
        self.copies[3].wait_recv()
        self.out[...] = self.last[...] + self.pair[1].astype(jnp.float32)
        for copy in self.pending:
            copy.wait_send()


STREAM_SEMS = 7
STREAM_SCRATCH = 7


def stream_scratch(columns):
    low = jnp.bfloat16
    return [
        pltpu.VMEM((2, 4, 2, 32, columns), low),
        pltpu.VMEM((2, 4, 2, 32, columns), low),
        pltpu.VMEM((2, 2, 32, columns), low),
        pltpu.VMEM((4, 2, 32, columns), low),
        pltpu.VMEM((2, 2, 32, columns), low),
        pltpu.VMEM((2, 32, columns), low),
        pltpu.VMEM((32, columns), jnp.float32),
    ]


def rank_places():
    rank = lax.axis_index("dp")
    return {"x": lax.div(rank, 8), "z": lax.rem(lax.div(rank, 2), 4), "y": lax.rem(rank, 2)}


def rank_where(place):
    def where(axis, index):
        at = dict(place)
        at[axis] = index
        return {"dp": at["x"] * 8 + at["z"] * 2 + at["y"]}

    return where


def reduce_kernel(orders, *refs):
    n = len(orders)
    grads, gains, outs, gain_out = refs[:n], refs[n], refs[n + 1 : 2 * n + 1], refs[2 * n + 1]
    rest = refs[2 * n + 2 :]
    gain_box, gain_send, gain_recv = rest[:3]
    send_sems, recv_sems = rest[3:5]
    rest = rest[5:]
    place = rank_places()
    where = rank_where(place)
    me = lax.axis_index("tensor")
    doubling = [
        where("x", partner(place["x"], FLIP)),
        where("x", partner(place["x"], MIRROR)),
        where("z", partner(place["z"], FLIP)),
        where("z", partner(place["z"], MIRROR)),
        where("y", 1 - place["y"]),
        {"tensor": partner(me, FLIP)},
        {"tensor": across(me)},
    ]
    greet(doubling)
    streams = [
        Stream(
            orders[i],
            grads[i],
            outs[i],
            rest[i * STREAM_SCRATCH : (i + 1) * STREAM_SCRATCH],
            (send_sems.at[i], recv_sems.at[i]),
            place,
            where,
        )
        for i in range(n)
    ]
    gain_copies = []
    gain_box[0] = gains[...]

    def gain_start(step):
        copy = send(
            gain_box.at[2 * step],
            gain_box.at[2 * step + 1],
            gain_send.at[step],
            gain_recv.at[step],
            doubling[step],
        )
        copy.start()
        gain_copies.append(copy)

    def gain_end(step):
        gain_copies[step].wait_recv()
        result = gain_box[2 * step] + gain_box[2 * step + 1]
        if step == 6:
            gain_out[...] = result
        else:
            gain_box[2 * step + 2] = result

    gain_start(0)
    for stream in streams:
        stream.halve(0)
    gain_end(0)
    gain_start(1)
    for stream in streams:
        stream.quarter(0)
    gain_end(1)
    gain_start(2)
    for stream in streams:
        stream.settle(0)
        stream.halve(1)
    gain_end(2)
    gain_start(3)
    for stream in streams:
        stream.quarter(1)
    gain_end(3)
    gain_start(4)
    for stream in streams:
        stream.settle(1)
    gain_end(4)
    gain_start(5)
    for stream in streams:
        stream.finish()
    gain_end(5)
    gain_start(6)
    gain_end(6)
    for copy in gain_copies:
        copy.wait_send()


def reduce_all(orders, grads, gains):
    grads = [g.reshape(4, 4, 2, 32, g.shape[1]) for g in grads]
    n = len(grads)
    scratch = [
        pltpu.VMEM((14,) + gains.shape, jnp.float32),
        pltpu.SemaphoreType.DMA((7,)),
        pltpu.SemaphoreType.DMA((7,)),
        pltpu.SemaphoreType.DMA((n, STREAM_SEMS)),
        pltpu.SemaphoreType.DMA((n, STREAM_SEMS)),
    ]
    for g in grads:
        scratch += stream_scratch(g.shape[-1])
    return pl.pallas_call(
        functools.partial(reduce_kernel, orders),
        out_shape=[jax.ShapeDtypeStruct((32, g.shape[-1]), jnp.float32) for g in grads]
        + [jax.ShapeDtypeStruct(gains.shape, jnp.float32)],
        in_specs=[VMEM_SPACE] * (n + 1),
        out_specs=[VMEM_SPACE] * (n + 1),
        scratch_shapes=scratch,
        compiler_params=pltpu.CompilerParams(
            collective_id=2, has_side_effects=True, vmem_limit_bytes=48 << 20
        ),
    )(*grads, gains)


epsilon = 1e-06
contract_rows = (((0,), (0,)), ((), ()))
contract_cols = (((1,), (1,)), ((), ()))


def rms_scale(values):
    return lax.rsqrt(jnp.mean(values * values, axis=-1, keepdims=True) + epsilon)


def rotary_tables():
    position = jnp.arange(SEQUENCE_TOKENS, dtype=jnp.float32)
    inverse = jnp.power(
        jnp.float32(1000000.0), -jnp.arange(HEAD_SIZE // 2, dtype=jnp.float32) * 2.0 / HEAD_SIZE
    )
    angles = position[:, None] * inverse[None, :]
    return (jnp.cos(angles)[:, None, :], jnp.sin(angles)[:, None, :])


def rotate(values, cosine_table, sine_table):
    half_size = values.shape[-1] // 2
    first_half = values[..., :half_size]
    second = values[..., half_size:]
    return jnp.concatenate(
        [
            first_half * cosine_table - second * sine_table,
            second * cosine_table + first_half * sine_table,
        ],
        axis=-1,
    )


def rotate_back(incoming, cosine_table, sine_table):
    half_size = incoming.shape[-1] // 2
    first_half = incoming[..., :half_size]
    second = incoming[..., half_size:]
    return jnp.concatenate(
        [
            first_half * cosine_table + second * sine_table,
            second * cosine_table - first_half * sine_table,
        ],
        axis=-1,
    )


def norm_back(incoming, values, row_scale, gain_vector):
    scaled = incoming * gain_vector
    input_grad = row_scale * scaled - values * row_scale**3 * jnp.mean(
        scaled * values, axis=-1, keepdims=True
    )
    return (input_grad, incoming * values * row_scale)


def causal_mask(row_start, block_size, key_end):
    query_pos = row_start + jnp.arange(block_size, dtype=jnp.int32)
    key_pos = jnp.arange(key_end, dtype=jnp.int32)
    return key_pos[None, :] <= query_pos[:, None]


def attend_forward(queries, split_key_heads, split_value_heads):
    block_size = min(512, SEQUENCE_TOKENS)
    score_scale = HEAD_SIZE ** (-0.5)
    outputs = []
    log_parts = []
    for block_index in range(SEQUENCE_TOKENS // block_size):
        row_start = block_index * block_size
        key_end = row_start + block_size
        query_part = queries[row_start:key_end]
        scores = (
            jnp.einsum(
                "qgrd,kgd->grqk",
                query_part,
                split_key_heads[:key_end],
                preferred_element_type=jnp.float32,
            )
            * score_scale
        )
        scores = jnp.where(causal_mask(row_start, block_size, key_end), scores, -jnp.inf)
        peak_score = jnp.max(scores, axis=-1, keepdims=True)
        exponent = jnp.exp(scores - peak_score)
        denominator = jnp.sum(exponent, axis=-1, keepdims=True)
        probabilities = (exponent / denominator).astype(jnp.bfloat16)
        outputs.append(
            jnp.einsum(
                "grqk,kgd->qgrd",
                probabilities,
                split_value_heads[:key_end],
                preferred_element_type=jnp.float32,
            )
        )
        log_parts.append(peak_score + jnp.log(denominator))
    return (jnp.concatenate(outputs, axis=0), jnp.concatenate(log_parts, axis=2))


def attend_backward(queries, split_key_heads, split_value_heads, grad_attended, log_totals):
    block_size = min(512, SEQUENCE_TOKENS)
    score_scale = HEAD_SIZE ** (-0.5)
    key_grads = jnp.zeros(split_key_heads.shape, jnp.float32)
    value_grads = jnp.zeros(split_value_heads.shape, jnp.float32)
    query_grads = []
    for block_index in range(SEQUENCE_TOKENS // block_size):
        row_start = block_index * block_size
        key_end = row_start + block_size
        query_part = queries[row_start:key_end]
        grad_part = grad_attended[row_start:key_end]
        scores = (
            jnp.einsum(
                "qgrd,kgd->grqk",
                query_part,
                split_key_heads[:key_end],
                preferred_element_type=jnp.float32,
            )
            * score_scale
        )
        probabilities = jnp.where(
            causal_mask(row_start, block_size, key_end),
            jnp.exp(scores - log_totals[:, :, row_start:key_end]),
            0.0,
        )
        probs_low = probabilities.astype(jnp.bfloat16)
        value_grads = value_grads.at[:key_end].add(
            jnp.einsum("grqk,qgrd->kgd", probs_low, grad_part, preferred_element_type=jnp.float32)
        )
        grad_probs = jnp.einsum(
            "qgrd,kgd->grqk",
            grad_part,
            split_value_heads[:key_end],
            preferred_element_type=jnp.float32,
        )
        row_delta = jnp.sum(grad_probs * probabilities, axis=-1, keepdims=True)
        grad_scores = (probabilities * (grad_probs - row_delta)).astype(jnp.bfloat16)
        query_grads.append(
            jnp.einsum(
                "grqk,kgd->qgrd",
                grad_scores,
                split_key_heads[:key_end],
                preferred_element_type=jnp.float32,
            )
            * score_scale
        )
        key_grads = key_grads.at[:key_end].add(
            jnp.einsum(
                "grqk,qgrd->kgd", grad_scores, query_part, preferred_element_type=jnp.float32
            )
            * score_scale
        )
    return (jnp.concatenate(query_grads, axis=0), key_grads, value_grads)


def per_device(
    tokens,
    norm_in,
    w_query,
    key_matrix,
    value_matrix,
    query_gain,
    key_gain,
    w_out,
    norm_mid,
    w_gate,
    w_up,
    w_down,
    cotangent,
):
    local_rows = tokens.shape[0]
    head_local = w_query.shape[1] // HEAD_SIZE
    kv_local = key_matrix.shape[1] // HEAD_SIZE
    repeat = head_local // kv_local
    total_rows = local_rows * lax.axis_size("tensor")
    seq_count = total_rows // SEQUENCE_TOKENS
    cosine_table, sine_table = rotary_tables()
    norm_in_f = norm_in.astype(jnp.float32)
    norm_mid_f = norm_mid.astype(jnp.float32)
    query_gain_f = query_gain.astype(jnp.float32)
    key_gain_f = key_gain.astype(jnp.float32)
    inputs = tokens.astype(jnp.float32)
    scale_in = rms_scale(inputs)
    normalized_rows = (inputs * scale_in * norm_in_f).astype(jnp.bfloat16)
    gathered = group_gather(normalized_rows)
    query_raw = jnp.dot(gathered, w_query, preferred_element_type=jnp.float32).reshape(
        total_rows, head_local, HEAD_SIZE
    )
    key_raw = jnp.dot(gathered, key_matrix, preferred_element_type=jnp.float32).reshape(
        total_rows, kv_local, HEAD_SIZE
    )
    value_low = jnp.dot(gathered, value_matrix, preferred_element_type=jnp.float32).astype(
        jnp.bfloat16
    )
    query_scale = rms_scale(query_raw)
    key_scale = rms_scale(key_raw)
    query_low = rotate(
        (query_raw * query_scale * query_gain_f).reshape(
            seq_count, SEQUENCE_TOKENS, head_local, HEAD_SIZE
        ),
        cosine_table,
        sine_table,
    ).astype(jnp.bfloat16)
    key_low = rotate(
        (key_raw * key_scale * key_gain_f).reshape(seq_count, SEQUENCE_TOKENS, kv_local, HEAD_SIZE),
        cosine_table,
        sine_table,
    ).astype(jnp.bfloat16)
    query_heads = query_low.reshape(seq_count, SEQUENCE_TOKENS, kv_local, repeat, HEAD_SIZE)
    split_value_heads = value_low.reshape(seq_count, SEQUENCE_TOKENS, kv_local, HEAD_SIZE)
    attended, log_totals = lax.map(
        lambda packed: attend_forward(packed[0], packed[1], packed[2]),
        (query_heads, key_low, split_value_heads),
    )
    attended = attended.reshape(total_rows, head_local * HEAD_SIZE).astype(jnp.bfloat16)
    hidden_state = inputs + group_scatter(
        jnp.dot(attended, w_out, preferred_element_type=jnp.float32).astype(jnp.bfloat16)
    )
    scale_mid = rms_scale(hidden_state)
    normed_mid = (hidden_state * scale_mid * norm_mid_f).astype(jnp.bfloat16)
    gathered_mid = group_gather(normed_mid)
    gate_proj = jnp.dot(gathered_mid, w_gate, preferred_element_type=jnp.float32)
    up_proj = jnp.dot(gathered_mid, w_up, preferred_element_type=jnp.float32)
    activated = (jax.nn.silu(gate_proj) * up_proj).astype(jnp.bfloat16)
    result = (
        hidden_state
        + group_scatter(
            jnp.dot(activated, w_down, preferred_element_type=jnp.float32).astype(jnp.bfloat16)
        )
    ).astype(jnp.bfloat16)
    grad_full = group_gather(cotangent)
    grad_down = lax.dot_general(
        grad_full, activated, contract_rows, preferred_element_type=jnp.float32
    )
    grad_act = lax.dot_general(grad_full, w_down, contract_cols, preferred_element_type=jnp.float32)
    sigmoid_gate = jax.nn.sigmoid(gate_proj)
    grad_up_low = (grad_act * gate_proj * sigmoid_gate).astype(jnp.bfloat16)
    grad_gate_low = (
        grad_act * up_proj * sigmoid_gate * (1.0 + gate_proj * (1.0 - sigmoid_gate))
    ).astype(jnp.bfloat16)
    grad_w_gate = lax.dot_general(
        gathered_mid, grad_gate_low, contract_rows, preferred_element_type=jnp.float32
    )
    grad_w_up = lax.dot_general(
        gathered_mid, grad_up_low, contract_rows, preferred_element_type=jnp.float32
    )
    grad_normed_mid = group_scatter(
        (
            lax.dot_general(grad_gate_low, w_gate, contract_cols, preferred_element_type=jnp.float32)
            + lax.dot_general(grad_up_low, w_up, contract_cols, preferred_element_type=jnp.float32)
        ).astype(jnp.bfloat16)
    )
    back_mid, gain_mid_terms = norm_back(grad_normed_mid, hidden_state, scale_mid, norm_mid_f)
    grad_hidden = cotangent.astype(jnp.float32) + back_mid
    grad_gathered = group_gather(grad_hidden.astype(jnp.bfloat16))
    grad_w_out = lax.dot_general(
        grad_gathered, attended, contract_rows, preferred_element_type=jnp.float32
    )
    grad_attended = lax.dot_general(
        grad_gathered, w_out, contract_cols, preferred_element_type=jnp.float32
    ).astype(jnp.bfloat16)
    query_grads, key_grads, value_grads = lax.map(
        lambda packed: attend_backward(packed[0], packed[1], packed[2], packed[3], packed[4]),
        (
            query_heads,
            key_low,
            split_value_heads,
            grad_attended.reshape(seq_count, SEQUENCE_TOKENS, kv_local, repeat, HEAD_SIZE),
            log_totals,
        ),
    )
    query_unrot = rotate_back(
        query_grads.reshape(seq_count, SEQUENCE_TOKENS, head_local, HEAD_SIZE),
        cosine_table,
        sine_table,
    )
    key_unrot = rotate_back(key_grads, cosine_table, sine_table)
    grad_query_raw, query_gain_terms = norm_back(
        query_unrot.reshape(total_rows, head_local, HEAD_SIZE), query_raw, query_scale, query_gain_f
    )
    grad_key_raw, key_gain_terms = norm_back(
        key_unrot.reshape(total_rows, kv_local, HEAD_SIZE), key_raw, key_scale, key_gain_f
    )
    query_grad_low = grad_query_raw.reshape(total_rows, head_local * HEAD_SIZE).astype(jnp.bfloat16)
    key_grad_low = grad_key_raw.reshape(total_rows, kv_local * HEAD_SIZE).astype(jnp.bfloat16)
    value_grad_low = value_grads.reshape(total_rows, kv_local * HEAD_SIZE).astype(jnp.bfloat16)
    grad_w_query = lax.dot_general(
        gathered, query_grad_low, contract_rows, preferred_element_type=jnp.float32
    )
    grad_w_key = lax.dot_general(
        gathered, key_grad_low, contract_rows, preferred_element_type=jnp.float32
    )
    grad_w_value = lax.dot_general(
        gathered, value_grad_low, contract_rows, preferred_element_type=jnp.float32
    )
    grad_normed = group_scatter(
        (
            lax.dot_general(
                query_grad_low, w_query, contract_cols, preferred_element_type=jnp.float32
            )
            + lax.dot_general(
                key_grad_low, key_matrix, contract_cols, preferred_element_type=jnp.float32
            )
            + lax.dot_general(
                value_grad_low, value_matrix, contract_cols, preferred_element_type=jnp.float32
            )
        ).astype(jnp.bfloat16)
    )
    back_in, gain_in_terms = norm_back(grad_normed, inputs, scale_in, norm_in_f)
    grad_tokens = (grad_hidden + back_in).astype(jnp.bfloat16)
    gains = jnp.concatenate(
        [
            jnp.sum(gain_in_terms, axis=0),
            jnp.sum(gain_mid_terms, axis=0),
            jnp.sum(query_gain_terms, axis=(0, 1)),
            jnp.sum(key_gain_terms, axis=(0, 1)),
            jnp.zeros((768,), jnp.float32),
        ]
    ).reshape(24, 128)
    low = jnp.bfloat16
    summed = reduce_all(
        (
            ("x", FLIP, FLIP),
            ("x", MIRROR, MIRROR),
            ("z", FLIP, FLIP),
            ("z", MIRROR, MIRROR),
            ("x", FLIP, MIRROR),
            ("x", MIRROR, FLIP),
            ("z", MIRROR, MIRROR),
        ),
        [
            grad_w_gate.astype(low),
            grad_w_up.astype(low),
            grad_down.astype(low),
            grad_w_out.astype(low),
            grad_w_key.astype(low),
            grad_w_value.astype(low),
            grad_w_query.astype(low),
        ],
        gains,
    )
    totals = summed[7].reshape(3072)
    return (
        result,
        grad_tokens,
        totals[:1024],
        summed[6],
        summed[4],
        summed[5],
        totals[2048:2176],
        totals[2176:2304],
        summed[3].T,
        totals[1024:2048],
        summed[0],
        summed[1],
        summed[2].T,
    )


def solution(mesh):
    placed = (
        P(("dp", "tensor"), None),
        P(),
        P(None, "tensor"),
        P(None, "tensor"),
        P(None, "tensor"),
        P(),
        P(),
        P("tensor", None),
        P(),
        P(None, "tensor"),
        P(None, "tensor"),
        P("tensor", None),
        P(("dp", "tensor"), None),
    )
    return jax.shard_map(
        per_device,
        mesh=mesh,
        in_specs=placed,
        out_specs=(
            P(("dp", "tensor"), None),
            P(("dp", "tensor"), None),
            P(),
            P("dp", "tensor"),
            P("dp", "tensor"),
            P("dp", "tensor"),
            P(),
            P(),
            P("tensor", "dp"),
            P(),
            P("dp", "tensor"),
            P("dp", "tensor"),
            P("tensor", "dp"),
        ),
        check_vma=False,
    )
```

```python
import functools

import jax
import jax.numpy as jnp
import numpy as np
from jax import lax
from jax.experimental import pallas as pl
from jax.experimental.pallas import tpu as pltpu
from jax.sharding import PartitionSpec as P

HEAD_SIZE = 128
SEQUENCE_TOKENS = 1024
GROUP = 4
CHUNKS = 4
VMEM_SPACE = pl.BlockSpec(memory_space=pltpu.VMEM)
FLIP, MIRROR = 1, 3
epsilon = 1e-06
contract_rows = (((0,), (0,)), ((), ()))
contract_cols = (((1,), (1,)), ((), ()))


def partner(index, pairing):
    if pairing == FLIP:
        return index + 1 - 2 * lax.rem(index, 2)
    return 3 - index


def across(index):
    return lax.rem(index + 2, 4)


def send(source, target, send_sem, recv_sem, where):
    return pltpu.make_async_remote_copy(
        src_ref=source,
        dst_ref=target,
        send_sem=send_sem,
        recv_sem=recv_sem,
        device_id=where,
        device_id_type=pl.DeviceIdType.MESH,
    )


def greet(others):
    barrier = pltpu.get_barrier_semaphore()
    for where in others:
        pl.semaphore_signal(barrier, inc=1, device_id=where, device_id_type=pl.DeviceIdType.MESH)
    pl.semaphore_wait(barrier, len(others))


def gather_kernel(shard, whole, own_sem, send_sems, recv_sems):
    me = lax.axis_index("tensor")
    sibling, far = {"tensor": partner(me, FLIP)}, {"tensor": across(me)}
    rows = shard.shape[0] // CHUNKS
    greet([sibling, far])
    copies = []
    for chunk in range(CHUNKS):
        part = pl.ds(chunk * rows, rows)
        copies.append(
            send(shard.at[part], whole.at[me, part], send_sems.at[0, chunk], recv_sems.at[0, chunk], far)
        )
    for copy in copies:
        copy.start()
    near = send(shard, whole.at[me], send_sems.at[1, 0], recv_sems.at[1, 0], sibling)
    near.start()
    own = pltpu.make_async_copy(shard, whole.at[me], own_sem)
    own.start()
    passed = []
    there = across(me)
    for chunk in range(CHUNKS):
        part = pl.ds(chunk * rows, rows)
        copies[chunk].wait_recv()
        onward = send(
            whole.at[there, part],
            whole.at[there, part],
            send_sems.at[2, chunk],
            recv_sems.at[2, chunk],
            sibling,
        )
        onward.start()
        passed.append(onward)
    own.wait()
    near.wait()
    for copy in copies:
        copy.wait_send()
    for copy in passed:
        copy.wait()


def group_gather(shard):
    rows, width = shard.shape
    return pl.pallas_call(
        gather_kernel,
        out_shape=jax.ShapeDtypeStruct((GROUP, rows, width), shard.dtype),
        in_specs=[VMEM_SPACE],
        out_specs=VMEM_SPACE,
        scratch_shapes=[
            pltpu.SemaphoreType.DMA,
            pltpu.SemaphoreType.DMA((3, CHUNKS)),
            pltpu.SemaphoreType.DMA((3, CHUNKS)),
        ],
        compiler_params=pltpu.CompilerParams(
            collective_id=0, has_side_effects=True, vmem_limit_bytes=32 << 20
        ),
    )(shard).reshape(GROUP * rows, width)


def scatter_kernel(partial, total, near, summed, arrived, send_sems, recv_sems):
    me = lax.axis_index("tensor")
    sibling, far = {"tensor": partner(me, FLIP)}, {"tensor": across(me)}
    rows = total.shape[0] // CHUNKS
    greet([sibling, far])
    copies = [[], [], []]
    for slot, block in ((0, partner(me, MIRROR)), (1, partner(me, FLIP))):
        for chunk in range(CHUNKS):
            part = pl.ds(chunk * rows, rows)
            copies[slot].append(
                send(
                    partial.at[block, part],
                    near.at[slot, part],
                    send_sems.at[slot, chunk],
                    recv_sems.at[slot, chunk],
                    sibling,
                )
            )
            copies[slot][chunk].start()
    there = across(me)
    for chunk in range(CHUNKS):
        part = pl.ds(chunk * rows, rows)
        copies[0][chunk].wait_recv()
        summed[part] = (
            partial[there, part].astype(jnp.float32) + near[0, part].astype(jnp.float32)
        ).astype(jnp.bfloat16)
        onward = send(
            summed.at[part], arrived.at[part], send_sems.at[2, chunk], recv_sems.at[2, chunk], far
        )
        onward.start()
        copies[2].append(onward)
    for chunk in range(CHUNKS):
        part = pl.ds(chunk * rows, rows)
        copies[1][chunk].wait_recv()
        copies[2][chunk].wait_recv()
        total[part] = (
            partial[me, part].astype(jnp.float32)
            + near[1, part].astype(jnp.float32)
            + arrived[part].astype(jnp.float32)
        )
    for group in copies:
        for copy in group:
            copy.wait_send()


def group_scatter(partial):
    rows, width = partial.shape[0] // GROUP, partial.shape[1]
    return pl.pallas_call(
        scatter_kernel,
        out_shape=jax.ShapeDtypeStruct((rows, width), jnp.float32),
        in_specs=[VMEM_SPACE],
        out_specs=VMEM_SPACE,
        scratch_shapes=[
            pltpu.VMEM((2, rows, width), jnp.bfloat16),
            pltpu.VMEM((rows, width), jnp.bfloat16),
            pltpu.VMEM((rows, width), jnp.bfloat16),
            pltpu.SemaphoreType.DMA((3, CHUNKS)),
            pltpu.SemaphoreType.DMA((3, CHUNKS)),
        ],
        compiler_params=pltpu.CompilerParams(
            collective_id=1, has_side_effects=True, vmem_limit_bytes=32 << 20
        ),
    )(partial.reshape(GROUP, rows, width))


class Stream:
    def __init__(self, order, grad, out, scratch, sems, place, where):
        self.first, self.orders = order[0], order[1:]
        self.grad, self.local, self.out = grad, grad, out
        self.early, self.mid, self.late, self.held, self.low, self.pair, self.last = scratch
        self.send_sems, self.recv_sems = sems
        self.place, self.where = place, where
        self.pending = []

    def axis(self, stage):
        return self.first if stage == 0 else ("z" if self.first == "x" else "x")

    def block(self, stage, index, local=True):
        if stage == 1:
            return self.held.at[index]
        grad = self.local if local else self.grad
        return grad.at[index] if self.first == "x" else grad.at[:, index]

    def launch(self, source, target, slot, where):
        copy = send(source, target, self.send_sems.at[slot], self.recv_sems.at[slot], where)
        copy.start()
        self.pending.append(copy)
        return copy

    def halve(self, stage):
        axis, here = self.axis(stage), self.place[self.axis(stage)]
        other = partner(here, self.orders[stage])
        box = self.early if stage == 0 else self.late
        self.copies = [
            self.launch(
                self.block(stage, index, False), box.at[slot], 4 * stage + slot, self.where(axis, other)
            )
            for slot, index in ((1, across(here)), (0, other))
        ]

    def quarter(self, stage):
        axis, here = self.axis(stage), self.place[self.axis(stage)]
        other = partner(here, FLIP + MIRROR - self.orders[stage])
        box, mid = (self.early, self.mid) if stage == 0 else (self.late, self.low)
        self.copies[0].wait_recv()
        mine = self.block(stage, other)

        def add(row, _):
            mid[0, row] = (
                mine[row].astype(jnp.float32) + box[1, row].astype(jnp.float32)
            ).astype(jnp.bfloat16)
            return _

        lax.fori_loop(0, mid.shape[1], add, 0)
        self.copies.append(
            self.launch(mid.at[0], mid.at[1], 4 * stage + 2, self.where(axis, other))
        )

    def settle(self, stage):
        here = self.place[self.axis(stage)]
        self.copies[1].wait_recv()
        self.copies[2].wait_recv()
        box, mid = (self.early, self.mid) if stage == 0 else (self.late, self.low)
        mine = self.block(stage, here)
        if stage == 0:

            def add(row, _):
                self.held[row] = (
                    mine[row].astype(jnp.float32)
                    + box[0, row].astype(jnp.float32)
                    + mid[1, row].astype(jnp.float32)
                ).astype(jnp.bfloat16)
                return _

            lax.fori_loop(0, mid.shape[1], add, 0)
            return
        keep = self.place["y"]
        give = 1 - keep
        self.pair[0] = (
            mine[give].astype(jnp.float32)
            + box[0, give].astype(jnp.float32)
            + mid[1, give].astype(jnp.float32)
        ).astype(jnp.bfloat16)
        self.copies.append(
            self.launch(self.pair.at[0], self.pair.at[1], 3, self.where("y", give))
        )
        self.last[...] = (
            mine[keep].astype(jnp.float32)
            + box[0, keep].astype(jnp.float32)
            + mid[1, keep].astype(jnp.float32)
        )

    def finish(self):
        self.copies[3].wait_recv()
        self.out[...] = self.last[...] + self.pair[1].astype(jnp.float32)
        for copy in self.pending:
            copy.wait_send()


STREAM_SEMS = 7
STREAM_SCRATCH = 7


def stream_scratch(columns):
    low = jnp.bfloat16
    return [
        pltpu.VMEM((2, 4, 2, 32, columns), low),
        pltpu.VMEM((2, 4, 2, 32, columns), low),
        pltpu.VMEM((2, 2, 32, columns), low),
        pltpu.VMEM((4, 2, 32, columns), low),
        pltpu.VMEM((2, 2, 32, columns), low),
        pltpu.VMEM((2, 32, columns), low),
        pltpu.VMEM((32, columns), jnp.float32),
    ]


def rank_places():
    rank = lax.axis_index("dp")
    return {"x": lax.div(rank, 8), "z": lax.rem(lax.div(rank, 2), 4), "y": lax.rem(rank, 2)}


def rank_where(place):
    def where(axis, index):
        at = dict(place)
        at[axis] = index
        return {"dp": at["x"] * 8 + at["z"] * 2 + at["y"]}

    return where


class Gather:
    def __init__(self, whole, send_sems, recv_sems, me):
        self.whole, self.send_sems, self.recv_sems, self.me = whole, send_sems, recv_sems, me
        self.sibling, self.far = {"tensor": partner(me, FLIP)}, {"tensor": across(me)}
        self.rows = whole.shape[1] // CHUNKS

    def copy(self, lane, chunk, block, where):
        part = pl.ds(chunk * self.rows, self.rows)
        spot = self.whole.at[block, part]
        return send(spot, spot, self.send_sems.at[lane, chunk], self.recv_sems.at[lane, chunk], where)

    def start_chunk(self, chunk):
        self.copy(0, chunk, self.me, self.far).start()
        self.copy(1, chunk, self.me, self.sibling).start()

    def start(self):
        for chunk in range(CHUNKS):
            self.copy(0, chunk, self.me, self.far).start()
        for chunk in range(CHUNKS):
            self.copy(1, chunk, self.me, self.sibling).start()

    def wait_sibling(self):
        for chunk in range(CHUNKS):
            self.copy(1, chunk, self.me, self.sibling).wait_recv()

    def wait_far(self):
        for chunk in range(CHUNKS):
            self.copy(0, chunk, self.me, self.far).wait_recv()
            self.copy(2, chunk, across(self.me), self.sibling).start()

    def wait_last(self):
        for chunk in range(CHUNKS):
            self.copy(2, chunk, across(self.me), self.sibling).wait_recv()

    def drain(self):
        for chunk in range(CHUNKS):
            self.copy(0, chunk, self.me, self.far).wait_send()
            self.copy(1, chunk, self.me, self.sibling).wait_send()
            self.copy(2, chunk, across(self.me), self.sibling).wait_send()


class Scatter:
    def __init__(self, partial, near, summed, arrived, send_sems, recv_sems, me):
        self.partial, self.near, self.summed, self.arrived = partial, near, summed, arrived
        self.send_sems, self.recv_sems, self.me = send_sems, recv_sems, me
        self.sibling, self.far = {"tensor": partner(me, FLIP)}, {"tensor": across(me)}
        self.rows = near.shape[1] // CHUNKS

    def part(self, chunk):
        return pl.ds(chunk * self.rows, self.rows)

    def near_copy(self, slot, chunk):
        block = partner(self.me, MIRROR if slot == 0 else FLIP)
        return send(
            self.partial.at[block, self.part(chunk)],
            self.near.at[slot, self.part(chunk)],
            self.send_sems.at[slot, chunk],
            self.recv_sems.at[slot, chunk],
            self.sibling,
        )

    def far_copy(self, chunk):
        return send(
            self.summed.at[self.part(chunk)],
            self.arrived.at[self.part(chunk)],
            self.send_sems.at[2, chunk],
            self.recv_sems.at[2, chunk],
            self.far,
        )

    def start(self, slot):
        for chunk in range(CHUNKS):
            self.near_copy(slot, chunk).start()

    def cross(self, mine):
        for chunk in range(CHUNKS):
            part = self.part(chunk)
            self.near_copy(0, chunk).wait_recv()
            self.summed[part] = (
                mine[part].astype(jnp.float32) + self.near[0, part].astype(jnp.float32)
            ).astype(jnp.bfloat16)
            self.far_copy(chunk).start()

    def total(self, chunk, mine):
        part = self.part(chunk)
        self.near_copy(1, chunk).wait_recv()
        self.far_copy(chunk).wait_recv()
        return (
            mine[part].astype(jnp.float32)
            + self.near[1, part].astype(jnp.float32)
            + self.arrived[part].astype(jnp.float32)
        )

    def drain(self):
        for chunk in range(CHUNKS):
            self.near_copy(0, chunk).wait_send()
            self.near_copy(1, chunk).wait_send()
            self.far_copy(chunk).wait_send()


def scatter_scratch(rows, width):
    return [
        pltpu.VMEM((2, rows, width), jnp.bfloat16),
        pltpu.VMEM((rows, width), jnp.bfloat16),
        pltpu.VMEM((rows, width), jnp.bfloat16),
        pltpu.SemaphoreType.DMA((3, CHUNKS)),
        pltpu.SemaphoreType.DMA((3, CHUNKS)),
    ]


def gather_scratch(rows, width):
    return [
        pltpu.VMEM((GROUP, rows, width), jnp.bfloat16),
        pltpu.SemaphoreType.DMA((3, CHUNKS)),
        pltpu.SemaphoreType.DMA((3, CHUNKS)),
    ]


def dot(left, right):
    return jnp.dot(left, right, preferred_element_type=jnp.float32)


def dot_cols(left, right):
    return lax.dot_general(left, right, contract_cols, preferred_element_type=jnp.float32)


def turn(values, cosine, sine):
    return values * cosine + pltpu.roll(values, HEAD_SIZE // 2, 1) * sine


def head_norm_back(incoming, values, gain):
    scale = lax.rsqrt(jnp.mean(values * values, axis=-1, keepdims=True) + epsilon)
    scaled = incoming * gain
    grad = scale * scaled - values * (
        scale * scale * scale * jnp.mean(scaled * values, axis=-1, keepdims=True)
    )
    return grad, jnp.sum(incoming * values * scale, axis=0, keepdims=True)


SCORE_SCALE = HEAD_SIZE**-0.5
LOG2_E = 1.4426950408889634
ROWS = 256


def back_kernel(names, layout, *refs):
    ref = dict(zip(names, refs))
    me = lax.axis_index("tensor")
    sibling, far, far_sibling = partner(me, FLIP), across(me), partner(me, MIRROR)
    place = rank_places()
    where = rank_where(place)
    doubling = [
        where("x", partner(place["x"], FLIP)),
        where("x", partner(place["x"], MIRROR)),
        where("z", partner(place["z"], FLIP)),
        where("z", partner(place["z"], MIRROR)),
        where("y", 1 - place["y"]),
        {"tensor": sibling},
        {"tensor": far},
    ]

    loads = {}
    parts = {
        "down_part_far": ref["down_part"].at[pl.ds(far, 1)],
        "down_part_own": ref["down_part"].at[pl.ds(me, 1)],
    }
    for slot, name in enumerate(layout["loads"]):
        source = parts[name] if name in parts else ref[name]
        copy = pltpu.make_async_copy(source, ref["v_" + name], ref["load_sems"].at[slot])
        copy.start()
        loads[name] = copy
    greet(doubling)

    gather = Gather(ref["gh_all"], ref["gh_send"], ref["gh_recv"], me)
    down = Scatter(
        ref["down_part"], ref["d_near"], ref["d_sum"], ref["d_arr"], ref["d_send"], ref["d_recv"], me
    )
    loads["gh"].wait()
    ref["gh_all"][me] = ref["v_gh"][...].astype(jnp.bfloat16)
    gather.start()

    def streams_of(kind):
        out = []
        for i, (source, start, size, order) in enumerate(layout[kind]):
            columns = pl.ds(start, size)
            scratch = [ref["%s%d_%d" % (kind, i, j)] for j in range(STREAM_SCRATCH)]
            stream = Stream(
                order,
                ref[source].at[:, :, :, :, columns],
                ref["o_" + source].at[:, columns],
                scratch,
                (ref[kind + "_send"].at[i], ref[kind + "_recv"].at[i]),
                place,
                where,
            )
            if kind == "ffn":
                stream.local = ref["v_" + source].at[:, :, :, :, columns]
            out.append(stream)
        return out

    ffn = streams_of("ffn")
    attn = streams_of("attn")
    for stream in ffn:
        stream.halve(0)
    down.start(0)
    down.start(1)

    loads["w_out"].wait()
    loads["att"].wait()

    def attended_grad(block):
        rows = ref["gh_all"][block]
        for g in range(2):
            part = dot_cols(rows, ref["v_w_out"][g * ROWS : (g + 1) * ROWS, :]).astype(jnp.bfloat16)
            for r in range(2):
                low = part[:, r * HEAD_SIZE : (r + 1) * HEAD_SIZE]
                start = (2 * g + r) * HEAD_SIZE
                ref["do"][g, block, r * ROWS : (r + 1) * ROWS, :] = low
                product = low.astype(jnp.float32) * ref["v_att"][
                    block, :, start : start + HEAD_SIZE
                ].astype(jnp.float32)
                ref["delta"][g, block, :, r * ROWS : (r + 1) * ROWS] = jnp.sum(
                    product.T, axis=0, keepdims=True
                )

    attended_grad(me)
    gather.wait_sibling()
    attended_grad(sibling)
    gather.wait_far()
    attended_grad(far)
    gather.wait_last()
    attended_grad(far_sibling)

    loads["down_part_far"].wait()
    down.cross(ref["v_down_part_far"].at[0])
    for source in ("gate", "up", "down"):
        loads[source].wait()
    for stream in ffn:
        stream.quarter(0)

    for name in ("q", "k", "v", "lse", "qraw", "kraw", "cos", "sin", "qg", "kg"):
        loads[name].wait()
    ref["qgain"][...] = jnp.zeros_like(ref["qgain"])
    ref["kgain"][...] = jnp.zeros_like(ref["kgain"])
    key_row = lax.broadcasted_iota(jnp.int32, (ROWS, 2 * ROWS), 0)
    query_col = lax.rem(lax.broadcasted_iota(jnp.int32, (ROWS, 2 * ROWS), 1), ROWS)
    allowed = key_row <= query_col

    def attend_group(g):
        def clear(block, carry):
            ref["dk"][block] = jnp.zeros((ROWS, HEAD_SIZE), jnp.float32)
            ref["dv"][block] = jnp.zeros((ROWS, HEAD_SIZE), jnp.float32)
            ref["kt"][block] = ref["v_k"][g, block].T
            return carry

        lax.fori_loop(0, 4, clear, 0)

        def unit(qb, carry):
            ref["qt"][...] = ref["v_q"][g, qb].T
            ref["dot"][...] = ref["do"][g, qb].T
            ref["dqt"][...] = jnp.zeros_like(ref["dqt"])

            def tile(kb, masked):
                scores = dot(ref["v_k"][g, kb], ref["qt"][...])
                probs = jnp.exp2(scores * (SCORE_SCALE * LOG2_E) - ref["v_lse"][g, qb])
                if masked:
                    probs = jnp.where(allowed, probs, 0.0)
                ref["dv"][kb] += dot(probs.astype(jnp.bfloat16), ref["do"][g, qb])
                grad_probs = dot(ref["v_v"][g, kb], ref["dot"][...])
                grad_scores = (probs * (grad_probs - ref["delta"][g, qb])).astype(jnp.bfloat16)
                ref["dk"][kb] += dot(grad_scores, ref["v_q"][g, qb])
                ref["dqt"][...] += dot(ref["kt"][kb], grad_scores)

            def body(kb, inner):
                tile(kb, False)
                return inner

            lax.fori_loop(0, qb, body, 0)
            tile(qb, True)
            grads = ref["dqt"][...].T * SCORE_SCALE
            for r in range(2):
                start = (2 * g + r) * HEAD_SIZE
                back = turn(
                    grads[r * ROWS : (r + 1) * ROWS], ref["v_cos"][qb], ref["v_sin"][qb]
                )
                grad, gain = head_norm_back(
                    back, ref["v_qraw"][qb, :, start : start + HEAD_SIZE], ref["v_qg"][...]
                )
                ref["dqkv"][qb, :, start : start + HEAD_SIZE] = grad.astype(jnp.bfloat16)
                ref["qgain"][...] += gain
            return carry

        lax.fori_loop(0, 4, unit, 0)

        def keys(kb, carry):
            start = g * HEAD_SIZE
            back = turn(ref["dk"][kb] * SCORE_SCALE, ref["v_cos"][kb], ref["v_sin"][kb])
            grad, gain = head_norm_back(
                back, ref["v_kraw"][kb, :, start : start + HEAD_SIZE], ref["v_kg"][...]
            )
            ref["dqkv"][kb, :, 512 + start : 512 + start + HEAD_SIZE] = grad.astype(jnp.bfloat16)
            ref["dqkv"][kb, :, 768 + start : 768 + start + HEAD_SIZE] = ref["dv"][kb].astype(
                jnp.bfloat16
            )
            ref["kgain"][...] += gain
            return carry

        lax.fori_loop(0, 4, keys, 0)

    attend_group(0)
    for stream in ffn:
        stream.settle(0)
        stream.halve(1)
    attend_group(1)
    for stream in ffn:
        stream.quarter(1)

    for name in ("wq", "wk", "wv"):
        loads[name].wait()
    inward = Scatter(
        ref["x_part"], ref["x_near"], ref["x_sum"], ref["x_arr"], ref["x_send"], ref["x_recv"], me
    )

    def inward_part(block, target):
        def column(j, carry):
            at = pl.ds(pl.multiple_of(j * ROWS, ROWS), ROWS)
            value = (
                dot_cols(ref["dqkv"][block, :, 0:512], ref["v_wq"][at, :])
                + dot_cols(ref["dqkv"][block, :, 512:768], ref["v_wk"][at, :])
                + dot_cols(ref["dqkv"][block, :, 768:1024], ref["v_wv"][at, :])
            )
            target[:, at] = value.astype(target.dtype)
            return carry

        lax.fori_loop(0, 4, column, 0)

    inward_part(far_sibling, ref["x_part"].at[far_sibling])
    inward.start(0)
    inward_part(far, ref["x_part"].at[far])
    inward.cross(ref["x_part"].at[far])
    inward_part(sibling, ref["x_part"].at[sibling])
    inward.start(1)
    inward_part(me, ref["x_own"])

    loads["norm_all"].wait()

    def weight_grad(rows, cols, target):
        def block(j, carry):
            at = pl.ds(pl.multiple_of(j * ROWS, ROWS), ROWS)
            total = jnp.zeros((ROWS, cols.shape[2]), jnp.float32)
            for b in range(4):
                total += dot(rows[b, :, at].T, cols[b])
            target[j] = total.astype(jnp.bfloat16).reshape(4, 2, 32, cols.shape[2])
            return carry

        lax.fori_loop(0, 4, block, 0)

    weight_grad(ref["gh_all"], ref["v_att"], ref["gw_out"])
    for stream, entry in zip(attn, layout["attn"]):
        if entry[0] == "gw_out":
            stream.halve(0)
    weight_grad(ref["v_norm_all"], ref["dqkv"], ref["gw_qkv"])
    for stream, entry in zip(attn, layout["attn"]):
        if entry[0] == "gw_qkv":
            stream.halve(0)
    for stream in ffn:
        stream.settle(1)

    loads["hidden"].wait()
    loads["down_part_own"].wait()
    for chunk in range(CHUNKS):
        part = down.part(chunk)
        total = down.total(chunk, ref["v_down_part_own"].at[0])
        ref["result"][part] = (ref["v_hidden"][part] + total).astype(jnp.bfloat16)

    for name in ("tokens", "norm_in", "gain_mid"):
        loads[name].wait()
    ref["gains"][...] = jnp.zeros_like(ref["gains"])
    ref["gains"][1:2] = ref["v_gain_mid"][...]
    ref["gains"][2:3, 0:128] = ref["qgain"][...]
    ref["gains"][2:3, 128:256] = ref["kgain"][...]
    for chunk in range(CHUNKS):
        part = inward.part(chunk)
        incoming = inward.total(chunk, ref["x_own"])
        values = ref["v_tokens"][part].astype(jnp.float32)
        grad, gain = head_norm_back(incoming, values, ref["v_norm_in"][...])
        ref["grad_tokens"][part] = (ref["v_gh"][part] + grad).astype(jnp.bfloat16)
        ref["gains"][0:1] += gain

    gain_box = ref["gain_box"]
    gain_box[0] = ref["gains"][...]

    def gain_copy(step):
        return send(
            gain_box.at[2 * step],
            gain_box.at[2 * step + 1],
            ref["gain_send"].at[step],
            ref["gain_recv"].at[step],
            doubling[step],
        )

    def gain_end(step):
        gain_copy(step).wait_recv()
        value = gain_box[2 * step] + gain_box[2 * step + 1]
        if step == 6:
            ref["gain_out"][...] = value
        else:
            gain_box[2 * step + 2] = value
            gain_copy(step + 1).start()

    gain_copy(0).start()
    for stream in attn:
        stream.quarter(0)
    gain_end(0)
    for stream in ffn:
        stream.finish()
    gain_end(1)
    for stream in attn:
        stream.settle(0)
        stream.halve(1)
    gain_end(2)
    for stream in attn:
        stream.quarter(1)
    gain_end(3)
    for stream in attn:
        stream.settle(1)
    gain_end(4)
    gain_end(5)
    for stream in attn:
        stream.finish()
    gain_end(6)
    for step in range(7):
        gain_copy(step).wait_send()
    gather.drain()
    down.drain()
    inward.drain()


def back_part(inputs):
    low, wide = jnp.bfloat16, jnp.float32
    loaded = [
        "gh", "w_out", "att", "down_part_far", "gate", "up", "down", "q", "k", "v", "lse", "qraw",
        "kraw", "cos", "sin", "qg", "kg", "wq", "wk", "wv", "norm_all", "down_part_own", "hidden",
        "tokens", "norm_in", "gain_mid",
    ]
    names = list(inputs)
    operands = [inputs[name] for name in names]
    outs = {
        "result": ((ROWS, 1024), low),
        "grad_tokens": ((ROWS, 1024), low),
        "o_gate": ((32, 768), wide),
        "o_up": ((32, 768), wide),
        "o_down": ((32, 768), wide),
        "o_gw_qkv": ((32, 1024), wide),
        "o_gw_out": ((32, 512), wide),
        "gain_out": ((8, 1024), wide),
    }
    xa, xb = ("x", FLIP, FLIP), ("x", MIRROR, MIRROR)
    za, zb = ("z", FLIP, MIRROR), ("z", MIRROR, FLIP)
    layout = {
        "loads": loaded,
        "ffn": [
            ("gate", 0, 384, xa), ("gate", 384, 384, xb), ("up", 0, 384, za), ("up", 384, 384, zb),
            ("down", 0, 256, xa), ("down", 256, 128, xb), ("down", 384, 256, za),
            ("down", 640, 128, zb),
        ],
        "attn": [
            ("gw_out", 0, 256, xa), ("gw_out", 256, 256, xb), ("gw_qkv", 0, 384, za),
            ("gw_qkv", 384, 384, zb), ("gw_qkv", 768, 128, xa), ("gw_qkv", 896, 128, xb),
        ],
    }
    scratch = {
        "v_" + name: pltpu.VMEM((1, ROWS, 1024), low)
        if name.startswith("down_part")
        else pltpu.VMEM(inputs[name].shape, inputs[name].dtype)
        for name in loaded
    }
    scratch["load_sems"] = pltpu.SemaphoreType.DMA((len(loaded),))
    scratch["gh_all"], scratch["gh_send"], scratch["gh_recv"] = gather_scratch(ROWS, 1024)
    for tag in ("d", "x"):
        for part, kind in zip(("near", "sum", "arr", "send", "recv"), scatter_scratch(ROWS, 1024)):
            scratch[tag + "_" + part] = kind
    scratch.update({
        "do": pltpu.VMEM((2, 4, 2 * ROWS, HEAD_SIZE), low),
        "delta": pltpu.VMEM((2, 4, 1, 2 * ROWS), wide),
        "qt": pltpu.VMEM((HEAD_SIZE, 2 * ROWS), low),
        "dot": pltpu.VMEM((HEAD_SIZE, 2 * ROWS), low),
        "dqt": pltpu.VMEM((HEAD_SIZE, 2 * ROWS), wide),
        "kt": pltpu.VMEM((4, HEAD_SIZE, ROWS), low),
        "dk": pltpu.VMEM((4, ROWS, HEAD_SIZE), wide),
        "dv": pltpu.VMEM((4, ROWS, HEAD_SIZE), wide),
        "dqkv": pltpu.VMEM((4, ROWS, 1024), low),
        "qgain": pltpu.VMEM((1, HEAD_SIZE), wide),
        "kgain": pltpu.VMEM((1, HEAD_SIZE), wide),
        "x_part": pltpu.VMEM((4, ROWS, 1024), low),
        "x_own": pltpu.VMEM((ROWS, 1024), wide),
        "gw_out": pltpu.VMEM((4, 4, 2, 32, 512), low),
        "gw_qkv": pltpu.VMEM((4, 4, 2, 32, 1024), low),
        "gains": pltpu.VMEM((8, 1024), wide),
        "gain_box": pltpu.VMEM((14, 8, 1024), wide),
        "gain_send": pltpu.SemaphoreType.DMA((7,)),
        "gain_recv": pltpu.SemaphoreType.DMA((7,)),
    })
    for kind in ("ffn", "attn"):
        for way in ("_send", "_recv"):
            scratch[kind + way] = pltpu.SemaphoreType.DMA((len(layout[kind]), STREAM_SEMS))
        for i, entry in enumerate(layout[kind]):
            for j, buffer in enumerate(stream_scratch(entry[2])):
                scratch["%s%d_%d" % (kind, i, j)] = buffer
    results = pl.pallas_call(
        functools.partial(back_kernel, names + list(outs) + list(scratch), layout),
        out_shape=[jax.ShapeDtypeStruct(*spec) for spec in outs.values()],
        in_specs=[pl.BlockSpec(memory_space=pl.ANY)] * len(names),
        out_specs=[VMEM_SPACE] * len(outs),
        scratch_shapes=list(scratch.values()),
        compiler_params=pltpu.CompilerParams(
            collective_id=3, has_side_effects=True, vmem_limit_bytes=60 << 20
        ),
    )(*operands)
    return dict(zip(outs, results))


def rms_scale(values):
    return lax.rsqrt(jnp.mean(values * values, axis=-1, keepdims=True) + epsilon)


def rotary_tables():
    position = np.arange(SEQUENCE_TOKENS, dtype=np.float64)
    inverse = 1000000.0 ** (-np.arange(HEAD_SIZE // 2, dtype=np.float64) * 2.0 / HEAD_SIZE)
    angles = position[:, None] * inverse[None, :]
    return tuple(
        jnp.asarray(table.astype(np.float32)[:, None, :]) for table in (np.cos(angles), np.sin(angles))
    )


def rotate(values, cosine_table, sine_table):
    half_size = values.shape[-1] // 2
    first_half = values[..., :half_size]
    second = values[..., half_size:]
    return jnp.concatenate(
        [
            first_half * cosine_table - second * sine_table,
            second * cosine_table + first_half * sine_table,
        ],
        axis=-1,
    )


def norm_back(incoming, values, row_scale, gain_vector):
    scaled = incoming * gain_vector
    input_grad = row_scale * scaled - values * row_scale**3 * jnp.mean(
        scaled * values, axis=-1, keepdims=True
    )
    return (input_grad, incoming * values * row_scale)


def causal_mask(row_start, block_size, key_end):
    query_pos = row_start + jnp.arange(block_size, dtype=jnp.int32)
    key_pos = jnp.arange(key_end, dtype=jnp.int32)
    return key_pos[None, :] <= query_pos[:, None]


def attend_forward(queries, split_key_heads, split_value_heads):
    block_size = min(512, SEQUENCE_TOKENS)
    score_scale = HEAD_SIZE ** (-0.5)
    outputs = []
    log_parts = []
    for block_index in range(SEQUENCE_TOKENS // block_size):
        row_start = block_index * block_size
        key_end = row_start + block_size
        query_part = queries[row_start:key_end]
        scores = (
            jnp.einsum(
                "qgrd,kgd->grqk",
                query_part,
                split_key_heads[:key_end],
                preferred_element_type=jnp.float32,
            )
            * score_scale
        )
        scores = jnp.where(causal_mask(row_start, block_size, key_end), scores, -jnp.inf)
        peak_score = jnp.max(scores, axis=-1, keepdims=True)
        exponent = jnp.exp(scores - peak_score)
        denominator = jnp.sum(exponent, axis=-1, keepdims=True)
        probabilities = (exponent / denominator).astype(jnp.bfloat16)
        outputs.append(
            jnp.einsum(
                "grqk,kgd->qgrd",
                probabilities,
                split_value_heads[:key_end],
                preferred_element_type=jnp.float32,
            )
        )
        log_parts.append(peak_score + jnp.log(denominator))
    return (jnp.concatenate(outputs, axis=0), jnp.concatenate(log_parts, axis=2))


def per_device(
    tokens,
    norm_in,
    w_query,
    key_matrix,
    value_matrix,
    query_gain,
    key_gain,
    w_out,
    norm_mid,
    w_gate,
    w_up,
    w_down,
    cotangent,
):
    local_rows = tokens.shape[0]
    head_local = w_query.shape[1] // HEAD_SIZE
    kv_local = key_matrix.shape[1] // HEAD_SIZE
    repeat = head_local // kv_local
    total_rows = local_rows * lax.axis_size("tensor")
    seq_count = total_rows // SEQUENCE_TOKENS
    cosine_table, sine_table = rotary_tables()
    norm_in_f = norm_in.astype(jnp.float32)
    norm_mid_f = norm_mid.astype(jnp.float32)
    query_gain_f = query_gain.astype(jnp.float32)
    key_gain_f = key_gain.astype(jnp.float32)
    inputs = tokens.astype(jnp.float32)
    scale_in = rms_scale(inputs)
    normalized_rows = (inputs * scale_in * norm_in_f).astype(jnp.bfloat16)
    gathered = group_gather(normalized_rows)
    query_raw = jnp.dot(gathered, w_query, preferred_element_type=jnp.float32).reshape(
        total_rows, head_local, HEAD_SIZE
    )
    key_raw = jnp.dot(gathered, key_matrix, preferred_element_type=jnp.float32).reshape(
        total_rows, kv_local, HEAD_SIZE
    )
    value_low = jnp.dot(gathered, value_matrix, preferred_element_type=jnp.float32).astype(
        jnp.bfloat16
    )
    query_scale = rms_scale(query_raw)
    key_scale = rms_scale(key_raw)
    query_low = rotate(
        (query_raw * query_scale * query_gain_f).reshape(
            seq_count, SEQUENCE_TOKENS, head_local, HEAD_SIZE
        ),
        cosine_table,
        sine_table,
    ).astype(jnp.bfloat16)
    key_low = rotate(
        (key_raw * key_scale * key_gain_f).reshape(seq_count, SEQUENCE_TOKENS, kv_local, HEAD_SIZE),
        cosine_table,
        sine_table,
    ).astype(jnp.bfloat16)
    query_heads = query_low.reshape(seq_count, SEQUENCE_TOKENS, kv_local, repeat, HEAD_SIZE)
    split_value_heads = value_low.reshape(seq_count, SEQUENCE_TOKENS, kv_local, HEAD_SIZE)
    attended, log_totals = lax.map(
        lambda packed: attend_forward(packed[0], packed[1], packed[2]),
        (query_heads, key_low, split_value_heads),
    )
    attended = attended.reshape(total_rows, head_local * HEAD_SIZE).astype(jnp.bfloat16)
    hidden_state = inputs + group_scatter(
        jnp.dot(attended, w_out, preferred_element_type=jnp.float32).astype(jnp.bfloat16)
    )
    scale_mid = rms_scale(hidden_state)
    normed_mid = (hidden_state * scale_mid * norm_mid_f).astype(jnp.bfloat16)
    gathered_mid = group_gather(normed_mid)
    gate_proj = jnp.dot(gathered_mid, w_gate, preferred_element_type=jnp.float32)
    up_proj = jnp.dot(gathered_mid, w_up, preferred_element_type=jnp.float32)
    activated = (jax.nn.silu(gate_proj) * up_proj).astype(jnp.bfloat16)
    down_part = jnp.dot(activated, w_down, preferred_element_type=jnp.float32).astype(jnp.bfloat16)
    grad_full = group_gather(cotangent)
    grad_down = lax.dot_general(
        grad_full, activated, contract_rows, preferred_element_type=jnp.float32
    )
    grad_act = lax.dot_general(grad_full, w_down, contract_cols, preferred_element_type=jnp.float32)
    sigmoid_gate = jax.nn.sigmoid(gate_proj)
    grad_up_low = (grad_act * gate_proj * sigmoid_gate).astype(jnp.bfloat16)
    grad_gate_low = (
        grad_act * up_proj * sigmoid_gate * (1.0 + gate_proj * (1.0 - sigmoid_gate))
    ).astype(jnp.bfloat16)
    grad_w_gate = lax.dot_general(
        gathered_mid, grad_gate_low, contract_rows, preferred_element_type=jnp.float32
    )
    grad_w_up = lax.dot_general(
        gathered_mid, grad_up_low, contract_rows, preferred_element_type=jnp.float32
    )
    grad_normed_mid = group_scatter(
        (
            lax.dot_general(grad_gate_low, w_gate, contract_cols, preferred_element_type=jnp.float32)
            + lax.dot_general(grad_up_low, w_up, contract_cols, preferred_element_type=jnp.float32)
        ).astype(jnp.bfloat16)
    )
    back_mid, gain_mid_terms = norm_back(grad_normed_mid, hidden_state, scale_mid, norm_mid_f)
    grad_hidden = cotangent.astype(jnp.float32) + back_mid
    cosine, sine = cosine_table[:, 0], sine_table[:, 0]
    cut = (2, 4, 2 * ROWS, HEAD_SIZE)
    outs = back_part(
        {
            "gh": grad_hidden,
            "w_out": w_out,
            "att": attended.reshape(4, ROWS, 512),
            "down_part": down_part.reshape(4, ROWS, 1024),
            "gate": grad_w_gate.astype(jnp.bfloat16).reshape(4, 4, 2, 32, 768),
            "up": grad_w_up.astype(jnp.bfloat16).reshape(4, 4, 2, 32, 768),
            "down": grad_down.astype(jnp.bfloat16).reshape(4, 4, 2, 32, 768),
            "q": query_low.reshape(4, ROWS, 2, 2, HEAD_SIZE).transpose(2, 0, 3, 1, 4).reshape(cut),
            "k": key_low.reshape(4, ROWS, 2, HEAD_SIZE).transpose(2, 0, 1, 3),
            "v": value_low.reshape(4, ROWS, 2, HEAD_SIZE).transpose(2, 0, 1, 3),
            "lse": (log_totals * LOG2_E)
            .reshape(2, 2, 4, ROWS)
            .transpose(0, 2, 1, 3)
            .reshape(2, 4, 1, 2 * ROWS),
            "qraw": query_raw.reshape(4, ROWS, 512),
            "kraw": key_raw.reshape(4, ROWS, 256),
            "cos": jnp.concatenate([cosine, cosine], axis=1).reshape(4, ROWS, HEAD_SIZE),
            "sin": jnp.concatenate([sine, -sine], axis=1).reshape(4, ROWS, HEAD_SIZE),
            "qg": query_gain_f.reshape(1, HEAD_SIZE),
            "kg": key_gain_f.reshape(1, HEAD_SIZE),
            "wq": w_query,
            "wk": key_matrix,
            "wv": value_matrix,
            "norm_all": gathered.reshape(4, ROWS, 1024),
            "hidden": hidden_state,
            "tokens": tokens,
            "norm_in": norm_in_f.reshape(1, 1024),
            "gain_mid": jnp.sum(gain_mid_terms, axis=0, keepdims=True),
        }
    )
    gains = outs["gain_out"]
    query_key_value = outs["o_gw_qkv"]
    return (
        outs["result"],
        outs["grad_tokens"],
        gains[0],
        query_key_value[:, :512],
        query_key_value[:, 512:768],
        query_key_value[:, 768:],
        gains[2, :128],
        gains[2, 128:256],
        outs["o_gw_out"].T,
        gains[1],
        outs["o_gate"],
        outs["o_up"],
        outs["o_down"].T,
    )


def solution(mesh):
    placed = (
        P(("dp", "tensor"), None),
        P(),
        P(None, "tensor"),
        P(None, "tensor"),
        P(None, "tensor"),
        P(),
        P(),
        P("tensor", None),
        P(),
        P(None, "tensor"),
        P(None, "tensor"),
        P("tensor", None),
        P(("dp", "tensor"), None),
    )
    return jax.shard_map(
        per_device,
        mesh=mesh,
        in_specs=placed,
        out_specs=(
            P(("dp", "tensor"), None),
            P(("dp", "tensor"), None),
            P(),
            P("dp", "tensor"),
            P("dp", "tensor"),
            P("dp", "tensor"),
            P(),
            P(),
            P("tensor", "dp"),
            P(),
            P("dp", "tensor"),
            P("dp", "tensor"),
            P("tensor", "dp"),
        ),
        check_vma=False,
    )
```

```python
import functools
from types import SimpleNamespace

import jax
import jax.numpy as jnp
import numpy as np
from jax import lax
from jax.experimental import pallas as pl
from jax.experimental.pallas import tpu as pltpu
from jax.sharding import PartitionSpec as P

HEAD_SIZE = 128
SEQUENCE_TOKENS = 1024
GROUP = 4
CHUNKS = 4
VMEM_SPACE = pl.BlockSpec(memory_space=pltpu.VMEM)
FLIP, MIRROR = 1, 3
epsilon = 1e-06
contract_cols = (((1,), (1,)), ((), ()))


def partner(index, pairing):
    if pairing == FLIP:
        return index + 1 - 2 * lax.rem(index, 2)
    return 3 - index


def across(index):
    return lax.rem(index + 2, 4)


def send(source, target, send_sem, recv_sem, where):
    return pltpu.make_async_remote_copy(
        src_ref=source,
        dst_ref=target,
        send_sem=send_sem,
        recv_sem=recv_sem,
        device_id=where,
        device_id_type=pl.DeviceIdType.MESH,
    )


def greet(others):
    barrier = pltpu.get_barrier_semaphore()
    for where in others:
        pl.semaphore_signal(barrier, inc=1, device_id=where, device_id_type=pl.DeviceIdType.MESH)
    pl.semaphore_wait(barrier, len(others))


class Stream:
    def __init__(self, order, grad, out, scratch, sems, place, where):
        self.first, self.orders = order[0], order[1:]
        self.grad, self.local, self.out = grad, grad, out
        self.early, self.mid, self.late, self.held, self.low, self.pair, self.last = scratch
        self.send_sems, self.recv_sems = sems
        self.place, self.where = place, where
        self.pending = []

    def axis(self, stage):
        return self.first if stage == 0 else ("z" if self.first == "x" else "x")

    def block(self, stage, index, local=True):
        if stage == 1:
            return self.held.at[index]
        grad = self.local if local else self.grad
        return grad.at[index] if self.first == "x" else grad.at[:, index]

    def launch(self, source, target, slot, where):
        copy = send(source, target, self.send_sems.at[slot], self.recv_sems.at[slot], where)
        copy.start()
        self.pending.append(copy)
        return copy

    def halve(self, stage):
        axis, here = self.axis(stage), self.place[self.axis(stage)]
        other = partner(here, self.orders[stage])
        box = self.early if stage == 0 else self.late
        self.copies = [
            self.launch(
                self.block(stage, index, False), box.at[slot], 4 * stage + slot, self.where(axis, other)
            )
            for slot, index in ((1, across(here)), (0, other))
        ]

    def quarter(self, stage):
        axis, here = self.axis(stage), self.place[self.axis(stage)]
        other = partner(here, FLIP + MIRROR - self.orders[stage])
        box, mid = (self.early, self.mid) if stage == 0 else (self.late, self.low)
        self.copies[0].wait_recv()
        mine = self.block(stage, other)

        def add(row, _):
            mid[0, row] = (
                mine[row].astype(jnp.float32) + box[1, row].astype(jnp.float32)
            ).astype(jnp.bfloat16)
            return _

        lax.fori_loop(0, mid.shape[1], add, 0)
        self.copies.append(
            self.launch(mid.at[0], mid.at[1], 4 * stage + 2, self.where(axis, other))
        )

    def settle(self, stage):
        here = self.place[self.axis(stage)]
        self.copies[1].wait_recv()
        self.copies[2].wait_recv()
        box, mid = (self.early, self.mid) if stage == 0 else (self.late, self.low)
        mine = self.block(stage, here)
        if stage == 0:

            def add(row, _):
                self.held[row] = (
                    mine[row].astype(jnp.float32)
                    + box[0, row].astype(jnp.float32)
                    + mid[1, row].astype(jnp.float32)
                ).astype(jnp.bfloat16)
                return _

            lax.fori_loop(0, mid.shape[1], add, 0)
            return
        keep = self.place["y"]
        give = 1 - keep
        self.pair[0] = (
            mine[give].astype(jnp.float32)
            + box[0, give].astype(jnp.float32)
            + mid[1, give].astype(jnp.float32)
        ).astype(jnp.bfloat16)
        self.copies.append(
            self.launch(self.pair.at[0], self.pair.at[1], 3, self.where("y", give))
        )
        self.last[...] = (
            mine[keep].astype(jnp.float32)
            + box[0, keep].astype(jnp.float32)
            + mid[1, keep].astype(jnp.float32)
        )

    def finish(self):
        self.copies[3].wait_recv()
        self.out[...] = self.last[...] + self.pair[1].astype(jnp.float32)
        for copy in self.pending:
            copy.wait_send()


STREAM_SEMS = 7
STREAM_SCRATCH = 7


def stream_scratch(columns):
    low = jnp.bfloat16
    return [
        pltpu.VMEM((2, 4, 2, 32, columns), low),
        pltpu.VMEM((2, 4, 2, 32, columns), low),
        pltpu.VMEM((2, 2, 32, columns), low),
        pltpu.VMEM((4, 2, 32, columns), low),
        pltpu.VMEM((2, 2, 32, columns), low),
        pltpu.VMEM((2, 32, columns), low),
        pltpu.VMEM((32, columns), jnp.float32),
    ]


def rank_places():
    rank = lax.axis_index("dp")
    return {"x": lax.div(rank, 8), "z": lax.rem(lax.div(rank, 2), 4), "y": lax.rem(rank, 2)}


def rank_where(place):
    def where(axis, index):
        at = dict(place)
        at[axis] = index
        return {"dp": at["x"] * 8 + at["z"] * 2 + at["y"]}

    return where


def rms_scale(values):
    return lax.rsqrt(jnp.mean(values * values, axis=-1, keepdims=True) + epsilon)


class Gather:
    def __init__(self, whole, send_sems, recv_sems, me):
        self.whole, self.send_sems, self.recv_sems, self.me = whole, send_sems, recv_sems, me
        self.sibling, self.far = {"tensor": partner(me, FLIP)}, {"tensor": across(me)}
        self.rows = whole.shape[1] // CHUNKS

    def copy(self, lane, chunk, block, where):
        part = pl.ds(chunk * self.rows, self.rows)
        spot = self.whole.at[block, part]
        return send(spot, spot, self.send_sems.at[lane, chunk], self.recv_sems.at[lane, chunk], where)

    def start_chunk(self, chunk):
        self.copy(0, chunk, self.me, self.far).start()
        self.copy(1, chunk, self.me, self.sibling).start()

    def start(self):
        for chunk in range(CHUNKS):
            self.copy(0, chunk, self.me, self.far).start()
        for chunk in range(CHUNKS):
            self.copy(1, chunk, self.me, self.sibling).start()

    def wait_sibling(self):
        for chunk in range(CHUNKS):
            self.copy(1, chunk, self.me, self.sibling).wait_recv()

    def wait_far(self):
        for chunk in range(CHUNKS):
            self.copy(0, chunk, self.me, self.far).wait_recv()
            self.copy(2, chunk, across(self.me), self.sibling).start()

    def wait_last(self):
        for chunk in range(CHUNKS):
            self.copy(2, chunk, across(self.me), self.sibling).wait_recv()

    def drain(self):
        for chunk in range(CHUNKS):
            self.copy(0, chunk, self.me, self.far).wait_send()
            self.copy(1, chunk, self.me, self.sibling).wait_send()
            self.copy(2, chunk, across(self.me), self.sibling).wait_send()


class Scatter:
    def __init__(self, partial, near, summed, arrived, send_sems, recv_sems, me):
        self.partial, self.near, self.summed, self.arrived = partial, near, summed, arrived
        self.send_sems, self.recv_sems, self.me = send_sems, recv_sems, me
        self.sibling, self.far = {"tensor": partner(me, FLIP)}, {"tensor": across(me)}
        self.rows = near.shape[1] // CHUNKS

    def part(self, chunk):
        return pl.ds(chunk * self.rows, self.rows)

    def near_copy(self, slot, chunk):
        block = partner(self.me, MIRROR if slot == 0 else FLIP)
        return send(
            self.partial.at[block, self.part(chunk)],
            self.near.at[slot, self.part(chunk)],
            self.send_sems.at[slot, chunk],
            self.recv_sems.at[slot, chunk],
            self.sibling,
        )

    def far_copy(self, chunk):
        return send(
            self.summed.at[self.part(chunk)],
            self.arrived.at[self.part(chunk)],
            self.send_sems.at[2, chunk],
            self.recv_sems.at[2, chunk],
            self.far,
        )

    def start(self, slot):
        for chunk in range(CHUNKS):
            self.near_copy(slot, chunk).start()

    def cross(self, mine):
        for chunk in range(CHUNKS):
            part = self.part(chunk)
            self.near_copy(0, chunk).wait_recv()
            self.summed[part] = (
                mine[part].astype(jnp.float32) + self.near[0, part].astype(jnp.float32)
            ).astype(jnp.bfloat16)
            self.far_copy(chunk).start()

    def total(self, chunk, mine):
        part = self.part(chunk)
        self.near_copy(1, chunk).wait_recv()
        self.far_copy(chunk).wait_recv()
        return (
            mine[part].astype(jnp.float32)
            + self.near[1, part].astype(jnp.float32)
            + self.arrived[part].astype(jnp.float32)
        )

    def drain(self):
        for chunk in range(CHUNKS):
            self.near_copy(0, chunk).wait_send()
            self.near_copy(1, chunk).wait_send()
            self.far_copy(chunk).wait_send()


def scatter_scratch(rows, width):
    return [
        pltpu.VMEM((2, rows, width), jnp.bfloat16),
        pltpu.VMEM((rows, width), jnp.bfloat16),
        pltpu.VMEM((rows, width), jnp.bfloat16),
        pltpu.SemaphoreType.DMA((3, CHUNKS)),
        pltpu.SemaphoreType.DMA((3, CHUNKS)),
    ]


def gather_scratch(rows, width):
    return [
        pltpu.VMEM((GROUP, rows, width), jnp.bfloat16),
        pltpu.SemaphoreType.DMA((3, CHUNKS)),
        pltpu.SemaphoreType.DMA((3, CHUNKS)),
    ]


def dot(left, right):
    return jnp.dot(left, right, preferred_element_type=jnp.float32)


def dot_cols(left, right):
    return lax.dot_general(left, right, contract_cols, preferred_element_type=jnp.float32)


def turn(values, cosine, sine):
    return values * cosine + pltpu.roll(values, HEAD_SIZE // 2, 1) * sine


def head_norm_back(incoming, values, gain):
    scale = lax.rsqrt(jnp.mean(values * values, axis=-1, keepdims=True) + epsilon)
    scaled = incoming * gain
    grad = scale * scaled - values * (
        scale * scale * scale * jnp.mean(scaled * values, axis=-1, keepdims=True)
    )
    return grad, jnp.sum(incoming * values * scale, axis=0, keepdims=True)


SCORE_SCALE = HEAD_SIZE**-0.5
LOG2_E = 1.4426950408889634
ROWS = 256
COTANGENT = "cot"
DOWN_PART = "down_part"
SCATTER_PARTS = ("_near", "_sum", "_arr", "_send", "_recv")


def start_loads(ref, layout, parts):
    loads = SimpleNamespace()
    table = vars(ref)
    for slot, name in enumerate(layout.loads):
        source = parts[name] if name in parts else table[name]
        copy = pltpu.make_async_copy(source, table["v_" + name], ref.load_sems.at[slot])
        copy.start()
        setattr(loads, name, copy)
    return loads


def weight_grad(rows, cols, target):
    def block(j, carry):
        at = pl.ds(pl.multiple_of(j * ROWS, ROWS), ROWS)
        total = jnp.zeros((ROWS, cols.shape[2]), jnp.float32)
        for b in range(4):
            total += dot(rows[b, :, at].T, cols[b])
        target[j] = total.astype(jnp.bfloat16).reshape(4, 2, 32, cols.shape[2])
        return carry

    lax.fori_loop(0, 4, block, 0)


def back_kernel(names, layout, *refs):
    ref = SimpleNamespace(**dict(zip(names, refs)))
    me = lax.axis_index("tensor")
    sibling, far, far_sibling = partner(me, FLIP), across(me), partner(me, MIRROR)
    place = rank_places()
    where = rank_where(place)
    doubling = [
        where("x", partner(place["x"], FLIP)),
        where("x", partner(place["x"], MIRROR)),
        where("z", partner(place["z"], FLIP)),
        where("z", partner(place["z"], MIRROR)),
        where("y", 1 - place["y"]),
        {"tensor": sibling},
        {"tensor": far},
    ]

    loads = start_loads(
        ref,
        layout,
        dict(
            down_part_far=ref.down_part.at[pl.ds(far, 1)],
            down_part_own=ref.down_part.at[pl.ds(me, 1)],
        ),
    )
    greet(doubling)

    gather = Gather(ref.gh_all, ref.gh_send, ref.gh_recv, me)
    down = Scatter(
        ref.down_part, ref.d_near, ref.d_sum, ref.d_arr, ref.d_send, ref.d_recv, me
    )
    loads.gh.wait()
    ref.gh_all[me] = ref.v_gh[...].astype(jnp.bfloat16)
    gather.start()

    def streams_of(kind, entries, send_sems, recv_sems):
        out = []
        table = vars(ref)
        for i, (source, start, size, order) in enumerate(entries):
            columns = pl.ds(start, size)
            stream = Stream(
                order,
                table[source].at[:, :, :, :, columns],
                table["o_" + source].at[:, columns],
                [table[kind + str(i) + "_" + str(j)] for j in range(STREAM_SCRATCH)],
                (send_sems.at[i], recv_sems.at[i]),
                place,
                where,
            )
            if "v_" + source in table:
                stream.local = table["v_" + source].at[:, :, :, :, columns]
            out.append(stream)
        return out

    ffn = streams_of("f", layout.ffn, ref.f_send, ref.f_recv)
    attn = streams_of("a", layout.attn, ref.a_send, ref.a_recv)
    for stream in ffn:
        stream.halve(0)
    down.start(0)
    down.start(1)

    loads.w_out.wait()
    loads.att.wait()

    def attended_grad(block):
        rows = ref.gh_all[block]
        for g in range(2):
            part = dot_cols(rows, ref.v_w_out[g * ROWS : (g + 1) * ROWS, :]).astype(jnp.bfloat16)
            for r in range(2):
                low = part[:, r * HEAD_SIZE : (r + 1) * HEAD_SIZE]
                start = (2 * g + r) * HEAD_SIZE
                ref.do[g, block, r * ROWS : (r + 1) * ROWS, :] = low
                product = low.astype(jnp.float32) * ref.v_att[
                    block, :, start : start + HEAD_SIZE
                ].astype(jnp.float32)
                ref.delta[g, block, :, r * ROWS : (r + 1) * ROWS] = jnp.sum(
                    product.T, axis=0, keepdims=True
                )

    attended_grad(me)
    gather.wait_sibling()
    attended_grad(sibling)
    gather.wait_far()
    attended_grad(far)
    gather.wait_last()
    attended_grad(far_sibling)

    loads.down_part_far.wait()
    down.cross(ref.v_down_part_far.at[0])
    for load in (loads.gate, loads.up, loads.down):
        load.wait()
    for stream in ffn:
        stream.quarter(0)

    for load in (
        loads.q, loads.k, loads.v, loads.lse, loads.qraw, loads.kraw, loads.cos, loads.sin,
        loads.qg, loads.kg,
    ):
        load.wait()
    ref.qgain[...] = jnp.zeros_like(ref.qgain)
    ref.kgain[...] = jnp.zeros_like(ref.kgain)
    key_row = lax.broadcasted_iota(jnp.int32, (ROWS, 2 * ROWS), 0)
    query_col = lax.rem(lax.broadcasted_iota(jnp.int32, (ROWS, 2 * ROWS), 1), ROWS)
    allowed = key_row <= query_col

    def attend_group(g):
        def clear(block, carry):
            ref.dk[block] = jnp.zeros((ROWS, HEAD_SIZE), jnp.float32)
            ref.dv[block] = jnp.zeros((ROWS, HEAD_SIZE), jnp.float32)
            ref.kt[block] = ref.v_k[g, block].T
            return carry

        lax.fori_loop(0, 4, clear, 0)

        def unit(qb, carry):
            ref.qt[...] = ref.v_q[g, qb].T
            ref.dot[...] = ref.do[g, qb].T
            ref.dqt[...] = jnp.zeros_like(ref.dqt)

            def tile(kb, masked):
                scores = dot(ref.v_k[g, kb], ref.qt[...])
                probs = jnp.exp2(scores * (SCORE_SCALE * LOG2_E) - ref.v_lse[g, qb])
                if masked:
                    probs = jnp.where(allowed, probs, 0.0)
                ref.dv[kb] += dot(probs.astype(jnp.bfloat16), ref.do[g, qb])
                grad_probs = dot(ref.v_v[g, kb], ref.dot[...])
                grad_scores = (probs * (grad_probs - ref.delta[g, qb])).astype(jnp.bfloat16)
                ref.dk[kb] += dot(grad_scores, ref.v_q[g, qb])
                ref.dqt[...] += dot(ref.kt[kb], grad_scores)

            def body(kb, inner):
                tile(kb, False)
                return inner

            lax.fori_loop(0, qb, body, 0)
            tile(qb, True)
            grads = ref.dqt[...].T * SCORE_SCALE
            for r in range(2):
                start = (2 * g + r) * HEAD_SIZE
                back = turn(
                    grads[r * ROWS : (r + 1) * ROWS], ref.v_cos[qb], ref.v_sin[qb]
                )
                grad, gain = head_norm_back(
                    back, ref.v_qraw[qb, :, start : start + HEAD_SIZE], ref.v_qg[...]
                )
                ref.dqkv[qb, :, start : start + HEAD_SIZE] = grad.astype(jnp.bfloat16)
                ref.qgain[...] += gain
            return carry

        lax.fori_loop(0, 4, unit, 0)

        def keys(kb, carry):
            start = g * HEAD_SIZE
            back = turn(ref.dk[kb] * SCORE_SCALE, ref.v_cos[kb], ref.v_sin[kb])
            grad, gain = head_norm_back(
                back, ref.v_kraw[kb, :, start : start + HEAD_SIZE], ref.v_kg[...]
            )
            ref.dqkv[kb, :, 512 + start : 512 + start + HEAD_SIZE] = grad.astype(jnp.bfloat16)
            ref.dqkv[kb, :, 768 + start : 768 + start + HEAD_SIZE] = ref.dv[kb].astype(
                jnp.bfloat16
            )
            ref.kgain[...] += gain
            return carry

        lax.fori_loop(0, 4, keys, 0)

    attend_group(0)
    for stream in ffn:
        stream.settle(0)
        stream.halve(1)
    attend_group(1)
    for stream in ffn:
        stream.quarter(1)

    for load in (loads.wq, loads.wk, loads.wv):
        load.wait()
    inward = Scatter(
        ref.x_part, ref.x_near, ref.x_sum, ref.x_arr, ref.x_send, ref.x_recv, me
    )

    def inward_part(block, target):
        def column(j, carry):
            at = pl.ds(pl.multiple_of(j * ROWS, ROWS), ROWS)
            value = (
                dot_cols(ref.dqkv[block, :, 0:512], ref.v_wq[at, :])
                + dot_cols(ref.dqkv[block, :, 512:768], ref.v_wk[at, :])
                + dot_cols(ref.dqkv[block, :, 768:1024], ref.v_wv[at, :])
            )
            target[:, at] = value.astype(target.dtype)
            return carry

        lax.fori_loop(0, 4, column, 0)

    inward_part(far_sibling, ref.x_part.at[far_sibling])
    inward.start(0)
    inward_part(far, ref.x_part.at[far])
    inward.cross(ref.x_part.at[far])
    inward_part(sibling, ref.x_part.at[sibling])
    inward.start(1)
    inward_part(me, ref.x_own)

    loads.norm_all.wait()

    weight_grad(ref.gh_all, ref.v_att, ref.gw_out)
    for stream in attn[:2]:
        stream.halve(0)
    weight_grad(ref.v_norm_all, ref.dqkv, ref.gw_qkv)
    for stream in attn[2:]:
        stream.halve(0)
    for stream in ffn:
        stream.settle(1)

    loads.hidden.wait()
    loads.down_part_own.wait()
    for chunk in range(CHUNKS):
        part = down.part(chunk)
        total = down.total(chunk, ref.v_down_part_own.at[0])
        ref.result[part] = (ref.v_hidden[part] + total).astype(jnp.bfloat16)

    for load in (loads.tokens, loads.norm_in, loads.gain_mid):
        load.wait()
    ref.gains[...] = jnp.zeros_like(ref.gains)
    ref.gains[1:2] = ref.v_gain_mid[...]
    ref.gains[2:3, 0:128] = ref.qgain[...]
    ref.gains[2:3, 128:256] = ref.kgain[...]
    for chunk in range(CHUNKS):
        part = inward.part(chunk)
        incoming = inward.total(chunk, ref.x_own)
        values = ref.v_tokens[part].astype(jnp.float32)
        grad, gain = head_norm_back(incoming, values, ref.v_norm_in[...])
        ref.grad_tokens[part] = (ref.v_gh[part] + grad).astype(jnp.bfloat16)
        ref.gains[0:1] += gain

    gain_box = ref.gain_box
    gain_box[0] = ref.gains[...]

    def gain_copy(step):
        return send(
            gain_box.at[2 * step],
            gain_box.at[2 * step + 1],
            ref.gain_send.at[step],
            ref.gain_recv.at[step],
            doubling[step],
        )

    def gain_end(step):
        gain_copy(step).wait_recv()
        value = gain_box[2 * step] + gain_box[2 * step + 1]
        if step == 6:
            ref.gain_out[...] = value
        else:
            gain_box[2 * step + 2] = value
            gain_copy(step + 1).start()

    gain_copy(0).start()
    for stream in attn:
        stream.quarter(0)
    gain_end(0)
    for stream in ffn:
        stream.finish()
    gain_end(1)
    for stream in attn:
        stream.settle(0)
        stream.halve(1)
    gain_end(2)
    for stream in attn:
        stream.quarter(1)
    gain_end(3)
    for stream in attn:
        stream.settle(1)
    gain_end(4)
    gain_end(5)
    for stream in attn:
        stream.finish()
    gain_end(6)
    for step in range(7):
        gain_copy(step).wait_send()
    gather.drain()
    down.drain()
    inward.drain()


def back_part(inputs):
    low, wide = jnp.bfloat16, jnp.float32
    names = list(inputs)
    loaded = [name for name in names if name != DOWN_PART] + [DOWN_PART + "_far", DOWN_PART + "_own"]
    operands = [inputs[name] for name in names]
    outs = dict(
        result=((ROWS, 1024), low),
        grad_tokens=((ROWS, 1024), low),
        o_gate=((32, 768), wide),
        o_up=((32, 768), wide),
        o_down=((32, 768), wide),
        o_gw_qkv=((32, 1024), wide),
        o_gw_out=((32, 512), wide),
        gain_out=((8, 1024), wide),
    )
    xa, xb = ("x", FLIP, FLIP), ("x", MIRROR, MIRROR)
    za, zb = ("z", FLIP, MIRROR), ("z", MIRROR, FLIP)
    gate, up, down, gw_qkv, gw_out = [name[2:] for name in list(outs)[2:7]]
    layout = SimpleNamespace(
        loads=loaded,
        ffn=[
            (gate, 0, 384, xa), (gate, 384, 384, xb), (up, 0, 384, za), (up, 384, 384, zb),
            (down, 0, 256, xa), (down, 256, 128, xb), (down, 384, 256, za), (down, 640, 128, zb),
        ],
        attn=[
            (gw_out, 0, 256, xa), (gw_out, 256, 256, xb), (gw_qkv, 0, 384, za),
            (gw_qkv, 384, 384, zb), (gw_qkv, 768, 128, xa), (gw_qkv, 896, 128, xb),
        ],
    )
    scratch = {
        "v_" + name: pltpu.VMEM((1, ROWS, 1024), low)
        if name.startswith(DOWN_PART)
        else pltpu.VMEM(inputs[name].shape, inputs[name].dtype)
        for name in loaded
    }
    scratch.update(
        load_sems=pltpu.SemaphoreType.DMA((len(loaded),)),
        do=pltpu.VMEM((2, 4, 2 * ROWS, HEAD_SIZE), low),
        delta=pltpu.VMEM((2, 4, 1, 2 * ROWS), wide),
        qt=pltpu.VMEM((HEAD_SIZE, 2 * ROWS), low),
        dot=pltpu.VMEM((HEAD_SIZE, 2 * ROWS), low),
        dqt=pltpu.VMEM((HEAD_SIZE, 2 * ROWS), wide),
        kt=pltpu.VMEM((4, HEAD_SIZE, ROWS), low),
        dk=pltpu.VMEM((4, ROWS, HEAD_SIZE), wide),
        dv=pltpu.VMEM((4, ROWS, HEAD_SIZE), wide),
        dqkv=pltpu.VMEM((4, ROWS, 1024), low),
        qgain=pltpu.VMEM((1, HEAD_SIZE), wide),
        kgain=pltpu.VMEM((1, HEAD_SIZE), wide),
        x_part=pltpu.VMEM((4, ROWS, 1024), low),
        x_own=pltpu.VMEM((ROWS, 1024), wide),
        gw_out=pltpu.VMEM((4, 4, 2, 32, 512), low),
        gw_qkv=pltpu.VMEM((4, 4, 2, 32, 1024), low),
        gains=pltpu.VMEM((8, 1024), wide),
        gain_box=pltpu.VMEM((14, 8, 1024), wide),
        gain_send=pltpu.SemaphoreType.DMA((7,)),
        gain_recv=pltpu.SemaphoreType.DMA((7,)),
    )
    scratch.update(zip(("gh_all", "gh_send", "gh_recv"), gather_scratch(ROWS, 1024)))
    for tag in "dx":
        scratch.update(zip((tag + end for end in SCATTER_PARTS), scatter_scratch(ROWS, 1024)))
    for kind, entries in (("f", layout.ffn), ("a", layout.attn)):
        for way in SCATTER_PARTS[3:]:
            scratch[kind + way] = pltpu.SemaphoreType.DMA((len(entries), STREAM_SEMS))
        for i, entry in enumerate(entries):
            for j, buffer in enumerate(stream_scratch(entry[2])):
                scratch[kind + str(i) + "_" + str(j)] = buffer
    results = pl.pallas_call(
        functools.partial(back_kernel, names + list(outs) + list(scratch), layout),
        out_shape=[jax.ShapeDtypeStruct(*spec) for spec in outs.values()],
        in_specs=[pl.BlockSpec(memory_space=pl.ANY)] * len(names),
        out_specs=[VMEM_SPACE] * len(outs),
        scratch_shapes=list(scratch.values()),
        compiler_params=pltpu.CompilerParams(
            collective_id=3, has_side_effects=True, vmem_limit_bytes=60 << 20
        ),
    )(*operands)
    return SimpleNamespace(**dict(zip(outs, results)))


def front_kernel(names, layout, *refs):
    ref = SimpleNamespace(**dict(zip(names, refs)))
    me = lax.axis_index("tensor")
    sibling, far, far_sibling = partner(me, FLIP), across(me), partner(me, MIRROR)
    loads = start_loads(ref, layout, {})
    cot_load = pltpu.make_async_copy(ref.cot, ref.dy_all.at[me], ref.cot_sem)
    cot_load.start()
    greet([{"tensor": sibling}, {"tensor": far}])
    stores = []

    def store(source, target):
        copy = pltpu.make_async_copy(source, target, ref.store_sems.at[len(stores)])
        copy.start()
        stores.append(copy)

    first = Gather(ref.norm_all, ref.n_send, ref.n_recv, me)
    cot = Gather(ref.dy_all, ref.c_send, ref.c_recv, me)
    middle = Gather(ref.mid_all, ref.m_send, ref.m_recv, me)
    loads.tokens.wait()
    loads.norm_in.wait()
    for chunk in range(CHUNKS):
        part = pl.ds(chunk * first.rows, first.rows)
        values = ref.v_tokens[part].astype(jnp.float32)
        ref.norm_all[me, part] = (values * rms_scale(values) * ref.v_norm_in[...]).astype(
            jnp.bfloat16
        )
        first.start_chunk(chunk)
    for load in (loads.wq, loads.wk, loads.wv, loads.cos, loads.sin, loads.qg, loads.kg):
        load.wait()

    def project(block):
        rows = ref.norm_all[block]
        raw = dot(rows, ref.v_wq[...])
        ref.qraw[block] = raw
        for head in range(4):
            values = raw[:, head * HEAD_SIZE : (head + 1) * HEAD_SIZE]
            values = values * rms_scale(values) * ref.v_qg[...]
            ref.q[head // 2, block, (head % 2) * ROWS : (head % 2 + 1) * ROWS, :] = turn(
                values, ref.v_cos[block], -ref.v_sin[block]
            ).astype(jnp.bfloat16)
        raw = dot(rows, ref.v_wk[...])
        ref.kraw[block] = raw
        for g in range(2):
            values = raw[:, g * HEAD_SIZE : (g + 1) * HEAD_SIZE]
            values = values * rms_scale(values) * ref.v_kg[...]
            ref.k[g, block] = turn(values, ref.v_cos[block], -ref.v_sin[block]).astype(jnp.bfloat16)
        low = dot(rows, ref.v_wv[...]).astype(jnp.bfloat16)
        for g in range(2):
            values = low[:, g * HEAD_SIZE : (g + 1) * HEAD_SIZE]
            ref.v[g, block] = values
            ref.vt[g, block] = values.T

    project(me)
    first.wait_sibling()
    project(sibling)
    first.wait_far()
    cot_load.wait()
    cot.start()
    project(far)
    first.wait_last()
    project(far_sibling)
    store(ref.norm_all, ref.o_norm_all)
    store(ref.q, ref.o_q)
    store(ref.k, ref.o_k)
    store(ref.v, ref.o_v)
    store(ref.qraw, ref.o_qraw)
    store(ref.kraw, ref.o_kraw)

    key_row = lax.broadcasted_iota(jnp.int32, (ROWS, 2 * ROWS), 0)
    query_col = lax.rem(lax.broadcasted_iota(jnp.int32, (ROWS, 2 * ROWS), 1), ROWS)
    allowed = key_row <= query_col
    loads.w_out.wait()

    def attend(block):
        for g in range(2):
            ref.qt[...] = ref.q[g, block].T
            ref.ot[...] = jnp.zeros_like(ref.ot)
            ref.total[...] = jnp.zeros_like(ref.total)

            def tile(kb, masked):
                scores = dot(ref.k[g, kb], ref.qt[...])
                probs = jnp.exp2(scores * (SCORE_SCALE * LOG2_E))
                if masked:
                    probs = jnp.where(allowed, probs, 0.0)
                ref.total[...] += jnp.sum(probs, axis=0, keepdims=True)
                ref.ot[...] += dot(ref.vt[g, kb], probs.astype(jnp.bfloat16))

            def body(kb, carry):
                tile(kb, False)
                return carry

            lax.fori_loop(0, block, body, 0)
            tile(block, True)
            total = ref.total[...]
            ref.lse[g, block] = jnp.log(total) * LOG2_E
            rows = (ref.ot[...] / total).T.astype(jnp.bfloat16)
            for r in range(2):
                start = (2 * g + r) * HEAD_SIZE
                ref.att[block, :, start : start + HEAD_SIZE] = rows[r * ROWS : (r + 1) * ROWS]

    def out_part(block, target):
        def column(j, carry):
            at = pl.ds(pl.multiple_of(j * ROWS, ROWS), ROWS)
            target[:, at] = dot(ref.att[block], ref.v_w_out[:, at]).astype(target.dtype)
            return carry

        lax.fori_loop(0, 4, column, 0)

    mixed = Scatter(ref.o_part, ref.p_near, ref.p_sum, ref.p_arr, ref.p_send, ref.p_recv, me)
    attend(far_sibling)
    out_part(far_sibling, ref.o_part.at[far_sibling])
    mixed.start(0)
    attend(far)
    out_part(far, ref.o_part.at[far])
    cot.wait_far()
    mixed.cross(ref.o_part.at[far])
    attend(sibling)
    out_part(sibling, ref.o_part.at[sibling])
    mixed.start(1)
    attend(me)
    out_part(me, ref.own)
    store(ref.att, ref.o_att)
    store(ref.lse, ref.o_lse)

    cot.wait_sibling()
    cot.wait_last()
    loads.w_down.wait()

    def act_grad(block, carry):
        for j in range(3):
            at = slice(j * ROWS, (j + 1) * ROWS)
            ref.gact[block, :, at] = dot_cols(ref.dy_all[block], ref.v_w_down[at, :])
        return carry

    lax.fori_loop(0, 4, act_grad, 0)

    loads.norm_mid.wait()
    for chunk in range(CHUNKS):
        part = mixed.part(chunk)
        values = ref.v_tokens[part].astype(jnp.float32) + mixed.total(chunk, ref.own)
        ref.hidden[part] = values
        ref.mid_all[me, part] = (values * rms_scale(values) * ref.v_norm_mid[...]).astype(
            jnp.bfloat16
        )
        middle.start_chunk(chunk)
    store(ref.hidden, ref.o_hidden)
    loads.w_gate.wait()
    loads.w_up.wait()

    def feed(block):
        def column(j, carry):
            at = pl.ds(pl.multiple_of(j * ROWS, ROWS), ROWS)
            gate = dot(ref.mid_all[block], ref.v_w_gate[:, at])
            up = dot(ref.mid_all[block], ref.v_w_up[:, at])
            sigmoid = jax.nn.sigmoid(gate)
            silu = gate * sigmoid
            ref.act[block, :, at] = (silu * up).astype(jnp.bfloat16)
            grad = ref.gact[block, :, at]
            ref.dup[block, :, at] = (grad * silu).astype(jnp.bfloat16)
            ref.dgate[block, :, at] = (
                grad * up * sigmoid * (1.0 + gate * (1.0 - sigmoid))
            ).astype(jnp.bfloat16)
            return carry

        lax.fori_loop(0, 3, column, 0)

    def mid_part(block, target):
        def column(j, carry):
            at = pl.ds(pl.multiple_of(j * ROWS, ROWS), ROWS)
            value = dot_cols(ref.dgate[block], ref.v_w_gate[at, :]) + dot_cols(
                ref.dup[block], ref.v_w_up[at, :]
            )
            target[:, at] = value.astype(target.dtype)
            return carry

        lax.fori_loop(0, 4, column, 0)

    back = Scatter(ref.b_part, ref.b_near, ref.b_sum, ref.b_arr, ref.b_send, ref.b_recv, me)
    feed(me)
    mid_part(me, ref.own)
    middle.wait_sibling()
    feed(sibling)
    mid_part(sibling, ref.b_part.at[sibling])
    back.start(1)
    middle.wait_far()
    feed(far)
    middle.wait_last()
    feed(far_sibling)
    mid_part(far_sibling, ref.b_part.at[far_sibling])
    back.start(0)
    mid_part(far, ref.b_part.at[far])
    back.cross(ref.b_part.at[far])

    weight_grad(ref.dy_all, ref.act, ref.gw_down)
    store(ref.gw_down, ref.o_down)
    weight_grad(ref.mid_all, ref.dgate, ref.gw_gate)
    store(ref.gw_gate, ref.o_gate)
    weight_grad(ref.mid_all, ref.dup, ref.gw_up)
    store(ref.gw_up, ref.o_up)

    def down_part(block, carry):
        for j in range(4):
            at = slice(j * ROWS, (j + 1) * ROWS)
            ref.down_part[block, :, at] = dot(ref.act[block], ref.v_w_down[:, at]).astype(
                jnp.bfloat16
            )
        return carry

    lax.fori_loop(0, 4, down_part, 0)
    store(ref.down_part, ref.o_down_part)

    ref.gain[...] = jnp.zeros_like(ref.gain)
    for chunk in range(CHUNKS):
        part = back.part(chunk)
        incoming = back.total(chunk, ref.own)
        grad, gain = head_norm_back(incoming, ref.hidden[part], ref.v_norm_mid[...])
        ref.gh[part] = ref.dy_all[me, part].astype(jnp.float32) + grad
        ref.gain[...] += gain
    store(ref.gh, ref.o_gh)
    store(ref.gain, ref.o_gain)
    for copy in stores:
        copy.wait()
    for moved in (first, cot, middle, mixed, back):
        moved.drain()


def front_part(inputs):
    low, wide = jnp.bfloat16, jnp.float32
    loaded = [name for name in inputs if name != COTANGENT]
    names = list(inputs)
    outs = dict(
        o_norm_all=((4, ROWS, 1024), low),
        o_q=((2, 4, 2 * ROWS, HEAD_SIZE), low),
        o_k=((2, 4, ROWS, HEAD_SIZE), low),
        o_v=((2, 4, ROWS, HEAD_SIZE), low),
        o_qraw=((4, ROWS, 512), wide),
        o_kraw=((4, ROWS, 256), wide),
        o_att=((4, ROWS, 512), low),
        o_lse=((2, 4, 1, 2 * ROWS), wide),
        o_hidden=((ROWS, 1024), wide),
        o_down=((4, 4, 2, 32, 768), low),
        o_gate=((4, 4, 2, 32, 768), low),
        o_up=((4, 4, 2, 32, 768), low),
        o_down_part=((4, ROWS, 1024), low),
        o_gh=((ROWS, 1024), wide),
        o_gain=((1, 1024), wide),
    )
    scratch = {"v_" + name: pltpu.VMEM(inputs[name].shape, inputs[name].dtype) for name in loaded}
    scratch.update(
        load_sems=pltpu.SemaphoreType.DMA((len(loaded),)),
        cot_sem=pltpu.SemaphoreType.DMA,
        store_sems=pltpu.SemaphoreType.DMA((len(outs),)),
        qraw=pltpu.VMEM((4, ROWS, 512), wide),
        kraw=pltpu.VMEM((4, ROWS, 256), wide),
        q=pltpu.VMEM((2, 4, 2 * ROWS, HEAD_SIZE), low),
        k=pltpu.VMEM((2, 4, ROWS, HEAD_SIZE), low),
        v=pltpu.VMEM((2, 4, ROWS, HEAD_SIZE), low),
        vt=pltpu.VMEM((2, 4, HEAD_SIZE, ROWS), low),
        qt=pltpu.VMEM((HEAD_SIZE, 2 * ROWS), low),
        ot=pltpu.VMEM((HEAD_SIZE, 2 * ROWS), wide),
        total=pltpu.VMEM((1, 2 * ROWS), wide),
        lse=pltpu.VMEM((2, 4, 1, 2 * ROWS), wide),
        att=pltpu.VMEM((4, ROWS, 512), low),
        o_part=pltpu.VMEM((4, ROWS, 1024), low),
        b_part=pltpu.VMEM((4, ROWS, 1024), low),
        own=pltpu.VMEM((ROWS, 1024), wide),
        hidden=pltpu.VMEM((ROWS, 1024), wide),
        gact=pltpu.VMEM((4, ROWS, 768), wide),
        act=pltpu.VMEM((4, ROWS, 768), low),
        dup=pltpu.VMEM((4, ROWS, 768), low),
        dgate=pltpu.VMEM((4, ROWS, 768), low),
        gw_down=pltpu.VMEM((4, 4, 2, 32, 768), low),
        gw_gate=pltpu.VMEM((4, 4, 2, 32, 768), low),
        gw_up=pltpu.VMEM((4, 4, 2, 32, 768), low),
        down_part=pltpu.VMEM((4, ROWS, 1024), low),
        gh=pltpu.VMEM((ROWS, 1024), wide),
        gain=pltpu.VMEM((1, 1024), wide),
    )
    scratch.update(
        zip(("norm_all", "n_send", "n_recv"), gather_scratch(ROWS, 1024)),
    )
    scratch.update(zip(("dy_all", "c_send", "c_recv"), gather_scratch(ROWS, 1024)))
    scratch.update(zip(("mid_all", "m_send", "m_recv"), gather_scratch(ROWS, 1024)))
    for tag in "pb":
        scratch.update(zip((tag + end for end in SCATTER_PARTS), scatter_scratch(ROWS, 1024)))
    results = pl.pallas_call(
        functools.partial(
            front_kernel, names + list(outs) + list(scratch), SimpleNamespace(loads=loaded)
        ),
        out_shape=[jax.ShapeDtypeStruct(*spec) for spec in outs.values()],
        in_specs=[pl.BlockSpec(memory_space=pl.ANY)] * len(names),
        out_specs=[pl.BlockSpec(memory_space=pl.ANY)] * len(outs),
        scratch_shapes=list(scratch.values()),
        compiler_params=pltpu.CompilerParams(
            collective_id=4, has_side_effects=True, vmem_limit_bytes=60 << 20
        ),
    )(*inputs.values())
    return SimpleNamespace(**dict(zip(outs, results)))


def rotary_tables():
    position = np.arange(SEQUENCE_TOKENS, dtype=np.float64)
    inverse = 1000000.0 ** (-np.arange(HEAD_SIZE // 2, dtype=np.float64) * 2.0 / HEAD_SIZE)
    angles = position[:, None] * inverse[None, :]
    cosine, sine = np.cos(angles), np.sin(angles)
    return (
        jnp.asarray(np.concatenate([table, tail], axis=1).astype(np.float32)).reshape(
            4, ROWS, HEAD_SIZE
        )
        for table, tail in ((cosine, cosine), (sine, -sine))
    )


def per_device(
    tokens,
    norm_in,
    w_query,
    key_matrix,
    value_matrix,
    query_gain,
    key_gain,
    w_out,
    norm_mid,
    w_gate,
    w_up,
    w_down,
    cotangent,
):
    wide = jnp.float32
    cosine, sine = rotary_tables()
    norm_in = norm_in.astype(wide).reshape(1, 1024)
    norm_mid = norm_mid.astype(wide).reshape(1, 1024)
    query_gain = query_gain.astype(wide).reshape(1, HEAD_SIZE)
    key_gain = key_gain.astype(wide).reshape(1, HEAD_SIZE)
    front = front_part(
        dict(
            tokens=tokens,
            norm_in=norm_in,
            wq=w_query,
            wk=key_matrix,
            wv=value_matrix,
            cos=cosine,
            sin=sine,
            qg=query_gain,
            kg=key_gain,
            cot=cotangent,
            w_out=w_out,
            w_down=w_down,
            norm_mid=norm_mid,
            w_gate=w_gate,
            w_up=w_up,
        )
    )
    outs = back_part(
        dict(
            gh=front.o_gh,
            w_out=w_out,
            att=front.o_att,
            down_part=front.o_down_part,
            gate=front.o_gate,
            up=front.o_up,
            down=front.o_down,
            q=front.o_q,
            k=front.o_k,
            v=front.o_v,
            lse=front.o_lse,
            qraw=front.o_qraw,
            kraw=front.o_kraw,
            cos=cosine,
            sin=sine,
            qg=query_gain,
            kg=key_gain,
            wq=w_query,
            wk=key_matrix,
            wv=value_matrix,
            norm_all=front.o_norm_all,
            hidden=front.o_hidden,
            tokens=tokens,
            norm_in=norm_in,
            gain_mid=front.o_gain,
        )
    )
    gains = outs.gain_out
    query_key_value = outs.o_gw_qkv
    return (
        outs.result,
        outs.grad_tokens,
        gains[0],
        query_key_value[:, :512],
        query_key_value[:, 512:768],
        query_key_value[:, 768:],
        gains[2, :128],
        gains[2, 128:256],
        outs.o_gw_out.T,
        gains[1],
        outs.o_gate,
        outs.o_up,
        outs.o_down.T,
    )


def solution(mesh):
    placed = (
        P(("dp", "tensor"), None),
        P(),
        P(None, "tensor"),
        P(None, "tensor"),
        P(None, "tensor"),
        P(),
        P(),
        P("tensor", None),
        P(),
        P(None, "tensor"),
        P(None, "tensor"),
        P("tensor", None),
        P(("dp", "tensor"), None),
    )
    return jax.shard_map(
        per_device,
        mesh=mesh,
        in_specs=placed,
        out_specs=(
            P(("dp", "tensor"), None),
            P(("dp", "tensor"), None),
            P(),
            P("dp", "tensor"),
            P("dp", "tensor"),
            P("dp", "tensor"),
            P(),
            P(),
            P("tensor", "dp"),
            P(),
            P("dp", "tensor"),
            P("dp", "tensor"),
            P("tensor", "dp"),
        ),
        check_vma=False,
    )
```

```python
import functools
from types import SimpleNamespace

import jax
import jax.numpy as jnp
import numpy as np
from jax import lax
from jax.experimental import pallas as pl
from jax.experimental.pallas import tpu as pltpu
from jax.sharding import PartitionSpec as P

HEAD_SIZE = 128
SEQUENCE_TOKENS = 1024
GROUP = 4
CHUNKS = 4
VMEM_SPACE = pl.BlockSpec(memory_space=pltpu.VMEM)
FLIP, MIRROR = 1, 3
epsilon = 1e-06
contract_cols = (((1,), (1,)), ((), ()))


def partner(index, pairing):
    if pairing == FLIP:
        return index + 1 - 2 * lax.rem(index, 2)
    return 3 - index


def across(index):
    return lax.rem(index + 2, 4)


def send(source, target, send_sem, recv_sem, where):
    return pltpu.make_async_remote_copy(
        src_ref=source,
        dst_ref=target,
        send_sem=send_sem,
        recv_sem=recv_sem,
        device_id=where,
        device_id_type=pl.DeviceIdType.MESH,
    )


def greet(others):
    barrier = pltpu.get_barrier_semaphore()
    for where in others:
        pl.semaphore_signal(barrier, inc=1, device_id=where, device_id_type=pl.DeviceIdType.MESH)
    pl.semaphore_wait(barrier, len(others))


class Stream:
    def __init__(self, order, grad, out, scratch, sems, place, where):
        self.first, self.orders = order[0], order[1:]
        self.grad, self.local, self.out = grad, grad, out
        self.early, self.mid, self.late, self.held, self.low, self.pair, self.last = scratch
        self.send_sems, self.recv_sems = sems
        self.place, self.where = place, where
        self.pending = []

    def axis(self, stage):
        return self.first if stage == 0 else ("z" if self.first == "x" else "x")

    def block(self, stage, index, local=True):
        if stage == 1:
            return self.held.at[index]
        grad = self.local if local else self.grad
        return grad.at[index] if self.first == "x" else grad.at[:, index]

    def launch(self, source, target, slot, where):
        copy = send(source, target, self.send_sems.at[slot], self.recv_sems.at[slot], where)
        copy.start()
        self.pending.append(copy)
        return copy

    def halve(self, stage):
        axis, here = self.axis(stage), self.place[self.axis(stage)]
        other = partner(here, self.orders[stage])
        box = self.early if stage == 0 else self.late
        self.copies = [
            self.launch(
                self.block(stage, index, False), box.at[slot], 4 * stage + slot, self.where(axis, other)
            )
            for slot, index in ((1, across(here)), (0, other))
        ]

    def quarter(self, stage):
        axis, here = self.axis(stage), self.place[self.axis(stage)]
        other = partner(here, FLIP + MIRROR - self.orders[stage])
        box, mid = (self.early, self.mid) if stage == 0 else (self.late, self.low)
        self.copies[0].wait_recv()
        mine = self.block(stage, other)

        def add(row, _):
            mid[0, row] = (
                mine[row].astype(jnp.float32) + box[1, row].astype(jnp.float32)
            ).astype(jnp.bfloat16)
            return _

        lax.fori_loop(0, mid.shape[1], add, 0)
        self.copies.append(
            self.launch(mid.at[0], mid.at[1], 4 * stage + 2, self.where(axis, other))
        )

    def settle(self, stage):
        here = self.place[self.axis(stage)]
        self.copies[1].wait_recv()
        self.copies[2].wait_recv()
        box, mid = (self.early, self.mid) if stage == 0 else (self.late, self.low)
        mine = self.block(stage, here)
        if stage == 0:

            def add(row, _):
                self.held[row] = (
                    mine[row].astype(jnp.float32)
                    + box[0, row].astype(jnp.float32)
                    + mid[1, row].astype(jnp.float32)
                ).astype(jnp.bfloat16)
                return _

            lax.fori_loop(0, mid.shape[1], add, 0)
            return
        keep = self.place["y"]
        give = 1 - keep
        self.pair[0] = (
            mine[give].astype(jnp.float32)
            + box[0, give].astype(jnp.float32)
            + mid[1, give].astype(jnp.float32)
        ).astype(jnp.bfloat16)
        self.copies.append(
            self.launch(self.pair.at[0], self.pair.at[1], 3, self.where("y", give))
        )
        self.last[...] = (
            mine[keep].astype(jnp.float32)
            + box[0, keep].astype(jnp.float32)
            + mid[1, keep].astype(jnp.float32)
        )

    def finish(self):
        self.copies[3].wait_recv()
        self.out[...] = self.last[...] + self.pair[1].astype(jnp.float32)
        for copy in self.pending:
            copy.wait_send()


STREAM_SEMS = 7
STREAM_SCRATCH = 7


def stream_scratch(columns):
    low = jnp.bfloat16
    return [
        pltpu.VMEM((2, 4, 2, 32, columns), low),
        pltpu.VMEM((2, 4, 2, 32, columns), low),
        pltpu.VMEM((2, 2, 32, columns), low),
        pltpu.VMEM((4, 2, 32, columns), low),
        pltpu.VMEM((2, 2, 32, columns), low),
        pltpu.VMEM((2, 32, columns), low),
        pltpu.VMEM((32, columns), jnp.float32),
    ]


def rank_places():
    rank = lax.axis_index("dp")
    return {"x": lax.div(rank, 8), "z": lax.rem(lax.div(rank, 2), 4), "y": lax.rem(rank, 2)}


def rank_where(place):
    def where(axis, index):
        at = dict(place)
        at[axis] = index
        return {"dp": at["x"] * 8 + at["z"] * 2 + at["y"]}

    return where


def rms_scale(values):
    return lax.rsqrt(jnp.mean(values * values, axis=-1, keepdims=True) + epsilon)


class Gather:
    def __init__(self, whole, send_sems, recv_sems, me):
        self.whole, self.send_sems, self.recv_sems, self.me = whole, send_sems, recv_sems, me
        self.sibling, self.far = {"tensor": partner(me, FLIP)}, {"tensor": across(me)}
        self.rows = whole.shape[1] // CHUNKS

    def copy(self, lane, chunk, block, where):
        part = pl.ds(chunk * self.rows, self.rows)
        spot = self.whole.at[block, part]
        return send(spot, spot, self.send_sems.at[lane, chunk], self.recv_sems.at[lane, chunk], where)

    def start_chunk(self, chunk):
        self.copy(0, chunk, self.me, self.far).start()
        self.copy(1, chunk, self.me, self.sibling).start()

    def start(self):
        for chunk in range(CHUNKS):
            self.copy(0, chunk, self.me, self.far).start()
        for chunk in range(CHUNKS):
            self.copy(1, chunk, self.me, self.sibling).start()

    def wait_sibling(self):
        for chunk in range(CHUNKS):
            self.copy(1, chunk, self.me, self.sibling).wait_recv()

    def wait_far(self):
        for chunk in range(CHUNKS):
            self.copy(0, chunk, self.me, self.far).wait_recv()
            self.copy(2, chunk, across(self.me), self.sibling).start()

    def wait_last(self):
        for chunk in range(CHUNKS):
            self.copy(2, chunk, across(self.me), self.sibling).wait_recv()

    def drain(self):
        for chunk in range(CHUNKS):
            self.copy(0, chunk, self.me, self.far).wait_send()
            self.copy(1, chunk, self.me, self.sibling).wait_send()
            self.copy(2, chunk, across(self.me), self.sibling).wait_send()


class Scatter:
    def __init__(self, partial, near, summed, arrived, send_sems, recv_sems, me):
        self.partial, self.near, self.summed, self.arrived = partial, near, summed, arrived
        self.send_sems, self.recv_sems, self.me = send_sems, recv_sems, me
        self.sibling, self.far = {"tensor": partner(me, FLIP)}, {"tensor": across(me)}
        self.rows = near.shape[1] // CHUNKS

    def part(self, chunk):
        return pl.ds(chunk * self.rows, self.rows)

    def near_copy(self, slot, chunk):
        block = partner(self.me, MIRROR if slot == 0 else FLIP)
        return send(
            self.partial.at[block, self.part(chunk)],
            self.near.at[slot, self.part(chunk)],
            self.send_sems.at[slot, chunk],
            self.recv_sems.at[slot, chunk],
            self.sibling,
        )

    def far_copy(self, chunk):
        return send(
            self.summed.at[self.part(chunk)],
            self.arrived.at[self.part(chunk)],
            self.send_sems.at[2, chunk],
            self.recv_sems.at[2, chunk],
            self.far,
        )

    def start(self, slot):
        for chunk in range(CHUNKS):
            self.near_copy(slot, chunk).start()

    def cross(self, mine):
        for chunk in range(CHUNKS):
            part = self.part(chunk)
            self.near_copy(0, chunk).wait_recv()
            self.summed[part] = (
                mine[part].astype(jnp.float32) + self.near[0, part].astype(jnp.float32)
            ).astype(jnp.bfloat16)
            self.far_copy(chunk).start()

    def total(self, chunk, mine):
        part = self.part(chunk)
        self.near_copy(1, chunk).wait_recv()
        self.far_copy(chunk).wait_recv()
        return (
            mine[part].astype(jnp.float32)
            + self.near[1, part].astype(jnp.float32)
            + self.arrived[part].astype(jnp.float32)
        )

    def drain(self):
        for chunk in range(CHUNKS):
            self.near_copy(0, chunk).wait_send()
            self.near_copy(1, chunk).wait_send()
            self.far_copy(chunk).wait_send()


def scatter_scratch(rows, width):
    return [
        pltpu.VMEM((2, rows, width), jnp.bfloat16),
        pltpu.VMEM((rows, width), jnp.bfloat16),
        pltpu.VMEM((rows, width), jnp.bfloat16),
        pltpu.SemaphoreType.DMA((3, CHUNKS)),
        pltpu.SemaphoreType.DMA((3, CHUNKS)),
    ]


def gather_scratch(rows, width):
    return [
        pltpu.VMEM((GROUP, rows, width), jnp.bfloat16),
        pltpu.SemaphoreType.DMA((3, CHUNKS)),
        pltpu.SemaphoreType.DMA((3, CHUNKS)),
    ]


def dot(left, right):
    return jnp.dot(left, right, preferred_element_type=jnp.float32)


def dot_cols(left, right):
    return lax.dot_general(left, right, contract_cols, preferred_element_type=jnp.float32)


def turn(values, cosine, sine):
    return values * cosine + pltpu.roll(values, HEAD_SIZE // 2, 1) * sine


def head_norm_back(incoming, values, gain):
    scale = lax.rsqrt(jnp.mean(values * values, axis=-1, keepdims=True) + epsilon)
    scaled = incoming * gain
    grad = scale * scaled - values * (
        scale * scale * scale * jnp.mean(scaled * values, axis=-1, keepdims=True)
    )
    return grad, jnp.sum(incoming * values * scale, axis=0, keepdims=True)


SCORE_SCALE = HEAD_SIZE**-0.5
LOG2_E = 1.4426950408889634
ROWS = 256
COTANGENT = "cot"
DOWN_PART = "down_part"
MATRICES = ("wq", "wk", "wv")
SCATTER_PARTS = ("_near", "_sum", "_arr", "_send", "_recv")


def start_loads(ref, layout, pairs):
    loads = SimpleNamespace()
    table = vars(ref)
    for slot, name in enumerate(layout.loads):
        source, target = pairs[name] if name in pairs else (table[name], table["v_" + name])
        copy = pltpu.make_async_copy(source, target, ref.load_sems.at[slot])
        copy.start()
        setattr(loads, name, copy)
    return loads


def weight_grad(rows, cols, target):
    width = cols.shape[-1]
    right = cols[...].reshape(SEQUENCE_TOKENS, width)
    for j in range(4):
        left = rows[:, :, j * ROWS : (j + 1) * ROWS].reshape(SEQUENCE_TOKENS, ROWS)
        target[j] = dot(left.T, right).astype(jnp.bfloat16).reshape(4, 2, 32, width)


class RingSum:
    def __init__(self, box, slot, others, send_sems, recv_sems):
        self.box, self.slot, self.others = box, slot, others
        self.send_sems, self.recv_sems = send_sems, recv_sems

    def copy(self, index, slot):
        spot = self.box.at[slot]
        return send(
            spot, spot, self.send_sems.at[index], self.recv_sems.at[slot], self.others[index][1]
        )

    def start(self, value):
        self.box[self.slot] = value
        for index in range(len(self.others)):
            self.copy(index, self.slot).start()

    def end(self):
        for index, (slot, _) in enumerate(self.others):
            self.copy(index, slot).wait_recv()
        total = self.box[0]
        for slot in range(1, self.box.shape[0]):
            total = total + self.box[slot]
        for index in range(len(self.others)):
            self.copy(index, self.slot).wait_send()
        return total


def back_kernel(names, layout, *refs):
    ref = SimpleNamespace(**dict(zip(names, refs)))
    me = lax.axis_index("tensor")
    sibling, far, far_sibling = partner(me, FLIP), across(me), partner(me, MIRROR)
    place = rank_places()
    where = rank_where(place)
    pairs = dict(
        down_part_far=(ref.down_part.at[pl.ds(far, 1)], ref.v_down_part_far),
        down_part_own=(ref.down_part.at[pl.ds(me, 1)], ref.v_down_part_own),
    )
    for g in range(2):
        base = g * 512
        for name, source, start, size in (
            ("wq", ref.wq, 0, 256), ("wk", ref.wk, 256, 128), ("wv", ref.wv, 384, 128)
        ):
            pairs[name + str(g)] = (
                source.at[:, pl.ds(g * size, size)],
                ref.wcat.at[:, pl.ds(base + start, size)],
            )
    loads = start_loads(ref, layout, pairs)

    rings = []
    for axis, box in (("x", ref.box_x), ("z", ref.box_z)):
        here = place[axis]
        slots = (partner(here, FLIP), partner(here, MIRROR), across(here))
        rings.append(
            RingSum(
                box,
                here,
                [(slot, where(axis, slot)) for slot in slots],
                ref.gain_send.at[len(rings)],
                ref.gain_recv.at[len(rings)],
            )
        )
    y = place["y"]
    eight = []
    for row in (y, 1 - y):
        for member in (me, sibling, far, far_sibling):
            if row is not y or member is not me:
                eight.append((row * 4 + member, dict(where("y", row), tensor=member)))
    rings.append(
        RingSum(ref.box_y, y * 4 + me, eight, ref.gain_send.at[2], ref.gain_recv.at[2])
    )
    greet([there for ring in rings for _, there in ring.others])

    gather = Gather(ref.gh_all, ref.gh_send, ref.gh_recv, me)
    down = Scatter(
        ref.down_part, ref.d_near, ref.d_sum, ref.d_arr, ref.d_send, ref.d_recv, me
    )
    loads.gh.wait()
    ref.gh_all[me] = ref.v_gh[...].astype(jnp.bfloat16)
    gather.start()

    table = vars(ref)

    def streams_of(kind, entries, send_sems, recv_sems):
        out = []
        for i, (source, start, size, order, target, at) in enumerate(entries):
            columns = pl.ds(start, size)
            stream = Stream(
                order,
                table[source].at[:, :, :, :, columns],
                table[target].at[:, pl.ds(at, size)],
                [table[kind + str(i) + "_" + str(j)] for j in range(STREAM_SCRATCH)],
                (send_sems.at[i], recv_sems.at[i]),
                place,
                where,
            )
            if "v_" + source in table:
                stream.local = table["v_" + source].at[:, :, :, :, columns]
            out.append(stream)
        return out

    ffn = streams_of("f", layout.ffn, ref.f_send, ref.f_recv)
    attn = streams_of("a", layout.attn, ref.a_send, ref.a_recv)
    out_streams, group_streams = attn[:4], (attn[4:8], attn[8:])

    def every(streams, *steps):
        for stream in streams:
            for step, *stage in steps:
                step(stream, *stage)

    every(ffn, (Stream.halve, 0))
    down.start(0)
    down.start(1)

    loads.w_out.wait()
    loads.att.wait()

    def attended_grad(block):
        part = dot_cols(ref.gh_all[block], ref.v_w_out[...]).astype(jnp.bfloat16)
        for head in range(4):
            g, r = head // 2, head % 2
            at = slice(head * HEAD_SIZE, (head + 1) * HEAD_SIZE)
            low = part[:, at]
            ref.do[g, block, r * ROWS : (r + 1) * ROWS, :] = low
            product = low.astype(jnp.float32) * ref.v_att[block, :, at].astype(jnp.float32)
            ref.delta[g, block, :, r * ROWS : (r + 1) * ROWS] = jnp.sum(
                product.T, axis=0, keepdims=True
            )

    attended_grad(me)
    gather.wait_sibling()
    attended_grad(sibling)
    gather.wait_far()
    attended_grad(far)
    gather.wait_last()
    attended_grad(far_sibling)

    loads.down_part_far.wait()
    down.cross(ref.v_down_part_far.at[0])
    for load in (loads.gate, loads.up, loads.down):
        load.wait()
    every(ffn, (Stream.quarter, 0))
    weight_grad(ref.gh_all, ref.v_att, ref.gw_out)
    every(out_streams, (Stream.halve, 0))

    for load in (
        loads.q, loads.k, loads.v, loads.lse, loads.qraw, loads.kraw, loads.cos, loads.sin,
        loads.qg, loads.kg,
    ):
        load.wait()
    ref.qgain[...] = jnp.zeros_like(ref.qgain)
    ref.kgain[...] = jnp.zeros_like(ref.kgain)
    key_row = lax.broadcasted_iota(jnp.int32, (ROWS, 2 * ROWS), 0)
    query_col = lax.rem(lax.broadcasted_iota(jnp.int32, (ROWS, 2 * ROWS), 1), ROWS)
    allowed = key_row <= query_col

    def attend_group(g):
        base = 512 * g
        for qb in (3, 2, 1, 0):
            keys = (qb + 1) * ROWS
            key = ref.v_k[g, 0 : qb + 1].reshape(keys, HEAD_SIZE)
            query, grad_out = ref.v_q[g, qb], ref.do[g, qb]
            probs = jnp.exp2(
                dot_cols(key, query) * (SCORE_SCALE * LOG2_E) - ref.v_lse[g, qb]
            )
            tail = jnp.where(allowed, probs[keys - ROWS :], 0.0)
            probs = jnp.concatenate([probs[: keys - ROWS], tail], axis=0) if qb else tail
            grad_probs = dot_cols(
                ref.v_v[g, 0 : qb + 1].reshape(keys, HEAD_SIZE), grad_out
            )
            grad_scores = (probs * (grad_probs - ref.delta[g, qb])).astype(jnp.bfloat16)
            grad_value = dot(probs.astype(jnp.bfloat16), grad_out).reshape(qb + 1, ROWS, HEAD_SIZE)
            grad_key = dot(grad_scores, query).reshape(qb + 1, ROWS, HEAD_SIZE)
            if qb == 3:
                ref.dv[...] = grad_value
                ref.dk[...] = grad_key
            else:
                ref.dv[0 : qb + 1] += grad_value
                ref.dk[0 : qb + 1] += grad_key
            grads = dot(key.T, grad_scores).T * SCORE_SCALE
            for r in range(2):
                start = (2 * g + r) * HEAD_SIZE
                back = turn(
                    grads[r * ROWS : (r + 1) * ROWS], ref.v_cos[qb], ref.v_sin[qb]
                )
                grad, gain = head_norm_back(
                    back, ref.v_qraw[qb, :, start : start + HEAD_SIZE], ref.v_qg[...]
                )
                at = base + r * HEAD_SIZE
                ref.dqkv[qb, :, at : at + HEAD_SIZE] = grad.astype(jnp.bfloat16)
                ref.qgain[...] += gain

        for kb in range(4):
            start = g * HEAD_SIZE
            back = turn(ref.dk[kb] * SCORE_SCALE, ref.v_cos[kb], ref.v_sin[kb])
            grad, gain = head_norm_back(
                back, ref.v_kraw[kb, :, start : start + HEAD_SIZE], ref.v_kg[...]
            )
            ref.dqkv[kb, :, base + 256 : base + 384] = grad.astype(jnp.bfloat16)
            ref.dqkv[kb, :, base + 384 : base + 512] = ref.dv[kb].astype(jnp.bfloat16)
            ref.kgain[...] += gain

    attend_group(0)
    every(ffn, (Stream.settle, 0), (Stream.halve, 1))
    loads.norm_all.wait()
    weight_grad(ref.v_norm_all, ref.dqkv.at[:, :, 0:512], ref.gw_0)
    every(group_streams[0], (Stream.halve, 0))
    every(out_streams, (Stream.quarter, 0))
    attend_group(1)

    for load in (loads.wq0, loads.wk0, loads.wv0, loads.wq1, loads.wk1, loads.wv1):
        load.wait()
    inward = Scatter(
        ref.x_part, ref.x_near, ref.x_sum, ref.x_arr, ref.x_send, ref.x_recv, me
    )

    def inward_part(block, target):
        target[...] = dot_cols(ref.dqkv[block], ref.wcat[...]).astype(target.dtype)

    inward_part(far_sibling, ref.x_part.at[far_sibling])
    inward.start(0)
    inward_part(far, ref.x_part.at[far])
    inward.cross(ref.x_part.at[far])
    inward_part(sibling, ref.x_part.at[sibling])
    inward.start(1)
    weight_grad(ref.v_norm_all, ref.dqkv.at[:, :, 512:1024], ref.gw_1)
    every(group_streams[1], (Stream.halve, 0))
    inward_part(me, ref.x_own)

    every(ffn, (Stream.quarter, 1))
    every(out_streams, (Stream.settle, 0), (Stream.halve, 1))
    every(group_streams[0], (Stream.quarter, 0))
    every(ffn, (Stream.settle, 1))
    every(out_streams, (Stream.quarter, 1))
    every(group_streams[0], (Stream.settle, 0), (Stream.halve, 1))

    loads.hidden.wait()
    loads.down_part_own.wait()
    for chunk in range(CHUNKS):
        part = down.part(chunk)
        total = down.total(chunk, ref.v_down_part_own.at[0])
        ref.result[part] = (ref.v_hidden[part] + total).astype(jnp.bfloat16)
    every(group_streams[1], (Stream.quarter, 0))
    every(out_streams, (Stream.settle, 1))
    every(group_streams[0], (Stream.quarter, 1))

    for load in (loads.tokens, loads.norm_in, loads.gain_mid):
        load.wait()
    ref.gains[...] = jnp.zeros_like(ref.gains)
    ref.gains[1:2] = ref.v_gain_mid[...]
    ref.gains[2:3, 0:128] = ref.qgain[...]
    ref.gains[2:3, 128:256] = ref.kgain[...]
    for chunk in range(CHUNKS):
        part = inward.part(chunk)
        incoming = inward.total(chunk, ref.x_own)
        values = ref.v_tokens[part].astype(jnp.float32)
        grad, gain = head_norm_back(incoming, values, ref.v_norm_in[...])
        ref.grad_tokens[part] = (ref.v_gh[part] + grad).astype(jnp.bfloat16)
        ref.gains[0:1] += gain

    rings[0].start(ref.gains[...])
    every(group_streams[1], (Stream.settle, 0), (Stream.halve, 1))
    every(ffn, (Stream.finish,))
    rings[1].start(rings[0].end())
    every(group_streams[1], (Stream.quarter, 1))
    every(group_streams[0], (Stream.settle, 1))
    every(out_streams, (Stream.finish,))
    rings[2].start(rings[1].end())
    every(group_streams[1], (Stream.settle, 1))
    ref.o_out[...] = ref.t_out[...].T
    ref.o_down[...] = ref.t_down[...].T
    every(group_streams[0], (Stream.finish,))
    total = rings[2].end()
    ref.o_norm_in[...] = total[0:1]
    ref.o_norm_mid[...] = total[1:2]
    ref.o_qgain[...] = total[2:3, 0:128]
    ref.o_kgain[...] = total[2:3, 128:256]
    every(group_streams[1], (Stream.finish,))
    gather.drain()
    down.drain()
    inward.drain()


def hand_over_kernel(n, *refs):
    copies = [
        pltpu.make_async_copy(refs[i], refs[n + i], refs[2 * n].at[i]) for i in range(n)
    ]
    for copy in copies:
        copy.start()
    for copy in copies:
        copy.wait()


def hand_over(arrays):
    n = len(arrays)
    anywhere = [pl.BlockSpec(memory_space=pl.ANY)] * n
    return pl.pallas_call(
        functools.partial(hand_over_kernel, n),
        out_shape=[jax.ShapeDtypeStruct(array.shape, array.dtype) for array in arrays],
        in_specs=anywhere,
        out_specs=anywhere,
        scratch_shapes=[pltpu.SemaphoreType.DMA((n,))],
    )(*arrays)


def back_part(inputs):
    low, wide = jnp.bfloat16, jnp.float32
    names = list(inputs)
    weights = [name for name in names if name in MATRICES]
    loaded = [name for name in names if name != DOWN_PART and name not in MATRICES]
    loaded += [DOWN_PART + "_far", DOWN_PART + "_own"]
    shapes = {name: (inputs[name].shape, inputs[name].dtype) for name in loaded[:-2]}
    shapes.update({name: ((1, ROWS, 1024), low) for name in loaded[-2:]})
    loaded += [name + str(g) for g in range(2) for name in weights]
    outs = dict(
        result=((ROWS, 1024), low),
        grad_tokens=((ROWS, 1024), low),
        o_gate=((32, 768), wide),
        o_up=((32, 768), wide),
        o_down=((768, 32), wide),
        o_q=((32, 512), wide),
        o_k=((32, 256), wide),
        o_v=((32, 256), wide),
        o_out=((512, 32), wide),
        o_norm_in=((1, 1024), wide),
        o_norm_mid=((1, 1024), wide),
        o_qgain=((1, HEAD_SIZE), wide),
        o_kgain=((1, HEAD_SIZE), wide),
    )
    xa, xb = ("x", FLIP, FLIP), ("x", MIRROR, MIRROR)
    za, zb = ("z", FLIP, MIRROR), ("z", MIRROR, FLIP)
    layout = SimpleNamespace(
        loads=loaded,
        ffn=[
            ("gate", 0, 384, xa, "o_gate", 0), ("gate", 384, 384, xb, "o_gate", 384),
            ("up", 0, 384, za, "o_up", 0), ("up", 384, 384, zb, "o_up", 384),
            ("down", 0, 256, xa, "t_down", 0), ("down", 256, 128, xb, "t_down", 256),
            ("down", 384, 256, za, "t_down", 384), ("down", 640, 128, zb, "t_down", 640),
        ],
        attn=[("gw_out", 128 * i, 128, way, "t_out", 128 * i) for i, way in enumerate((xb, zb, xa, za))]
        + [
            ("gw_" + str(g), 128 * i, 128, way, target, at + step * g)
            for g in range(2)
            for i, (way, target, at, step) in enumerate(
                ((xa, "o_q", 0, 256), (xb, "o_q", 128, 256), (za, "o_k", 0, 128), (zb, "o_v", 0, 128))
            )
        ],
    )
    scratch = {"v_" + name: pltpu.VMEM(*spec) for name, spec in shapes.items()}
    scratch.update(
        load_sems=pltpu.SemaphoreType.DMA((len(loaded),)),
        do=pltpu.VMEM((2, 4, 2 * ROWS, HEAD_SIZE), low),
        delta=pltpu.VMEM((2, 4, 1, 2 * ROWS), wide),
        dk=pltpu.VMEM((4, ROWS, HEAD_SIZE), wide),
        dv=pltpu.VMEM((4, ROWS, HEAD_SIZE), wide),
        dqkv=pltpu.VMEM((4, ROWS, 1024), low),
        wcat=pltpu.VMEM((1024, 1024), low),
        qgain=pltpu.VMEM((1, HEAD_SIZE), wide),
        kgain=pltpu.VMEM((1, HEAD_SIZE), wide),
        x_part=pltpu.VMEM((4, ROWS, 1024), low),
        x_own=pltpu.VMEM((ROWS, 1024), wide),
        gw_out=pltpu.VMEM((4, 4, 2, 32, 512), low),
        gw_0=pltpu.VMEM((4, 4, 2, 32, 512), low),
        gw_1=pltpu.VMEM((4, 4, 2, 32, 512), low),
        t_out=pltpu.VMEM((32, 512), wide),
        t_down=pltpu.VMEM((32, 768), wide),
        gains=pltpu.VMEM((8, 1024), wide),
        box_x=pltpu.VMEM((4, 8, 1024), wide),
        box_z=pltpu.VMEM((4, 8, 1024), wide),
        box_y=pltpu.VMEM((8, 8, 1024), wide),
        gain_send=pltpu.SemaphoreType.DMA((3, 8)),
        gain_recv=pltpu.SemaphoreType.DMA((3, 8)),
    )
    scratch.update(zip(("gh_all", "gh_send", "gh_recv"), gather_scratch(ROWS, 1024)))
    for tag in "dx":
        scratch.update(zip((tag + end for end in SCATTER_PARTS), scatter_scratch(ROWS, 1024)))
    for kind, entries in (("f", layout.ffn), ("a", layout.attn)):
        for way in SCATTER_PARTS[3:]:
            scratch[kind + way] = pltpu.SemaphoreType.DMA((len(entries), STREAM_SEMS))
        for i, entry in enumerate(entries):
            for j, buffer in enumerate(stream_scratch(entry[2])):
                scratch[kind + str(i) + "_" + str(j)] = buffer
    results = pl.pallas_call(
        functools.partial(back_kernel, names + list(outs) + list(scratch), layout),
        out_shape=[jax.ShapeDtypeStruct(*spec) for spec in outs.values()],
        in_specs=[pl.BlockSpec(memory_space=pl.ANY)] * len(names),
        out_specs=[VMEM_SPACE] * len(outs),
        scratch_shapes=list(scratch.values()),
        compiler_params=pltpu.CompilerParams(
            collective_id=3, has_side_effects=True, vmem_limit_bytes=61 << 20
        ),
    )(*inputs.values())
    return SimpleNamespace(**dict(zip(outs, hand_over(results))))


def front_kernel(names, layout, *refs):
    ref = SimpleNamespace(**dict(zip(names, refs)))
    me = lax.axis_index("tensor")
    sibling, far, far_sibling = partner(me, FLIP), across(me), partner(me, MIRROR)
    loads = start_loads(ref, layout, {})
    cot_load = pltpu.make_async_copy(ref.cot, ref.dy_all.at[me], ref.cot_sem)
    cot_load.start()
    greet([{"tensor": sibling}, {"tensor": far}])
    stores = []

    def store(source, target):
        copy = pltpu.make_async_copy(source, target, ref.store_sems.at[len(stores)])
        copy.start()
        stores.append(copy)

    first = Gather(ref.norm_all, ref.n_send, ref.n_recv, me)
    cot = Gather(ref.dy_all, ref.c_send, ref.c_recv, me)
    middle = Gather(ref.mid_all, ref.m_send, ref.m_recv, me)
    loads.tokens.wait()
    loads.norm_in.wait()
    for chunk in range(CHUNKS):
        part = pl.ds(chunk * first.rows, first.rows)
        values = ref.v_tokens[part].astype(jnp.float32)
        ref.norm_all[me, part] = (values * rms_scale(values) * ref.v_norm_in[...]).astype(
            jnp.bfloat16
        )
        first.start_chunk(chunk)
    for load in (loads.wq, loads.wk, loads.wv, loads.cos, loads.sin, loads.qg, loads.kg):
        load.wait()

    def project(block):
        rows = ref.norm_all[block]
        raw = dot(rows, ref.v_wq[...])
        ref.qraw[block] = raw
        for head in range(4):
            values = raw[:, head * HEAD_SIZE : (head + 1) * HEAD_SIZE]
            values = values * rms_scale(values) * ref.v_qg[...]
            ref.q[head // 2, block, (head % 2) * ROWS : (head % 2 + 1) * ROWS, :] = turn(
                values, ref.v_cos[block], -ref.v_sin[block]
            ).astype(jnp.bfloat16)
        raw = dot(rows, ref.v_wk[...])
        ref.kraw[block] = raw
        for g in range(2):
            values = raw[:, g * HEAD_SIZE : (g + 1) * HEAD_SIZE]
            values = values * rms_scale(values) * ref.v_kg[...]
            ref.k[g, block] = turn(values, ref.v_cos[block], -ref.v_sin[block]).astype(jnp.bfloat16)
        low = dot(rows, ref.v_wv[...]).astype(jnp.bfloat16)
        for g in range(2):
            values = low[:, g * HEAD_SIZE : (g + 1) * HEAD_SIZE]
            ref.v[g, block] = values
            ref.vt[g, block] = values.T

    project(me)
    first.wait_sibling()
    project(sibling)
    first.wait_far()
    cot_load.wait()
    cot.start()
    project(far)
    first.wait_last()
    project(far_sibling)
    store(ref.norm_all, ref.o_norm_all)
    store(ref.q, ref.o_q)
    store(ref.k, ref.o_k)
    store(ref.v, ref.o_v)
    store(ref.qraw, ref.o_qraw)
    store(ref.kraw, ref.o_kraw)

    key_row = lax.broadcasted_iota(jnp.int32, (ROWS, 2 * ROWS), 0)
    query_col = lax.rem(lax.broadcasted_iota(jnp.int32, (ROWS, 2 * ROWS), 1), ROWS)
    allowed = key_row <= query_col
    loads.w_out.wait()

    def attend(block):
        for g in range(2):
            ref.qt[...] = ref.q[g, block].T
            ref.ot[...] = jnp.zeros_like(ref.ot)
            ref.total[...] = jnp.zeros_like(ref.total)

            def tile(kb, masked):
                scores = dot(ref.k[g, kb], ref.qt[...])
                probs = jnp.exp2(scores * (SCORE_SCALE * LOG2_E))
                if masked:
                    probs = jnp.where(allowed, probs, 0.0)
                ref.total[...] += jnp.sum(probs, axis=0, keepdims=True)
                ref.ot[...] += dot(ref.vt[g, kb], probs.astype(jnp.bfloat16))

            def body(kb, carry):
                tile(kb, False)
                return carry

            lax.fori_loop(0, block, body, 0)
            tile(block, True)
            total = ref.total[...]
            ref.lse[g, block] = jnp.log(total) * LOG2_E
            rows = (ref.ot[...] / total).T.astype(jnp.bfloat16)
            for r in range(2):
                start = (2 * g + r) * HEAD_SIZE
                ref.att[block, :, start : start + HEAD_SIZE] = rows[r * ROWS : (r + 1) * ROWS]

    def out_part(block, target):
        target[...] = dot(ref.att[block], ref.v_w_out[...]).astype(target.dtype)

    mixed = Scatter(ref.o_part, ref.p_near, ref.p_sum, ref.p_arr, ref.p_send, ref.p_recv, me)
    attend(far_sibling)
    out_part(far_sibling, ref.o_part.at[far_sibling])
    mixed.start(0)
    attend(far)
    out_part(far, ref.o_part.at[far])
    cot.wait_far()
    mixed.cross(ref.o_part.at[far])
    attend(sibling)
    out_part(sibling, ref.o_part.at[sibling])
    mixed.start(1)
    attend(me)
    out_part(me, ref.own)
    store(ref.att, ref.o_att)
    store(ref.lse, ref.o_lse)

    cot.wait_sibling()
    cot.wait_last()
    loads.w_down.wait()

    def act_grad(block, carry):
        ref.gact[block] = dot_cols(ref.dy_all[block], ref.v_w_down[...])
        return carry

    lax.fori_loop(0, 4, act_grad, 0)

    loads.norm_mid.wait()
    for chunk in range(CHUNKS):
        part = mixed.part(chunk)
        values = ref.v_tokens[part].astype(jnp.float32) + mixed.total(chunk, ref.own)
        ref.hidden[part] = values
        ref.mid_all[me, part] = (values * rms_scale(values) * ref.v_norm_mid[...]).astype(
            jnp.bfloat16
        )
        middle.start_chunk(chunk)
    store(ref.hidden, ref.o_hidden)
    loads.w_gate.wait()
    loads.w_up.wait()

    def feed(block):
        gate = dot(ref.mid_all[block], ref.v_w_gate[...])
        up = dot(ref.mid_all[block], ref.v_w_up[...])
        sigmoid = jax.nn.sigmoid(gate)
        silu = gate * sigmoid
        ref.act[block] = (silu * up).astype(jnp.bfloat16)
        grad = ref.gact[block]
        ref.dup[block] = (grad * silu).astype(jnp.bfloat16)
        ref.dgate[block] = (grad * up * sigmoid * (1.0 + gate * (1.0 - sigmoid))).astype(jnp.bfloat16)

    def mid_part(block, target):
        value = dot_cols(ref.dgate[block], ref.v_w_gate[...])
        value += dot_cols(ref.dup[block], ref.v_w_up[...])
        target[...] = value.astype(target.dtype)

    back = Scatter(ref.b_part, ref.b_near, ref.b_sum, ref.b_arr, ref.b_send, ref.b_recv, me)
    feed(me)
    mid_part(me, ref.own)
    middle.wait_sibling()
    feed(sibling)
    mid_part(sibling, ref.b_part.at[sibling])
    back.start(1)
    middle.wait_far()
    feed(far)
    middle.wait_last()
    feed(far_sibling)
    mid_part(far_sibling, ref.b_part.at[far_sibling])
    back.start(0)
    mid_part(far, ref.b_part.at[far])
    back.cross(ref.b_part.at[far])

    weight_grad(ref.dy_all, ref.act, ref.gw_down)
    store(ref.gw_down, ref.o_down)
    weight_grad(ref.mid_all, ref.dgate, ref.gw_gate)
    store(ref.gw_gate, ref.o_gate)
    weight_grad(ref.mid_all, ref.dup, ref.gw_up)
    store(ref.gw_up, ref.o_up)

    def down_part(block, carry):
        ref.down_part[block] = dot(ref.act[block], ref.v_w_down[...]).astype(jnp.bfloat16)
        return carry

    lax.fori_loop(0, 4, down_part, 0)
    store(ref.down_part, ref.o_down_part)

    ref.gain[...] = jnp.zeros_like(ref.gain)
    for chunk in range(CHUNKS):
        part = back.part(chunk)
        incoming = back.total(chunk, ref.own)
        grad, gain = head_norm_back(incoming, ref.hidden[part], ref.v_norm_mid[...])
        ref.gh[part] = ref.dy_all[me, part].astype(jnp.float32) + grad
        ref.gain[...] += gain
    store(ref.gh, ref.o_gh)
    store(ref.gain, ref.o_gain)
    for copy in stores:
        copy.wait()
    for moved in (first, cot, middle, mixed, back):
        moved.drain()


def front_part(inputs):
    low, wide = jnp.bfloat16, jnp.float32
    loaded = [name for name in inputs if name != COTANGENT]
    names = list(inputs)
    outs = dict(
        o_norm_all=((4, ROWS, 1024), low),
        o_q=((2, 4, 2 * ROWS, HEAD_SIZE), low),
        o_k=((2, 4, ROWS, HEAD_SIZE), low),
        o_v=((2, 4, ROWS, HEAD_SIZE), low),
        o_qraw=((4, ROWS, 512), wide),
        o_kraw=((4, ROWS, 256), wide),
        o_att=((4, ROWS, 512), low),
        o_lse=((2, 4, 1, 2 * ROWS), wide),
        o_hidden=((ROWS, 1024), wide),
        o_down=((4, 4, 2, 32, 768), low),
        o_gate=((4, 4, 2, 32, 768), low),
        o_up=((4, 4, 2, 32, 768), low),
        o_down_part=((4, ROWS, 1024), low),
        o_gh=((ROWS, 1024), wide),
        o_gain=((1, 1024), wide),
    )
    scratch = {"v_" + name: pltpu.VMEM(inputs[name].shape, inputs[name].dtype) for name in loaded}
    scratch.update(
        load_sems=pltpu.SemaphoreType.DMA((len(loaded),)),
        cot_sem=pltpu.SemaphoreType.DMA,
        store_sems=pltpu.SemaphoreType.DMA((len(outs),)),
        qraw=pltpu.VMEM((4, ROWS, 512), wide),
        kraw=pltpu.VMEM((4, ROWS, 256), wide),
        q=pltpu.VMEM((2, 4, 2 * ROWS, HEAD_SIZE), low),
        k=pltpu.VMEM((2, 4, ROWS, HEAD_SIZE), low),
        v=pltpu.VMEM((2, 4, ROWS, HEAD_SIZE), low),
        vt=pltpu.VMEM((2, 4, HEAD_SIZE, ROWS), low),
        qt=pltpu.VMEM((HEAD_SIZE, 2 * ROWS), low),
        ot=pltpu.VMEM((HEAD_SIZE, 2 * ROWS), wide),
        total=pltpu.VMEM((1, 2 * ROWS), wide),
        lse=pltpu.VMEM((2, 4, 1, 2 * ROWS), wide),
        att=pltpu.VMEM((4, ROWS, 512), low),
        o_part=pltpu.VMEM((4, ROWS, 1024), low),
        b_part=pltpu.VMEM((4, ROWS, 1024), low),
        own=pltpu.VMEM((ROWS, 1024), wide),
        hidden=pltpu.VMEM((ROWS, 1024), wide),
        gact=pltpu.VMEM((4, ROWS, 768), wide),
        act=pltpu.VMEM((4, ROWS, 768), low),
        dup=pltpu.VMEM((4, ROWS, 768), low),
        dgate=pltpu.VMEM((4, ROWS, 768), low),
        gw_down=pltpu.VMEM((4, 4, 2, 32, 768), low),
        gw_gate=pltpu.VMEM((4, 4, 2, 32, 768), low),
        gw_up=pltpu.VMEM((4, 4, 2, 32, 768), low),
        down_part=pltpu.VMEM((4, ROWS, 1024), low),
        gh=pltpu.VMEM((ROWS, 1024), wide),
        gain=pltpu.VMEM((1, 1024), wide),
    )
    scratch.update(
        zip(("norm_all", "n_send", "n_recv"), gather_scratch(ROWS, 1024)),
    )
    scratch.update(zip(("dy_all", "c_send", "c_recv"), gather_scratch(ROWS, 1024)))
    scratch.update(zip(("mid_all", "m_send", "m_recv"), gather_scratch(ROWS, 1024)))
    for tag in "pb":
        scratch.update(zip((tag + end for end in SCATTER_PARTS), scatter_scratch(ROWS, 1024)))
    results = pl.pallas_call(
        functools.partial(
            front_kernel, names + list(outs) + list(scratch), SimpleNamespace(loads=loaded)
        ),
        out_shape=[jax.ShapeDtypeStruct(*spec) for spec in outs.values()],
        in_specs=[pl.BlockSpec(memory_space=pl.ANY)] * len(names),
        out_specs=[pl.BlockSpec(memory_space=pl.ANY)] * len(outs),
        scratch_shapes=list(scratch.values()),
        compiler_params=pltpu.CompilerParams(
            collective_id=4, has_side_effects=True, vmem_limit_bytes=60 << 20
        ),
    )(*inputs.values())
    return SimpleNamespace(**dict(zip(outs, results)))


def rotary_tables():
    position = np.arange(SEQUENCE_TOKENS, dtype=np.float64)
    inverse = 1000000.0 ** (-np.arange(HEAD_SIZE // 2, dtype=np.float64) * 2.0 / HEAD_SIZE)
    angles = position[:, None] * inverse[None, :]
    cosine, sine = np.cos(angles), np.sin(angles)
    return (
        jnp.asarray(
            np.concatenate([table, tail], axis=1).astype(np.float32).reshape(4, ROWS, HEAD_SIZE)
        )
        for table, tail in ((cosine, cosine), (sine, -sine))
    )


def per_device(
    tokens,
    norm_in,
    w_query,
    key_matrix,
    value_matrix,
    query_gain,
    key_gain,
    w_out,
    norm_mid,
    w_gate,
    w_up,
    w_down,
    cotangent,
):
    wide = jnp.float32
    cosine, sine = rotary_tables()
    norm_in = norm_in.astype(wide).reshape(1, 1024)
    norm_mid = norm_mid.astype(wide).reshape(1, 1024)
    query_gain = query_gain.astype(wide).reshape(1, HEAD_SIZE)
    key_gain = key_gain.astype(wide).reshape(1, HEAD_SIZE)
    front = front_part(
        dict(
            tokens=tokens,
            norm_in=norm_in,
            wq=w_query,
            wk=key_matrix,
            wv=value_matrix,
            cos=cosine,
            sin=sine,
            qg=query_gain,
            kg=key_gain,
            cot=cotangent,
            w_out=w_out,
            w_down=w_down,
            norm_mid=norm_mid,
            w_gate=w_gate,
            w_up=w_up,
        )
    )
    outs = back_part(
        dict(
            gh=front.o_gh,
            w_out=w_out,
            att=front.o_att,
            down_part=front.o_down_part,
            gate=front.o_gate,
            up=front.o_up,
            down=front.o_down,
            q=front.o_q,
            k=front.o_k,
            v=front.o_v,
            lse=front.o_lse,
            qraw=front.o_qraw,
            kraw=front.o_kraw,
            cos=cosine,
            sin=sine,
            qg=query_gain,
            kg=key_gain,
            wq=w_query,
            wk=key_matrix,
            wv=value_matrix,
            norm_all=front.o_norm_all,
            hidden=front.o_hidden,
            tokens=tokens,
            norm_in=norm_in,
            gain_mid=front.o_gain,
        )
    )
    return (
        outs.result,
        outs.grad_tokens,
        outs.o_norm_in.reshape(1024),
        outs.o_q,
        outs.o_k,
        outs.o_v,
        outs.o_qgain.reshape(HEAD_SIZE),
        outs.o_kgain.reshape(HEAD_SIZE),
        outs.o_out,
        outs.o_norm_mid.reshape(1024),
        outs.o_gate,
        outs.o_up,
        outs.o_down,
    )


def solution(mesh):
    placed = (
        P(("dp", "tensor"), None),
        P(),
        P(None, "tensor"),
        P(None, "tensor"),
        P(None, "tensor"),
        P(),
        P(),
        P("tensor", None),
        P(),
        P(None, "tensor"),
        P(None, "tensor"),
        P("tensor", None),
        P(("dp", "tensor"), None),
    )
    return jax.shard_map(
        per_device,
        mesh=mesh,
        in_specs=placed,
        out_specs=(
            P(("dp", "tensor"), None),
            P(("dp", "tensor"), None),
            P(),
            P("dp", "tensor"),
            P("dp", "tensor"),
            P("dp", "tensor"),
            P(),
            P(),
            P("tensor", "dp"),
            P(),
            P("dp", "tensor"),
            P("dp", "tensor"),
            P("tensor", "dp"),
        ),
        check_vma=False,
    )
```

```python
import functools
from types import SimpleNamespace

import jax
import jax.numpy as jnp
import numpy as np
from jax import lax
from jax.experimental import pallas as pl
from jax.experimental.pallas import tpu as pltpu
from jax.sharding import PartitionSpec as P

HEAD_SIZE = 128
SEQUENCE_TOKENS = 1024
GROUP = 4
CHUNKS = 4
VMEM_SPACE = pl.BlockSpec(memory_space=pltpu.VMEM)
FLIP, MIRROR = 1, 3
epsilon = 1e-06
contract_cols = (((1,), (1,)), ((), ()))


def partner(index, pairing):
    if pairing == FLIP:
        return index + 1 - 2 * lax.rem(index, 2)
    return 3 - index


def across(index):
    return lax.rem(index + 2, 4)


def send(source, target, send_sem, recv_sem, where):
    return pltpu.make_async_remote_copy(
        src_ref=source,
        dst_ref=target,
        send_sem=send_sem,
        recv_sem=recv_sem,
        device_id=where,
        device_id_type=pl.DeviceIdType.MESH,
    )


def greet(others):
    barrier = pltpu.get_barrier_semaphore()
    for where in others:
        pl.semaphore_signal(barrier, inc=1, device_id=where, device_id_type=pl.DeviceIdType.MESH)
    pl.semaphore_wait(barrier, len(others))


class Stream:
    def __init__(self, order, grad, out, scratch, sems, place, where):
        self.first, self.orders = order[0], order[1:]
        self.grad, self.local, self.out = grad, grad, out
        self.early, self.mid, self.late, self.held, self.low, self.pair, self.last = scratch
        self.send_sems, self.recv_sems = sems
        self.place, self.where = place, where
        self.pending = []

    def axis(self, stage):
        return self.first if stage == 0 else ("z" if self.first == "x" else "x")

    def block(self, stage, index, local=True):
        if stage == 1:
            return self.held.at[index]
        grad = self.local if local else self.grad
        return grad.at[index] if self.first == "x" else grad.at[:, index]

    def launch(self, source, target, slot, where):
        copy = send(source, target, self.send_sems.at[slot], self.recv_sems.at[slot], where)
        copy.start()
        self.pending.append(copy)
        return copy

    def halve(self, stage):
        axis, here = self.axis(stage), self.place[self.axis(stage)]
        other = partner(here, self.orders[stage])
        box = self.early if stage == 0 else self.late
        self.copies = [
            self.launch(
                self.block(stage, index, False), box.at[slot], 4 * stage + slot, self.where(axis, other)
            )
            for slot, index in ((1, across(here)), (0, other))
        ]

    def quarter(self, stage):
        axis, here = self.axis(stage), self.place[self.axis(stage)]
        other = partner(here, FLIP + MIRROR - self.orders[stage])
        box, mid = (self.early, self.mid) if stage == 0 else (self.late, self.low)
        self.copies[0].wait_recv()
        mine = self.block(stage, other)

        def add(row, _):
            mid[0, row] = mine[row] + box[1, row]
            return _

        lax.fori_loop(0, mid.shape[1], add, 0)
        self.copies.append(
            self.launch(mid.at[0], mid.at[1], 4 * stage + 2, self.where(axis, other))
        )

    def settle(self, stage):
        here = self.place[self.axis(stage)]
        self.copies[1].wait_recv()
        self.copies[2].wait_recv()
        box, mid = (self.early, self.mid) if stage == 0 else (self.late, self.low)
        mine = self.block(stage, here)
        if stage == 0:

            def add(row, _):
                self.held[row] = mine[row] + box[0, row] + mid[1, row]
                return _

            lax.fori_loop(0, mid.shape[1], add, 0)
            return
        keep = self.place["y"]
        give = 1 - keep
        self.pair[0] = (
            mine[give].astype(jnp.float32)
            + box[0, give].astype(jnp.float32)
            + mid[1, give].astype(jnp.float32)
        ).astype(jnp.bfloat16)
        self.copies.append(
            self.launch(self.pair.at[0], self.pair.at[1], 3, self.where("y", give))
        )
        self.last[...] = (
            mine[keep].astype(jnp.float32)
            + box[0, keep].astype(jnp.float32)
            + mid[1, keep].astype(jnp.float32)
        )

    def finish(self):
        self.copies[3].wait_recv()
        self.out[...] = self.last[...] + self.pair[1].astype(jnp.float32)
        for copy in self.pending:
            copy.wait_send()


STREAM_SEMS = 7
STREAM_SCRATCH = 7


def stream_scratch(columns):
    low = jnp.bfloat16
    return [
        pltpu.VMEM((2, 4, 2, 32, columns), low),
        pltpu.VMEM((2, 4, 2, 32, columns), low),
        pltpu.VMEM((2, 2, 32, columns), low),
        pltpu.VMEM((4, 2, 32, columns), low),
        pltpu.VMEM((2, 2, 32, columns), low),
        pltpu.VMEM((2, 32, columns), low),
        pltpu.VMEM((32, columns), jnp.float32),
    ]


def rank_places():
    rank = lax.axis_index("dp")
    return {"x": lax.div(rank, 8), "z": lax.rem(lax.div(rank, 2), 4), "y": lax.rem(rank, 2)}


def rank_where(place):
    def where(axis, index):
        at = dict(place)
        at[axis] = index
        return {"dp": at["x"] * 8 + at["z"] * 2 + at["y"]}

    return where


def rms_scale(values):
    return lax.rsqrt(jnp.mean(values * values, axis=-1, keepdims=True) + epsilon)


class Gather:
    def __init__(self, whole, send_sems, recv_sems, me):
        self.whole, self.send_sems, self.recv_sems, self.me = whole, send_sems, recv_sems, me
        self.sibling, self.far = {"tensor": partner(me, FLIP)}, {"tensor": across(me)}
        self.rows = whole.shape[1] // CHUNKS

    def copy(self, lane, chunk, block, where):
        part = pl.ds(chunk * self.rows, self.rows)
        spot = self.whole.at[block, part]
        return send(spot, spot, self.send_sems.at[lane, chunk], self.recv_sems.at[lane, chunk], where)

    def start_chunk(self, chunk):
        self.copy(0, chunk, self.me, self.far).start()
        self.copy(1, chunk, self.me, self.sibling).start()

    def start(self):
        for chunk in range(CHUNKS):
            self.copy(0, chunk, self.me, self.far).start()
        for chunk in range(CHUNKS):
            self.copy(1, chunk, self.me, self.sibling).start()

    def wait_sibling(self):
        for chunk in range(CHUNKS):
            self.copy(1, chunk, self.me, self.sibling).wait_recv()

    def wait_far(self):
        for chunk in range(CHUNKS):
            self.copy(0, chunk, self.me, self.far).wait_recv()
            self.copy(2, chunk, across(self.me), self.sibling).start()

    def wait_last(self):
        for chunk in range(CHUNKS):
            self.copy(2, chunk, across(self.me), self.sibling).wait_recv()

    def drain(self):
        for chunk in range(CHUNKS):
            self.copy(0, chunk, self.me, self.far).wait_send()
            self.copy(1, chunk, self.me, self.sibling).wait_send()
            self.copy(2, chunk, across(self.me), self.sibling).wait_send()


class Scatter:
    def __init__(self, partial, near, summed, arrived, send_sems, recv_sems, me):
        self.partial, self.near, self.summed, self.arrived = partial, near, summed, arrived
        self.send_sems, self.recv_sems, self.me = send_sems, recv_sems, me
        self.sibling, self.far = {"tensor": partner(me, FLIP)}, {"tensor": across(me)}
        self.rows = near.shape[1] // CHUNKS

    def part(self, chunk):
        return pl.ds(chunk * self.rows, self.rows)

    def near_copy(self, slot, chunk):
        block = partner(self.me, MIRROR if slot == 0 else FLIP)
        return send(
            self.partial.at[block, self.part(chunk)],
            self.near.at[slot, self.part(chunk)],
            self.send_sems.at[slot, chunk],
            self.recv_sems.at[slot, chunk],
            self.sibling,
        )

    def far_copy(self, chunk):
        return send(
            self.summed.at[self.part(chunk)],
            self.arrived.at[self.part(chunk)],
            self.send_sems.at[2, chunk],
            self.recv_sems.at[2, chunk],
            self.far,
        )

    def start(self, slot):
        for chunk in range(CHUNKS):
            self.near_copy(slot, chunk).start()

    def cross(self, mine):
        for chunk in range(CHUNKS):
            part = self.part(chunk)
            self.near_copy(0, chunk).wait_recv()
            self.summed[part] = (
                mine[part].astype(jnp.float32) + self.near[0, part].astype(jnp.float32)
            ).astype(jnp.bfloat16)
            self.far_copy(chunk).start()

    def total(self, chunk, mine):
        part = self.part(chunk)
        self.near_copy(1, chunk).wait_recv()
        self.far_copy(chunk).wait_recv()
        return (
            mine[part].astype(jnp.float32)
            + self.near[1, part].astype(jnp.float32)
            + self.arrived[part].astype(jnp.float32)
        )

    def drain(self):
        for chunk in range(CHUNKS):
            self.near_copy(0, chunk).wait_send()
            self.near_copy(1, chunk).wait_send()
            self.far_copy(chunk).wait_send()


def scatter_scratch(rows, width):
    return [
        pltpu.VMEM((2, rows, width), jnp.bfloat16),
        pltpu.VMEM((rows, width), jnp.bfloat16),
        pltpu.VMEM((rows, width), jnp.bfloat16),
        pltpu.SemaphoreType.DMA((3, CHUNKS)),
        pltpu.SemaphoreType.DMA((3, CHUNKS)),
    ]


def gather_scratch(rows, width):
    return [
        pltpu.VMEM((GROUP, rows, width), jnp.bfloat16),
        pltpu.SemaphoreType.DMA((3, CHUNKS)),
        pltpu.SemaphoreType.DMA((3, CHUNKS)),
    ]


def dot(left, right):
    return jnp.dot(left, right, preferred_element_type=jnp.float32)


def dot_cols(left, right):
    return lax.dot_general(left, right, contract_cols, preferred_element_type=jnp.float32)


def turn(values, cosine, sine):
    return values * cosine + pltpu.roll(values, HEAD_SIZE // 2, 1) * sine


def head_norm_back(incoming, values, gain):
    scale = lax.rsqrt(jnp.mean(values * values, axis=-1, keepdims=True) + epsilon)
    scaled = incoming * gain
    grad = scale * scaled - values * (
        scale * scale * scale * jnp.mean(scaled * values, axis=-1, keepdims=True)
    )
    return grad, jnp.sum(incoming * values * scale, axis=0, keepdims=True)


SCORE_SCALE = HEAD_SIZE**-0.5
LOG2_E = 1.4426950408889634
ROWS = 256
COTANGENT = "cot"
DOWN_PART = "down_part"
MATRICES = ("wq", "wk", "wv")
SCATTER_PARTS = ("_near", "_sum", "_arr", "_send", "_recv")


def start_loads(ref, layout, pairs):
    loads = SimpleNamespace()
    table = vars(ref)
    for slot, name in enumerate(layout.loads):
        source, target = pairs[name] if name in pairs else (table[name], table["v_" + name])
        copy = pltpu.make_async_copy(source, target, ref.load_sems.at[slot])
        copy.start()
        setattr(loads, name, copy)
    return loads


def weight_grad(rows, cols, target):
    width = cols.shape[-1]
    right = cols[...].reshape(SEQUENCE_TOKENS, width)
    for j in range(4):
        left = rows[:, :, j * ROWS : (j + 1) * ROWS].reshape(SEQUENCE_TOKENS, ROWS)
        target[j] = dot(left.T, right).astype(jnp.bfloat16).reshape(4, 2, 32, width)


class RingSum:
    def __init__(self, box, slot, others, send_sems, recv_sems):
        self.box, self.slot, self.others = box, slot, others
        self.send_sems, self.recv_sems = send_sems, recv_sems

    def copy(self, index, slot):
        spot = self.box.at[slot]
        return send(
            spot, spot, self.send_sems.at[index], self.recv_sems.at[slot], self.others[index][1]
        )

    def start(self, value):
        self.box[self.slot] = value
        for index in range(len(self.others)):
            self.copy(index, self.slot).start()

    def end(self):
        for index, (slot, _) in enumerate(self.others):
            self.copy(index, slot).wait_recv()
        total = self.box[0]
        for slot in range(1, self.box.shape[0]):
            total = total + self.box[slot]
        for index in range(len(self.others)):
            self.copy(index, self.slot).wait_send()
        return total


def back_kernel(names, layout, *refs):
    ref = SimpleNamespace(**dict(zip(names, refs)))
    me = lax.axis_index("tensor")
    sibling, far, far_sibling = partner(me, FLIP), across(me), partner(me, MIRROR)
    place = rank_places()
    where = rank_where(place)
    pairs = dict(
        down_part_far=(ref.down_part.at[pl.ds(far, 1)], ref.v_down_part_far),
        down_part_own=(ref.down_part.at[pl.ds(me, 1)], ref.v_down_part_own),
    )
    for g in range(2):
        base = g * 512
        for name, source, start, size in (
            ("wq", ref.wq, 0, 256), ("wk", ref.wk, 256, 128), ("wv", ref.wv, 384, 128)
        ):
            pairs[name + str(g)] = (
                source.at[:, pl.ds(g * size, size)],
                ref.wcat.at[:, pl.ds(base + start, size)],
            )
    loads = start_loads(ref, layout, pairs)

    rings = []
    for axis, box in (("x", ref.box_x), ("z", ref.box_z)):
        here = place[axis]
        slots = (partner(here, FLIP), partner(here, MIRROR), across(here))
        rings.append(
            RingSum(
                box,
                here,
                [(slot, where(axis, slot)) for slot in slots],
                ref.gain_send.at[len(rings)],
                ref.gain_recv.at[len(rings)],
            )
        )
    y = place["y"]
    eight = []
    for row in (y, 1 - y):
        for member in (me, sibling, far, far_sibling):
            if row is not y or member is not me:
                eight.append((row * 4 + member, dict(where("y", row), tensor=member)))
    rings.append(
        RingSum(ref.box_y, y * 4 + me, eight, ref.gain_send.at[2], ref.gain_recv.at[2])
    )
    greet([there for ring in rings for _, there in ring.others])

    gather = Gather(ref.gh_all, ref.gh_send, ref.gh_recv, me)
    down = Scatter(
        ref.down_part, ref.d_near, ref.d_sum, ref.d_arr, ref.d_send, ref.d_recv, me
    )
    loads.gh.wait()
    ref.gh_all[me] = ref.v_gh[...].astype(jnp.bfloat16)
    gather.start()

    table = vars(ref)

    def streams_of(kind, entries, send_sems, recv_sems):
        out = []
        for i, (source, start, size, order, target, at) in enumerate(entries):
            columns = pl.ds(start, size)
            stream = Stream(
                order,
                table[source].at[:, :, :, :, columns],
                table[target].at[:, pl.ds(at, size)],
                [table[kind + str(i) + "_" + str(j)] for j in range(STREAM_SCRATCH)],
                (send_sems.at[i], recv_sems.at[i]),
                place,
                where,
            )
            if "v_" + source in table:
                stream.local = table["v_" + source].at[:, :, :, :, columns]
            out.append(stream)
        return out

    ffn = streams_of("f", layout.ffn, ref.f_send, ref.f_recv)
    attn = streams_of("a", layout.attn, ref.a_send, ref.a_recv)
    out_streams, group_streams = attn[:4], (attn[4:8], attn[8:])

    def every(streams, *steps):
        for stream in streams:
            for step, *stage in steps:
                step(stream, *stage)

    every(ffn, (Stream.halve, 0))
    down.start(0)
    down.start(1)

    loads.w_out.wait()
    loads.att.wait()

    def attended_grad(block):
        part = dot_cols(ref.gh_all[block], ref.v_w_out[...]).astype(jnp.bfloat16)
        for head in range(4):
            g, r = head // 2, head % 2
            at = slice(head * HEAD_SIZE, (head + 1) * HEAD_SIZE)
            low = part[:, at]
            ref.do[g, block, r * ROWS : (r + 1) * ROWS, :] = low
            product = low.astype(jnp.float32) * ref.v_att[block, :, at].astype(jnp.float32)
            ref.delta[g, block, :, r * ROWS : (r + 1) * ROWS] = jnp.sum(
                product.T, axis=0, keepdims=True
            )

    attended_grad(me)
    gather.wait_sibling()
    attended_grad(sibling)
    gather.wait_far()
    attended_grad(far)
    gather.wait_last()
    attended_grad(far_sibling)

    loads.down_part_far.wait()
    down.cross(ref.v_down_part_far.at[0])
    for load in (loads.gate, loads.up, loads.down):
        load.wait()
    every(ffn, (Stream.quarter, 0))
    weight_grad(ref.gh_all, ref.v_att, ref.gw_out)
    every(out_streams, (Stream.halve, 0))

    for load in (
        loads.q, loads.k, loads.v, loads.lse, loads.qraw, loads.kraw, loads.cos, loads.sin,
        loads.qg, loads.kg,
    ):
        load.wait()
    ref.qgain[...] = jnp.zeros_like(ref.qgain)
    ref.kgain[...] = jnp.zeros_like(ref.kgain)
    key_row = lax.broadcasted_iota(jnp.int32, (ROWS, 2 * ROWS), 0)
    query_col = lax.rem(lax.broadcasted_iota(jnp.int32, (ROWS, 2 * ROWS), 1), ROWS)
    allowed = key_row <= query_col

    def attend_group(g):
        base = 512 * g
        for qb in (3, 2, 1, 0):
            keys = (qb + 1) * ROWS
            key = ref.v_k[g, 0 : qb + 1].reshape(keys, HEAD_SIZE)
            query, grad_out = ref.v_q[g, qb], ref.do[g, qb]
            probs = jnp.exp2(
                dot_cols(key, query) * (SCORE_SCALE * LOG2_E) - ref.v_lse[g, qb]
            )
            tail = jnp.where(allowed, probs[keys - ROWS :], 0.0)
            probs = jnp.concatenate([probs[: keys - ROWS], tail], axis=0) if qb else tail
            grad_probs = dot_cols(
                ref.v_v[g, 0 : qb + 1].reshape(keys, HEAD_SIZE), grad_out
            )
            grad_scores = (probs * (grad_probs - ref.delta[g, qb])).astype(jnp.bfloat16)
            grad_value = dot(probs.astype(jnp.bfloat16), grad_out).reshape(qb + 1, ROWS, HEAD_SIZE)
            grad_key = dot(grad_scores, query).reshape(qb + 1, ROWS, HEAD_SIZE)
            if qb == 3:
                ref.dv[...] = grad_value
                ref.dk[...] = grad_key
            else:
                ref.dv[0 : qb + 1] += grad_value
                ref.dk[0 : qb + 1] += grad_key
            grads = dot(key.T, grad_scores).T * SCORE_SCALE
            for r in range(2):
                start = (2 * g + r) * HEAD_SIZE
                back = turn(
                    grads[r * ROWS : (r + 1) * ROWS], ref.v_cos[qb], ref.v_sin[qb]
                )
                grad, gain = head_norm_back(
                    back, ref.v_qraw[qb, :, start : start + HEAD_SIZE], ref.v_qg[...]
                )
                at = base + r * HEAD_SIZE
                ref.dqkv[qb, :, at : at + HEAD_SIZE] = grad.astype(jnp.bfloat16)
                ref.qgain[...] += gain

        for kb in range(4):
            start = g * HEAD_SIZE
            back = turn(ref.dk[kb] * SCORE_SCALE, ref.v_cos[kb], ref.v_sin[kb])
            grad, gain = head_norm_back(
                back, ref.v_kraw[kb, :, start : start + HEAD_SIZE], ref.v_kg[...]
            )
            ref.dqkv[kb, :, base + 256 : base + 384] = grad.astype(jnp.bfloat16)
            ref.dqkv[kb, :, base + 384 : base + 512] = ref.dv[kb].astype(jnp.bfloat16)
            ref.kgain[...] += gain

    attend_group(0)
    loads.norm_all.wait()
    weight_grad(ref.v_norm_all, ref.dqkv.at[:, :, 0:512], ref.gw_0)
    every(group_streams[0], (Stream.halve, 0))
    every(ffn, (Stream.settle, 0), (Stream.halve, 1))
    every(out_streams, (Stream.quarter, 0))
    attend_group(1)

    for load in (loads.wq0, loads.wk0, loads.wv0, loads.wq1, loads.wk1, loads.wv1):
        load.wait()
    inward = Scatter(
        ref.x_part, ref.x_near, ref.x_sum, ref.x_arr, ref.x_send, ref.x_recv, me
    )

    def inward_part(block, target):
        target[...] = dot_cols(ref.dqkv[block], ref.wcat[...]).astype(target.dtype)

    inward_part(far_sibling, ref.x_part.at[far_sibling])
    inward.start(0)
    inward_part(far, ref.x_part.at[far])
    inward.cross(ref.x_part.at[far])
    inward_part(sibling, ref.x_part.at[sibling])
    inward.start(1)
    weight_grad(ref.v_norm_all, ref.dqkv.at[:, :, 512:1024], ref.gw_1)
    every(group_streams[1], (Stream.halve, 0))
    inward_part(me, ref.x_own)

    every(ffn, (Stream.quarter, 1))
    every(out_streams, (Stream.settle, 0), (Stream.halve, 1))
    every(group_streams[0], (Stream.quarter, 0))
    every(ffn, (Stream.settle, 1))
    every(out_streams, (Stream.quarter, 1))
    every(group_streams[0], (Stream.settle, 0), (Stream.halve, 1))

    loads.hidden.wait()
    loads.down_part_own.wait()
    for chunk in range(CHUNKS):
        part = down.part(chunk)
        total = down.total(chunk, ref.v_down_part_own.at[0])
        ref.result[part] = (ref.v_hidden[part] + total).astype(jnp.bfloat16)
    every(group_streams[1], (Stream.quarter, 0))
    every(out_streams, (Stream.settle, 1))
    every(group_streams[0], (Stream.quarter, 1))

    for load in (loads.tokens, loads.norm_in, loads.gain_mid):
        load.wait()
    ref.gains[...] = jnp.zeros_like(ref.gains)
    ref.gains[1:2] = ref.v_gain_mid[...]
    ref.gains[2:3, 0:128] = ref.qgain[...]
    ref.gains[2:3, 128:256] = ref.kgain[...]
    for chunk in range(CHUNKS):
        part = inward.part(chunk)
        incoming = inward.total(chunk, ref.x_own)
        values = ref.v_tokens[part].astype(jnp.float32)
        grad, gain = head_norm_back(incoming, values, ref.v_norm_in[...])
        ref.grad_tokens[part] = (ref.v_gh[part] + grad).astype(jnp.bfloat16)
        ref.gains[0:1] += gain

    rings[0].start(ref.gains[...])
    every(group_streams[1], (Stream.settle, 0), (Stream.halve, 1))
    every(ffn, (Stream.finish,))
    rings[1].start(rings[0].end())
    every(group_streams[1], (Stream.quarter, 1))
    every(group_streams[0], (Stream.settle, 1))
    every(out_streams, (Stream.finish,))
    rings[2].start(rings[1].end())
    every(group_streams[1], (Stream.settle, 1))
    every(group_streams[0], (Stream.finish,))
    total = rings[2].end()
    ref.o_norm_in[...] = total[0:1]
    ref.o_norm_mid[...] = total[1:2]
    ref.o_qgain[...] = total[2:3, 0:128]
    ref.o_kgain[...] = total[2:3, 128:256]
    every(group_streams[1], (Stream.finish,))
    gather.drain()
    down.drain()
    inward.drain()


def hand_over_kernel(n, *refs):
    sources, targets, buffers, sems = refs[:n], refs[n : 2 * n], refs[2 * n : 3 * n], refs[3 * n]
    pulls = [pltpu.make_async_copy(sources[i], buffers[i], sems.at[0, i]) for i in range(n)]
    pushes = [pltpu.make_async_copy(buffers[i], targets[i], sems.at[1, i]) for i in range(n)]
    for pull in pulls:
        pull.start()
    for pull, push in zip(pulls, pushes):
        pull.wait()
        push.start()
    for push in pushes:
        push.wait()


def hand_over(arrays):
    n = len(arrays)
    anywhere = [pl.BlockSpec(memory_space=pl.ANY)] * n
    return pl.pallas_call(
        functools.partial(hand_over_kernel, n),
        out_shape=[jax.ShapeDtypeStruct(array.shape, array.dtype) for array in arrays],
        in_specs=anywhere,
        out_specs=anywhere,
        scratch_shapes=[pltpu.VMEM(array.shape, array.dtype) for array in arrays]
        + [pltpu.SemaphoreType.DMA((2, n))],
    )(*arrays)


def back_part(inputs):
    low, wide = jnp.bfloat16, jnp.float32
    names = list(inputs)
    weights = [name for name in names if name in MATRICES]
    loaded = [name for name in names if name != DOWN_PART and name not in MATRICES]
    loaded += [DOWN_PART + "_far", DOWN_PART + "_own"]
    shapes = {name: (inputs[name].shape, inputs[name].dtype) for name in loaded[:-2]}
    shapes.update({name: ((1, ROWS, 1024), low) for name in loaded[-2:]})
    loaded += [name + str(g) for g in range(2) for name in weights]
    outs = dict(
        result=((ROWS, 1024), low),
        grad_tokens=((ROWS, 1024), low),
        o_gate=((32, 768), wide),
        o_up=((32, 768), wide),
        o_down=((32, 768), wide),
        o_q=((32, 512), wide),
        o_k=((32, 256), wide),
        o_v=((32, 256), wide),
        o_out=((32, 512), wide),
        o_norm_in=((1, 1024), wide),
        o_norm_mid=((1, 1024), wide),
        o_qgain=((1, HEAD_SIZE), wide),
        o_kgain=((1, HEAD_SIZE), wide),
    )
    xa, xb = ("x", FLIP, FLIP), ("x", MIRROR, MIRROR)
    za, zb = ("z", FLIP, MIRROR), ("z", MIRROR, FLIP)
    layout = SimpleNamespace(
        loads=loaded,
        ffn=[
            ("gate", 0, 384, xa, "o_gate", 0), ("gate", 384, 384, xb, "o_gate", 384),
            ("up", 0, 384, za, "o_up", 0), ("up", 384, 384, zb, "o_up", 384),
            ("down", 0, 256, xa, "o_down", 0), ("down", 256, 128, xb, "o_down", 256),
            ("down", 384, 256, za, "o_down", 384), ("down", 640, 128, zb, "o_down", 640),
        ],
        attn=[("gw_out", 128 * i, 128, way, "o_out", 128 * i) for i, way in enumerate((xb, zb, xa, za))]
        + [
            ("gw_" + str(g), 128 * i, 128, way, target, at + step * g)
            for g in range(2)
            for i, (way, target, at, step) in enumerate(
                ((xa, "o_q", 0, 256), (xb, "o_q", 128, 256), (za, "o_k", 0, 128), (zb, "o_v", 0, 128))
            )
        ],
    )
    scratch = {"v_" + name: pltpu.VMEM(*spec) for name, spec in shapes.items()}
    scratch.update(
        load_sems=pltpu.SemaphoreType.DMA((len(loaded),)),
        do=pltpu.VMEM((2, 4, 2 * ROWS, HEAD_SIZE), low),
        delta=pltpu.VMEM((2, 4, 1, 2 * ROWS), wide),
        dk=pltpu.VMEM((4, ROWS, HEAD_SIZE), wide),
        dv=pltpu.VMEM((4, ROWS, HEAD_SIZE), wide),
        dqkv=pltpu.VMEM((4, ROWS, 1024), low),
        wcat=pltpu.VMEM((1024, 1024), low),
        qgain=pltpu.VMEM((1, HEAD_SIZE), wide),
        kgain=pltpu.VMEM((1, HEAD_SIZE), wide),
        x_part=pltpu.VMEM((4, ROWS, 1024), low),
        x_own=pltpu.VMEM((ROWS, 1024), wide),
        gw_out=pltpu.VMEM((4, 4, 2, 32, 512), low),
        gw_0=pltpu.VMEM((4, 4, 2, 32, 512), low),
        gw_1=pltpu.VMEM((4, 4, 2, 32, 512), low),
        gains=pltpu.VMEM((8, 1024), wide),
        box_x=pltpu.VMEM((4, 8, 1024), wide),
        box_z=pltpu.VMEM((4, 8, 1024), wide),
        box_y=pltpu.VMEM((8, 8, 1024), wide),
        gain_send=pltpu.SemaphoreType.DMA((3, 8)),
        gain_recv=pltpu.SemaphoreType.DMA((3, 8)),
    )
    scratch.update(zip(("gh_all", "gh_send", "gh_recv"), gather_scratch(ROWS, 1024)))
    for tag in "dx":
        scratch.update(zip((tag + end for end in SCATTER_PARTS), scatter_scratch(ROWS, 1024)))
    for kind, entries in (("f", layout.ffn), ("a", layout.attn)):
        for way in SCATTER_PARTS[3:]:
            scratch[kind + way] = pltpu.SemaphoreType.DMA((len(entries), STREAM_SEMS))
        for i, entry in enumerate(entries):
            for j, buffer in enumerate(stream_scratch(entry[2])):
                scratch[kind + str(i) + "_" + str(j)] = buffer
    results = pl.pallas_call(
        functools.partial(back_kernel, names + list(outs) + list(scratch), layout),
        out_shape=[jax.ShapeDtypeStruct(*spec) for spec in outs.values()],
        in_specs=[pl.BlockSpec(memory_space=pl.ANY)] * len(names),
        out_specs=[VMEM_SPACE] * len(outs),
        scratch_shapes=list(scratch.values()),
        compiler_params=pltpu.CompilerParams(
            collective_id=3, has_side_effects=True, vmem_limit_bytes=61 << 20
        ),
    )(*inputs.values())
    return SimpleNamespace(**dict(zip(outs, hand_over(results))))


def front_kernel(names, layout, *refs):
    ref = SimpleNamespace(**dict(zip(names, refs)))
    me = lax.axis_index("tensor")
    sibling, far, far_sibling = partner(me, FLIP), across(me), partner(me, MIRROR)
    loads = start_loads(ref, layout, {})
    cot_load = pltpu.make_async_copy(ref.cot, ref.dy_all.at[me], ref.cot_sem)
    cot_load.start()
    greet([{"tensor": sibling}, {"tensor": far}])
    stores = []

    def store(source, target):
        copy = pltpu.make_async_copy(source, target, ref.store_sems.at[len(stores)])
        copy.start()
        stores.append(copy)

    first = Gather(ref.norm_all, ref.n_send, ref.n_recv, me)
    cot = Gather(ref.dy_all, ref.c_send, ref.c_recv, me)
    middle = Gather(ref.mid_all, ref.m_send, ref.m_recv, me)
    loads.tokens.wait()
    loads.norm_in.wait()
    for chunk in range(CHUNKS):
        part = pl.ds(chunk * first.rows, first.rows)
        values = ref.v_tokens[part].astype(jnp.float32)
        ref.norm_all[me, part] = (values * rms_scale(values) * ref.v_norm_in[...]).astype(
            jnp.bfloat16
        )
        first.start_chunk(chunk)
    for load in (loads.wq, loads.wk, loads.wv, loads.cos, loads.sin, loads.qg, loads.kg):
        load.wait()

    def project(block):
        rows = ref.norm_all[block]
        raw = dot(rows, ref.v_wq[...])
        ref.qraw[block] = raw
        for head in range(4):
            values = raw[:, head * HEAD_SIZE : (head + 1) * HEAD_SIZE]
            values = values * rms_scale(values) * ref.v_qg[...]
            ref.q[head // 2, block, (head % 2) * ROWS : (head % 2 + 1) * ROWS, :] = turn(
                values, ref.v_cos[block], -ref.v_sin[block]
            ).astype(jnp.bfloat16)
        raw = dot(rows, ref.v_wk[...])
        ref.kraw[block] = raw
        for g in range(2):
            values = raw[:, g * HEAD_SIZE : (g + 1) * HEAD_SIZE]
            values = values * rms_scale(values) * ref.v_kg[...]
            ref.k[g, block] = turn(values, ref.v_cos[block], -ref.v_sin[block]).astype(jnp.bfloat16)
        low = dot(rows, ref.v_wv[...]).astype(jnp.bfloat16)
        for g in range(2):
            values = low[:, g * HEAD_SIZE : (g + 1) * HEAD_SIZE]
            ref.v[g, block] = values
            ref.vt[g, block] = values.T

    project(me)
    first.wait_sibling()
    project(sibling)
    first.wait_far()
    cot_load.wait()
    cot.start()
    project(far)
    first.wait_last()
    project(far_sibling)
    store(ref.norm_all, ref.o_norm_all)
    store(ref.q, ref.o_q)
    store(ref.k, ref.o_k)
    store(ref.v, ref.o_v)
    store(ref.qraw, ref.o_qraw)
    store(ref.kraw, ref.o_kraw)

    key_row = lax.broadcasted_iota(jnp.int32, (ROWS, 2 * ROWS), 0)
    query_col = lax.rem(lax.broadcasted_iota(jnp.int32, (ROWS, 2 * ROWS), 1), ROWS)
    allowed = key_row <= query_col
    loads.w_out.wait()

    def attend(block):
        for g in range(2):
            ref.qt[...] = ref.q[g, block].T
            ref.ot[...] = jnp.zeros_like(ref.ot)
            ref.total[...] = jnp.zeros_like(ref.total)

            def tile(kb, masked):
                scores = dot(ref.k[g, kb], ref.qt[...])
                probs = jnp.exp2(scores * (SCORE_SCALE * LOG2_E))
                if masked:
                    probs = jnp.where(allowed, probs, 0.0)
                ref.total[...] += jnp.sum(probs, axis=0, keepdims=True)
                ref.ot[...] += dot(ref.vt[g, kb], probs.astype(jnp.bfloat16))

            def body(kb, carry):
                tile(kb, False)
                return carry

            lax.fori_loop(0, block, body, 0)
            tile(block, True)
            total = ref.total[...]
            ref.lse[g, block] = jnp.log(total) * LOG2_E
            rows = (ref.ot[...] / total).T.astype(jnp.bfloat16)
            for r in range(2):
                start = (2 * g + r) * HEAD_SIZE
                ref.att[block, :, start : start + HEAD_SIZE] = rows[r * ROWS : (r + 1) * ROWS]

    def out_part(block, target):
        target[...] = dot(ref.att[block], ref.v_w_out[...]).astype(target.dtype)

    mixed = Scatter(ref.o_part, ref.p_near, ref.p_sum, ref.p_arr, ref.p_send, ref.p_recv, me)
    attend(far_sibling)
    out_part(far_sibling, ref.o_part.at[far_sibling])
    mixed.start(0)
    attend(far)
    out_part(far, ref.o_part.at[far])
    cot.wait_far()
    mixed.cross(ref.o_part.at[far])
    attend(sibling)
    out_part(sibling, ref.o_part.at[sibling])
    mixed.start(1)
    attend(me)
    out_part(me, ref.own)
    store(ref.att, ref.o_att)
    store(ref.lse, ref.o_lse)

    cot.wait_sibling()
    cot.wait_last()
    loads.w_down.wait()

    def act_grad(block, carry):
        ref.gact[block] = dot_cols(ref.dy_all[block], ref.v_w_down[...])
        return carry

    lax.fori_loop(0, 4, act_grad, 0)

    loads.norm_mid.wait()
    for chunk in range(CHUNKS):
        part = mixed.part(chunk)
        values = ref.v_tokens[part].astype(jnp.float32) + mixed.total(chunk, ref.own)
        ref.hidden[part] = values
        ref.mid_all[me, part] = (values * rms_scale(values) * ref.v_norm_mid[...]).astype(
            jnp.bfloat16
        )
        middle.start_chunk(chunk)
    store(ref.hidden, ref.o_hidden)
    loads.w_gate.wait()
    loads.w_up.wait()

    def feed(block):
        gate = dot(ref.mid_all[block], ref.v_w_gate[...])
        up = dot(ref.mid_all[block], ref.v_w_up[...])
        sigmoid = jax.nn.sigmoid(gate)
        silu = gate * sigmoid
        ref.act[block] = (silu * up).astype(jnp.bfloat16)
        grad = ref.gact[block]
        ref.dup[block] = (grad * silu).astype(jnp.bfloat16)
        ref.dgate[block] = (grad * up * sigmoid * (1.0 + gate * (1.0 - sigmoid))).astype(jnp.bfloat16)

    def mid_part(block, target):
        value = dot_cols(ref.dgate[block], ref.v_w_gate[...])
        value += dot_cols(ref.dup[block], ref.v_w_up[...])
        target[...] = value.astype(target.dtype)

    back = Scatter(ref.b_part, ref.b_near, ref.b_sum, ref.b_arr, ref.b_send, ref.b_recv, me)
    feed(me)
    mid_part(me, ref.own)
    middle.wait_sibling()
    feed(sibling)
    mid_part(sibling, ref.b_part.at[sibling])
    back.start(1)
    middle.wait_far()
    feed(far)
    middle.wait_last()
    feed(far_sibling)
    mid_part(far_sibling, ref.b_part.at[far_sibling])
    back.start(0)
    mid_part(far, ref.b_part.at[far])
    back.cross(ref.b_part.at[far])

    weight_grad(ref.dy_all, ref.act, ref.gw_down)
    store(ref.gw_down, ref.o_down)
    weight_grad(ref.mid_all, ref.dgate, ref.gw_gate)
    store(ref.gw_gate, ref.o_gate)
    weight_grad(ref.mid_all, ref.dup, ref.gw_up)
    store(ref.gw_up, ref.o_up)

    def down_part(block, carry):
        ref.down_part[block] = dot(ref.act[block], ref.v_w_down[...]).astype(jnp.bfloat16)
        return carry

    lax.fori_loop(0, 4, down_part, 0)
    store(ref.down_part, ref.o_down_part)

    ref.gain[...] = jnp.zeros_like(ref.gain)
    for chunk in range(CHUNKS):
        part = back.part(chunk)
        incoming = back.total(chunk, ref.own)
        grad, gain = head_norm_back(incoming, ref.hidden[part], ref.v_norm_mid[...])
        ref.gh[part] = ref.dy_all[me, part].astype(jnp.float32) + grad
        ref.gain[...] += gain
    store(ref.gh, ref.o_gh)
    store(ref.gain, ref.o_gain)
    for copy in stores:
        copy.wait()
    for moved in (first, cot, middle, mixed, back):
        moved.drain()


def front_part(inputs):
    low, wide = jnp.bfloat16, jnp.float32
    loaded = [name for name in inputs if name != COTANGENT]
    names = list(inputs)
    outs = dict(
        o_norm_all=((4, ROWS, 1024), low),
        o_q=((2, 4, 2 * ROWS, HEAD_SIZE), low),
        o_k=((2, 4, ROWS, HEAD_SIZE), low),
        o_v=((2, 4, ROWS, HEAD_SIZE), low),
        o_qraw=((4, ROWS, 512), wide),
        o_kraw=((4, ROWS, 256), wide),
        o_att=((4, ROWS, 512), low),
        o_lse=((2, 4, 1, 2 * ROWS), wide),
        o_hidden=((ROWS, 1024), wide),
        o_down=((4, 4, 2, 32, 768), low),
        o_gate=((4, 4, 2, 32, 768), low),
        o_up=((4, 4, 2, 32, 768), low),
        o_down_part=((4, ROWS, 1024), low),
        o_gh=((ROWS, 1024), wide),
        o_gain=((1, 1024), wide),
    )
    scratch = {"v_" + name: pltpu.VMEM(inputs[name].shape, inputs[name].dtype) for name in loaded}
    scratch.update(
        load_sems=pltpu.SemaphoreType.DMA((len(loaded),)),
        cot_sem=pltpu.SemaphoreType.DMA,
        store_sems=pltpu.SemaphoreType.DMA((len(outs),)),
        qraw=pltpu.VMEM((4, ROWS, 512), wide),
        kraw=pltpu.VMEM((4, ROWS, 256), wide),
        q=pltpu.VMEM((2, 4, 2 * ROWS, HEAD_SIZE), low),
        k=pltpu.VMEM((2, 4, ROWS, HEAD_SIZE), low),
        v=pltpu.VMEM((2, 4, ROWS, HEAD_SIZE), low),
        vt=pltpu.VMEM((2, 4, HEAD_SIZE, ROWS), low),
        qt=pltpu.VMEM((HEAD_SIZE, 2 * ROWS), low),
        ot=pltpu.VMEM((HEAD_SIZE, 2 * ROWS), wide),
        total=pltpu.VMEM((1, 2 * ROWS), wide),
        lse=pltpu.VMEM((2, 4, 1, 2 * ROWS), wide),
        att=pltpu.VMEM((4, ROWS, 512), low),
        o_part=pltpu.VMEM((4, ROWS, 1024), low),
        b_part=pltpu.VMEM((4, ROWS, 1024), low),
        own=pltpu.VMEM((ROWS, 1024), wide),
        hidden=pltpu.VMEM((ROWS, 1024), wide),
        gact=pltpu.VMEM((4, ROWS, 768), wide),
        act=pltpu.VMEM((4, ROWS, 768), low),
        dup=pltpu.VMEM((4, ROWS, 768), low),
        dgate=pltpu.VMEM((4, ROWS, 768), low),
        gw_down=pltpu.VMEM((4, 4, 2, 32, 768), low),
        gw_gate=pltpu.VMEM((4, 4, 2, 32, 768), low),
        gw_up=pltpu.VMEM((4, 4, 2, 32, 768), low),
        down_part=pltpu.VMEM((4, ROWS, 1024), low),
        gh=pltpu.VMEM((ROWS, 1024), wide),
        gain=pltpu.VMEM((1, 1024), wide),
    )
    scratch.update(
        zip(("norm_all", "n_send", "n_recv"), gather_scratch(ROWS, 1024)),
    )
    scratch.update(zip(("dy_all", "c_send", "c_recv"), gather_scratch(ROWS, 1024)))
    scratch.update(zip(("mid_all", "m_send", "m_recv"), gather_scratch(ROWS, 1024)))
    for tag in "pb":
        scratch.update(zip((tag + end for end in SCATTER_PARTS), scatter_scratch(ROWS, 1024)))
    results = pl.pallas_call(
        functools.partial(
            front_kernel, names + list(outs) + list(scratch), SimpleNamespace(loads=loaded)
        ),
        out_shape=[jax.ShapeDtypeStruct(*spec) for spec in outs.values()],
        in_specs=[pl.BlockSpec(memory_space=pl.ANY)] * len(names),
        out_specs=[pl.BlockSpec(memory_space=pl.ANY)] * len(outs),
        scratch_shapes=list(scratch.values()),
        compiler_params=pltpu.CompilerParams(
            collective_id=4, has_side_effects=True, vmem_limit_bytes=60 << 20
        ),
    )(*inputs.values())
    return SimpleNamespace(**dict(zip(outs, results)))


def rotary_tables():
    position = np.arange(SEQUENCE_TOKENS, dtype=np.float64)
    inverse = 1000000.0 ** (-np.arange(HEAD_SIZE // 2, dtype=np.float64) * 2.0 / HEAD_SIZE)
    angles = position[:, None] * inverse[None, :]
    cosine, sine = np.cos(angles), np.sin(angles)
    return (
        jnp.asarray(
            np.concatenate([table, tail], axis=1).astype(np.float32).reshape(4, ROWS, HEAD_SIZE)
        )
        for table, tail in ((cosine, cosine), (sine, -sine))
    )


def per_device(
    tokens,
    norm_in,
    w_query,
    key_matrix,
    value_matrix,
    query_gain,
    key_gain,
    w_out,
    norm_mid,
    w_gate,
    w_up,
    w_down,
    cotangent,
):
    wide = jnp.float32
    cosine, sine = rotary_tables()
    norm_in = norm_in.astype(wide).reshape(1, 1024)
    norm_mid = norm_mid.astype(wide).reshape(1, 1024)
    query_gain = query_gain.astype(wide).reshape(1, HEAD_SIZE)
    key_gain = key_gain.astype(wide).reshape(1, HEAD_SIZE)
    front = front_part(
        dict(
            tokens=tokens,
            norm_in=norm_in,
            wq=w_query,
            wk=key_matrix,
            wv=value_matrix,
            cos=cosine,
            sin=sine,
            qg=query_gain,
            kg=key_gain,
            cot=cotangent,
            w_out=w_out,
            w_down=w_down,
            norm_mid=norm_mid,
            w_gate=w_gate,
            w_up=w_up,
        )
    )
    outs = back_part(
        dict(
            gh=front.o_gh,
            w_out=w_out,
            att=front.o_att,
            down_part=front.o_down_part,
            gate=front.o_gate,
            up=front.o_up,
            down=front.o_down,
            q=front.o_q,
            k=front.o_k,
            v=front.o_v,
            lse=front.o_lse,
            qraw=front.o_qraw,
            kraw=front.o_kraw,
            cos=cosine,
            sin=sine,
            qg=query_gain,
            kg=key_gain,
            wq=w_query,
            wk=key_matrix,
            wv=value_matrix,
            norm_all=front.o_norm_all,
            hidden=front.o_hidden,
            tokens=tokens,
            norm_in=norm_in,
            gain_mid=front.o_gain,
        )
    )
    return (
        outs.result,
        outs.grad_tokens,
        outs.o_norm_in.reshape(1024),
        outs.o_q,
        outs.o_k,
        outs.o_v,
        outs.o_qgain.reshape(HEAD_SIZE),
        outs.o_kgain.reshape(HEAD_SIZE),
        outs.o_out.T,
        outs.o_norm_mid.reshape(1024),
        outs.o_gate,
        outs.o_up,
        outs.o_down.T,
    )


def solution(mesh):
    placed = (
        P(("dp", "tensor"), None),
        P(),
        P(None, "tensor"),
        P(None, "tensor"),
        P(None, "tensor"),
        P(),
        P(),
        P("tensor", None),
        P(),
        P(None, "tensor"),
        P(None, "tensor"),
        P("tensor", None),
        P(("dp", "tensor"), None),
    )
    return jax.shard_map(
        per_device,
        mesh=mesh,
        in_specs=placed,
        out_specs=(
            P(("dp", "tensor"), None),
            P(("dp", "tensor"), None),
            P(),
            P("dp", "tensor"),
            P("dp", "tensor"),
            P("dp", "tensor"),
            P(),
            P(),
            P("tensor", "dp"),
            P(),
            P("dp", "tensor"),
            P("dp", "tensor"),
            P("tensor", "dp"),
        ),
        check_vma=False,
    )
```

```python
import functools
from types import SimpleNamespace

import jax
import jax.numpy as jnp
import numpy as np
from jax import lax
from jax.experimental import pallas as pl
from jax.experimental.pallas import tpu as pltpu
from jax.sharding import PartitionSpec as P

HEAD_SIZE = 128
SEQUENCE_TOKENS = 1024
GROUP = 4
CHUNKS = 4
VMEM_SPACE = pl.BlockSpec(memory_space=pltpu.VMEM)
FLIP, MIRROR = 1, 3
epsilon = 1e-06
contract_cols = (((1,), (1,)), ((), ()))


def partner(index, pairing):
    if pairing == FLIP:
        return index + 1 - 2 * lax.rem(index, 2)
    return 3 - index


def across(index):
    return lax.rem(index + 2, 4)


def send(source, target, send_sem, recv_sem, where):
    return pltpu.make_async_remote_copy(
        src_ref=source,
        dst_ref=target,
        send_sem=send_sem,
        recv_sem=recv_sem,
        device_id=where,
        device_id_type=pl.DeviceIdType.MESH,
    )


def greet(others):
    barrier = pltpu.get_barrier_semaphore()
    for where in others:
        pl.semaphore_signal(barrier, inc=1, device_id=where, device_id_type=pl.DeviceIdType.MESH)
    pl.semaphore_wait(barrier, len(others))


class Stream:
    def __init__(self, order, grad, out, scratch, sems, place, where):
        self.first, self.orders = order[0], order[1:]
        self.grad, self.local, self.out = grad, grad, out
        self.early, self.mid, self.late, self.held, self.low, self.pair, self.last = scratch
        self.send_sems, self.recv_sems = sems
        self.place, self.where = place, where
        self.pending = []
        self.copies = [None, None]

    def axis(self, stage):
        return self.first if stage == 0 else ("z" if self.first == "x" else "x")

    def block(self, stage, index, local=True):
        if stage == 1:
            return self.held.at[index]
        grad = self.local if local else self.grad
        return grad.at[index] if self.first == "x" else grad.at[:, index]

    def launch(self, source, target, slot, where):
        copy = send(source, target, self.send_sems.at[slot], self.recv_sems.at[slot], where)
        copy.start()
        self.pending.append(copy)
        return copy

    def halve(self, stage):
        axis, here = self.axis(stage), self.place[self.axis(stage)]
        other = partner(here, self.orders[stage])
        box = self.early if stage == 0 else self.late
        self.copies = [
            self.launch(
                self.block(stage, index, False), box.at[slot], 4 * stage + slot, self.where(axis, other)
            )
            for slot, index in ((1, across(here)), (0, other))
        ]

    def quarter(self, stage):
        axis, here = self.axis(stage), self.place[self.axis(stage)]
        other = partner(here, FLIP + MIRROR - self.orders[stage])
        box, mid = (self.early, self.mid) if stage == 0 else (self.late, self.low)
        if self.copies[0]:
            self.copies[0].wait_recv()
        mine = self.block(stage, other)

        def add(row, _):
            mid[0, row] = mine[row] + box[1, row]
            return _

        lax.fori_loop(0, mid.shape[1], add, 0)
        self.copies.append(
            self.launch(mid.at[0], mid.at[1], 4 * stage + 2, self.where(axis, other))
        )

    def settle(self, stage):
        here = self.place[self.axis(stage)]
        if self.copies[1]:
            self.copies[1].wait_recv()
        self.copies[2].wait_recv()
        box, mid = (self.early, self.mid) if stage == 0 else (self.late, self.low)
        mine = self.block(stage, here)
        if stage == 0:

            def add(row, _):
                self.held[row] = mine[row] + box[0, row] + mid[1, row]
                return _

            lax.fori_loop(0, mid.shape[1], add, 0)
            return
        keep = self.place["y"]
        give = 1 - keep
        self.pair[0] = (
            mine[give].astype(jnp.float32)
            + box[0, give].astype(jnp.float32)
            + mid[1, give].astype(jnp.float32)
        ).astype(jnp.bfloat16)
        self.copies.append(
            self.launch(self.pair.at[0], self.pair.at[1], 3, self.where("y", give))
        )
        self.last[...] = (
            mine[keep].astype(jnp.float32)
            + box[0, keep].astype(jnp.float32)
            + mid[1, keep].astype(jnp.float32)
        )

    def finish(self):
        self.copies[3].wait_recv()
        self.out[...] = self.last[...] + self.pair[1].astype(jnp.float32)
        for copy in self.pending:
            copy.wait_send()


STREAM_SEMS = 7
STREAM_SCRATCH = 7


def stream_scratch(columns):
    low = jnp.bfloat16
    return [
        pltpu.VMEM((2, 4, 2, 32, columns), low),
        pltpu.VMEM((2, 4, 2, 32, columns), low),
        pltpu.VMEM((2, 2, 32, columns), low),
        pltpu.VMEM((4, 2, 32, columns), low),
        pltpu.VMEM((2, 2, 32, columns), low),
        pltpu.VMEM((2, 32, columns), low),
        pltpu.VMEM((32, columns), jnp.float32),
    ]


def rank_places():
    rank = lax.axis_index("dp")
    return {"x": lax.div(rank, 8), "z": lax.rem(lax.div(rank, 2), 4), "y": lax.rem(rank, 2)}


def rank_where(place):
    def where(axis, index):
        at = dict(place)
        at[axis] = index
        return {"dp": at["x"] * 8 + at["z"] * 2 + at["y"]}

    return where


def rms_scale(values):
    return lax.rsqrt(jnp.mean(values * values, axis=-1, keepdims=True) + epsilon)


class Gather:
    def __init__(self, whole, send_sems, recv_sems, me):
        self.whole, self.send_sems, self.recv_sems, self.me = whole, send_sems, recv_sems, me
        self.sibling, self.far = {"tensor": partner(me, FLIP)}, {"tensor": across(me)}
        self.rows = whole.shape[1] // CHUNKS

    def copy(self, lane, chunk, block, where):
        part = pl.ds(chunk * self.rows, self.rows)
        spot = self.whole.at[block, part]
        return send(spot, spot, self.send_sems.at[lane, chunk], self.recv_sems.at[lane, chunk], where)

    def start_chunk(self, chunk):
        self.copy(0, chunk, self.me, self.far).start()
        self.copy(1, chunk, self.me, self.sibling).start()

    def start(self):
        for chunk in range(CHUNKS):
            self.copy(0, chunk, self.me, self.far).start()
        for chunk in range(CHUNKS):
            self.copy(1, chunk, self.me, self.sibling).start()

    def wait_sibling(self):
        for chunk in range(CHUNKS):
            self.copy(1, chunk, self.me, self.sibling).wait_recv()

    def wait_far(self):
        for chunk in range(CHUNKS):
            self.copy(0, chunk, self.me, self.far).wait_recv()
            self.copy(2, chunk, across(self.me), self.sibling).start()

    def wait_last(self):
        for chunk in range(CHUNKS):
            self.copy(2, chunk, across(self.me), self.sibling).wait_recv()

    def drain(self):
        for chunk in range(CHUNKS):
            self.copy(0, chunk, self.me, self.far).wait_send()
            self.copy(1, chunk, self.me, self.sibling).wait_send()
            self.copy(2, chunk, across(self.me), self.sibling).wait_send()


class Scatter:
    def __init__(self, partial, near, summed, arrived, send_sems, recv_sems, me):
        self.partial, self.near, self.summed, self.arrived = partial, near, summed, arrived
        self.send_sems, self.recv_sems, self.me = send_sems, recv_sems, me
        self.sibling, self.far = {"tensor": partner(me, FLIP)}, {"tensor": across(me)}
        self.rows = near.shape[1] // CHUNKS

    def part(self, chunk):
        return pl.ds(chunk * self.rows, self.rows)

    def near_copy(self, slot, chunk):
        block = partner(self.me, MIRROR if slot == 0 else FLIP)
        return send(
            self.partial.at[block, self.part(chunk)],
            self.near.at[slot, self.part(chunk)],
            self.send_sems.at[slot, chunk],
            self.recv_sems.at[slot, chunk],
            self.sibling,
        )

    def far_copy(self, chunk):
        return send(
            self.summed.at[self.part(chunk)],
            self.arrived.at[self.part(chunk)],
            self.send_sems.at[2, chunk],
            self.recv_sems.at[2, chunk],
            self.far,
        )

    def start(self, slot):
        for chunk in range(CHUNKS):
            self.near_copy(slot, chunk).start()

    def cross(self, mine):
        for chunk in range(CHUNKS):
            part = self.part(chunk)
            self.near_copy(0, chunk).wait_recv()
            self.summed[part] = (
                mine[part].astype(jnp.float32) + self.near[0, part].astype(jnp.float32)
            ).astype(jnp.bfloat16)
            self.far_copy(chunk).start()

    def total(self, chunk, mine):
        part = self.part(chunk)
        self.near_copy(1, chunk).wait_recv()
        self.far_copy(chunk).wait_recv()
        return (
            mine[part].astype(jnp.float32)
            + self.near[1, part].astype(jnp.float32)
            + self.arrived[part].astype(jnp.float32)
        )

    def drain(self):
        for chunk in range(CHUNKS):
            self.near_copy(0, chunk).wait_send()
            self.near_copy(1, chunk).wait_send()
            self.far_copy(chunk).wait_send()


def scatter_scratch(rows, width):
    return [
        pltpu.VMEM((2, rows, width), jnp.bfloat16),
        pltpu.VMEM((rows, width), jnp.bfloat16),
        pltpu.VMEM((rows, width), jnp.bfloat16),
        pltpu.SemaphoreType.DMA((3, CHUNKS)),
        pltpu.SemaphoreType.DMA((3, CHUNKS)),
    ]


def gather_scratch(rows, width):
    return [
        pltpu.VMEM((GROUP, rows, width), jnp.bfloat16),
        pltpu.SemaphoreType.DMA((3, CHUNKS)),
        pltpu.SemaphoreType.DMA((3, CHUNKS)),
    ]


def dot(left, right):
    return jnp.dot(left, right, preferred_element_type=jnp.float32)


def dot_cols(left, right):
    return lax.dot_general(left, right, contract_cols, preferred_element_type=jnp.float32)


def turn(values, cosine, sine):
    return values * cosine + pltpu.roll(values, HEAD_SIZE // 2, 1) * sine


def head_norm_back(incoming, values, gain):
    scale = lax.rsqrt(jnp.mean(values * values, axis=-1, keepdims=True) + epsilon)
    scaled = incoming * gain
    grad = scale * scaled - values * (
        scale * scale * scale * jnp.mean(scaled * values, axis=-1, keepdims=True)
    )
    return grad, jnp.sum(incoming * values * scale, axis=0, keepdims=True)


SCORE_SCALE = HEAD_SIZE**-0.5
LOG2_E = 1.4426950408889634
ROWS = 256
HALF = 128
COTANGENT = "cot"
DOWN_PART = "down_part"
MATRICES = ("wq", "wk", "wv")
SCATTER_PARTS = ("_near", "_sum", "_arr", "_send", "_recv")


def start_loads(ref, layout, pairs):
    loads = SimpleNamespace()
    table = vars(ref)
    for slot, name in enumerate(layout.loads):
        source, target = pairs[name] if name in pairs else (table[name], table["v_" + name])
        copy = pltpu.make_async_copy(source, target, ref.load_sems.at[slot])
        copy.start()
        setattr(loads, name, copy)
    return loads


def weight_grad(rows, cols, target):
    width = cols.shape[-1]
    right = cols[...].reshape(SEQUENCE_TOKENS, width)
    for j in range(4):
        left = rows[:, :, j * ROWS : (j + 1) * ROWS].reshape(SEQUENCE_TOKENS, ROWS)
        target[j] = dot(left.T, right).astype(jnp.bfloat16).reshape(4, 2, 32, width)


class RingSum:
    def __init__(self, box, slot, others, send_sems, recv_sems):
        self.box, self.slot, self.others = box, slot, others
        self.send_sems, self.recv_sems = send_sems, recv_sems

    def copy(self, index, slot):
        spot = self.box.at[slot]
        return send(
            spot, spot, self.send_sems.at[index], self.recv_sems.at[slot], self.others[index][1]
        )

    def start(self, value):
        self.box[self.slot] = value
        for index in range(len(self.others)):
            self.copy(index, self.slot).start()

    def end(self):
        for index, (slot, _) in enumerate(self.others):
            self.copy(index, slot).wait_recv()
        total = self.box[0]
        for slot in range(1, self.box.shape[0]):
            total = total + self.box[slot]
        for index in range(len(self.others)):
            self.copy(index, self.slot).wait_send()
        return total


def back_kernel(names, layout, *refs):
    ref = SimpleNamespace(**dict(zip(names, refs)))
    me = lax.axis_index("tensor")
    sibling, far, far_sibling = partner(me, FLIP), across(me), partner(me, MIRROR)
    place = rank_places()
    where = rank_where(place)
    pairs = dict(
        down_part_far=(ref.down_part.at[pl.ds(far, 1)], ref.v_down_part_far),
        down_part_own=(ref.down_part.at[pl.ds(me, 1)], ref.v_down_part_own),
    )
    for g in range(2):
        base = g * 512
        for name, source, start, size in (
            ("wq", ref.wq, 0, 256), ("wk", ref.wk, 256, 128), ("wv", ref.wv, 384, 128)
        ):
            pairs[name + str(g)] = (
                source.at[:, pl.ds(g * size, size)],
                ref.wcat.at[:, pl.ds(base + start, size)],
            )
    for i in range(len(layout.ffn)):
        name = "early" + str(i)
        pairs[name] = (vars(ref)[name], vars(ref)["f" + str(i) + "_0"])
    loads = start_loads(ref, layout, pairs)

    rings = []
    for axis, box in (("x", ref.box_x), ("z", ref.box_z)):
        here = place[axis]
        slots = (partner(here, FLIP), partner(here, MIRROR), across(here))
        rings.append(
            RingSum(
                box,
                here,
                [(slot, where(axis, slot)) for slot in slots],
                ref.gain_send.at[len(rings)],
                ref.gain_recv.at[len(rings)],
            )
        )
    y = place["y"]
    eight = []
    for row in (y, 1 - y):
        for member in (me, sibling, far, far_sibling):
            if row is not y or member is not me:
                eight.append((row * 4 + member, dict(where("y", row), tensor=member)))
    rings.append(
        RingSum(ref.box_y, y * 4 + me, eight, ref.gain_send.at[2], ref.gain_recv.at[2])
    )
    greet([there for ring in rings for _, there in ring.others])

    down = Scatter(
        ref.down_part, ref.d_near, ref.d_sum, ref.d_arr, ref.d_send, ref.d_recv, me
    )
    down.start(0)
    down.start(1)

    table = vars(ref)

    def streams_of(kind, entries, send_sems, recv_sems):
        out = []
        for i, (source, start, size, order, target, at) in enumerate(entries):
            columns = pl.ds(start, size)
            stream = Stream(
                order,
                table[source].at[:, :, :, :, columns],
                table[target].at[:, pl.ds(at, size)],
                [table[kind + str(i) + "_" + str(j)] for j in range(STREAM_SCRATCH)],
                (send_sems.at[i], recv_sems.at[i]),
                place,
                where,
            )
            if "v_" + source in table:
                stream.local = table["v_" + source].at[:, :, :, :, columns]
            out.append(stream)
        return out

    ffn = streams_of("f", layout.ffn, ref.f_send, ref.f_recv)
    attn = streams_of("a", layout.attn, ref.a_send, ref.a_recv)
    out_streams, group_streams = attn[:4], (attn[4:8], attn[8:])

    def every(streams, *steps):
        for stream in streams:
            for step, *stage in steps:
                step(stream, *stage)

    loads.down_part_far.wait()
    down.cross(ref.v_down_part_far.at[0])
    for load in [loads.gate, loads.up, loads.down] + [
        vars(loads)["early" + str(i)] for i in range(len(ffn))
    ]:
        load.wait()
    every(ffn, (Stream.quarter, 0))

    for load in (loads.w_out, loads.att, loads.gh):
        load.wait()

    def attended_grad(block):
        part = dot_cols(ref.v_gh[block], ref.v_w_out[...]).astype(jnp.bfloat16)
        for head in range(4):
            g, r = head // 2, head % 2
            at = slice(head * HEAD_SIZE, (head + 1) * HEAD_SIZE)
            low = part[:, at]
            ref.do[g, block, r * ROWS : (r + 1) * ROWS, :] = low
            product = low.astype(jnp.float32) * ref.v_att[block, :, at].astype(jnp.float32)
            ref.delta[g, block, :, r * ROWS : (r + 1) * ROWS] = jnp.sum(
                product.T, axis=0, keepdims=True
            )

    for block in (3, 2, 1, 0):
        attended_grad(block)
    weight_grad(ref.v_gh, ref.v_att, ref.gw_out)
    every(out_streams, (Stream.halve, 0))

    for load in (
        loads.q, loads.k, loads.v, loads.lse, loads.qraw, loads.kraw, loads.cos, loads.sin,
        loads.qg, loads.kg,
    ):
        load.wait()
    ref.qgain[...] = jnp.zeros_like(ref.qgain)
    ref.kgain[...] = jnp.zeros_like(ref.kgain)
    key_row = lax.broadcasted_iota(jnp.int32, (ROWS, 2 * ROWS), 0)
    query_col = lax.rem(lax.broadcasted_iota(jnp.int32, (ROWS, 2 * ROWS), 1), ROWS)
    allowed = key_row <= query_col

    def attend_group(g):
        base = 512 * g
        for qb in (3, 2, 1, 0):
            keys = (qb + 1) * ROWS
            key = ref.v_k[g, 0 : qb + 1].reshape(keys, HEAD_SIZE)
            query, grad_out = ref.v_q[g, qb], ref.do[g, qb]
            probs = jnp.exp2(
                dot_cols(key, query) * (SCORE_SCALE * LOG2_E) - ref.v_lse[g, qb]
            )
            tail = jnp.where(allowed, probs[keys - ROWS :], 0.0)
            probs = jnp.concatenate([probs[: keys - ROWS], tail], axis=0) if qb else tail
            grad_probs = dot_cols(
                ref.v_v[g, 0 : qb + 1].reshape(keys, HEAD_SIZE), grad_out
            )
            grad_scores = (probs * (grad_probs - ref.delta[g, qb])).astype(jnp.bfloat16)
            grad_value = dot(probs.astype(jnp.bfloat16), grad_out).reshape(qb + 1, ROWS, HEAD_SIZE)
            grad_key = dot(grad_scores, query).reshape(qb + 1, ROWS, HEAD_SIZE)
            if qb == 3:
                ref.dv[...] = grad_value
                ref.dk[...] = grad_key
            else:
                ref.dv[0 : qb + 1] += grad_value
                ref.dk[0 : qb + 1] += grad_key
            grads = dot(key.T, grad_scores).T * SCORE_SCALE
            for r in range(2):
                start = (2 * g + r) * HEAD_SIZE
                back = turn(
                    grads[r * ROWS : (r + 1) * ROWS], ref.v_cos[qb], ref.v_sin[qb]
                )
                grad, gain = head_norm_back(
                    back, ref.v_qraw[qb, :, start : start + HEAD_SIZE], ref.v_qg[...]
                )
                at = base + r * HEAD_SIZE
                ref.dqkv[qb, :, at : at + HEAD_SIZE] = grad.astype(jnp.bfloat16)
                ref.qgain[...] += gain

        for kb in range(4):
            start = g * HEAD_SIZE
            back = turn(ref.dk[kb] * SCORE_SCALE, ref.v_cos[kb], ref.v_sin[kb])
            grad, gain = head_norm_back(
                back, ref.v_kraw[kb, :, start : start + HEAD_SIZE], ref.v_kg[...]
            )
            ref.dqkv[kb, :, base + 256 : base + 384] = grad.astype(jnp.bfloat16)
            ref.dqkv[kb, :, base + 384 : base + 512] = ref.dv[kb].astype(jnp.bfloat16)
            ref.kgain[...] += gain

    attend_group(0)
    loads.norm_all.wait()
    weight_grad(ref.v_norm_all, ref.dqkv.at[:, :, 0:512], ref.gw_0)
    every(group_streams[0], (Stream.halve, 0))
    every(ffn, (Stream.settle, 0), (Stream.halve, 1))
    every(out_streams, (Stream.quarter, 0))
    attend_group(1)

    for load in (loads.wq0, loads.wk0, loads.wv0, loads.wq1, loads.wk1, loads.wv1):
        load.wait()
    inward = Scatter(
        ref.x_part, ref.x_near, ref.x_sum, ref.x_arr, ref.x_send, ref.x_recv, me
    )

    def inward_part(block, target):
        target[...] = dot_cols(ref.dqkv[block], ref.wcat[...]).astype(target.dtype)

    inward_part(far_sibling, ref.x_part.at[far_sibling])
    inward.start(0)
    inward_part(far, ref.x_part.at[far])
    inward.cross(ref.x_part.at[far])
    inward_part(sibling, ref.x_part.at[sibling])
    inward.start(1)
    weight_grad(ref.v_norm_all, ref.dqkv.at[:, :, 512:1024], ref.gw_1)
    every(group_streams[1], (Stream.halve, 0))
    inward_part(me, ref.x_own)

    every(ffn, (Stream.quarter, 1))
    every(out_streams, (Stream.settle, 0), (Stream.halve, 1))
    every(group_streams[0], (Stream.quarter, 0))
    every(ffn, (Stream.settle, 1))
    every(out_streams, (Stream.quarter, 1))
    every(group_streams[0], (Stream.settle, 0), (Stream.halve, 1))

    loads.hidden.wait()
    loads.down_part_own.wait()
    for chunk in range(CHUNKS):
        part = down.part(chunk)
        total = down.total(chunk, ref.v_down_part_own.at[0])
        ref.result[part] = (ref.v_hidden[part] + total).astype(jnp.bfloat16)
    every(group_streams[1], (Stream.quarter, 0))
    every(out_streams, (Stream.settle, 1))
    every(group_streams[0], (Stream.quarter, 1))

    for load in (loads.tokens, loads.norm_in, loads.gain_mid):
        load.wait()
    ref.gains[...] = jnp.zeros_like(ref.gains)
    ref.gains[1:2] = ref.v_gain_mid[...]
    ref.gains[2:3, 0:128] = ref.qgain[...]
    ref.gains[2:3, 128:256] = ref.kgain[...]
    for chunk in range(CHUNKS):
        part = inward.part(chunk)
        incoming = inward.total(chunk, ref.x_own)
        values = ref.v_tokens[part].astype(jnp.float32)
        grad, gain = head_norm_back(incoming, values, ref.v_norm_in[...])
        ref.grad_tokens[part] = (ref.v_gh[me, part].astype(jnp.float32) + grad).astype(
            jnp.bfloat16
        )
        ref.gains[0:1] += gain

    rings[0].start(ref.gains[...])
    every(group_streams[1], (Stream.settle, 0), (Stream.halve, 1))
    every(ffn, (Stream.finish,))
    rings[1].start(rings[0].end())
    every(group_streams[1], (Stream.quarter, 1))
    every(group_streams[0], (Stream.settle, 1))
    every(out_streams, (Stream.finish,))
    rings[2].start(rings[1].end())
    every(group_streams[1], (Stream.settle, 1))
    every(group_streams[0], (Stream.finish,))
    total = rings[2].end()
    ref.o_norm_in[...] = total[0:1]
    ref.o_norm_mid[...] = total[1:2]
    ref.o_qgain[...] = total[2:3, 0:128]
    ref.o_kgain[...] = total[2:3, 128:256]
    every(group_streams[1], (Stream.finish,))
    down.drain()
    inward.drain()


def hand_over_kernel(n, *refs):
    sources, targets, buffers, sems = refs[:n], refs[n : 2 * n], refs[2 * n : 3 * n], refs[3 * n]
    pulls = [pltpu.make_async_copy(sources[i], buffers[i], sems.at[0, i]) for i in range(n)]
    pushes = [pltpu.make_async_copy(buffers[i], targets[i], sems.at[1, i]) for i in range(n)]
    for pull in pulls:
        pull.start()
    for pull, push in zip(pulls, pushes):
        pull.wait()
        push.start()
    for push in pushes:
        push.wait()


def hand_over(arrays):
    n = len(arrays)
    anywhere = [pl.BlockSpec(memory_space=pl.ANY)] * n
    return pl.pallas_call(
        functools.partial(hand_over_kernel, n),
        out_shape=[jax.ShapeDtypeStruct(array.shape, array.dtype) for array in arrays],
        in_specs=anywhere,
        out_specs=anywhere,
        scratch_shapes=[pltpu.VMEM(array.shape, array.dtype) for array in arrays]
        + [pltpu.SemaphoreType.DMA((2, n))],
    )(*arrays)


def ffn_streams():
    xa, xb = ("x", FLIP, FLIP), ("x", MIRROR, MIRROR)
    za, zb = ("z", FLIP, MIRROR), ("z", MIRROR, FLIP)
    return [
        ("gate", 0, 384, xa, "o_gate", 0), ("gate", 384, 384, xb, "o_gate", 384),
        ("up", 0, 384, za, "o_up", 0), ("up", 384, 384, zb, "o_up", 384),
        ("down", 0, 256, xa, "o_down", 0), ("down", 256, 128, xb, "o_down", 256),
        ("down", 384, 256, za, "o_down", 384), ("down", 640, 128, zb, "o_down", 640),
    ]


def back_part(inputs, ffn):
    low, wide = jnp.bfloat16, jnp.float32
    names = list(inputs)
    weights = [name for name in names if name in MATRICES]
    loaded = [name for name in names if name != DOWN_PART and name not in MATRICES]
    loaded += [DOWN_PART + "_far", DOWN_PART + "_own"]
    shapes = {name: (inputs[name].shape, inputs[name].dtype) for name in loaded[:-2]}
    shapes.update({name: ((1, ROWS, 1024), low) for name in loaded[-2:]})
    loaded += [name + str(g) for g in range(2) for name in weights]
    early = [name for name in loaded if name.startswith(("down", "gate", "up", "early"))]
    loaded = loaded[:3] + early + [name for name in loaded[3:] if name not in early]
    outs = dict(
        result=((ROWS, 1024), low),
        grad_tokens=((ROWS, 1024), low),
        o_gate=((32, 768), wide),
        o_up=((32, 768), wide),
        o_down=((32, 768), wide),
        o_q=((32, 512), wide),
        o_k=((32, 256), wide),
        o_v=((32, 256), wide),
        o_out=((32, 512), wide),
        o_norm_in=((1, 1024), wide),
        o_norm_mid=((1, 1024), wide),
        o_qgain=((1, HEAD_SIZE), wide),
        o_kgain=((1, HEAD_SIZE), wide),
    )
    xa, xb = ("x", FLIP, FLIP), ("x", MIRROR, MIRROR)
    za, zb = ("z", FLIP, MIRROR), ("z", MIRROR, FLIP)
    layout = SimpleNamespace(
        loads=loaded,
        ffn=ffn,
        attn=[("gw_out", 128 * i, 128, way, "o_out", 128 * i) for i, way in enumerate((xb, zb, xa, za))]
        + [
            ("gw_" + str(g), 128 * i, 128, way, target, at + step * g)
            for g in range(2)
            for i, (way, target, at, step) in enumerate(
                ((xa, "o_q", 0, 256), (xb, "o_q", 128, 256), (za, "o_k", 0, 128), (zb, "o_v", 0, 128))
            )
        ],
    )
    scratch = {"v_" + name: pltpu.VMEM(*spec) for name, spec in shapes.items()}
    scratch.update(
        load_sems=pltpu.SemaphoreType.DMA((len(loaded),)),
        do=pltpu.VMEM((2, 4, 2 * ROWS, HEAD_SIZE), low),
        delta=pltpu.VMEM((2, 4, 1, 2 * ROWS), wide),
        dk=pltpu.VMEM((4, ROWS, HEAD_SIZE), wide),
        dv=pltpu.VMEM((4, ROWS, HEAD_SIZE), wide),
        dqkv=pltpu.VMEM((4, ROWS, 1024), low),
        wcat=pltpu.VMEM((1024, 1024), low),
        qgain=pltpu.VMEM((1, HEAD_SIZE), wide),
        kgain=pltpu.VMEM((1, HEAD_SIZE), wide),
        x_part=pltpu.VMEM((4, ROWS, 1024), low),
        x_own=pltpu.VMEM((ROWS, 1024), wide),
        gw_out=pltpu.VMEM((4, 4, 2, 32, 512), low),
        gw_0=pltpu.VMEM((4, 4, 2, 32, 512), low),
        gw_1=pltpu.VMEM((4, 4, 2, 32, 512), low),
        gains=pltpu.VMEM((8, 1024), wide),
        box_x=pltpu.VMEM((4, 8, 1024), wide),
        box_z=pltpu.VMEM((4, 8, 1024), wide),
        box_y=pltpu.VMEM((8, 8, 1024), wide),
        gain_send=pltpu.SemaphoreType.DMA((3, 8)),
        gain_recv=pltpu.SemaphoreType.DMA((3, 8)),
    )
    for tag in "dx":
        scratch.update(zip((tag + end for end in SCATTER_PARTS), scatter_scratch(ROWS, 1024)))
    for kind, entries in (("f", layout.ffn), ("a", layout.attn)):
        for way in SCATTER_PARTS[3:]:
            scratch[kind + way] = pltpu.SemaphoreType.DMA((len(entries), STREAM_SEMS))
        for i, entry in enumerate(entries):
            for j, buffer in enumerate(stream_scratch(entry[2])):
                scratch[kind + str(i) + "_" + str(j)] = buffer
    for i in range(len(ffn)):
        scratch["f" + str(i) + "_0"] = scratch.pop("v_early" + str(i))
    results = pl.pallas_call(
        functools.partial(back_kernel, names + list(outs) + list(scratch), layout),
        out_shape=[jax.ShapeDtypeStruct(*spec) for spec in outs.values()],
        in_specs=[pl.BlockSpec(memory_space=pl.ANY)] * len(names),
        out_specs=[VMEM_SPACE] * len(outs),
        scratch_shapes=list(scratch.values()),
        compiler_params=pltpu.CompilerParams(
            collective_id=3, has_side_effects=True, vmem_limit_bytes=61 << 20
        ),
    )(*inputs.values())
    return SimpleNamespace(**dict(zip(outs, hand_over(results))))


class Exchange:
    def __init__(self, own, near_out, near_in, summed, arrived, send_sems, recv_sems, me):
        self.own, self.near_out, self.near_in = own, near_out, near_in
        self.summed, self.arrived = summed, arrived
        self.send_sems, self.recv_sems = send_sems, recv_sems
        self.sibling, self.far = {"tensor": partner(me, FLIP)}, {"tensor": across(me)}
        core = lax.rem(me, 2)
        self.mine = pl.ds(pl.multiple_of(core * HALF, HALF), HALF)
        self.other = pl.ds(pl.multiple_of((1 - core) * HALF, HALF), HALF)

    def near(self, block):
        return send(
            self.near_out.at[block],
            self.near_in.at[block],
            self.send_sems.at[0, block],
            self.recv_sems.at[0, block],
            self.sibling,
        )

    def swap(self, block):
        return send(
            self.summed.at[block],
            self.arrived.at[block],
            self.send_sems.at[1, block],
            self.recv_sems.at[1, block],
            self.far,
        )

    def share(self, block, whole):
        spot = whole.at[block, self.mine]
        return send(
            spot, spot, self.send_sems.at[2, block], self.recv_sems.at[2, block], self.sibling
        )

    def give(self, block, part):
        self.near_out[block] = part[self.other].astype(jnp.bfloat16)
        self.near(block).start()
        self.own[block] = part[self.mine]

    def cross(self, block):
        self.near(block).wait()
        self.summed[block] = (
            self.own[block] + self.near_in[block].astype(jnp.float32)
        ).astype(jnp.bfloat16)
        self.swap(block).start()

    def total(self, block):
        self.swap(block).wait()
        return self.summed[block].astype(jnp.float32) + self.arrived[block].astype(jnp.float32)


def exchange_scratch():
    half = pltpu.VMEM((4, HALF, 1024), jnp.bfloat16)
    sems = pltpu.SemaphoreType.DMA((3, 4))
    return [half, half, half, sems, sems]


def front_kernel(names, layout, *refs):
    ref = SimpleNamespace(**dict(zip(names, refs)))
    me = lax.axis_index("tensor")
    sibling, far, far_sibling = partner(me, FLIP), across(me), partner(me, MIRROR)
    place = rank_places()
    where = rank_where(place)
    loads = start_loads(
        ref,
        layout,
        dict(tokens=(ref.tokens, ref.tokens_all.at[me]), cot=(ref.cot, ref.dy_all.at[me])),
    )
    greet(
        [{"tensor": sibling}, {"tensor": far}]
        + [
            where(axis, partner(place[axis], pairing))
            for axis in ("x", "z")
            for pairing in (FLIP, MIRROR)
        ]
    )
    stores = []

    def store(source, target):
        copy = pltpu.make_async_copy(source, target, ref.store_sems.at[len(stores)])
        copy.start()
        stores.append(copy)

    first = Gather(ref.tokens_all, ref.n_send, ref.n_recv, me)
    cot = Gather(ref.dy_all, ref.c_send, ref.c_recv, me)
    loads.tokens.wait()
    first.start()
    for load in (
        loads.norm_in, loads.wq, loads.wk, loads.wv, loads.cos, loads.sin, loads.qg, loads.kg
    ):
        load.wait()

    def project(block):
        values = ref.tokens_all[block].astype(jnp.float32)
        rows = (values * rms_scale(values) * ref.v_norm_in[...]).astype(jnp.bfloat16)
        ref.norm_all[block] = rows
        raw = dot(rows, ref.v_wq[...])
        ref.qraw[block] = raw
        for head in range(4):
            values = raw[:, head * HEAD_SIZE : (head + 1) * HEAD_SIZE]
            values = values * rms_scale(values) * ref.v_qg[...]
            ref.q[head // 2, block, (head % 2) * ROWS : (head % 2 + 1) * ROWS, :] = turn(
                values, ref.v_cos[block], -ref.v_sin[block]
            ).astype(jnp.bfloat16)
        raw = dot(rows, ref.v_wk[...])
        ref.kraw[block] = raw
        for g in range(2):
            values = raw[:, g * HEAD_SIZE : (g + 1) * HEAD_SIZE]
            values = values * rms_scale(values) * ref.v_kg[...]
            ref.k[g, block] = turn(values, ref.v_cos[block], -ref.v_sin[block]).astype(jnp.bfloat16)
        low = dot(rows, ref.v_wv[...]).astype(jnp.bfloat16)
        for g in range(2):
            ref.v[g, block] = low[:, g * HEAD_SIZE : (g + 1) * HEAD_SIZE]

    project(me)
    first.wait_sibling()
    project(sibling)
    first.wait_far()
    loads.cot.wait()
    cot.start()
    project(far)
    first.wait_last()
    project(far_sibling)
    store(ref.norm_all, ref.o_norm_all)
    store(ref.q, ref.o_q)
    store(ref.k, ref.o_k)
    store(ref.v, ref.o_v)
    store(ref.qraw, ref.o_qraw)
    store(ref.kraw, ref.o_kraw)

    key_row = lax.broadcasted_iota(jnp.int32, (ROWS, 2 * ROWS), 0)
    query_col = lax.rem(lax.broadcasted_iota(jnp.int32, (ROWS, 2 * ROWS), 1), ROWS)
    allowed = key_row <= query_col
    loads.w_out.wait()
    mixed = Exchange(
        ref.own, ref.p_out, ref.p_near, ref.p_sum, ref.p_arr, ref.p_send, ref.p_recv, me
    )
    back = Exchange(
        ref.own, ref.p_out, ref.b_near, ref.b_sum, ref.b_arr, ref.b_send, ref.b_recv, me
    )

    def attend(block):
        keys = (block + 1) * ROWS
        for g in range(2):
            scores = dot_cols(
                ref.k[g, 0 : block + 1].reshape(keys, HEAD_SIZE), ref.q[g, block]
            )
            probs = jnp.exp2(scores * (SCORE_SCALE * LOG2_E))
            tail = jnp.where(allowed, probs[keys - ROWS :], 0.0)
            probs = jnp.concatenate([probs[: keys - ROWS], tail], axis=0) if block else tail
            total = jnp.sum(probs, axis=0, keepdims=True)
            ref.lse[g, block] = jnp.log(total) * LOG2_E
            values = ref.v[g, 0 : block + 1].reshape(keys, HEAD_SIZE)
            rows = (dot(values.T, probs.astype(jnp.bfloat16)) / total).T.astype(jnp.bfloat16)
            for r in range(2):
                start = (2 * g + r) * HEAD_SIZE
                ref.att[block, :, start : start + HEAD_SIZE] = rows[r * ROWS : (r + 1) * ROWS]
        ref.part[...] = dot(ref.att[block], ref.v_w_out[...])
        mixed.give(block, ref.part)

    attend(3)
    attend(2)
    mixed.cross(3)
    attend(1)
    mixed.cross(2)
    attend(0)
    mixed.cross(1)
    cot.wait_far()
    mixed.cross(0)
    store(ref.att, ref.o_att)
    store(ref.lse, ref.o_lse)
    cot.wait_sibling()
    cot.wait_last()
    for load in (loads.w_down, loads.norm_mid, loads.w_gate, loads.w_up):
        load.wait()

    def mid_norm(block):
        values = ref.tokens_all[block, mixed.mine].astype(jnp.float32) + mixed.total(block)
        ref.hidden[block] = values
        ref.mid_all[block, mixed.mine] = (
            values * rms_scale(values) * ref.v_norm_mid[...]
        ).astype(jnp.bfloat16)
        mixed.share(block, ref.mid_all).start()

    def feed(block):
        grad = dot_cols(ref.dy_all[block], ref.v_w_down[...])
        mixed.share(block, ref.mid_all).wait()
        gate = dot(ref.mid_all[block], ref.v_w_gate[...])
        up = dot(ref.mid_all[block], ref.v_w_up[...])
        sigmoid = jax.nn.sigmoid(gate)
        silu = gate * sigmoid
        ref.act[block] = (silu * up).astype(jnp.bfloat16)
        ref.dup[block] = (grad * silu).astype(jnp.bfloat16)
        ref.dgate[block] = (grad * up * sigmoid * (1.0 + gate * (1.0 - sigmoid))).astype(jnp.bfloat16)
        value = dot_cols(ref.dgate[block], ref.v_w_gate[...])
        ref.part[...] = value + dot_cols(ref.dup[block], ref.v_w_up[...])
        back.give(block, ref.part)

    for block in (3, 2, 1, 0):
        mid_norm(block)
        feed(block)
        if block < 3:
            back.cross(block + 1)
    back.cross(0)

    streams = []
    table = vars(ref)
    for i, (source, start, size, order) in enumerate(layout.ffn):
        streams.append(
            Stream(
                order,
                table["gw_" + source].at[:, :, :, :, pl.ds(start, size)],
                None,
                [table["early" + str(i)]] + [None] * (STREAM_SCRATCH - 1),
                (ref.f_send.at[i], ref.f_recv.at[i]),
                place,
                where,
            )
        )

    weight_grad(ref.mid_all, ref.dgate, ref.gw_gate)
    for stream in streams[:2]:
        stream.halve(0)
    weight_grad(ref.mid_all, ref.dup, ref.gw_up)
    for stream in streams[2:4]:
        stream.halve(0)
    weight_grad(ref.dy_all, ref.act, ref.gw_down)
    for stream in streams[4:]:
        stream.halve(0)
    store(ref.gw_gate, ref.o_gate)
    store(ref.gw_up, ref.o_up)
    store(ref.gw_down, ref.o_down)
    for block in range(4):
        ref.down_part[block] = dot(ref.act[block], ref.v_w_down[...]).astype(jnp.bfloat16)
    store(ref.down_part, ref.o_down_part)

    own_half = send(
        ref.hidden.at[sibling], ref.hid.at[mixed.mine], ref.h_send, ref.h_recv, mixed.sibling
    )
    own_half.start()
    ref.hid[mixed.mine] = ref.hidden[me]

    ref.gain[...] = jnp.zeros_like(ref.gain)
    for block in (3, 2, 1, 0):
        incoming = back.total(block)
        grad, gain = head_norm_back(incoming, ref.hidden[block], ref.v_norm_mid[...])
        ref.gh_all[block, back.mine] = (
            ref.dy_all[block, back.mine].astype(jnp.float32) + grad
        ).astype(jnp.bfloat16)
        back.share(block, ref.gh_all).start()
        ref.gain[...] += gain
    ref.gain[...] *= 0.5
    store(ref.gain, ref.o_gain)
    own_half.wait()
    store(ref.hid, ref.o_hidden)
    for block in (3, 2, 1, 0):
        back.share(block, ref.gh_all).wait()
    store(ref.gh_all, ref.o_gh)
    for i, stream in enumerate(streams):
        for copy in stream.copies:
            copy.wait()
        store(table["early" + str(i)], table["o_early" + str(i)])
    for copy in stores:
        copy.wait()
    first.drain()
    cot.drain()


def front_part(inputs, ffn):
    low, wide = jnp.bfloat16, jnp.float32
    names = list(inputs)
    outs = dict(
        o_norm_all=((4, ROWS, 1024), low),
        o_q=((2, 4, 2 * ROWS, HEAD_SIZE), low),
        o_k=((2, 4, ROWS, HEAD_SIZE), low),
        o_v=((2, 4, ROWS, HEAD_SIZE), low),
        o_qraw=((4, ROWS, 512), wide),
        o_kraw=((4, ROWS, 256), wide),
        o_att=((4, ROWS, 512), low),
        o_lse=((2, 4, 1, 2 * ROWS), wide),
        o_hidden=((ROWS, 1024), wide),
        o_down=((4, 4, 2, 32, 768), low),
        o_gate=((4, 4, 2, 32, 768), low),
        o_up=((4, 4, 2, 32, 768), low),
        o_down_part=((4, ROWS, 1024), low),
        o_gh=((4, ROWS, 1024), low),
        o_gain=((1, 1024), wide),
    )
    early = {"early" + str(i): ((2, 4, 2, 32, entry[2]), low) for i, entry in enumerate(ffn)}
    outs.update({"o_" + name: spec for name, spec in early.items()})
    whole = ("tokens", COTANGENT)
    scratch = {
        "v_" + name: pltpu.VMEM(inputs[name].shape, inputs[name].dtype)
        for name in names
        if name not in whole
    }
    scratch.update({name: pltpu.VMEM(*spec) for name, spec in early.items()})
    scratch.update(
        load_sems=pltpu.SemaphoreType.DMA((len(names),)),
        store_sems=pltpu.SemaphoreType.DMA((len(outs),)),
        f_send=pltpu.SemaphoreType.DMA((len(ffn), 2)),
        f_recv=pltpu.SemaphoreType.DMA((len(ffn), 2)),
        h_send=pltpu.SemaphoreType.DMA,
        h_recv=pltpu.SemaphoreType.DMA,
        norm_all=pltpu.VMEM((4, ROWS, 1024), low),
        mid_all=pltpu.VMEM((4, ROWS, 1024), low),
        gh_all=pltpu.VMEM((4, ROWS, 1024), low),
        qraw=pltpu.VMEM((4, ROWS, 512), wide),
        kraw=pltpu.VMEM((4, ROWS, 256), wide),
        q=pltpu.VMEM((2, 4, 2 * ROWS, HEAD_SIZE), low),
        k=pltpu.VMEM((2, 4, ROWS, HEAD_SIZE), low),
        v=pltpu.VMEM((2, 4, ROWS, HEAD_SIZE), low),
        lse=pltpu.VMEM((2, 4, 1, 2 * ROWS), wide),
        att=pltpu.VMEM((4, ROWS, 512), low),
        part=pltpu.VMEM((ROWS, 1024), wide),
        own=pltpu.VMEM((4, HALF, 1024), wide),
        hidden=pltpu.VMEM((4, HALF, 1024), wide),
        hid=pltpu.VMEM((ROWS, 1024), wide),
        p_out=pltpu.VMEM((4, HALF, 1024), low),
        act=pltpu.VMEM((4, ROWS, 768), low),
        dup=pltpu.VMEM((4, ROWS, 768), low),
        dgate=pltpu.VMEM((4, ROWS, 768), low),
        gw_down=pltpu.VMEM((4, 4, 2, 32, 768), low),
        gw_gate=pltpu.VMEM((4, 4, 2, 32, 768), low),
        gw_up=pltpu.VMEM((4, 4, 2, 32, 768), low),
        down_part=pltpu.VMEM((4, ROWS, 1024), low),
        gain=pltpu.VMEM((1, 1024), wide),
    )
    scratch.update(zip(("tokens_all", "n_send", "n_recv"), gather_scratch(ROWS, 1024)))
    scratch.update(zip(("dy_all", "c_send", "c_recv"), gather_scratch(ROWS, 1024)))
    for tag in "pb":
        scratch.update(zip((tag + end for end in SCATTER_PARTS), exchange_scratch()))
    results = pl.pallas_call(
        functools.partial(
            front_kernel,
            names + list(outs) + list(scratch),
            SimpleNamespace(loads=names, ffn=[entry[:4] for entry in ffn]),
        ),
        out_shape=[jax.ShapeDtypeStruct(*spec) for spec in outs.values()],
        in_specs=[pl.BlockSpec(memory_space=pl.ANY)] * len(names),
        out_specs=[pl.BlockSpec(memory_space=pl.ANY)] * len(outs),
        scratch_shapes=list(scratch.values()),
        compiler_params=pltpu.CompilerParams(
            collective_id=4, has_side_effects=True, vmem_limit_bytes=62 << 20
        ),
    )(*inputs.values())
    return SimpleNamespace(**dict(zip(outs, results)))


def rotary_tables():
    position = np.arange(SEQUENCE_TOKENS, dtype=np.float64)
    inverse = 1000000.0 ** (-np.arange(HEAD_SIZE // 2, dtype=np.float64) * 2.0 / HEAD_SIZE)
    angles = position[:, None] * inverse[None, :]
    cosine, sine = np.cos(angles), np.sin(angles)
    return (
        jnp.asarray(
            np.concatenate([table, tail], axis=1).astype(np.float32).reshape(4, ROWS, HEAD_SIZE)
        )
        for table, tail in ((cosine, cosine), (sine, -sine))
    )


def per_device(
    tokens,
    norm_in,
    w_query,
    key_matrix,
    value_matrix,
    query_gain,
    key_gain,
    w_out,
    norm_mid,
    w_gate,
    w_up,
    w_down,
    cotangent,
):
    wide = jnp.float32
    cosine, sine = rotary_tables()
    norm_in = norm_in.astype(wide).reshape(1, 1024)
    norm_mid = norm_mid.astype(wide).reshape(1, 1024)
    query_gain = query_gain.astype(wide).reshape(1, HEAD_SIZE)
    key_gain = key_gain.astype(wide).reshape(1, HEAD_SIZE)
    ffn = ffn_streams()
    front = front_part(
        dict(
            tokens=tokens,
            norm_in=norm_in,
            wq=w_query,
            wk=key_matrix,
            wv=value_matrix,
            cos=cosine,
            sin=sine,
            qg=query_gain,
            kg=key_gain,
            cot=cotangent,
            w_out=w_out,
            w_down=w_down,
            norm_mid=norm_mid,
            w_gate=w_gate,
            w_up=w_up,
        ),
        ffn,
    )
    outs = back_part(
        dict(
            gh=front.o_gh,
            w_out=w_out,
            att=front.o_att,
            down_part=front.o_down_part,
            gate=front.o_gate,
            up=front.o_up,
            down=front.o_down,
            q=front.o_q,
            k=front.o_k,
            v=front.o_v,
            lse=front.o_lse,
            qraw=front.o_qraw,
            kraw=front.o_kraw,
            cos=cosine,
            sin=sine,
            qg=query_gain,
            kg=key_gain,
            wq=w_query,
            wk=key_matrix,
            wv=value_matrix,
            norm_all=front.o_norm_all,
            hidden=front.o_hidden,
            tokens=tokens,
            norm_in=norm_in,
            gain_mid=front.o_gain,
            **{"early" + str(i): vars(front)["o_early" + str(i)] for i in range(len(ffn))},
        ),
        ffn,
    )
    return (
        outs.result,
        outs.grad_tokens,
        outs.o_norm_in.reshape(1024),
        outs.o_q,
        outs.o_k,
        outs.o_v,
        outs.o_qgain.reshape(HEAD_SIZE),
        outs.o_kgain.reshape(HEAD_SIZE),
        outs.o_out.T,
        outs.o_norm_mid.reshape(1024),
        outs.o_gate,
        outs.o_up,
        outs.o_down.T,
    )


def solution(mesh):
    placed = (
        P(("dp", "tensor"), None),
        P(),
        P(None, "tensor"),
        P(None, "tensor"),
        P(None, "tensor"),
        P(),
        P(),
        P("tensor", None),
        P(),
        P(None, "tensor"),
        P(None, "tensor"),
        P("tensor", None),
        P(("dp", "tensor"), None),
    )
    return jax.shard_map(
        per_device,
        mesh=mesh,
        in_specs=placed,
        out_specs=(
            P(("dp", "tensor"), None),
            P(("dp", "tensor"), None),
            P(),
            P("dp", "tensor"),
            P("dp", "tensor"),
            P("dp", "tensor"),
            P(),
            P(),
            P("tensor", "dp"),
            P(),
            P("dp", "tensor"),
            P("dp", "tensor"),
            P("tensor", "dp"),
        ),
        check_vma=False,
    )
```

```python
import functools
from types import SimpleNamespace

import jax
import jax.numpy as jnp
import numpy as np
from jax import lax
from jax.experimental import pallas as pl
from jax.experimental.pallas import tpu as pltpu
from jax.sharding import PartitionSpec as P

HEAD_SIZE = 128
SEQUENCE_TOKENS = 1024
GROUP = 4
CHUNKS = 4
VMEM_SPACE = pl.BlockSpec(memory_space=pltpu.VMEM)
FLIP, MIRROR = 1, 3
epsilon = 1e-06
contract_cols = (((1,), (1,)), ((), ()))


def partner(index, pairing):
    if pairing == FLIP:
        return index + 1 - 2 * lax.rem(index, 2)
    return 3 - index


def across(index):
    return lax.rem(index + 2, 4)


def send(source, target, send_sem, recv_sem, where):
    return pltpu.make_async_remote_copy(
        src_ref=source,
        dst_ref=target,
        send_sem=send_sem,
        recv_sem=recv_sem,
        device_id=where,
        device_id_type=pl.DeviceIdType.MESH,
    )


def greet(others):
    barrier = pltpu.get_barrier_semaphore()
    for where in others:
        pl.semaphore_signal(barrier, inc=1, device_id=where, device_id_type=pl.DeviceIdType.MESH)
    pl.semaphore_wait(barrier, len(others))


class Stream:
    def __init__(self, order, grad, out, scratch, sems, place, where):
        self.first, self.orders = order[0], order[1:]
        self.grad, self.local, self.out = grad, grad, out
        self.early, self.mid, self.late, self.held, self.low, self.pair, self.last = scratch
        self.send_sems, self.recv_sems = sems
        self.place, self.where = place, where
        self.pending = []
        self.copies = [None, None]

    def axis(self, stage):
        return self.first if stage == 0 else ("z" if self.first == "x" else "x")

    def block(self, stage, index, local=True):
        if stage == 1:
            return self.held.at[index]
        grad = self.local if local else self.grad
        return grad.at[index] if self.first == "x" else grad.at[:, index]

    def launch(self, source, target, slot, where):
        copy = send(source, target, self.send_sems.at[slot], self.recv_sems.at[slot], where)
        copy.start()
        self.pending.append(copy)
        return copy

    def halve(self, stage):
        axis, here = self.axis(stage), self.place[self.axis(stage)]
        other = partner(here, self.orders[stage])
        box = self.early if stage == 0 else self.late
        self.copies = [
            self.launch(
                self.block(stage, index, False), box.at[slot], 4 * stage + slot, self.where(axis, other)
            )
            for slot, index in ((1, across(here)), (0, other))
        ]

    def quarter(self, stage):
        axis, here = self.axis(stage), self.place[self.axis(stage)]
        other = partner(here, FLIP + MIRROR - self.orders[stage])
        box, mid = (self.early, self.mid) if stage == 0 else (self.late, self.low)
        if self.copies[0]:
            self.copies[0].wait_recv()
        mine = self.block(stage, other)

        def add(row, _):
            mid[0, row] = mine[row] + box[1, row]
            return _

        lax.fori_loop(0, mid.shape[1], add, 0)
        self.copies.append(
            self.launch(mid.at[0], mid.at[1], 4 * stage + 2, self.where(axis, other))
        )

    def settle(self, stage):
        here = self.place[self.axis(stage)]
        if self.copies[1]:
            self.copies[1].wait_recv()
        self.copies[2].wait_recv()
        box, mid = (self.early, self.mid) if stage == 0 else (self.late, self.low)
        mine = self.block(stage, here)
        if stage == 0:

            def add(row, _):
                self.held[row] = mine[row] + box[0, row] + mid[1, row]
                return _

            lax.fori_loop(0, mid.shape[1], add, 0)
            return
        keep = self.place["y"]
        give = 1 - keep
        self.pair[0] = (
            mine[give].astype(jnp.float32)
            + box[0, give].astype(jnp.float32)
            + mid[1, give].astype(jnp.float32)
        ).astype(jnp.bfloat16)
        self.copies.append(
            self.launch(self.pair.at[0], self.pair.at[1], 3, self.where("y", give))
        )
        self.last[...] = (
            mine[keep].astype(jnp.float32)
            + box[0, keep].astype(jnp.float32)
            + mid[1, keep].astype(jnp.float32)
        )

    def finish(self):
        self.copies[3].wait_recv()
        self.out[...] = self.last[...] + self.pair[1].astype(jnp.float32)
        for copy in self.pending:
            copy.wait_send()


STREAM_SEMS = 7
STREAM_SCRATCH = 7


def stream_scratch(columns):
    low = jnp.bfloat16
    return [
        pltpu.VMEM((2, 4, 2, 32, columns), low),
        pltpu.VMEM((2, 4, 2, 32, columns), low),
        pltpu.VMEM((2, 2, 32, columns), low),
        pltpu.VMEM((4, 2, 32, columns), low),
        pltpu.VMEM((2, 2, 32, columns), low),
        pltpu.VMEM((2, 32, columns), low),
        pltpu.VMEM((32, columns), jnp.float32),
    ]


def rank_places():
    rank = lax.axis_index("dp")
    return {"x": lax.div(rank, 8), "z": lax.rem(lax.div(rank, 2), 4), "y": lax.rem(rank, 2)}


def rank_where(place):
    def where(axis, index):
        at = dict(place)
        at[axis] = index
        return {"dp": at["x"] * 8 + at["z"] * 2 + at["y"]}

    return where


def rms_scale(values):
    return lax.rsqrt(jnp.mean(values * values, axis=-1, keepdims=True) + epsilon)


class Gather:
    def __init__(self, whole, send_sems, recv_sems, me):
        self.whole, self.send_sems, self.recv_sems, self.me = whole, send_sems, recv_sems, me
        self.sibling, self.far = {"tensor": partner(me, FLIP)}, {"tensor": across(me)}
        self.rows = whole.shape[1] // CHUNKS

    def copy(self, lane, chunk, block, where):
        part = pl.ds(chunk * self.rows, self.rows)
        spot = self.whole.at[block, part]
        return send(spot, spot, self.send_sems.at[lane, chunk], self.recv_sems.at[lane, chunk], where)

    def start_chunk(self, chunk):
        self.copy(0, chunk, self.me, self.far).start()
        self.copy(1, chunk, self.me, self.sibling).start()

    def start(self):
        for chunk in range(CHUNKS):
            self.copy(0, chunk, self.me, self.far).start()
        for chunk in range(CHUNKS):
            self.copy(1, chunk, self.me, self.sibling).start()

    def wait_sibling(self):
        for chunk in range(CHUNKS):
            self.copy(1, chunk, self.me, self.sibling).wait_recv()

    def wait_far(self):
        for chunk in range(CHUNKS):
            self.copy(0, chunk, self.me, self.far).wait_recv()
            self.copy(2, chunk, across(self.me), self.sibling).start()

    def wait_last(self):
        for chunk in range(CHUNKS):
            self.copy(2, chunk, across(self.me), self.sibling).wait_recv()

    def drain(self):
        for chunk in range(CHUNKS):
            self.copy(0, chunk, self.me, self.far).wait_send()
            self.copy(1, chunk, self.me, self.sibling).wait_send()
            self.copy(2, chunk, across(self.me), self.sibling).wait_send()


class Scatter:
    def __init__(self, partial, near, summed, arrived, send_sems, recv_sems, me):
        self.partial, self.near, self.summed, self.arrived = partial, near, summed, arrived
        self.send_sems, self.recv_sems, self.me = send_sems, recv_sems, me
        self.sibling, self.far = {"tensor": partner(me, FLIP)}, {"tensor": across(me)}
        self.rows = near.shape[1] // CHUNKS

    def part(self, chunk):
        return pl.ds(chunk * self.rows, self.rows)

    def near_copy(self, slot, chunk):
        block = partner(self.me, MIRROR if slot == 0 else FLIP)
        return send(
            self.partial.at[block, self.part(chunk)],
            self.near.at[slot, self.part(chunk)],
            self.send_sems.at[slot, chunk],
            self.recv_sems.at[slot, chunk],
            self.sibling,
        )

    def far_copy(self, chunk):
        return send(
            self.summed.at[self.part(chunk)],
            self.arrived.at[self.part(chunk)],
            self.send_sems.at[2, chunk],
            self.recv_sems.at[2, chunk],
            self.far,
        )

    def start(self, slot):
        for chunk in range(CHUNKS):
            self.near_copy(slot, chunk).start()

    def cross(self, mine):
        for chunk in range(CHUNKS):
            part = self.part(chunk)
            self.near_copy(0, chunk).wait_recv()
            self.summed[part] = (
                mine[part].astype(jnp.float32) + self.near[0, part].astype(jnp.float32)
            ).astype(jnp.bfloat16)
            self.far_copy(chunk).start()

    def total(self, chunk, mine):
        part = self.part(chunk)
        self.near_copy(1, chunk).wait_recv()
        self.far_copy(chunk).wait_recv()
        return (
            mine[part].astype(jnp.float32)
            + self.near[1, part].astype(jnp.float32)
            + self.arrived[part].astype(jnp.float32)
        )

    def drain(self):
        for chunk in range(CHUNKS):
            self.near_copy(0, chunk).wait_send()
            self.near_copy(1, chunk).wait_send()
            self.far_copy(chunk).wait_send()


def scatter_scratch(rows, width):
    return [
        pltpu.VMEM((2, rows, width), jnp.bfloat16),
        pltpu.VMEM((rows, width), jnp.bfloat16),
        pltpu.VMEM((rows, width), jnp.bfloat16),
        pltpu.SemaphoreType.DMA((3, CHUNKS)),
        pltpu.SemaphoreType.DMA((3, CHUNKS)),
    ]


def gather_scratch(rows, width):
    return [
        pltpu.VMEM((GROUP, rows, width), jnp.bfloat16),
        pltpu.SemaphoreType.DMA((3, CHUNKS)),
        pltpu.SemaphoreType.DMA((3, CHUNKS)),
    ]


def vector(ref):
    return ref[...].astype(jnp.float32).reshape(1, ref.shape[0])


def dot(left, right):
    return jnp.dot(left, right, preferred_element_type=jnp.float32)


def dot_cols(left, right):
    return lax.dot_general(left, right, contract_cols, preferred_element_type=jnp.float32)


def turn(values, cosine, sine):
    return values * cosine + pltpu.roll(values, HEAD_SIZE // 2, 1) * sine


def head_norm_back(incoming, values, gain):
    scale = lax.rsqrt(jnp.mean(values * values, axis=-1, keepdims=True) + epsilon)
    scaled = incoming * gain
    grad = scale * scaled - values * (
        scale * scale * scale * jnp.mean(scaled * values, axis=-1, keepdims=True)
    )
    return grad, jnp.sum(incoming * values * scale, axis=0, keepdims=True)


SCORE_SCALE = HEAD_SIZE**-0.5
LOG2_E = 1.4426950408889634
ROWS = 256
HALF = 128
COTANGENT = "cot"
DOWN_PART = "down_part"
MATRICES = ("wq", "wk", "wv")
SCATTER_PARTS = ("_near", "_sum", "_arr", "_send", "_recv")


def start_loads(ref, layout, pairs):
    loads = SimpleNamespace()
    table = vars(ref)
    for slot, name in enumerate(layout.loads):
        source, target = pairs[name] if name in pairs else (table[name], table["v_" + name])
        copy = pltpu.make_async_copy(source, target, ref.load_sems.at[slot])
        copy.start()
        setattr(loads, name, copy)
    return loads


def weight_grad(rows, cols, target):
    width = cols.shape[-1]
    right = cols[...].reshape(SEQUENCE_TOKENS, width)
    for j in range(4):
        left = rows[:, :, j * ROWS : (j + 1) * ROWS].reshape(SEQUENCE_TOKENS, ROWS)
        target[j] = dot(left.T, right).astype(jnp.bfloat16).reshape(4, 2, 32, width)


class RingSum:
    def __init__(self, box, slot, others, send_sems, recv_sems):
        self.box, self.slot, self.others = box, slot, others
        self.send_sems, self.recv_sems = send_sems, recv_sems

    def copy(self, index, slot):
        spot = self.box.at[slot]
        return send(
            spot, spot, self.send_sems.at[index], self.recv_sems.at[slot], self.others[index][1]
        )

    def start(self, value):
        self.box[self.slot] = value
        for index in range(len(self.others)):
            self.copy(index, self.slot).start()

    def end(self):
        for index, (slot, _) in enumerate(self.others):
            self.copy(index, slot).wait_recv()
        total = self.box[0]
        for slot in range(1, self.box.shape[0]):
            total = total + self.box[slot]
        for index in range(len(self.others)):
            self.copy(index, self.slot).wait_send()
        return total


def back_kernel(names, layout, *refs):
    ref = SimpleNamespace(**dict(zip(names, refs)))
    me = lax.axis_index("tensor")
    sibling, far, far_sibling = partner(me, FLIP), across(me), partner(me, MIRROR)
    place = rank_places()
    where = rank_where(place)
    pairs = dict(
        down_part_far=(ref.down_part.at[pl.ds(far, 1)], ref.v_down_part_far),
        down_part_own=(ref.down_part.at[pl.ds(me, 1)], ref.v_down_part_own),
    )
    for g in range(2):
        base = g * 512
        for name, source, start, size in (
            ("wq", ref.wq, 0, 256), ("wk", ref.wk, 256, 128), ("wv", ref.wv, 384, 128)
        ):
            pairs[name + str(g)] = (
                source.at[:, pl.ds(g * size, size)],
                ref.wcat.at[:, pl.ds(base + start, size)],
            )
    for i in range(len(layout.ffn)):
        name = "early" + str(i)
        pairs[name] = (vars(ref)[name], vars(ref)["f" + str(i) + "_0"])
    loads = start_loads(ref, layout, pairs)

    def turns(here):
        return here, partner(here, FLIP), partner(here, MIRROR), across(here)

    def far_place(x, z):
        return {"dp": x * 8 + z * 2 + place["y"]}

    y = place["y"]
    plane = [(x * 4 + z, far_place(x, z)) for x in turns(place["x"]) for z in turns(place["z"])]
    eight = [
        (row * 4 + member, dict(where("y", row), tensor=member))
        for row in (y, 1 - y)
        for member in turns(me)
    ]
    rings = []
    for box, members in (
        (ref.box_plane, plane), (ref.box_eight, eight), (ref.late_plane, plane), (ref.late_eight, eight)
    ):
        rings.append(
            RingSum(
                box,
                members[0][0],
                members[1:],
                ref.gain_send.at[len(rings)],
                ref.gain_recv.at[len(rings)],
            )
        )
    greet([there for ring in rings[:2] for _, there in ring.others])

    down = Scatter(
        ref.down_part, ref.d_near, ref.d_sum, ref.d_arr, ref.d_send, ref.d_recv, me
    )
    down.start(0)
    down.start(1)

    table = vars(ref)

    def streams_of(kind, entries, send_sems, recv_sems):
        out = []
        for i, (source, start, size, order, target, at) in enumerate(entries):
            columns = pl.ds(start, size)
            stream = Stream(
                order,
                table[source].at[:, :, :, :, columns],
                table[target].at[:, pl.ds(at, size)],
                [table[kind + str(i) + "_" + str(j)] for j in range(STREAM_SCRATCH)],
                (send_sems.at[i], recv_sems.at[i]),
                place,
                where,
            )
            if "v_" + source in table:
                stream.local = table["v_" + source].at[:, :, :, :, columns]
            out.append(stream)
        return out

    ffn = streams_of("f", layout.ffn, ref.f_send, ref.f_recv)
    attn = streams_of("a", layout.attn, ref.a_send, ref.a_recv)
    out_streams, group_streams = attn[:4], (attn[4:8], attn[8:])

    def every(streams, *steps):
        for stream in streams:
            for step, *stage in steps:
                step(stream, *stage)

    for load in (loads.w_out, loads.att, loads.gh):
        load.wait()

    def attended_grad(block):
        part = dot_cols(ref.v_gh[block], ref.v_w_out[...]).astype(jnp.bfloat16)
        for head in range(4):
            g, r = head // 2, head % 2
            at = slice(head * HEAD_SIZE, (head + 1) * HEAD_SIZE)
            low = part[:, at]
            ref.do[g, block, r * ROWS : (r + 1) * ROWS, :] = low
            product = low.astype(jnp.float32) * ref.v_att[block, :, at].astype(jnp.float32)
            ref.delta[g, block, :, r * ROWS : (r + 1) * ROWS] = jnp.sum(
                product.T, axis=0, keepdims=True
            )

    attended_grad(3)
    attended_grad(2)

    loads.down_part_far.wait()
    down.cross(ref.v_down_part_far.at[0])
    for load in [loads.gate, loads.up, loads.down] + [
        vars(loads)["early" + str(i)] for i in range(len(ffn))
    ]:
        load.wait()
    every(ffn, (Stream.quarter, 0))
    attended_grad(1)
    attended_grad(0)
    weight_grad(ref.v_gh, ref.v_att, ref.gw_out)
    every(out_streams, (Stream.halve, 0))

    for load in (
        loads.q, loads.k, loads.v, loads.lse, loads.qraw, loads.kraw, loads.cos, loads.sin,
        loads.qg, loads.kg,
    ):
        load.wait()
    ref.qgain[...] = jnp.zeros_like(ref.qgain)
    ref.kgain[...] = jnp.zeros_like(ref.kgain)
    key_row = lax.broadcasted_iota(jnp.int32, (ROWS, 2 * ROWS), 0)
    query_col = lax.rem(lax.broadcasted_iota(jnp.int32, (ROWS, 2 * ROWS), 1), ROWS)
    allowed = key_row <= query_col

    def attend_group(g):
        base = 512 * g
        for qb in (3, 2, 1, 0):
            keys = (qb + 1) * ROWS
            key = ref.v_k[g, 0 : qb + 1].reshape(keys, HEAD_SIZE)
            query, grad_out = ref.v_q[g, qb], ref.do[g, qb]
            probs = jnp.exp2(
                dot_cols(key, query) * (SCORE_SCALE * LOG2_E) - ref.v_lse[g, qb]
            )
            tail = jnp.where(allowed, probs[keys - ROWS :], 0.0)
            probs = jnp.concatenate([probs[: keys - ROWS], tail], axis=0) if qb else tail
            grad_probs = dot_cols(
                ref.v_v[g, 0 : qb + 1].reshape(keys, HEAD_SIZE), grad_out
            )
            grad_scores = (probs * (grad_probs - ref.delta[g, qb])).astype(jnp.bfloat16)
            grad_value = dot(probs.astype(jnp.bfloat16), grad_out).reshape(qb + 1, ROWS, HEAD_SIZE)
            grad_key = dot(grad_scores, query).reshape(qb + 1, ROWS, HEAD_SIZE)
            if qb == 3:
                ref.dv[...] = grad_value
                ref.dk[...] = grad_key
            else:
                ref.dv[0 : qb + 1] += grad_value
                ref.dk[0 : qb + 1] += grad_key
            grads = dot(key.T, grad_scores).T * SCORE_SCALE
            for r in range(2):
                start = (2 * g + r) * HEAD_SIZE
                back = turn(
                    grads[r * ROWS : (r + 1) * ROWS], ref.v_cos[qb], ref.v_sin[qb]
                )
                grad, gain = head_norm_back(
                    back, ref.v_qraw[qb, :, start : start + HEAD_SIZE], vector(ref.v_qg)
                )
                at = base + r * HEAD_SIZE
                ref.dqkv[qb, :, at : at + HEAD_SIZE] = grad.astype(jnp.bfloat16)
                ref.qgain[...] += gain

        for kb in range(4):
            start = g * HEAD_SIZE
            back = turn(ref.dk[kb] * SCORE_SCALE, ref.v_cos[kb], ref.v_sin[kb])
            grad, gain = head_norm_back(
                back, ref.v_kraw[kb, :, start : start + HEAD_SIZE], vector(ref.v_kg)
            )
            ref.dqkv[kb, :, base + 256 : base + 384] = grad.astype(jnp.bfloat16)
            ref.dqkv[kb, :, base + 384 : base + 512] = ref.dv[kb].astype(jnp.bfloat16)
            ref.kgain[...] += gain

    attend_group(0)
    loads.norm_all.wait()
    weight_grad(ref.v_norm_all, ref.dqkv.at[:, :, 0:512], ref.gw_0)
    every(group_streams[0], (Stream.halve, 0))
    every(ffn, (Stream.settle, 0), (Stream.halve, 1))
    every(out_streams, (Stream.quarter, 0))
    attend_group(1)
    loads.gain_mid.wait()
    ref.gains[...] = jnp.zeros_like(ref.gains)
    for row in range(8):
        ref.gains[row : row + 1] = ref.v_gain_mid[:, row * HEAD_SIZE : (row + 1) * HEAD_SIZE]
    ref.gains[8:9] = ref.qgain[...]
    ref.gains[9:10] = ref.kgain[...]
    rings[0].start(ref.gains[...])

    for load in (loads.wq0, loads.wk0, loads.wv0, loads.wq1, loads.wk1, loads.wv1):
        load.wait()
    inward = Scatter(
        ref.x_part, ref.x_near, ref.x_sum, ref.x_arr, ref.x_send, ref.x_recv, me
    )

    def inward_part(block, target):
        target[...] = dot_cols(ref.dqkv[block], ref.wcat[...]).astype(target.dtype)

    inward_part(far_sibling, ref.x_part.at[far_sibling])
    inward.start(0)
    inward_part(far, ref.x_part.at[far])
    inward.cross(ref.x_part.at[far])
    inward_part(sibling, ref.x_part.at[sibling])
    inward.start(1)
    weight_grad(ref.v_norm_all, ref.dqkv.at[:, :, 512:1024], ref.gw_1)
    every(group_streams[1], (Stream.halve, 0))
    inward_part(me, ref.x_own)
    rings[1].start(rings[0].end())

    every(ffn, (Stream.quarter, 1))
    every(out_streams, (Stream.settle, 0), (Stream.halve, 1))
    every(group_streams[0], (Stream.quarter, 0))
    every(ffn, (Stream.settle, 1))
    every(out_streams, (Stream.quarter, 1))
    every(group_streams[0], (Stream.settle, 0), (Stream.halve, 1))

    loads.hidden.wait()
    loads.down_part_own.wait()
    for chunk in range(CHUNKS):
        part = down.part(chunk)
        total = down.total(chunk, ref.v_down_part_own.at[0])
        ref.result[part] = (ref.v_hidden[part] + total).astype(jnp.bfloat16)
    every(group_streams[1], (Stream.quarter, 0))
    every(out_streams, (Stream.settle, 1))
    every(group_streams[0], (Stream.quarter, 1))

    early = rings[1].end()
    for row in range(8):
        ref.o_norm_mid[:, row * HEAD_SIZE : (row + 1) * HEAD_SIZE] = early[row : row + 1]
    ref.o_qgain[...] = early[8:9]
    ref.o_kgain[...] = early[9:10]

    for load in (loads.tokens, loads.norm_in):
        load.wait()
    ref.gain_in[...] = jnp.zeros_like(ref.gain_in)
    for chunk in range(CHUNKS):
        part = inward.part(chunk)
        incoming = inward.total(chunk, ref.x_own)
        values = ref.v_tokens[part].astype(jnp.float32)
        grad, gain = head_norm_back(incoming, values, vector(ref.v_norm_in))
        ref.grad_tokens[part] = (ref.v_gh[me, part].astype(jnp.float32) + grad).astype(
            jnp.bfloat16
        )
        ref.gain_in[...] += gain
    for row in range(8):
        ref.gains[row : row + 1] = ref.gain_in[:, row * HEAD_SIZE : (row + 1) * HEAD_SIZE]

    rings[2].start(ref.gains[0:8])
    every(group_streams[1], (Stream.settle, 0), (Stream.halve, 1))
    every(ffn, (Stream.finish,))
    rings[3].start(rings[2].end())
    every(group_streams[1], (Stream.quarter, 1))
    every(group_streams[0], (Stream.settle, 1))
    every(out_streams, (Stream.finish,))
    every(group_streams[1], (Stream.settle, 1))
    every(group_streams[0], (Stream.finish,))
    total = rings[3].end()
    for row in range(8):
        ref.o_norm_in[:, row * HEAD_SIZE : (row + 1) * HEAD_SIZE] = total[row : row + 1]
    every(group_streams[1], (Stream.finish,))
    down.drain()
    inward.drain()


def hand_over_kernel(n, *refs):
    sources, targets, buffers, sems = refs[:n], refs[n : 2 * n], refs[2 * n : 3 * n], refs[3 * n]
    pulls = [pltpu.make_async_copy(sources[i], buffers[i], sems.at[0, i]) for i in range(n)]
    pushes = [pltpu.make_async_copy(buffers[i], targets[i], sems.at[1, i]) for i in range(n)]
    for pull in pulls:
        pull.start()
    for pull, push in zip(pulls, pushes):
        pull.wait()
        push.start()
    for push in pushes:
        push.wait()


def hand_over(arrays):
    n = len(arrays)
    anywhere = [pl.BlockSpec(memory_space=pl.ANY)] * n
    return pl.pallas_call(
        functools.partial(hand_over_kernel, n),
        out_shape=[jax.ShapeDtypeStruct(array.shape, array.dtype) for array in arrays],
        in_specs=anywhere,
        out_specs=anywhere,
        scratch_shapes=[pltpu.VMEM(array.shape, array.dtype) for array in arrays]
        + [pltpu.SemaphoreType.DMA((2, n))],
    )(*arrays)


def ffn_streams():
    xa, xb = ("x", FLIP, FLIP), ("x", MIRROR, MIRROR)
    za, zb = ("z", FLIP, MIRROR), ("z", MIRROR, FLIP)
    return [
        ("gate", 0, 384, xa, "o_gate", 0), ("gate", 384, 384, xb, "o_gate", 384),
        ("up", 0, 384, za, "o_up", 0), ("up", 384, 384, zb, "o_up", 384),
        ("down", 0, 256, xa, "o_down", 0), ("down", 256, 128, xb, "o_down", 256),
        ("down", 384, 256, za, "o_down", 384), ("down", 640, 128, zb, "o_down", 640),
    ]


def back_part(inputs, ffn):
    low, wide = jnp.bfloat16, jnp.float32
    names = list(inputs)
    weights = [name for name in names if name in MATRICES]
    loaded = [name for name in names if name != DOWN_PART and name not in MATRICES]
    loaded += [DOWN_PART + "_far", DOWN_PART + "_own"]
    shapes = {name: (inputs[name].shape, inputs[name].dtype) for name in loaded[:-2]}
    shapes.update({name: ((1, ROWS, 1024), low) for name in loaded[-2:]})
    loaded += [name + str(g) for g in range(2) for name in weights]
    early = [name for name in loaded if name.startswith(("down", "gate", "up", "early"))]
    loaded = loaded[:3] + early + [name for name in loaded[3:] if name not in early]
    outs = dict(
        result=((ROWS, 1024), low),
        grad_tokens=((ROWS, 1024), low),
        o_gate=((32, 768), wide),
        o_up=((32, 768), wide),
        o_down=((32, 768), wide),
        o_q=((32, 512), wide),
        o_k=((32, 256), wide),
        o_v=((32, 256), wide),
        o_out=((32, 512), wide),
        o_norm_in=((1, 1024), wide),
        o_norm_mid=((1, 1024), wide),
        o_qgain=((1, HEAD_SIZE), wide),
        o_kgain=((1, HEAD_SIZE), wide),
    )
    xa, xb = ("x", FLIP, FLIP), ("x", MIRROR, MIRROR)
    za, zb = ("z", FLIP, MIRROR), ("z", MIRROR, FLIP)
    layout = SimpleNamespace(
        loads=loaded,
        ffn=ffn,
        attn=[("gw_out", 128 * i, 128, way, "o_out", 128 * i) for i, way in enumerate((xb, zb, xa, za))]
        + [
            ("gw_" + str(g), 128 * i, 128, way, target, at + step * g)
            for g in range(2)
            for i, (way, target, at, step) in enumerate(
                ((xa, "o_q", 0, 256), (xb, "o_q", 128, 256), (za, "o_k", 0, 128), (zb, "o_v", 0, 128))
            )
        ],
    )
    scratch = {"v_" + name: pltpu.VMEM(*spec) for name, spec in shapes.items()}
    scratch.update(
        load_sems=pltpu.SemaphoreType.DMA((len(loaded),)),
        do=pltpu.VMEM((2, 4, 2 * ROWS, HEAD_SIZE), low),
        delta=pltpu.VMEM((2, 4, 1, 2 * ROWS), wide),
        dk=pltpu.VMEM((4, ROWS, HEAD_SIZE), wide),
        dv=pltpu.VMEM((4, ROWS, HEAD_SIZE), wide),
        dqkv=pltpu.VMEM((4, ROWS, 1024), low),
        wcat=pltpu.VMEM((1024, 1024), low),
        qgain=pltpu.VMEM((1, HEAD_SIZE), wide),
        kgain=pltpu.VMEM((1, HEAD_SIZE), wide),
        x_part=pltpu.VMEM((4, ROWS, 1024), low),
        x_own=pltpu.VMEM((ROWS, 1024), wide),
        gw_out=pltpu.VMEM((4, 4, 2, 32, 512), low),
        gw_0=pltpu.VMEM((4, 4, 2, 32, 512), low),
        gw_1=pltpu.VMEM((4, 4, 2, 32, 512), low),
        gains=pltpu.VMEM((16, HEAD_SIZE), wide),
        gain_in=pltpu.VMEM((1, 1024), wide),
        box_plane=pltpu.VMEM((16, 16, HEAD_SIZE), wide),
        box_eight=pltpu.VMEM((8, 16, HEAD_SIZE), wide),
        late_plane=pltpu.VMEM((16, 8, HEAD_SIZE), wide),
        late_eight=pltpu.VMEM((8, 8, HEAD_SIZE), wide),
        gain_send=pltpu.SemaphoreType.DMA((4, 16)),
        gain_recv=pltpu.SemaphoreType.DMA((4, 16)),
    )
    for tag in "dx":
        scratch.update(zip((tag + end for end in SCATTER_PARTS), scatter_scratch(ROWS, 1024)))
    for kind, entries in (("f", layout.ffn), ("a", layout.attn)):
        for way in SCATTER_PARTS[3:]:
            scratch[kind + way] = pltpu.SemaphoreType.DMA((len(entries), STREAM_SEMS))
        for i, entry in enumerate(entries):
            for j, buffer in enumerate(stream_scratch(entry[2])):
                scratch[kind + str(i) + "_" + str(j)] = buffer
    for i in range(len(ffn)):
        scratch["f" + str(i) + "_0"] = scratch.pop("v_early" + str(i))
    results = pl.pallas_call(
        functools.partial(back_kernel, names + list(outs) + list(scratch), layout),
        out_shape=[jax.ShapeDtypeStruct(*spec) for spec in outs.values()],
        in_specs=[pl.BlockSpec(memory_space=pl.ANY)] * len(names),
        out_specs=[VMEM_SPACE] * len(outs),
        scratch_shapes=list(scratch.values()),
        compiler_params=pltpu.CompilerParams(
            collective_id=3, has_side_effects=True, vmem_limit_bytes=61 << 20
        ),
    )(*inputs.values())
    return SimpleNamespace(**dict(zip(outs, hand_over(results))))


class Exchange:
    def __init__(self, own, near_out, near_in, summed, arrived, send_sems, recv_sems, me):
        self.own, self.near_out, self.near_in = own, near_out, near_in
        self.summed, self.arrived = summed, arrived
        self.send_sems, self.recv_sems = send_sems, recv_sems
        self.sibling, self.far = {"tensor": partner(me, FLIP)}, {"tensor": across(me)}
        core = lax.rem(me, 2)
        self.mine = pl.ds(pl.multiple_of(core * HALF, HALF), HALF)
        self.other = pl.ds(pl.multiple_of((1 - core) * HALF, HALF), HALF)

    def near(self, block):
        return send(
            self.near_out.at[block],
            self.near_in.at[block],
            self.send_sems.at[0, block],
            self.recv_sems.at[0, block],
            self.sibling,
        )

    def swap(self, block):
        return send(
            self.summed.at[block],
            self.arrived.at[block],
            self.send_sems.at[1, block],
            self.recv_sems.at[1, block],
            self.far,
        )

    def share(self, block, whole):
        spot = whole.at[block, self.mine]
        return send(
            spot, spot, self.send_sems.at[2, block], self.recv_sems.at[2, block], self.sibling
        )

    def give(self, block, part):
        self.near_out[block] = part[self.other].astype(jnp.bfloat16)
        self.near(block).start()
        self.own[block] = part[self.mine]

    def cross(self, block):
        self.near(block).wait()
        self.summed[block] = (
            self.own[block] + self.near_in[block].astype(jnp.float32)
        ).astype(jnp.bfloat16)
        self.swap(block).start()

    def total(self, block):
        self.swap(block).wait()
        return self.summed[block].astype(jnp.float32) + self.arrived[block].astype(jnp.float32)


def exchange_scratch():
    half = pltpu.VMEM((4, HALF, 1024), jnp.bfloat16)
    sems = pltpu.SemaphoreType.DMA((3, 4))
    return [half, half, half, sems, sems]


def front_kernel(names, layout, *refs):
    ref = SimpleNamespace(**dict(zip(names, refs)))
    me = lax.axis_index("tensor")
    sibling, far, far_sibling = partner(me, FLIP), across(me), partner(me, MIRROR)
    place = rank_places()
    where = rank_where(place)
    loads = start_loads(
        ref,
        layout,
        dict(tokens=(ref.tokens, ref.tokens_all.at[me]), cot=(ref.cot, ref.dy_all.at[me])),
    )
    greet(
        [{"tensor": sibling}, {"tensor": far}]
        + [
            where(axis, partner(place[axis], pairing))
            for axis in ("x", "z")
            for pairing in (FLIP, MIRROR)
        ]
    )
    stores = []

    def store(source, target):
        copy = pltpu.make_async_copy(source, target, ref.store_sems.at[len(stores)])
        copy.start()
        stores.append(copy)

    first = Gather(ref.tokens_all, ref.n_send, ref.n_recv, me)
    cot = Gather(ref.dy_all, ref.c_send, ref.c_recv, me)
    loads.tokens.wait()
    first.start()
    for load in (
        loads.norm_in, loads.wq, loads.wk, loads.wv, loads.cos, loads.sin, loads.qg, loads.kg
    ):
        load.wait()

    def project(block):
        values = ref.tokens_all[block].astype(jnp.float32)
        rows = (values * rms_scale(values) * vector(ref.v_norm_in)).astype(jnp.bfloat16)
        ref.norm_all[block] = rows
        raw = dot(rows, ref.v_wq[...])
        ref.qraw[block] = raw
        for head in range(4):
            values = raw[:, head * HEAD_SIZE : (head + 1) * HEAD_SIZE]
            values = values * rms_scale(values) * vector(ref.v_qg)
            ref.q[head // 2, block, (head % 2) * ROWS : (head % 2 + 1) * ROWS, :] = turn(
                values, ref.v_cos[block], -ref.v_sin[block]
            ).astype(jnp.bfloat16)
        raw = dot(rows, ref.v_wk[...])
        ref.kraw[block] = raw
        for g in range(2):
            values = raw[:, g * HEAD_SIZE : (g + 1) * HEAD_SIZE]
            values = values * rms_scale(values) * vector(ref.v_kg)
            ref.k[g, block] = turn(values, ref.v_cos[block], -ref.v_sin[block]).astype(jnp.bfloat16)
        low = dot(rows, ref.v_wv[...]).astype(jnp.bfloat16)
        for g in range(2):
            ref.v[g, block] = low[:, g * HEAD_SIZE : (g + 1) * HEAD_SIZE]

    project(me)
    first.wait_sibling()
    project(sibling)
    first.wait_far()
    loads.cot.wait()
    cot.start()
    project(far)
    first.wait_last()
    project(far_sibling)
    store(ref.norm_all, ref.o_norm_all)
    store(ref.q, ref.o_q)
    store(ref.k, ref.o_k)
    store(ref.v, ref.o_v)
    store(ref.qraw, ref.o_qraw)
    store(ref.kraw, ref.o_kraw)

    key_row = lax.broadcasted_iota(jnp.int32, (ROWS, 2 * ROWS), 0)
    query_col = lax.rem(lax.broadcasted_iota(jnp.int32, (ROWS, 2 * ROWS), 1), ROWS)
    allowed = key_row <= query_col
    loads.w_out.wait()
    mixed = Exchange(
        ref.own, ref.p_out, ref.p_near, ref.p_sum, ref.p_arr, ref.p_send, ref.p_recv, me
    )
    back = Exchange(
        ref.own, ref.p_out, ref.b_near, ref.b_sum, ref.b_arr, ref.b_send, ref.b_recv, me
    )

    def attend(block):
        keys = (block + 1) * ROWS
        for g in range(2):
            scores = dot_cols(
                ref.k[g, 0 : block + 1].reshape(keys, HEAD_SIZE), ref.q[g, block]
            )
            probs = jnp.exp2(scores * (SCORE_SCALE * LOG2_E))
            tail = jnp.where(allowed, probs[keys - ROWS :], 0.0)
            probs = jnp.concatenate([probs[: keys - ROWS], tail], axis=0) if block else tail
            total = jnp.sum(probs, axis=0, keepdims=True)
            ref.lse[g, block] = jnp.log(total) * LOG2_E
            values = ref.v[g, 0 : block + 1].reshape(keys, HEAD_SIZE)
            rows = (dot(values.T, probs.astype(jnp.bfloat16)) / total).T.astype(jnp.bfloat16)
            for r in range(2):
                start = (2 * g + r) * HEAD_SIZE
                ref.att[block, :, start : start + HEAD_SIZE] = rows[r * ROWS : (r + 1) * ROWS]
        ref.part[...] = dot(ref.att[block], ref.v_w_out[...])
        mixed.give(block, ref.part)

    attend(3)
    attend(2)
    mixed.cross(3)
    attend(1)
    mixed.cross(2)
    attend(0)
    mixed.cross(1)
    cot.wait_far()
    mixed.cross(0)
    store(ref.att, ref.o_att)
    store(ref.lse, ref.o_lse)
    cot.wait_sibling()
    cot.wait_last()
    for load in (loads.w_down, loads.norm_mid, loads.w_gate, loads.w_up):
        load.wait()

    def mid_norm(block):
        values = ref.tokens_all[block, mixed.mine].astype(jnp.float32) + mixed.total(block)
        ref.hidden[block] = values
        ref.mid_all[block, mixed.mine] = (
            values * rms_scale(values) * vector(ref.v_norm_mid)
        ).astype(jnp.bfloat16)
        mixed.share(block, ref.mid_all).start()

    def feed(block):
        grad = dot_cols(ref.dy_all[block], ref.v_w_down[...])
        mixed.share(block, ref.mid_all).wait()
        gate = dot(ref.mid_all[block], ref.v_w_gate[...])
        up = dot(ref.mid_all[block], ref.v_w_up[...])
        sigmoid = jax.nn.sigmoid(gate)
        silu = gate * sigmoid
        ref.act[block] = (silu * up).astype(jnp.bfloat16)
        ref.dup[block] = (grad * silu).astype(jnp.bfloat16)
        ref.dgate[block] = (grad * up * sigmoid * (1.0 + gate * (1.0 - sigmoid))).astype(jnp.bfloat16)
        value = dot_cols(ref.dgate[block], ref.v_w_gate[...])
        ref.part[...] = value + dot_cols(ref.dup[block], ref.v_w_up[...])
        back.give(block, ref.part)

    for block in (3, 2, 1, 0):
        mid_norm(block)
        feed(block)
        if block < 3:
            back.cross(block + 1)
    back.cross(0)

    streams = []
    table = vars(ref)
    for i, (source, start, size, order) in enumerate(layout.ffn):
        streams.append(
            Stream(
                order,
                table["gw_" + source].at[:, :, :, :, pl.ds(start, size)],
                None,
                [table["early" + str(i)]] + [None] * (STREAM_SCRATCH - 1),
                (ref.f_send.at[i], ref.f_recv.at[i]),
                place,
                where,
            )
        )

    weight_grad(ref.mid_all, ref.dgate, ref.gw_gate)
    for stream in streams[:2]:
        stream.halve(0)
    weight_grad(ref.mid_all, ref.dup, ref.gw_up)
    for stream in streams[2:4]:
        stream.halve(0)
    weight_grad(ref.dy_all, ref.act, ref.gw_down)
    for stream in streams[4:]:
        stream.halve(0)
    store(ref.gw_gate, ref.o_gate)
    store(ref.gw_up, ref.o_up)
    store(ref.gw_down, ref.o_down)
    for block in range(4):
        ref.down_part[block] = dot(ref.act[block], ref.v_w_down[...]).astype(jnp.bfloat16)
    store(ref.down_part, ref.o_down_part)

    own_half = send(
        ref.hidden.at[sibling], ref.hid.at[mixed.mine], ref.h_send, ref.h_recv, mixed.sibling
    )
    own_half.start()
    ref.hid[mixed.mine] = ref.hidden[me]

    ref.gain[...] = jnp.zeros_like(ref.gain)
    for block in (3, 2, 1, 0):
        incoming = back.total(block)
        grad, gain = head_norm_back(incoming, ref.hidden[block], vector(ref.v_norm_mid))
        ref.gh_all[block, back.mine] = (
            ref.dy_all[block, back.mine].astype(jnp.float32) + grad
        ).astype(jnp.bfloat16)
        back.share(block, ref.gh_all).start()
        ref.gain[...] += gain
    ref.gain[...] *= 0.5
    store(ref.gain, ref.o_gain)
    own_half.wait()
    store(ref.hid, ref.o_hidden)
    for block in (3, 2, 1, 0):
        back.share(block, ref.gh_all).wait()
    store(ref.gh_all, ref.o_gh)
    for i, stream in enumerate(streams):
        for copy in stream.copies:
            copy.wait()
        store(table["early" + str(i)], table["o_early" + str(i)])
    for copy in stores:
        copy.wait()
    first.drain()
    cot.drain()


def front_part(inputs, ffn):
    low, wide = jnp.bfloat16, jnp.float32
    names = list(inputs)
    outs = dict(
        o_norm_all=((4, ROWS, 1024), low),
        o_q=((2, 4, 2 * ROWS, HEAD_SIZE), low),
        o_k=((2, 4, ROWS, HEAD_SIZE), low),
        o_v=((2, 4, ROWS, HEAD_SIZE), low),
        o_qraw=((4, ROWS, 512), wide),
        o_kraw=((4, ROWS, 256), wide),
        o_att=((4, ROWS, 512), low),
        o_lse=((2, 4, 1, 2 * ROWS), wide),
        o_hidden=((ROWS, 1024), wide),
        o_down=((4, 4, 2, 32, 768), low),
        o_gate=((4, 4, 2, 32, 768), low),
        o_up=((4, 4, 2, 32, 768), low),
        o_down_part=((4, ROWS, 1024), low),
        o_gh=((4, ROWS, 1024), low),
        o_gain=((1, 1024), wide),
    )
    early = {"early" + str(i): ((2, 4, 2, 32, entry[2]), low) for i, entry in enumerate(ffn)}
    outs.update({"o_" + name: spec for name, spec in early.items()})
    whole = ("tokens", COTANGENT)
    scratch = {
        "v_" + name: pltpu.VMEM(inputs[name].shape, inputs[name].dtype)
        for name in names
        if name not in whole
    }
    scratch.update({name: pltpu.VMEM(*spec) for name, spec in early.items()})
    scratch.update(
        load_sems=pltpu.SemaphoreType.DMA((len(names),)),
        store_sems=pltpu.SemaphoreType.DMA((len(outs),)),
        f_send=pltpu.SemaphoreType.DMA((len(ffn), 2)),
        f_recv=pltpu.SemaphoreType.DMA((len(ffn), 2)),
        h_send=pltpu.SemaphoreType.DMA,
        h_recv=pltpu.SemaphoreType.DMA,
        norm_all=pltpu.VMEM((4, ROWS, 1024), low),
        mid_all=pltpu.VMEM((4, ROWS, 1024), low),
        gh_all=pltpu.VMEM((4, ROWS, 1024), low),
        qraw=pltpu.VMEM((4, ROWS, 512), wide),
        kraw=pltpu.VMEM((4, ROWS, 256), wide),
        q=pltpu.VMEM((2, 4, 2 * ROWS, HEAD_SIZE), low),
        k=pltpu.VMEM((2, 4, ROWS, HEAD_SIZE), low),
        v=pltpu.VMEM((2, 4, ROWS, HEAD_SIZE), low),
        lse=pltpu.VMEM((2, 4, 1, 2 * ROWS), wide),
        att=pltpu.VMEM((4, ROWS, 512), low),
        part=pltpu.VMEM((ROWS, 1024), wide),
        own=pltpu.VMEM((4, HALF, 1024), wide),
        hidden=pltpu.VMEM((4, HALF, 1024), wide),
        hid=pltpu.VMEM((ROWS, 1024), wide),
        p_out=pltpu.VMEM((4, HALF, 1024), low),
        act=pltpu.VMEM((4, ROWS, 768), low),
        dup=pltpu.VMEM((4, ROWS, 768), low),
        dgate=pltpu.VMEM((4, ROWS, 768), low),
        gw_down=pltpu.VMEM((4, 4, 2, 32, 768), low),
        gw_gate=pltpu.VMEM((4, 4, 2, 32, 768), low),
        gw_up=pltpu.VMEM((4, 4, 2, 32, 768), low),
        down_part=pltpu.VMEM((4, ROWS, 1024), low),
        gain=pltpu.VMEM((1, 1024), wide),
    )
    scratch.update(zip(("tokens_all", "n_send", "n_recv"), gather_scratch(ROWS, 1024)))
    scratch.update(zip(("dy_all", "c_send", "c_recv"), gather_scratch(ROWS, 1024)))
    for tag in "pb":
        scratch.update(zip((tag + end for end in SCATTER_PARTS), exchange_scratch()))
    results = pl.pallas_call(
        functools.partial(
            front_kernel,
            names + list(outs) + list(scratch),
            SimpleNamespace(loads=names, ffn=[entry[:4] for entry in ffn]),
        ),
        out_shape=[jax.ShapeDtypeStruct(*spec) for spec in outs.values()],
        in_specs=[pl.BlockSpec(memory_space=pl.ANY)] * len(names),
        out_specs=[pl.BlockSpec(memory_space=pl.ANY)] * len(outs),
        scratch_shapes=list(scratch.values()),
        compiler_params=pltpu.CompilerParams(
            collective_id=4, has_side_effects=True, vmem_limit_bytes=62 << 20
        ),
    )(*inputs.values())
    return SimpleNamespace(**dict(zip(outs, results)))


def rotary_tables():
    position = np.arange(SEQUENCE_TOKENS, dtype=np.float64)
    inverse = 1000000.0 ** (-np.arange(HEAD_SIZE // 2, dtype=np.float64) * 2.0 / HEAD_SIZE)
    angles = position[:, None] * inverse[None, :]
    cosine, sine = np.cos(angles), np.sin(angles)
    return (
        jnp.asarray(
            np.concatenate([table, tail], axis=1).astype(np.float32).reshape(4, ROWS, HEAD_SIZE)
        )
        for table, tail in ((cosine, cosine), (sine, -sine))
    )


def per_device(
    tokens,
    norm_in,
    w_query,
    key_matrix,
    value_matrix,
    query_gain,
    key_gain,
    w_out,
    norm_mid,
    w_gate,
    w_up,
    w_down,
    cotangent,
):
    cosine, sine = rotary_tables()
    ffn = ffn_streams()
    front = front_part(
        dict(
            tokens=tokens,
            norm_in=norm_in,
            wq=w_query,
            wk=key_matrix,
            wv=value_matrix,
            cos=cosine,
            sin=sine,
            qg=query_gain,
            kg=key_gain,
            cot=cotangent,
            w_out=w_out,
            w_down=w_down,
            norm_mid=norm_mid,
            w_gate=w_gate,
            w_up=w_up,
        ),
        ffn,
    )
    outs = back_part(
        dict(
            gh=front.o_gh,
            w_out=w_out,
            att=front.o_att,
            down_part=front.o_down_part,
            gate=front.o_gate,
            up=front.o_up,
            down=front.o_down,
            q=front.o_q,
            k=front.o_k,
            v=front.o_v,
            lse=front.o_lse,
            qraw=front.o_qraw,
            kraw=front.o_kraw,
            cos=cosine,
            sin=sine,
            qg=query_gain,
            kg=key_gain,
            wq=w_query,
            wk=key_matrix,
            wv=value_matrix,
            norm_all=front.o_norm_all,
            hidden=front.o_hidden,
            tokens=tokens,
            norm_in=norm_in,
            gain_mid=front.o_gain,
            **{"early" + str(i): vars(front)["o_early" + str(i)] for i in range(len(ffn))},
        ),
        ffn,
    )
    return (
        outs.result,
        outs.grad_tokens,
        outs.o_norm_in.reshape(1024),
        outs.o_q,
        outs.o_k,
        outs.o_v,
        outs.o_qgain.reshape(HEAD_SIZE),
        outs.o_kgain.reshape(HEAD_SIZE),
        outs.o_out.T,
        outs.o_norm_mid.reshape(1024),
        outs.o_gate,
        outs.o_up,
        outs.o_down.T,
    )


def solution(mesh):
    placed = (
        P(("dp", "tensor"), None),
        P(),
        P(None, "tensor"),
        P(None, "tensor"),
        P(None, "tensor"),
        P(),
        P(),
        P("tensor", None),
        P(),
        P(None, "tensor"),
        P(None, "tensor"),
        P("tensor", None),
        P(("dp", "tensor"), None),
    )
    return jax.shard_map(
        per_device,
        mesh=mesh,
        in_specs=placed,
        out_specs=(
            P(("dp", "tensor"), None),
            P(("dp", "tensor"), None),
            P(),
            P("dp", "tensor"),
            P("dp", "tensor"),
            P("dp", "tensor"),
            P(),
            P(),
            P("tensor", "dp"),
            P(),
            P("dp", "tensor"),
            P("dp", "tensor"),
            P("tensor", "dp"),
        ),
        check_vma=False,
    )
```

```python
import functools
from types import SimpleNamespace

import jax
import jax.numpy as jnp
import numpy as np
from jax import lax
from jax.experimental import pallas as pl
from jax.experimental.pallas import tpu as pltpu
from jax.sharding import PartitionSpec as P

HEAD_SIZE = 128
SEQUENCE_TOKENS = 1024
GROUP = 4
CHUNKS = 4
VMEM_SPACE = pl.BlockSpec(memory_space=pltpu.VMEM)
FLIP, MIRROR = 1, 3
epsilon = 1e-06
contract_cols = (((1,), (1,)), ((), ()))


def partner(index, pairing):
    if pairing == FLIP:
        return index + 1 - 2 * lax.rem(index, 2)
    return 3 - index


def across(index):
    return lax.rem(index + 2, 4)


def send(source, target, send_sem, recv_sem, where):
    return pltpu.make_async_remote_copy(
        src_ref=source,
        dst_ref=target,
        send_sem=send_sem,
        recv_sem=recv_sem,
        device_id=where,
        device_id_type=pl.DeviceIdType.MESH,
    )


def greet(others):
    barrier = pltpu.get_barrier_semaphore()
    for where in others:
        pl.semaphore_signal(barrier, inc=1, device_id=where, device_id_type=pl.DeviceIdType.MESH)
    pl.semaphore_wait(barrier, len(others))


class Stream:
    def __init__(self, order, grad, out, scratch, sems, place, where):
        self.first, self.orders = order[0], order[1:]
        self.grad, self.local, self.out = grad, grad, out
        self.early, self.mid, self.late, self.held, self.low, self.pair, self.last = scratch
        self.send_sems, self.recv_sems = sems
        self.place, self.where = place, where
        self.pending = []
        self.copies = [None, None]

    def axis(self, stage):
        return self.first if stage == 0 else ("z" if self.first == "x" else "x")

    def block(self, stage, index, local=True):
        if stage == 1:
            return self.held.at[index]
        grad = self.local if local else self.grad
        return grad.at[index] if self.first == "x" else grad.at[:, index]

    def launch(self, source, target, slot, where):
        copy = send(source, target, self.send_sems.at[slot], self.recv_sems.at[slot], where)
        copy.start()
        self.pending.append(copy)
        return copy

    def halve(self, stage):
        axis, here = self.axis(stage), self.place[self.axis(stage)]
        other = partner(here, self.orders[stage])
        box = self.early if stage == 0 else self.late
        self.copies = [
            self.launch(
                self.block(stage, index, False), box.at[slot], 4 * stage + slot, self.where(axis, other)
            )
            for slot, index in ((1, across(here)), (0, other))
        ]

    def quarter(self, stage):
        axis, here = self.axis(stage), self.place[self.axis(stage)]
        other = partner(here, FLIP + MIRROR - self.orders[stage])
        box, mid = (self.early, self.mid) if stage == 0 else (self.late, self.low)
        if self.copies[0]:
            self.copies[0].wait_recv()
        mine = self.block(stage, other)

        def add(row, _):
            mid[0, row] = mine[row] + box[1, row]
            return _

        lax.fori_loop(0, mid.shape[1], add, 0)
        self.copies.append(
            self.launch(mid.at[0], mid.at[1], 4 * stage + 2, self.where(axis, other))
        )

    def settle(self, stage):
        here = self.place[self.axis(stage)]
        if self.copies[1]:
            self.copies[1].wait_recv()
        self.copies[2].wait_recv()
        box, mid = (self.early, self.mid) if stage == 0 else (self.late, self.low)
        mine = self.block(stage, here)
        if stage == 0:

            def add(row, _):
                self.held[row] = mine[row] + box[0, row] + mid[1, row]
                return _

            lax.fori_loop(0, mid.shape[1], add, 0)
            return
        keep = self.place["y"]
        give = 1 - keep
        self.pair[0] = (
            mine[give].astype(jnp.float32)
            + box[0, give].astype(jnp.float32)
            + mid[1, give].astype(jnp.float32)
        ).astype(jnp.bfloat16)
        self.copies.append(
            self.launch(self.pair.at[0], self.pair.at[1], 3, self.where("y", give))
        )
        self.last[...] = (
            mine[keep].astype(jnp.float32)
            + box[0, keep].astype(jnp.float32)
            + mid[1, keep].astype(jnp.float32)
        )

    def finish(self):
        self.copies[3].wait_recv()
        self.out[...] = self.last[...] + self.pair[1].astype(jnp.float32)
        for copy in self.pending:
            copy.wait_send()


STREAM_SEMS = 7
STREAM_SCRATCH = 7


def stream_scratch(columns):
    low = jnp.bfloat16
    return [
        pltpu.VMEM((2, 4, 2, 32, columns), low),
        pltpu.VMEM((2, 4, 2, 32, columns), low),
        pltpu.VMEM((2, 2, 32, columns), low),
        pltpu.VMEM((4, 2, 32, columns), low),
        pltpu.VMEM((2, 2, 32, columns), low),
        pltpu.VMEM((2, 32, columns), low),
        pltpu.VMEM((32, columns), jnp.float32),
    ]


def rank_places():
    rank = lax.axis_index("dp")
    return {"x": lax.div(rank, 8), "z": lax.rem(lax.div(rank, 2), 4), "y": lax.rem(rank, 2)}


def rank_where(place):
    def where(axis, index):
        at = dict(place)
        at[axis] = index
        return {"dp": at["x"] * 8 + at["z"] * 2 + at["y"]}

    return where


def rms_scale(values):
    return lax.rsqrt(jnp.mean(values * values, axis=-1, keepdims=True) + epsilon)


class Gather:
    def __init__(self, whole, send_sems, recv_sems, me, shard=None):
        self.shard = shard
        self.whole, self.send_sems, self.recv_sems, self.me = whole, send_sems, recv_sems, me
        self.sibling, self.far = {"tensor": partner(me, FLIP)}, {"tensor": across(me)}
        self.rows = whole.shape[1] // CHUNKS

    def copy(self, lane, chunk, block, where):
        part = pl.ds(chunk * self.rows, self.rows)
        spot = self.whole.at[block, part]
        source = spot if self.shard is None or lane == 2 else self.shard.at[part]
        return send(source, spot, self.send_sems.at[lane, chunk], self.recv_sems.at[lane, chunk], where)

    def start_chunk(self, chunk):
        self.copy(0, chunk, self.me, self.far).start()
        self.copy(1, chunk, self.me, self.sibling).start()

    def start(self):
        for chunk in range(CHUNKS):
            self.copy(0, chunk, self.me, self.far).start()
        for chunk in range(CHUNKS):
            self.copy(1, chunk, self.me, self.sibling).start()

    def wait_sibling(self):
        for chunk in range(CHUNKS):
            self.copy(1, chunk, self.me, self.sibling).wait_recv()

    def wait_far(self):
        for chunk in range(CHUNKS):
            self.copy(0, chunk, self.me, self.far).wait_recv()
            self.copy(2, chunk, across(self.me), self.sibling).start()

    def wait_last(self):
        for chunk in range(CHUNKS):
            self.copy(2, chunk, across(self.me), self.sibling).wait_recv()

    def drain(self):
        for chunk in range(CHUNKS):
            self.copy(0, chunk, self.me, self.far).wait_send()
            self.copy(1, chunk, self.me, self.sibling).wait_send()
            self.copy(2, chunk, across(self.me), self.sibling).wait_send()


class Scatter:
    def __init__(self, partial, near, summed, arrived, send_sems, recv_sems, me):
        self.partial, self.near, self.summed, self.arrived = partial, near, summed, arrived
        self.send_sems, self.recv_sems, self.me = send_sems, recv_sems, me
        self.sibling, self.far = {"tensor": partner(me, FLIP)}, {"tensor": across(me)}
        self.rows = near.shape[1] // CHUNKS

    def part(self, chunk):
        return pl.ds(chunk * self.rows, self.rows)

    def near_copy(self, slot, chunk):
        block = partner(self.me, MIRROR if slot == 0 else FLIP)
        return send(
            self.partial.at[block, self.part(chunk)],
            self.near.at[slot, self.part(chunk)],
            self.send_sems.at[slot, chunk],
            self.recv_sems.at[slot, chunk],
            self.sibling,
        )

    def far_copy(self, chunk):
        return send(
            self.summed.at[self.part(chunk)],
            self.arrived.at[self.part(chunk)],
            self.send_sems.at[2, chunk],
            self.recv_sems.at[2, chunk],
            self.far,
        )

    def start(self, slot):
        for chunk in range(CHUNKS):
            self.near_copy(slot, chunk).start()

    def cross(self, mine):
        for chunk in range(CHUNKS):
            part = self.part(chunk)
            self.near_copy(0, chunk).wait_recv()
            self.summed[part] = (
                mine[part].astype(jnp.float32) + self.near[0, part].astype(jnp.float32)
            ).astype(jnp.bfloat16)
            self.far_copy(chunk).start()

    def total(self, chunk, mine):
        part = self.part(chunk)
        self.near_copy(1, chunk).wait_recv()
        self.far_copy(chunk).wait_recv()
        return (
            mine[part].astype(jnp.float32)
            + self.near[1, part].astype(jnp.float32)
            + self.arrived[part].astype(jnp.float32)
        )

    def drain(self):
        for chunk in range(CHUNKS):
            self.near_copy(0, chunk).wait_send()
            self.near_copy(1, chunk).wait_send()
            self.far_copy(chunk).wait_send()


def scatter_scratch(rows, width):
    return [
        pltpu.VMEM((2, rows, width), jnp.bfloat16),
        pltpu.VMEM((rows, width), jnp.bfloat16),
        pltpu.VMEM((rows, width), jnp.bfloat16),
        pltpu.SemaphoreType.DMA((3, CHUNKS)),
        pltpu.SemaphoreType.DMA((3, CHUNKS)),
    ]


def gather_scratch(rows, width):
    return [
        pltpu.VMEM((GROUP, rows, width), jnp.bfloat16),
        pltpu.SemaphoreType.DMA((3, CHUNKS)),
        pltpu.SemaphoreType.DMA((3, CHUNKS)),
    ]


def vector(ref):
    return ref[...].astype(jnp.float32).reshape(1, ref.shape[0])


def dot(left, right):
    return jnp.dot(left, right, preferred_element_type=jnp.float32)


def dot_cols(left, right):
    return lax.dot_general(left, right, contract_cols, preferred_element_type=jnp.float32)


def turn(values, cosine, sine):
    return values * cosine + pltpu.roll(values, HEAD_SIZE // 2, 1) * sine


def head_norm_back(incoming, values, gain):
    scale = lax.rsqrt(jnp.mean(values * values, axis=-1, keepdims=True) + epsilon)
    scaled = incoming * gain
    grad = scale * scaled - values * (
        scale * scale * scale * jnp.mean(scaled * values, axis=-1, keepdims=True)
    )
    return grad, jnp.sum(incoming * values * scale, axis=0, keepdims=True)


SCORE_SCALE = HEAD_SIZE**-0.5
LOG2_E = 1.4426950408889634
ROWS = 256
HALF = 128
COTANGENT = "cot"
DOWN_PART = "down_part"
MATRICES = ("wq", "wk", "wv")
SCATTER_PARTS = ("_near", "_sum", "_arr", "_send", "_recv")


def start_loads(ref, layout, pairs):
    loads = SimpleNamespace()
    table = vars(ref)
    for slot, name in enumerate(layout.loads):
        source, target = pairs[name] if name in pairs else (table[name], table["v_" + name])
        copy = pltpu.make_async_copy(source, target, ref.load_sems.at[slot])
        copy.start()
        setattr(loads, name, copy)
    return loads


def weight_grad(rows, cols, target):
    width = cols.shape[-1]
    right = cols[...].reshape(SEQUENCE_TOKENS, width)
    for j in range(4):
        left = rows[:, :, j * ROWS : (j + 1) * ROWS].reshape(SEQUENCE_TOKENS, ROWS)
        target[j] = dot(left.T, right).astype(jnp.bfloat16).reshape(4, 2, 32, width)


class RingSum:
    def __init__(self, box, slot, others, send_sems, recv_sems):
        self.box, self.slot, self.others = box, slot, others
        self.send_sems, self.recv_sems = send_sems, recv_sems

    def copy(self, index, slot):
        spot = self.box.at[slot]
        return send(
            spot, spot, self.send_sems.at[index], self.recv_sems.at[slot], self.others[index][1]
        )

    def start(self, value):
        self.box[self.slot] = value
        for index in range(len(self.others)):
            self.copy(index, self.slot).start()

    def end(self):
        for index, (slot, _) in enumerate(self.others):
            self.copy(index, slot).wait_recv()
        total = self.box[0]
        for slot in range(1, self.box.shape[0]):
            total = total + self.box[slot]
        for index in range(len(self.others)):
            self.copy(index, self.slot).wait_send()
        return total


def back_kernel(names, layout, *refs):
    ref = SimpleNamespace(**dict(zip(names, refs)))
    me = lax.axis_index("tensor")
    sibling, far, far_sibling = partner(me, FLIP), across(me), partner(me, MIRROR)
    place = rank_places()
    where = rank_where(place)
    pairs = dict(
        down_part_far=(ref.down_part.at[pl.ds(far, 1)], ref.v_down_part_far),
        down_part_own=(ref.down_part.at[pl.ds(me, 1)], ref.v_down_part_own),
    )
    for g in range(2):
        base = g * 512
        for name, source, start, size in (
            ("wq", ref.wq, 0, 256), ("wk", ref.wk, 256, 128), ("wv", ref.wv, 384, 128)
        ):
            pairs[name + str(g)] = (
                source.at[:, pl.ds(g * size, size)],
                ref.wcat.at[:, pl.ds(base + start, size)],
            )
    for i in range(len(layout.ffn)):
        name = "early" + str(i)
        pairs[name] = (vars(ref)[name], vars(ref)["f" + str(i) + "_0"])
    loads = start_loads(ref, layout, pairs)

    def turns(here):
        return here, partner(here, FLIP), partner(here, MIRROR), across(here)

    y = place["y"]
    eight = [
        (row * 4 + member, dict(where("y", row), tensor=member))
        for row in (y, 1 - y)
        for member in turns(me)
    ]
    rings = []
    for box, members in (
        (ref.box_x, [(x, where("x", x)) for x in turns(place["x"])]),
        (ref.box_z, [(z, where("z", z)) for z in turns(place["z"])]),
        (ref.box_eight, eight),
    ):
        rings.append(
            RingSum(
                box,
                members[0][0],
                members[1:],
                ref.gain_send.at[len(rings)],
                ref.gain_recv.at[len(rings)],
            )
        )
    greet([there for ring in rings for _, there in ring.others])

    down = Scatter(
        ref.down_part, ref.d_near, ref.d_sum, ref.d_arr, ref.d_send, ref.d_recv, me
    )
    down.start(0)
    down.start(1)

    table = vars(ref)

    def streams_of(kind, entries, send_sems, recv_sems):
        out = []
        for i, (source, start, size, order, target, at) in enumerate(entries):
            columns = pl.ds(start, size)
            stream = Stream(
                order,
                table[source].at[:, :, :, :, columns],
                table[target].at[:, pl.ds(at, size)],
                [table[kind + str(i) + "_" + str(j)] for j in range(STREAM_SCRATCH)],
                (send_sems.at[i], recv_sems.at[i]),
                place,
                where,
            )
            if "v_" + source in table:
                stream.local = table["v_" + source].at[:, :, :, :, columns]
            out.append(stream)
        return out

    ffn = streams_of("f", layout.ffn, ref.f_send, ref.f_recv)
    attn = streams_of("a", layout.attn, ref.a_send, ref.a_recv)
    out_streams, group_streams = attn[:4], (attn[4:8], attn[8:])

    def every(streams, *steps):
        for stream in streams:
            for step, *stage in steps:
                step(stream, *stage)

    for load in (loads.w_out, loads.att, loads.gh):
        load.wait()

    def attended_grad(block):
        part = dot_cols(ref.v_gh[block], ref.v_w_out[...]).astype(jnp.bfloat16)
        for head in range(4):
            g, r = head // 2, head % 2
            at = slice(head * HEAD_SIZE, (head + 1) * HEAD_SIZE)
            low = part[:, at]
            ref.do[g, block, r * ROWS : (r + 1) * ROWS, :] = low
            product = low.astype(jnp.float32) * ref.v_att[block, :, at].astype(jnp.float32)
            ref.delta[g, block, :, r * ROWS : (r + 1) * ROWS] = jnp.sum(
                product.T, axis=0, keepdims=True
            )

    attended_grad(3)
    attended_grad(2)

    loads.down_part_far.wait()
    down.cross(ref.v_down_part_far.at[0])
    for load in [loads.gate, loads.up, loads.down] + [
        vars(loads)["early" + str(i)] for i in range(len(ffn))
    ]:
        load.wait()
    every(ffn, (Stream.quarter, 0))
    attended_grad(1)
    attended_grad(0)
    weight_grad(ref.v_gh, ref.v_att, ref.gw_out)
    every(out_streams, (Stream.halve, 0))

    for load in (
        loads.q, loads.k, loads.v, loads.lse, loads.qraw, loads.kraw, loads.cos, loads.sin,
        loads.qg, loads.kg,
    ):
        load.wait()
    ref.qgain[...] = jnp.zeros_like(ref.qgain)
    ref.kgain[...] = jnp.zeros_like(ref.kgain)
    key_row = lax.broadcasted_iota(jnp.int32, (ROWS, 2 * ROWS), 0)
    query_col = lax.rem(lax.broadcasted_iota(jnp.int32, (ROWS, 2 * ROWS), 1), ROWS)
    allowed = key_row <= query_col

    def attend_group(g):
        base = 512 * g
        for qb in (3, 2, 1, 0):
            keys = (qb + 1) * ROWS
            key = ref.v_k[g, 0 : qb + 1].reshape(keys, HEAD_SIZE)
            query, grad_out = ref.v_q[g, qb], ref.do[g, qb]
            probs = jnp.exp2(
                dot_cols(key, query) * (SCORE_SCALE * LOG2_E) - ref.v_lse[g, qb]
            )
            tail = jnp.where(allowed, probs[keys - ROWS :], 0.0)
            probs = jnp.concatenate([probs[: keys - ROWS], tail], axis=0) if qb else tail
            grad_probs = dot_cols(
                ref.v_v[g, 0 : qb + 1].reshape(keys, HEAD_SIZE), grad_out
            )
            grad_scores = (probs * (grad_probs - ref.delta[g, qb])).astype(jnp.bfloat16)
            grad_value = dot(probs.astype(jnp.bfloat16), grad_out).reshape(qb + 1, ROWS, HEAD_SIZE)
            grad_key = dot(grad_scores, query).reshape(qb + 1, ROWS, HEAD_SIZE)
            if qb == 3:
                ref.dv[...] = grad_value
                ref.dk[...] = grad_key
            else:
                ref.dv[0 : qb + 1] += grad_value
                ref.dk[0 : qb + 1] += grad_key
            grads = dot(key.T, grad_scores).T * SCORE_SCALE
            for r in range(2):
                start = (2 * g + r) * HEAD_SIZE
                back = turn(
                    grads[r * ROWS : (r + 1) * ROWS], ref.v_cos[qb], ref.v_sin[qb]
                )
                grad, gain = head_norm_back(
                    back, ref.v_qraw[qb, :, start : start + HEAD_SIZE], vector(ref.v_qg)
                )
                at = base + r * HEAD_SIZE
                ref.dqkv[qb, :, at : at + HEAD_SIZE] = grad.astype(jnp.bfloat16)
                ref.qgain[...] += gain

        for kb in range(4):
            start = g * HEAD_SIZE
            back = turn(ref.dk[kb] * SCORE_SCALE, ref.v_cos[kb], ref.v_sin[kb])
            grad, gain = head_norm_back(
                back, ref.v_kraw[kb, :, start : start + HEAD_SIZE], vector(ref.v_kg)
            )
            ref.dqkv[kb, :, base + 256 : base + 384] = grad.astype(jnp.bfloat16)
            ref.dqkv[kb, :, base + 384 : base + 512] = ref.dv[kb].astype(jnp.bfloat16)
            ref.kgain[...] += gain

    attend_group(0)
    attend_group(1)

    for load in (loads.wq0, loads.wk0, loads.wv0, loads.wq1, loads.wk1, loads.wv1):
        load.wait()
    inward = Scatter(
        ref.x_part, ref.x_near, ref.x_sum, ref.x_arr, ref.x_send, ref.x_recv, me
    )

    loads.norm_all.wait()
    loads.norm_in.wait()
    loads.gain_mid.wait()
    ref.gain_in[...] = jnp.zeros_like(ref.gain_in)

    def inward_part(block, target):
        value = dot_cols(ref.dqkv[block], ref.wcat[...])
        target[...] = value.astype(target.dtype)
        ref.gain_in[...] += jnp.sum(
            value * ref.v_norm_all[block].astype(jnp.float32), axis=0, keepdims=True
        )

    inward_part(far_sibling, ref.x_part.at[far_sibling])
    inward.start(0)
    inward_part(far, ref.x_part.at[far])
    inward.cross(ref.x_part.at[far])
    inward_part(sibling, ref.x_part.at[sibling])
    inward.start(1)
    inward_part(me, ref.x_own)

    ref.gains[...] = jnp.zeros_like(ref.gains)
    gain_in = ref.gain_in[...] / vector(ref.v_norm_in)
    for row in range(8):
        at = slice(row * HEAD_SIZE, (row + 1) * HEAD_SIZE)
        ref.gains[row : row + 1] = gain_in[:, at]
        ref.gains[8 + row : 9 + row] = ref.v_gain_mid[:, at]
    ref.gains[16:17] = ref.qgain[...]
    ref.gains[17:18] = ref.kgain[...]
    rings[0].start(ref.gains[...])

    both = group_streams[0] + group_streams[1]
    every(ffn, (Stream.settle, 0), (Stream.halve, 1))
    every(out_streams, (Stream.quarter, 0))
    weight_grad(ref.v_norm_all, ref.dqkv.at[:, :, 0:512], ref.gw_0)
    every(group_streams[0], (Stream.halve, 0))
    weight_grad(ref.v_norm_all, ref.dqkv.at[:, :, 512:1024], ref.gw_1)
    every(group_streams[1], (Stream.halve, 0))
    rings[1].start(rings[0].end())
    every(ffn, (Stream.quarter, 1))
    every(out_streams, (Stream.settle, 0), (Stream.halve, 1))
    every(both, (Stream.quarter, 0))
    rings[2].start(rings[1].end())
    every(ffn, (Stream.settle, 1))
    every(out_streams, (Stream.quarter, 1))
    every(both, (Stream.settle, 0), (Stream.halve, 1))

    loads.hidden.wait()
    loads.down_part_own.wait()
    for chunk in range(CHUNKS):
        part = down.part(chunk)
        total = down.total(chunk, ref.v_down_part_own.at[0])
        ref.result[part] = (ref.v_hidden[part] + total).astype(jnp.bfloat16)
    every(out_streams, (Stream.settle, 1))
    every(both, (Stream.quarter, 1))
    every(ffn, (Stream.finish,))
    total = rings[2].end()
    for row in range(8):
        at = slice(row * HEAD_SIZE, (row + 1) * HEAD_SIZE)
        ref.o_norm_in[:, at] = total[row : row + 1]
        ref.o_norm_mid[:, at] = total[8 + row : 9 + row]
    ref.o_qgain[...] = total[16:17]
    ref.o_kgain[...] = total[17:18]
    every(both, (Stream.settle, 1))

    loads.tokens.wait()
    for chunk in range(CHUNKS):
        part = inward.part(chunk)
        incoming = inward.total(chunk, ref.x_own)
        values = ref.v_tokens[part].astype(jnp.float32)
        grad, _ = head_norm_back(incoming, values, vector(ref.v_norm_in))
        ref.grad_tokens[part] = (ref.v_gh[me, part].astype(jnp.float32) + grad).astype(
            jnp.bfloat16
        )
    every(out_streams, (Stream.finish,))
    every(both, (Stream.finish,))
    down.drain()
    inward.drain()


def hand_over_kernel(n, *refs):
    sources, targets, buffers, sems = refs[:n], refs[n : 2 * n], refs[2 * n : 3 * n], refs[3 * n]
    pulls = [pltpu.make_async_copy(sources[i], buffers[i], sems.at[0, i]) for i in range(n)]
    pushes = [pltpu.make_async_copy(buffers[i], targets[i], sems.at[1, i]) for i in range(n)]
    for pull in pulls:
        pull.start()
    for pull, push in zip(pulls, pushes):
        pull.wait()
        push.start()
    for push in pushes:
        push.wait()


def hand_over(arrays):
    n = len(arrays)
    anywhere = [pl.BlockSpec(memory_space=pl.ANY)] * n
    return pl.pallas_call(
        functools.partial(hand_over_kernel, n),
        out_shape=[jax.ShapeDtypeStruct(array.shape, array.dtype) for array in arrays],
        in_specs=anywhere,
        out_specs=anywhere,
        scratch_shapes=[pltpu.VMEM(array.shape, array.dtype) for array in arrays]
        + [pltpu.SemaphoreType.DMA((2, n))],
    )(*arrays)


def ffn_streams():
    xa, xb = ("x", FLIP, FLIP), ("x", MIRROR, MIRROR)
    za, zb = ("z", FLIP, MIRROR), ("z", MIRROR, FLIP)
    return [
        ("gate", 0, 384, xa, "o_gate", 0), ("gate", 384, 384, xb, "o_gate", 384),
        ("up", 0, 384, za, "o_up", 0), ("up", 384, 384, zb, "o_up", 384),
        ("down", 0, 256, xa, "o_down", 0), ("down", 256, 128, xb, "o_down", 256),
        ("down", 384, 256, za, "o_down", 384), ("down", 640, 128, zb, "o_down", 640),
    ]


def back_part(inputs, ffn):
    low, wide = jnp.bfloat16, jnp.float32
    names = list(inputs)
    weights = [name for name in names if name in MATRICES]
    loaded = [name for name in names if name != DOWN_PART and name not in MATRICES]
    loaded += [DOWN_PART + "_far", DOWN_PART + "_own"]
    shapes = {name: (inputs[name].shape, inputs[name].dtype) for name in loaded[:-2]}
    shapes.update({name: ((1, ROWS, 1024), low) for name in loaded[-2:]})
    loaded += [name + str(g) for g in range(2) for name in weights]
    early = [name for name in loaded if name.startswith(("down", "gate", "up", "early"))]
    loaded = loaded[:3] + early + [name for name in loaded[3:] if name not in early]
    outs = dict(
        result=((ROWS, 1024), low),
        grad_tokens=((ROWS, 1024), low),
        o_gate=((32, 768), wide),
        o_up=((32, 768), wide),
        o_down=((32, 768), wide),
        o_q=((32, 512), wide),
        o_k=((32, 256), wide),
        o_v=((32, 256), wide),
        o_out=((32, 512), wide),
        o_norm_in=((1, 1024), wide),
        o_norm_mid=((1, 1024), wide),
        o_qgain=((1, HEAD_SIZE), wide),
        o_kgain=((1, HEAD_SIZE), wide),
    )
    xa, xb = ("x", FLIP, FLIP), ("x", MIRROR, MIRROR)
    za, zb = ("z", FLIP, MIRROR), ("z", MIRROR, FLIP)
    layout = SimpleNamespace(
        loads=loaded,
        ffn=ffn,
        attn=[("gw_out", 128 * i, 128, way, "o_out", 128 * i) for i, way in enumerate((xb, zb, xa, za))]
        + [
            ("gw_" + str(g), 128 * i, 128, way, target, at + step * g)
            for g in range(2)
            for i, (way, target, at, step) in enumerate(
                ((xa, "o_q", 0, 256), (xb, "o_q", 128, 256), (za, "o_k", 0, 128), (zb, "o_v", 0, 128))
            )
        ],
    )
    scratch = {"v_" + name: pltpu.VMEM(*spec) for name, spec in shapes.items()}
    scratch.update(
        load_sems=pltpu.SemaphoreType.DMA((len(loaded),)),
        do=pltpu.VMEM((2, 4, 2 * ROWS, HEAD_SIZE), low),
        delta=pltpu.VMEM((2, 4, 1, 2 * ROWS), wide),
        dk=pltpu.VMEM((4, ROWS, HEAD_SIZE), wide),
        dv=pltpu.VMEM((4, ROWS, HEAD_SIZE), wide),
        dqkv=pltpu.VMEM((4, ROWS, 1024), low),
        wcat=pltpu.VMEM((1024, 1024), low),
        qgain=pltpu.VMEM((1, HEAD_SIZE), wide),
        kgain=pltpu.VMEM((1, HEAD_SIZE), wide),
        x_part=pltpu.VMEM((4, ROWS, 1024), low),
        x_own=pltpu.VMEM((ROWS, 1024), wide),
        gw_out=pltpu.VMEM((4, 4, 2, 32, 512), low),
        gw_0=pltpu.VMEM((4, 4, 2, 32, 512), low),
        gw_1=pltpu.VMEM((4, 4, 2, 32, 512), low),
        gains=pltpu.VMEM((24, HEAD_SIZE), wide),
        gain_in=pltpu.VMEM((1, 1024), wide),
        box_x=pltpu.VMEM((4, 24, HEAD_SIZE), wide),
        box_z=pltpu.VMEM((4, 24, HEAD_SIZE), wide),
        box_eight=pltpu.VMEM((8, 24, HEAD_SIZE), wide),
        gain_send=pltpu.SemaphoreType.DMA((3, 8)),
        gain_recv=pltpu.SemaphoreType.DMA((3, 8)),
    )
    for tag in "dx":
        scratch.update(zip((tag + end for end in SCATTER_PARTS), scatter_scratch(ROWS, 1024)))
    for kind, entries in (("f", layout.ffn), ("a", layout.attn)):
        for way in SCATTER_PARTS[3:]:
            scratch[kind + way] = pltpu.SemaphoreType.DMA((len(entries), STREAM_SEMS))
        for i, entry in enumerate(entries):
            for j, buffer in enumerate(stream_scratch(entry[2])):
                scratch[kind + str(i) + "_" + str(j)] = buffer
    for i in range(len(ffn)):
        scratch["f" + str(i) + "_0"] = scratch.pop("v_early" + str(i))
    results = pl.pallas_call(
        functools.partial(back_kernel, names + list(outs) + list(scratch), layout),
        out_shape=[jax.ShapeDtypeStruct(*spec) for spec in outs.values()],
        in_specs=[pl.BlockSpec(memory_space=pl.ANY)] * len(names),
        out_specs=[VMEM_SPACE] * len(outs),
        scratch_shapes=list(scratch.values()),
        compiler_params=pltpu.CompilerParams(
            collective_id=3, has_side_effects=True, vmem_limit_bytes=61 << 20
        ),
    )(*inputs.values())
    return SimpleNamespace(**dict(zip(outs, hand_over(results))))


class Exchange:
    def __init__(self, own, near_out, near_in, summed, arrived, send_sems, recv_sems, me):
        self.own, self.near_out, self.near_in = own, near_out, near_in
        self.summed, self.arrived = summed, arrived
        self.send_sems, self.recv_sems = send_sems, recv_sems
        self.sibling, self.far = {"tensor": partner(me, FLIP)}, {"tensor": across(me)}
        core = lax.rem(me, 2)
        self.mine = pl.ds(pl.multiple_of(core * HALF, HALF), HALF)
        self.other = pl.ds(pl.multiple_of((1 - core) * HALF, HALF), HALF)

    def near(self, block):
        return send(
            self.near_out.at[block],
            self.near_in.at[block],
            self.send_sems.at[0, block],
            self.recv_sems.at[0, block],
            self.sibling,
        )

    def swap(self, block):
        return send(
            self.summed.at[block],
            self.arrived.at[block],
            self.send_sems.at[1, block],
            self.recv_sems.at[1, block],
            self.far,
        )

    def share(self, block, whole):
        spot = whole.at[block, self.mine]
        return send(
            spot, spot, self.send_sems.at[2, block], self.recv_sems.at[2, block], self.sibling
        )

    def give(self, block, part):
        self.near_out[block] = part[self.other].astype(jnp.bfloat16)
        self.near(block).start()
        self.own[block] = part[self.mine]

    def cross(self, block):
        self.near(block).wait()
        self.summed[block] = (
            self.own[block] + self.near_in[block].astype(jnp.float32)
        ).astype(jnp.bfloat16)
        self.swap(block).start()

    def total(self, block):
        self.swap(block).wait()
        return self.summed[block].astype(jnp.float32) + self.arrived[block].astype(jnp.float32)


def exchange_scratch():
    half = pltpu.VMEM((4, HALF, 1024), jnp.bfloat16)
    sems = pltpu.SemaphoreType.DMA((3, 4))
    return [half, half, half, sems, sems]


def front_kernel(names, layout, *refs):
    ref = SimpleNamespace(**dict(zip(names, refs)))
    me = lax.axis_index("tensor")
    sibling, far, far_sibling = partner(me, FLIP), across(me), partner(me, MIRROR)
    place = rank_places()
    where = rank_where(place)
    loads = start_loads(
        ref,
        layout,
        dict(tokens=(ref.tokens, ref.tokens_all.at[me]), cot=(ref.cot, ref.dy_all.at[me])),
    )
    greet(
        [{"tensor": sibling}, {"tensor": far}]
        + [
            where(axis, partner(place[axis], pairing))
            for axis in ("x", "z")
            for pairing in (FLIP, MIRROR)
        ]
    )
    stores = []

    def store(source, target):
        copy = pltpu.make_async_copy(source, target, ref.store_sems.at[len(stores)])
        copy.start()
        stores.append(copy)

    first = Gather(ref.tokens_all, ref.n_send, ref.n_recv, me, ref.tokens)
    cot = Gather(ref.dy_all, ref.c_send, ref.c_recv, me, ref.cot)
    first.start()
    loads.tokens.wait()
    for load in (
        loads.norm_in, loads.wq, loads.wk, loads.wv, loads.cos, loads.sin, loads.qg, loads.kg
    ):
        load.wait()

    def project(block):
        values = ref.tokens_all[block].astype(jnp.float32)
        rows = (values * rms_scale(values) * vector(ref.v_norm_in)).astype(jnp.bfloat16)
        ref.norm_all[block] = rows
        raw = dot(rows, ref.v_wq[...])
        ref.qraw[block] = raw
        for head in range(4):
            values = raw[:, head * HEAD_SIZE : (head + 1) * HEAD_SIZE]
            values = values * rms_scale(values) * vector(ref.v_qg)
            ref.q[head // 2, block, (head % 2) * ROWS : (head % 2 + 1) * ROWS, :] = turn(
                values, ref.v_cos[block], -ref.v_sin[block]
            ).astype(jnp.bfloat16)
        raw = dot(rows, ref.v_wk[...])
        ref.kraw[block] = raw
        for g in range(2):
            values = raw[:, g * HEAD_SIZE : (g + 1) * HEAD_SIZE]
            values = values * rms_scale(values) * vector(ref.v_kg)
            ref.k[g, block] = turn(values, ref.v_cos[block], -ref.v_sin[block]).astype(jnp.bfloat16)
        low = dot(rows, ref.v_wv[...]).astype(jnp.bfloat16)
        for g in range(2):
            ref.v[g, block] = low[:, g * HEAD_SIZE : (g + 1) * HEAD_SIZE]

    project(me)
    first.wait_sibling()
    project(sibling)
    first.wait_far()
    loads.cot.wait()
    cot.start()
    project(far)
    first.wait_last()
    project(far_sibling)
    store(ref.norm_all, ref.o_norm_all)
    store(ref.q, ref.o_q)
    store(ref.k, ref.o_k)
    store(ref.v, ref.o_v)
    store(ref.qraw, ref.o_qraw)
    store(ref.kraw, ref.o_kraw)

    key_row = lax.broadcasted_iota(jnp.int32, (ROWS, 2 * ROWS), 0)
    query_col = lax.rem(lax.broadcasted_iota(jnp.int32, (ROWS, 2 * ROWS), 1), ROWS)
    allowed = key_row <= query_col
    loads.w_out.wait()
    mixed = Exchange(
        ref.own, ref.p_out, ref.p_near, ref.p_sum, ref.p_arr, ref.p_send, ref.p_recv, me
    )
    back = Exchange(
        ref.own, ref.p_out, ref.b_near, ref.b_sum, ref.b_arr, ref.b_send, ref.b_recv, me
    )

    def attend(block):
        keys = (block + 1) * ROWS
        for g in range(2):
            scores = dot_cols(
                ref.k[g, 0 : block + 1].reshape(keys, HEAD_SIZE), ref.q[g, block]
            )
            probs = jnp.exp2(scores * (SCORE_SCALE * LOG2_E))
            tail = jnp.where(allowed, probs[keys - ROWS :], 0.0)
            probs = jnp.concatenate([probs[: keys - ROWS], tail], axis=0) if block else tail
            total = jnp.sum(probs, axis=0, keepdims=True)
            ref.lse[g, block] = jnp.log(total) * LOG2_E
            values = ref.v[g, 0 : block + 1].reshape(keys, HEAD_SIZE)
            rows = (dot(values.T, probs.astype(jnp.bfloat16)) / total).T.astype(jnp.bfloat16)
            for r in range(2):
                start = (2 * g + r) * HEAD_SIZE
                ref.att[block, :, start : start + HEAD_SIZE] = rows[r * ROWS : (r + 1) * ROWS]
        ref.part[...] = dot(ref.att[block], ref.v_w_out[...])
        mixed.give(block, ref.part)

    attend(3)
    attend(2)
    mixed.cross(3)
    attend(1)
    mixed.cross(2)
    attend(0)
    mixed.cross(1)
    cot.wait_far()
    mixed.cross(0)
    store(ref.att, ref.o_att)
    store(ref.lse, ref.o_lse)
    cot.wait_sibling()
    cot.wait_last()
    for load in (loads.w_down, loads.norm_mid, loads.w_gate, loads.w_up):
        load.wait()

    def mid_norm(block):
        values = ref.tokens_all[block, mixed.mine].astype(jnp.float32) + mixed.total(block)
        ref.hidden[block] = values
        ref.mid_all[block, mixed.mine] = (
            values * rms_scale(values) * vector(ref.v_norm_mid)
        ).astype(jnp.bfloat16)
        mixed.share(block, ref.mid_all).start()

    def feed(block):
        grad = dot_cols(ref.dy_all[block], ref.v_w_down[...])
        mixed.share(block, ref.mid_all).wait()
        gate = dot(ref.mid_all[block], ref.v_w_gate[...])
        up = dot(ref.mid_all[block], ref.v_w_up[...])
        sigmoid = jax.nn.sigmoid(gate)
        silu = gate * sigmoid
        ref.act[block] = (silu * up).astype(jnp.bfloat16)
        ref.dup[block] = (grad * silu).astype(jnp.bfloat16)
        ref.dgate[block] = (grad * up * sigmoid * (1.0 + gate * (1.0 - sigmoid))).astype(jnp.bfloat16)
        value = dot_cols(ref.dgate[block], ref.v_w_gate[...])
        ref.part[...] = value + dot_cols(ref.dup[block], ref.v_w_up[...])
        back.give(block, ref.part)

    for block in (3, 2, 1, 0):
        mid_norm(block)
        feed(block)
        if block < 3:
            back.cross(block + 1)
    back.cross(0)

    streams = []
    table = vars(ref)
    for i, (source, start, size, order) in enumerate(layout.ffn):
        streams.append(
            Stream(
                order,
                table["gw_" + source].at[:, :, :, :, pl.ds(start, size)],
                None,
                [table["early" + str(i)]] + [None] * (STREAM_SCRATCH - 1),
                (ref.f_send.at[i], ref.f_recv.at[i]),
                place,
                where,
            )
        )

    weight_grad(ref.mid_all, ref.dgate, ref.gw_gate)
    for stream in streams[:2]:
        stream.halve(0)
    weight_grad(ref.mid_all, ref.dup, ref.gw_up)
    for stream in streams[2:4]:
        stream.halve(0)
    weight_grad(ref.dy_all, ref.act, ref.gw_down)
    for stream in streams[4:]:
        stream.halve(0)
    store(ref.gw_gate, ref.o_gate)
    store(ref.gw_up, ref.o_up)
    store(ref.gw_down, ref.o_down)
    for block in range(4):
        ref.down_part[block] = dot(ref.act[block], ref.v_w_down[...]).astype(jnp.bfloat16)
    store(ref.down_part, ref.o_down_part)

    own_half = send(
        ref.hidden.at[sibling], ref.hid.at[mixed.mine], ref.h_send, ref.h_recv, mixed.sibling
    )
    own_half.start()
    ref.hid[mixed.mine] = ref.hidden[me]

    ref.gain[...] = jnp.zeros_like(ref.gain)
    for block in (3, 2, 1, 0):
        incoming = back.total(block)
        grad, gain = head_norm_back(incoming, ref.hidden[block], vector(ref.v_norm_mid))
        ref.gh_all[block, back.mine] = (
            ref.dy_all[block, back.mine].astype(jnp.float32) + grad
        ).astype(jnp.bfloat16)
        back.share(block, ref.gh_all).start()
        ref.gain[...] += gain
    ref.gain[...] *= 0.5
    store(ref.gain, ref.o_gain)
    own_half.wait()
    store(ref.hid, ref.o_hidden)
    for block in (3, 2, 1, 0):
        back.share(block, ref.gh_all).wait()
        store(ref.gh_all.at[block], ref.o_gh.at[block])
    for i, stream in enumerate(streams):
        for copy in stream.copies:
            copy.wait()
        store(table["early" + str(i)], table["o_early" + str(i)])
    for copy in stores:
        copy.wait()
    first.drain()
    cot.drain()


def front_part(inputs, ffn):
    low, wide = jnp.bfloat16, jnp.float32
    names = list(inputs)
    outs = dict(
        o_norm_all=((4, ROWS, 1024), low),
        o_q=((2, 4, 2 * ROWS, HEAD_SIZE), low),
        o_k=((2, 4, ROWS, HEAD_SIZE), low),
        o_v=((2, 4, ROWS, HEAD_SIZE), low),
        o_qraw=((4, ROWS, 512), wide),
        o_kraw=((4, ROWS, 256), wide),
        o_att=((4, ROWS, 512), low),
        o_lse=((2, 4, 1, 2 * ROWS), wide),
        o_hidden=((ROWS, 1024), wide),
        o_down=((4, 4, 2, 32, 768), low),
        o_gate=((4, 4, 2, 32, 768), low),
        o_up=((4, 4, 2, 32, 768), low),
        o_down_part=((4, ROWS, 1024), low),
        o_gh=((4, ROWS, 1024), low),
        o_gain=((1, 1024), wide),
    )
    early = {"early" + str(i): ((2, 4, 2, 32, entry[2]), low) for i, entry in enumerate(ffn)}
    outs.update({"o_" + name: spec for name, spec in early.items()})
    whole = ("tokens", COTANGENT)
    scratch = {
        "v_" + name: pltpu.VMEM(inputs[name].shape, inputs[name].dtype)
        for name in names
        if name not in whole
    }
    scratch.update({name: pltpu.VMEM(*spec) for name, spec in early.items()})
    scratch.update(
        load_sems=pltpu.SemaphoreType.DMA((len(names),)),
        store_sems=pltpu.SemaphoreType.DMA((len(outs) + 3,)),
        f_send=pltpu.SemaphoreType.DMA((len(ffn), 2)),
        f_recv=pltpu.SemaphoreType.DMA((len(ffn), 2)),
        h_send=pltpu.SemaphoreType.DMA,
        h_recv=pltpu.SemaphoreType.DMA,
        norm_all=pltpu.VMEM((4, ROWS, 1024), low),
        mid_all=pltpu.VMEM((4, ROWS, 1024), low),
        gh_all=pltpu.VMEM((4, ROWS, 1024), low),
        qraw=pltpu.VMEM((4, ROWS, 512), wide),
        kraw=pltpu.VMEM((4, ROWS, 256), wide),
        q=pltpu.VMEM((2, 4, 2 * ROWS, HEAD_SIZE), low),
        k=pltpu.VMEM((2, 4, ROWS, HEAD_SIZE), low),
        v=pltpu.VMEM((2, 4, ROWS, HEAD_SIZE), low),
        lse=pltpu.VMEM((2, 4, 1, 2 * ROWS), wide),
        att=pltpu.VMEM((4, ROWS, 512), low),
        part=pltpu.VMEM((ROWS, 1024), wide),
        own=pltpu.VMEM((4, HALF, 1024), wide),
        hidden=pltpu.VMEM((4, HALF, 1024), wide),
        hid=pltpu.VMEM((ROWS, 1024), wide),
        p_out=pltpu.VMEM((4, HALF, 1024), low),
        act=pltpu.VMEM((4, ROWS, 768), low),
        dup=pltpu.VMEM((4, ROWS, 768), low),
        dgate=pltpu.VMEM((4, ROWS, 768), low),
        gw_down=pltpu.VMEM((4, 4, 2, 32, 768), low),
        gw_gate=pltpu.VMEM((4, 4, 2, 32, 768), low),
        gw_up=pltpu.VMEM((4, 4, 2, 32, 768), low),
        down_part=pltpu.VMEM((4, ROWS, 1024), low),
        gain=pltpu.VMEM((1, 1024), wide),
    )
    scratch.update(zip(("tokens_all", "n_send", "n_recv"), gather_scratch(ROWS, 1024)))
    scratch.update(zip(("dy_all", "c_send", "c_recv"), gather_scratch(ROWS, 1024)))
    for tag in "pb":
        scratch.update(zip((tag + end for end in SCATTER_PARTS), exchange_scratch()))
    results = pl.pallas_call(
        functools.partial(
            front_kernel,
            names + list(outs) + list(scratch),
            SimpleNamespace(loads=names, ffn=[entry[:4] for entry in ffn]),
        ),
        out_shape=[jax.ShapeDtypeStruct(*spec) for spec in outs.values()],
        in_specs=[pl.BlockSpec(memory_space=pl.ANY)] * len(names),
        out_specs=[pl.BlockSpec(memory_space=pl.ANY)] * len(outs),
        scratch_shapes=list(scratch.values()),
        compiler_params=pltpu.CompilerParams(
            collective_id=4, has_side_effects=True, vmem_limit_bytes=62 << 20
        ),
    )(*inputs.values())
    return SimpleNamespace(**dict(zip(outs, results)))


def rotary_tables():
    position = np.arange(SEQUENCE_TOKENS, dtype=np.float64)
    inverse = 1000000.0 ** (-np.arange(HEAD_SIZE // 2, dtype=np.float64) * 2.0 / HEAD_SIZE)
    angles = position[:, None] * inverse[None, :]
    cosine, sine = np.cos(angles), np.sin(angles)
    return (
        jnp.asarray(
            np.concatenate([table, tail], axis=1).astype(np.float32).reshape(4, ROWS, HEAD_SIZE)
        )
        for table, tail in ((cosine, cosine), (sine, -sine))
    )


def per_device(
    tokens,
    norm_in,
    w_query,
    key_matrix,
    value_matrix,
    query_gain,
    key_gain,
    w_out,
    norm_mid,
    w_gate,
    w_up,
    w_down,
    cotangent,
):
    cosine, sine = rotary_tables()
    ffn = ffn_streams()
    front = front_part(
        dict(
            tokens=tokens,
            norm_in=norm_in,
            wq=w_query,
            wk=key_matrix,
            wv=value_matrix,
            cos=cosine,
            sin=sine,
            qg=query_gain,
            kg=key_gain,
            cot=cotangent,
            w_out=w_out,
            w_down=w_down,
            norm_mid=norm_mid,
            w_gate=w_gate,
            w_up=w_up,
        ),
        ffn,
    )
    outs = back_part(
        dict(
            gh=front.o_gh,
            w_out=w_out,
            att=front.o_att,
            down_part=front.o_down_part,
            gate=front.o_gate,
            up=front.o_up,
            down=front.o_down,
            q=front.o_q,
            k=front.o_k,
            v=front.o_v,
            lse=front.o_lse,
            qraw=front.o_qraw,
            kraw=front.o_kraw,
            cos=cosine,
            sin=sine,
            qg=query_gain,
            kg=key_gain,
            wq=w_query,
            wk=key_matrix,
            wv=value_matrix,
            norm_all=front.o_norm_all,
            hidden=front.o_hidden,
            tokens=tokens,
            norm_in=norm_in,
            gain_mid=front.o_gain,
            **{"early" + str(i): vars(front)["o_early" + str(i)] for i in range(len(ffn))},
        ),
        ffn,
    )
    return (
        outs.result,
        outs.grad_tokens,
        outs.o_norm_in.reshape(1024),
        outs.o_q,
        outs.o_k,
        outs.o_v,
        outs.o_qgain.reshape(HEAD_SIZE),
        outs.o_kgain.reshape(HEAD_SIZE),
        outs.o_out.T,
        outs.o_norm_mid.reshape(1024),
        outs.o_gate,
        outs.o_up,
        outs.o_down.T,
    )


def solution(mesh):
    placed = (
        P(("dp", "tensor"), None),
        P(),
        P(None, "tensor"),
        P(None, "tensor"),
        P(None, "tensor"),
        P(),
        P(),
        P("tensor", None),
        P(),
        P(None, "tensor"),
        P(None, "tensor"),
        P("tensor", None),
        P(("dp", "tensor"), None),
    )
    return jax.shard_map(
        per_device,
        mesh=mesh,
        in_specs=placed,
        out_specs=(
            P(("dp", "tensor"), None),
            P(("dp", "tensor"), None),
            P(),
            P("dp", "tensor"),
            P("dp", "tensor"),
            P("dp", "tensor"),
            P(),
            P(),
            P("tensor", "dp"),
            P(),
            P("dp", "tensor"),
            P("dp", "tensor"),
            P("tensor", "dp"),
        ),
        check_vma=False,
    )
```

```python
import functools
from types import SimpleNamespace

import jax
import jax.numpy as jnp
import numpy as np
from jax import lax
from jax.experimental import pallas as pl
from jax.experimental.pallas import tpu as pltpu
from jax.sharding import PartitionSpec as P

HEAD_SIZE = 128
SEQUENCE_TOKENS = 1024
GROUP = 4
CHUNKS = 4
VMEM_SPACE = pl.BlockSpec(memory_space=pltpu.VMEM)
FLIP, MIRROR = 1, 3
epsilon = 1e-06
contract_cols = (((1,), (1,)), ((), ()))


def partner(index, pairing):
    if pairing == FLIP:
        return index + 1 - 2 * lax.rem(index, 2)
    return 3 - index


def across(index):
    return lax.rem(index + 2, 4)


def send(source, target, send_sem, recv_sem, where):
    return pltpu.make_async_remote_copy(
        src_ref=source,
        dst_ref=target,
        send_sem=send_sem,
        recv_sem=recv_sem,
        device_id=where,
        device_id_type=pl.DeviceIdType.MESH,
    )


def greet(others):
    barrier = pltpu.get_barrier_semaphore()
    for where in others:
        pl.semaphore_signal(barrier, inc=1, device_id=where, device_id_type=pl.DeviceIdType.MESH)
    pl.semaphore_wait(barrier, len(others))


class Stream:
    def __init__(self, order, grad, out, scratch, sems, place, where):
        self.first, self.orders = order[0], order[1:]
        self.grad, self.local, self.out = grad, grad, out
        self.early, self.mid, self.late, self.held, self.low, self.pair, self.last = scratch
        self.send_sems, self.recv_sems = sems
        self.place, self.where = place, where
        self.pending = []
        self.copies = [None, None]

    def axis(self, stage):
        return self.first if stage == 0 else ("z" if self.first == "x" else "x")

    def block(self, stage, index, local=True):
        if stage == 1:
            return self.held.at[index]
        grad = self.local if local else self.grad
        return grad.at[index] if self.first == "x" else grad.at[:, index]

    def launch(self, source, target, slot, where):
        copy = send(source, target, self.send_sems.at[slot], self.recv_sems.at[slot], where)
        copy.start()
        self.pending.append(copy)
        return copy

    def halve(self, stage):
        axis, here = self.axis(stage), self.place[self.axis(stage)]
        other = partner(here, self.orders[stage])
        box = self.early if stage == 0 else self.late
        self.copies = [
            self.launch(
                self.block(stage, index, False), box.at[slot], 4 * stage + slot, self.where(axis, other)
            )
            for slot, index in ((1, across(here)), (0, other))
        ]

    def quarter(self, stage):
        axis, here = self.axis(stage), self.place[self.axis(stage)]
        other = partner(here, FLIP + MIRROR - self.orders[stage])
        box, mid = (self.early, self.mid) if stage == 0 else (self.late, self.low)
        if self.copies[0]:
            self.copies[0].wait_recv()
        mine = self.block(stage, other)

        def add(row, _):
            mid[0, row] = mine[row] + box[1, row]
            return _

        lax.fori_loop(0, mid.shape[1], add, 0)
        self.copies.append(
            self.launch(mid.at[0], mid.at[1], 4 * stage + 2, self.where(axis, other))
        )

    def settle(self, stage):
        here = self.place[self.axis(stage)]
        if self.copies[1]:
            self.copies[1].wait_recv()
        self.copies[2].wait_recv()
        box, mid = (self.early, self.mid) if stage == 0 else (self.late, self.low)
        mine = self.block(stage, here)
        if stage == 0:

            def add(row, _):
                self.held[row] = mine[row] + box[0, row] + mid[1, row]
                return _

            lax.fori_loop(0, mid.shape[1], add, 0)
            return
        keep = self.place["y"]
        give = 1 - keep
        self.pair[0] = (
            mine[give].astype(jnp.float32)
            + box[0, give].astype(jnp.float32)
            + mid[1, give].astype(jnp.float32)
        ).astype(jnp.bfloat16)
        self.copies.append(
            self.launch(self.pair.at[0], self.pair.at[1], 3, self.where("y", give))
        )
        self.last[...] = (
            mine[keep].astype(jnp.float32)
            + box[0, keep].astype(jnp.float32)
            + mid[1, keep].astype(jnp.float32)
        )

    def finish(self):
        self.copies[3].wait_recv()
        self.out[...] = self.last[...] + self.pair[1].astype(jnp.float32)
        for copy in self.pending:
            copy.wait_send()


STREAM_SEMS = 7
STREAM_SCRATCH = 7


def stream_scratch(columns):
    low = jnp.bfloat16
    return [
        pltpu.VMEM((2, 4, 2, 32, columns), low),
        pltpu.VMEM((2, 4, 2, 32, columns), low),
        pltpu.VMEM((2, 2, 32, columns), low),
        pltpu.VMEM((4, 2, 32, columns), low),
        pltpu.VMEM((2, 2, 32, columns), low),
        pltpu.VMEM((2, 32, columns), low),
        pltpu.VMEM((32, columns), jnp.float32),
    ]


def rank_places():
    rank = lax.axis_index("dp")
    return {"x": lax.div(rank, 8), "z": lax.rem(lax.div(rank, 2), 4), "y": lax.rem(rank, 2)}


def rank_where(place):
    def where(axis, index):
        at = dict(place)
        at[axis] = index
        return {"dp": at["x"] * 8 + at["z"] * 2 + at["y"]}

    return where


def rms_scale(values):
    return lax.rsqrt(jnp.mean(values * values, axis=-1, keepdims=True) + epsilon)


class Gather:
    def __init__(self, whole, send_sems, recv_sems, me, shard=None):
        self.shard = shard
        self.whole, self.send_sems, self.recv_sems, self.me = whole, send_sems, recv_sems, me
        self.sibling, self.far = {"tensor": partner(me, FLIP)}, {"tensor": across(me)}
        self.rows = whole.shape[1] // CHUNKS

    def copy(self, lane, chunk, block, where):
        part = pl.ds(chunk * self.rows, self.rows)
        spot = self.whole.at[block, part]
        source = spot if self.shard is None or lane == 2 else self.shard.at[part]
        return send(source, spot, self.send_sems.at[lane, chunk], self.recv_sems.at[lane, chunk], where)

    def start_chunk(self, chunk):
        self.copy(0, chunk, self.me, self.far).start()
        self.copy(1, chunk, self.me, self.sibling).start()

    def start(self):
        for chunk in range(CHUNKS):
            self.copy(0, chunk, self.me, self.far).start()
        for chunk in range(CHUNKS):
            self.copy(1, chunk, self.me, self.sibling).start()

    def wait_sibling(self):
        for chunk in range(CHUNKS):
            self.copy(1, chunk, self.me, self.sibling).wait_recv()

    def wait_far(self):
        for chunk in range(CHUNKS):
            self.copy(0, chunk, self.me, self.far).wait_recv()
            self.copy(2, chunk, across(self.me), self.sibling).start()

    def wait_last(self):
        for chunk in range(CHUNKS):
            self.copy(2, chunk, across(self.me), self.sibling).wait_recv()

    def drain(self):
        for chunk in range(CHUNKS):
            self.copy(0, chunk, self.me, self.far).wait_send()
            self.copy(1, chunk, self.me, self.sibling).wait_send()
            self.copy(2, chunk, across(self.me), self.sibling).wait_send()


class Scatter:
    def __init__(self, partial, near, summed, arrived, send_sems, recv_sems, me):
        self.partial, self.near, self.summed, self.arrived = partial, near, summed, arrived
        self.send_sems, self.recv_sems, self.me = send_sems, recv_sems, me
        self.sibling, self.far = {"tensor": partner(me, FLIP)}, {"tensor": across(me)}
        self.rows = near.shape[1] // CHUNKS

    def part(self, chunk):
        return pl.ds(chunk * self.rows, self.rows)

    def near_copy(self, slot, chunk):
        block = partner(self.me, MIRROR if slot == 0 else FLIP)
        return send(
            self.partial.at[block, self.part(chunk)],
            self.near.at[slot, self.part(chunk)],
            self.send_sems.at[slot, chunk],
            self.recv_sems.at[slot, chunk],
            self.sibling,
        )

    def far_copy(self, chunk):
        return send(
            self.summed.at[self.part(chunk)],
            self.arrived.at[self.part(chunk)],
            self.send_sems.at[2, chunk],
            self.recv_sems.at[2, chunk],
            self.far,
        )

    def start(self, slot):
        for chunk in range(CHUNKS):
            self.near_copy(slot, chunk).start()

    def cross(self, mine):
        for chunk in range(CHUNKS):
            part = self.part(chunk)
            self.near_copy(0, chunk).wait_recv()
            self.summed[part] = (
                mine[part].astype(jnp.float32) + self.near[0, part].astype(jnp.float32)
            ).astype(jnp.bfloat16)
            self.far_copy(chunk).start()

    def total(self, chunk, mine):
        part = self.part(chunk)
        self.near_copy(1, chunk).wait_recv()
        self.far_copy(chunk).wait_recv()
        return (
            mine[part].astype(jnp.float32)
            + self.near[1, part].astype(jnp.float32)
            + self.arrived[part].astype(jnp.float32)
        )

    def drain(self):
        for chunk in range(CHUNKS):
            self.near_copy(0, chunk).wait_send()
            self.near_copy(1, chunk).wait_send()
            self.far_copy(chunk).wait_send()


def scatter_scratch(rows, width):
    return [
        pltpu.VMEM((2, rows, width), jnp.bfloat16),
        pltpu.VMEM((rows, width), jnp.bfloat16),
        pltpu.VMEM((rows, width), jnp.bfloat16),
        pltpu.SemaphoreType.DMA((3, CHUNKS)),
        pltpu.SemaphoreType.DMA((3, CHUNKS)),
    ]


def gather_scratch(rows, width):
    return [
        pltpu.VMEM((GROUP, rows, width), jnp.bfloat16),
        pltpu.SemaphoreType.DMA((3, CHUNKS)),
        pltpu.SemaphoreType.DMA((3, CHUNKS)),
    ]


def vector(ref):
    return ref[...].astype(jnp.float32).reshape(1, ref.shape[0])


def dot(left, right):
    return jnp.dot(left, right, preferred_element_type=jnp.float32)


def dot_cols(left, right):
    return lax.dot_general(left, right, contract_cols, preferred_element_type=jnp.float32)


def turn(values, cosine, sine):
    return values * cosine + pltpu.roll(values, HEAD_SIZE // 2, 1) * sine


def head_norm_back(incoming, values, gain):
    scale = lax.rsqrt(jnp.mean(values * values, axis=-1, keepdims=True) + epsilon)
    scaled = incoming * gain
    grad = scale * scaled - values * (
        scale * scale * scale * jnp.mean(scaled * values, axis=-1, keepdims=True)
    )
    return grad, jnp.sum(incoming * values * scale, axis=0, keepdims=True)


SCORE_SCALE = HEAD_SIZE**-0.5
LOG2_E = 1.4426950408889634
ROWS = 256
HALF = 128
COTANGENT = "cot"
DOWN_PART = "down_part"
MATRICES = ("wq", "wk", "wv")
SCATTER_PARTS = ("_near", "_sum", "_arr", "_send", "_recv")


def start_loads(ref, layout, pairs):
    loads = SimpleNamespace()
    table = vars(ref)
    for slot, name in enumerate(layout.loads):
        source, target = pairs[name] if name in pairs else (table[name], table["v_" + name])
        copy = pltpu.make_async_copy(source, target, ref.load_sems.at[slot])
        copy.start()
        setattr(loads, name, copy)
    return loads


def weight_grad(rows, cols, target):
    width = cols.shape[-1]
    right = cols[...].reshape(SEQUENCE_TOKENS, width)
    for j in range(4):
        left = rows[:, :, j * ROWS : (j + 1) * ROWS].reshape(SEQUENCE_TOKENS, ROWS)
        target[j] = dot(left.T, right).astype(jnp.bfloat16).reshape(4, 2, 32, width)


class RingSum:
    def __init__(self, box, slot, others, send_sems, recv_sems):
        self.box, self.slot, self.others = box, slot, others
        self.send_sems, self.recv_sems = send_sems, recv_sems

    def copy(self, index, slot):
        spot = self.box.at[slot]
        return send(
            spot, spot, self.send_sems.at[index], self.recv_sems.at[slot], self.others[index][1]
        )

    def start(self, value):
        self.box[self.slot] = value
        for index in range(len(self.others)):
            self.copy(index, self.slot).start()

    def end(self):
        for index, (slot, _) in enumerate(self.others):
            self.copy(index, slot).wait_recv()
        total = self.box[0]
        for slot in range(1, self.box.shape[0]):
            total = total + self.box[slot]
        for index in range(len(self.others)):
            self.copy(index, self.slot).wait_send()
        return total


def back_kernel(names, layout, *refs):
    ref = SimpleNamespace(**dict(zip(names, refs)))
    me = lax.axis_index("tensor")
    sibling, far, far_sibling = partner(me, FLIP), across(me), partner(me, MIRROR)
    place = rank_places()
    where = rank_where(place)
    pairs = dict(
        down_part_far=(ref.down_part.at[pl.ds(far, 1)], ref.v_down_part_far),
        down_part_own=(ref.down_part.at[pl.ds(me, 1)], ref.v_down_part_own),
    )
    for g in range(2):
        base = g * 512
        for name, source, start, size in (
            ("wq", ref.wq, 0, 256), ("wk", ref.wk, 256, 128), ("wv", ref.wv, 384, 128)
        ):
            pairs[name + str(g)] = (
                source.at[:, pl.ds(g * size, size)],
                ref.wcat.at[:, pl.ds(base + start, size)],
            )
    for i in range(len(layout.ffn)):
        name = "early" + str(i)
        pairs[name] = (vars(ref)[name], vars(ref)["f" + str(i) + "_0"])
    loads = start_loads(ref, layout, pairs)

    def turns(here):
        return here, partner(here, FLIP), partner(here, MIRROR), across(here)

    y = place["y"]
    eight = [
        (row * 4 + member, dict(where("y", row), tensor=member))
        for row in (y, 1 - y)
        for member in turns(me)
    ]
    rings = []
    for box, members in (
        (ref.box_x, [(x, where("x", x)) for x in turns(place["x"])]),
        (ref.box_z, [(z, where("z", z)) for z in turns(place["z"])]),
        (ref.box_eight, eight),
    ):
        rings.append(
            RingSum(
                box,
                members[0][0],
                members[1:],
                ref.gain_send.at[len(rings)],
                ref.gain_recv.at[len(rings)],
            )
        )
    greet([there for ring in rings for _, there in ring.others])

    down = Scatter(
        ref.down_part, ref.d_near, ref.d_sum, ref.d_arr, ref.d_send, ref.d_recv, me
    )
    down.start(0)
    down.start(1)

    table = vars(ref)

    def streams_of(kind, entries, send_sems, recv_sems):
        out = []
        for i, (source, start, size, order, target, at) in enumerate(entries):
            columns = pl.ds(start, size)
            stream = Stream(
                order,
                table[source].at[:, :, :, :, columns],
                table[target].at[:, pl.ds(at, size)],
                [table[kind + str(i) + "_" + str(j)] for j in range(STREAM_SCRATCH)],
                (send_sems.at[i], recv_sems.at[i]),
                place,
                where,
            )
            if "v_" + source in table:
                stream.local = table["v_" + source].at[:, :, :, :, columns]
            out.append(stream)
        return out

    ffn = streams_of("f", layout.ffn, ref.f_send, ref.f_recv)
    attn = streams_of("a", layout.attn, ref.a_send, ref.a_recv)
    out_streams, group_streams = attn[:4], (attn[4:8], attn[8:])

    def every(streams, *steps):
        for stream in streams:
            for step, *stage in steps:
                step(stream, *stage)

    for load in (loads.w_out, loads.att, loads.gh):
        load.wait()

    def attended_grad(block):
        part = dot_cols(ref.v_gh[block], ref.v_w_out[...]).astype(jnp.bfloat16)
        for head in range(4):
            g, r = head // 2, head % 2
            at = slice(head * HEAD_SIZE, (head + 1) * HEAD_SIZE)
            low = part[:, at]
            ref.do[g, block, r * ROWS : (r + 1) * ROWS, :] = low
            product = low.astype(jnp.float32) * ref.v_att[block, :, at].astype(jnp.float32)
            ref.delta[g, block, :, r * ROWS : (r + 1) * ROWS] = jnp.sum(
                product.T, axis=0, keepdims=True
            )

    attended_grad(3)
    attended_grad(2)

    loads.down_part_far.wait()
    down.cross(ref.v_down_part_far.at[0])
    for load in [loads.gate, loads.up, loads.down] + [
        vars(loads)["early" + str(i)] for i in range(len(ffn))
    ]:
        load.wait()
    every(ffn, (Stream.quarter, 0))
    attended_grad(1)
    attended_grad(0)
    weight_grad(ref.v_gh, ref.v_att, ref.gw_out)
    every(out_streams, (Stream.halve, 0))

    for load in (
        loads.q, loads.k, loads.v, loads.lse, loads.qraw, loads.kraw, loads.cos, loads.sin,
        loads.qg, loads.kg,
    ):
        load.wait()
    ref.qgain[...] = jnp.zeros_like(ref.qgain)
    ref.kgain[...] = jnp.zeros_like(ref.kgain)
    key_row = lax.broadcasted_iota(jnp.int32, (ROWS, 2 * ROWS), 0)
    query_col = lax.rem(lax.broadcasted_iota(jnp.int32, (ROWS, 2 * ROWS), 1), ROWS)
    allowed = key_row <= query_col

    def attend_group(g):
        base = 512 * g
        for qb in (3, 2, 1, 0):
            keys = (qb + 1) * ROWS
            key = ref.v_k[g, 0 : qb + 1].reshape(keys, HEAD_SIZE)
            query, grad_out = ref.v_q[g, qb], ref.do[g, qb]
            probs = jnp.exp2(
                dot_cols(key, query) * (SCORE_SCALE * LOG2_E) - ref.v_lse[g, qb]
            )
            tail = jnp.where(allowed, probs[keys - ROWS :], 0.0)
            probs = jnp.concatenate([probs[: keys - ROWS], tail], axis=0) if qb else tail
            grad_probs = dot_cols(
                ref.v_v[g, 0 : qb + 1].reshape(keys, HEAD_SIZE), grad_out
            )
            grad_scores = (probs * (grad_probs - ref.delta[g, qb])).astype(jnp.bfloat16)
            grad_value = dot(probs.astype(jnp.bfloat16), grad_out).reshape(qb + 1, ROWS, HEAD_SIZE)
            grad_key = dot(grad_scores, query).reshape(qb + 1, ROWS, HEAD_SIZE)
            if qb == 3:
                ref.dv[...] = grad_value
                ref.dk[...] = grad_key
            else:
                ref.dv[0 : qb + 1] += grad_value
                ref.dk[0 : qb + 1] += grad_key
            grads = dot(key.T, grad_scores).T * SCORE_SCALE
            for r in range(2):
                start = (2 * g + r) * HEAD_SIZE
                back = turn(
                    grads[r * ROWS : (r + 1) * ROWS], ref.v_cos[qb], ref.v_sin[qb]
                )
                grad, gain = head_norm_back(
                    back, ref.v_qraw[qb, :, start : start + HEAD_SIZE], vector(ref.v_qg)
                )
                at = base + r * HEAD_SIZE
                ref.dqkv[qb, :, at : at + HEAD_SIZE] = grad.astype(jnp.bfloat16)
                ref.qgain[...] += gain

        for kb in range(4):
            start = g * HEAD_SIZE
            back = turn(ref.dk[kb] * SCORE_SCALE, ref.v_cos[kb], ref.v_sin[kb])
            grad, gain = head_norm_back(
                back, ref.v_kraw[kb, :, start : start + HEAD_SIZE], vector(ref.v_kg)
            )
            ref.dqkv[kb, :, base + 256 : base + 384] = grad.astype(jnp.bfloat16)
            ref.dqkv[kb, :, base + 384 : base + 512] = ref.dv[kb].astype(jnp.bfloat16)
            ref.kgain[...] += gain

    attend_group(0)
    loads.norm_all.wait()
    weight_grad(ref.v_norm_all, ref.dqkv.at[:, :, 0:512], ref.gw_0)
    every(group_streams[0], (Stream.halve, 0))
    every(ffn, (Stream.settle, 0), (Stream.halve, 1))
    every(out_streams, (Stream.quarter, 0))
    attend_group(1)
    weight_grad(ref.v_norm_all, ref.dqkv.at[:, :, 512:1024], ref.gw_1)
    every(group_streams[1], (Stream.halve, 0))

    for load in (loads.wq0, loads.wk0, loads.wv0, loads.wq1, loads.wk1, loads.wv1):
        load.wait()
    inward = Scatter(
        ref.x_part, ref.x_near, ref.x_sum, ref.x_arr, ref.x_send, ref.x_recv, me
    )

    loads.norm_in.wait()
    loads.gain_mid.wait()
    ref.gain_in[...] = jnp.zeros_like(ref.gain_in)

    def inward_part(block, target):
        value = dot_cols(ref.dqkv[block], ref.wcat[...])
        target[...] = value.astype(target.dtype)
        ref.gain_in[...] += jnp.sum(
            value * ref.v_norm_all[block].astype(jnp.float32), axis=0, keepdims=True
        )

    inward_part(far_sibling, ref.x_part.at[far_sibling])
    inward.start(0)
    inward_part(far, ref.x_part.at[far])
    inward.cross(ref.x_part.at[far])
    inward_part(sibling, ref.x_part.at[sibling])
    inward.start(1)
    inward_part(me, ref.x_own)

    ref.gains[...] = jnp.zeros_like(ref.gains)
    gain_in = ref.gain_in[...] / vector(ref.v_norm_in)
    for row in range(8):
        at = slice(row * HEAD_SIZE, (row + 1) * HEAD_SIZE)
        ref.gains[row : row + 1] = gain_in[:, at]
        ref.gains[8 + row : 9 + row] = ref.v_gain_mid[:, at]
    ref.gains[16:17] = ref.qgain[...]
    ref.gains[17:18] = ref.kgain[...]
    rings[0].start(ref.gains[...])

    both = group_streams[0] + group_streams[1]
    every(both, (Stream.quarter, 0))
    every(ffn, (Stream.quarter, 1))
    every(out_streams, (Stream.settle, 0), (Stream.halve, 1))
    rings[1].start(rings[0].end())
    every(both, (Stream.settle, 0), (Stream.halve, 1))
    every(ffn, (Stream.settle, 1))
    every(out_streams, (Stream.quarter, 1))
    rings[2].start(rings[1].end())
    every(both, (Stream.quarter, 1))
    every(out_streams, (Stream.settle, 1))

    loads.hidden.wait()
    loads.down_part_own.wait()
    for chunk in range(CHUNKS):
        part = down.part(chunk)
        total = down.total(chunk, ref.v_down_part_own.at[0])
        ref.result[part] = (ref.v_hidden[part] + total).astype(jnp.bfloat16)
    every(both, (Stream.settle, 1))
    every(ffn, (Stream.finish,))
    total = rings[2].end()
    for row in range(8):
        at = slice(row * HEAD_SIZE, (row + 1) * HEAD_SIZE)
        ref.o_norm_in[:, at] = total[row : row + 1]
        ref.o_norm_mid[:, at] = total[8 + row : 9 + row]
    ref.o_qgain[...] = total[16:17]
    ref.o_kgain[...] = total[17:18]

    loads.tokens.wait()
    for chunk in range(CHUNKS):
        part = inward.part(chunk)
        incoming = inward.total(chunk, ref.x_own)
        values = ref.v_tokens[part].astype(jnp.float32)
        grad, _ = head_norm_back(incoming, values, vector(ref.v_norm_in))
        ref.grad_tokens[part] = (ref.v_gh[me, part].astype(jnp.float32) + grad).astype(
            jnp.bfloat16
        )
    every(out_streams, (Stream.finish,))
    every(both, (Stream.finish,))
    down.drain()
    inward.drain()


def hand_over_kernel(n, *refs):
    sources, targets, buffers, sems = refs[:n], refs[n : 2 * n], refs[2 * n : 3 * n], refs[3 * n]
    pulls = [pltpu.make_async_copy(sources[i], buffers[i], sems.at[0, i]) for i in range(n)]
    pushes = [pltpu.make_async_copy(buffers[i], targets[i], sems.at[1, i]) for i in range(n)]
    for pull in pulls:
        pull.start()
    for pull, push in zip(pulls, pushes):
        pull.wait()
        push.start()
    for push in pushes:
        push.wait()


def hand_over(arrays):
    n = len(arrays)
    anywhere = [pl.BlockSpec(memory_space=pl.ANY)] * n
    return pl.pallas_call(
        functools.partial(hand_over_kernel, n),
        out_shape=[jax.ShapeDtypeStruct(array.shape, array.dtype) for array in arrays],
        in_specs=anywhere,
        out_specs=anywhere,
        scratch_shapes=[pltpu.VMEM(array.shape, array.dtype) for array in arrays]
        + [pltpu.SemaphoreType.DMA((2, n))],
    )(*arrays)


def ffn_streams():
    xa, xb = ("x", FLIP, FLIP), ("x", MIRROR, MIRROR)
    za, zb = ("z", FLIP, MIRROR), ("z", MIRROR, FLIP)
    return [
        ("gate", 0, 384, xa, "o_gate", 0), ("gate", 384, 384, xb, "o_gate", 384),
        ("up", 0, 384, za, "o_up", 0), ("up", 384, 384, zb, "o_up", 384),
        ("down", 0, 256, xa, "o_down", 0), ("down", 256, 128, xb, "o_down", 256),
        ("down", 384, 256, za, "o_down", 384), ("down", 640, 128, zb, "o_down", 640),
    ]


def back_part(inputs, ffn):
    low, wide = jnp.bfloat16, jnp.float32
    names = list(inputs)
    weights = [name for name in names if name in MATRICES]
    loaded = [name for name in names if name != DOWN_PART and name not in MATRICES]
    loaded += [DOWN_PART + "_far", DOWN_PART + "_own"]
    shapes = {name: (inputs[name].shape, inputs[name].dtype) for name in loaded[:-2]}
    shapes.update({name: ((1, ROWS, 1024), low) for name in loaded[-2:]})
    loaded += [name + str(g) for g in range(2) for name in weights]
    early = [name for name in loaded if name.startswith(("down", "gate", "up", "early"))]
    loaded = loaded[:3] + early + [name for name in loaded[3:] if name not in early]
    outs = dict(
        result=((ROWS, 1024), low),
        grad_tokens=((ROWS, 1024), low),
        o_gate=((32, 768), wide),
        o_up=((32, 768), wide),
        o_down=((32, 768), wide),
        o_q=((32, 512), wide),
        o_k=((32, 256), wide),
        o_v=((32, 256), wide),
        o_out=((32, 512), wide),
        o_norm_in=((1, 1024), wide),
        o_norm_mid=((1, 1024), wide),
        o_qgain=((1, HEAD_SIZE), wide),
        o_kgain=((1, HEAD_SIZE), wide),
    )
    xa, xb = ("x", FLIP, FLIP), ("x", MIRROR, MIRROR)
    za, zb = ("z", FLIP, MIRROR), ("z", MIRROR, FLIP)
    layout = SimpleNamespace(
        loads=loaded,
        ffn=ffn,
        attn=[("gw_out", 128 * i, 128, way, "o_out", 128 * i) for i, way in enumerate((xb, zb, xa, za))]
        + [
            ("gw_" + str(g), 128 * i, 128, way, target, at + step * g)
            for g in range(2)
            for i, (way, target, at, step) in enumerate(
                ((xa, "o_q", 0, 256), (xb, "o_q", 128, 256), (za, "o_k", 0, 128), (zb, "o_v", 0, 128))
            )
        ],
    )
    scratch = {"v_" + name: pltpu.VMEM(*spec) for name, spec in shapes.items()}
    scratch.update(
        load_sems=pltpu.SemaphoreType.DMA((len(loaded),)),
        do=pltpu.VMEM((2, 4, 2 * ROWS, HEAD_SIZE), low),
        delta=pltpu.VMEM((2, 4, 1, 2 * ROWS), wide),
        dk=pltpu.VMEM((4, ROWS, HEAD_SIZE), wide),
        dv=pltpu.VMEM((4, ROWS, HEAD_SIZE), wide),
        dqkv=pltpu.VMEM((4, ROWS, 1024), low),
        wcat=pltpu.VMEM((1024, 1024), low),
        qgain=pltpu.VMEM((1, HEAD_SIZE), wide),
        kgain=pltpu.VMEM((1, HEAD_SIZE), wide),
        x_part=pltpu.VMEM((4, ROWS, 1024), low),
        x_own=pltpu.VMEM((ROWS, 1024), wide),
        gw_out=pltpu.VMEM((4, 4, 2, 32, 512), low),
        gw_0=pltpu.VMEM((4, 4, 2, 32, 512), low),
        gw_1=pltpu.VMEM((4, 4, 2, 32, 512), low),
        gains=pltpu.VMEM((24, HEAD_SIZE), wide),
        gain_in=pltpu.VMEM((1, 1024), wide),
        box_x=pltpu.VMEM((4, 24, HEAD_SIZE), wide),
        box_z=pltpu.VMEM((4, 24, HEAD_SIZE), wide),
        box_eight=pltpu.VMEM((8, 24, HEAD_SIZE), wide),
        gain_send=pltpu.SemaphoreType.DMA((3, 8)),
        gain_recv=pltpu.SemaphoreType.DMA((3, 8)),
    )
    for tag in "dx":
        scratch.update(zip((tag + end for end in SCATTER_PARTS), scatter_scratch(ROWS, 1024)))
    for kind, entries in (("f", layout.ffn), ("a", layout.attn)):
        for way in SCATTER_PARTS[3:]:
            scratch[kind + way] = pltpu.SemaphoreType.DMA((len(entries), STREAM_SEMS))
        for i, entry in enumerate(entries):
            for j, buffer in enumerate(stream_scratch(entry[2])):
                scratch[kind + str(i) + "_" + str(j)] = buffer
    for i in range(len(ffn)):
        scratch["f" + str(i) + "_0"] = scratch.pop("v_early" + str(i))
    results = pl.pallas_call(
        functools.partial(back_kernel, names + list(outs) + list(scratch), layout),
        out_shape=[jax.ShapeDtypeStruct(*spec) for spec in outs.values()],
        in_specs=[pl.BlockSpec(memory_space=pl.ANY)] * len(names),
        out_specs=[VMEM_SPACE] * len(outs),
        scratch_shapes=list(scratch.values()),
        compiler_params=pltpu.CompilerParams(
            collective_id=3, has_side_effects=True, vmem_limit_bytes=61 << 20
        ),
    )(*inputs.values())
    return SimpleNamespace(**dict(zip(outs, hand_over(results))))


class Exchange:
    def __init__(self, own, near_out, near_in, summed, arrived, send_sems, recv_sems, me):
        self.own, self.near_out, self.near_in = own, near_out, near_in
        self.summed, self.arrived = summed, arrived
        self.send_sems, self.recv_sems = send_sems, recv_sems
        self.sibling, self.far = {"tensor": partner(me, FLIP)}, {"tensor": across(me)}
        core = lax.rem(me, 2)
        self.mine = pl.ds(pl.multiple_of(core * HALF, HALF), HALF)
        self.other = pl.ds(pl.multiple_of((1 - core) * HALF, HALF), HALF)

    def near(self, block):
        return send(
            self.near_out.at[block],
            self.near_in.at[block],
            self.send_sems.at[0, block],
            self.recv_sems.at[0, block],
            self.sibling,
        )

    def swap(self, block):
        return send(
            self.summed.at[block],
            self.arrived.at[block],
            self.send_sems.at[1, block],
            self.recv_sems.at[1, block],
            self.far,
        )

    def share(self, block, whole):
        spot = whole.at[block, self.mine]
        return send(
            spot, spot, self.send_sems.at[2, block], self.recv_sems.at[2, block], self.sibling
        )

    def give(self, block, part):
        self.near_out[block] = part[self.other].astype(jnp.bfloat16)
        self.near(block).start()
        self.own[block] = part[self.mine]

    def cross(self, block):
        self.near(block).wait()
        self.summed[block] = (
            self.own[block] + self.near_in[block].astype(jnp.float32)
        ).astype(jnp.bfloat16)
        self.swap(block).start()

    def total(self, block):
        self.swap(block).wait()
        return self.summed[block].astype(jnp.float32) + self.arrived[block].astype(jnp.float32)


def exchange_scratch():
    half = pltpu.VMEM((4, HALF, 1024), jnp.bfloat16)
    sems = pltpu.SemaphoreType.DMA((3, 4))
    return [half, half, half, sems, sems]


def front_kernel(names, layout, *refs):
    ref = SimpleNamespace(**dict(zip(names, refs)))
    me = lax.axis_index("tensor")
    sibling, far, far_sibling = partner(me, FLIP), across(me), partner(me, MIRROR)
    place = rank_places()
    where = rank_where(place)
    loads = start_loads(
        ref,
        layout,
        dict(tokens=(ref.tokens, ref.tokens_all.at[me]), cot=(ref.cot, ref.dy_all.at[me])),
    )
    greet(
        [{"tensor": sibling}, {"tensor": far}]
        + [
            where(axis, partner(place[axis], pairing))
            for axis in ("x", "z")
            for pairing in (FLIP, MIRROR)
        ]
    )
    stores = []

    def store(source, target):
        copy = pltpu.make_async_copy(source, target, ref.store_sems.at[len(stores)])
        copy.start()
        stores.append(copy)

    first = Gather(ref.tokens_all, ref.n_send, ref.n_recv, me, ref.tokens)
    cot = Gather(ref.dy_all, ref.c_send, ref.c_recv, me, ref.cot)
    first.start()
    loads.tokens.wait()
    for load in (
        loads.norm_in, loads.wq, loads.wk, loads.wv, loads.cos, loads.sin, loads.qg, loads.kg
    ):
        load.wait()

    def project(block):
        values = ref.tokens_all[block].astype(jnp.float32)
        rows = (values * rms_scale(values) * vector(ref.v_norm_in)).astype(jnp.bfloat16)
        ref.norm_all[block] = rows
        raw = dot(rows, ref.v_wq[...])
        ref.qraw[block] = raw
        for head in range(4):
            values = raw[:, head * HEAD_SIZE : (head + 1) * HEAD_SIZE]
            values = values * rms_scale(values) * vector(ref.v_qg)
            ref.q[head // 2, block, (head % 2) * ROWS : (head % 2 + 1) * ROWS, :] = turn(
                values, ref.v_cos[block], -ref.v_sin[block]
            ).astype(jnp.bfloat16)
        raw = dot(rows, ref.v_wk[...])
        ref.kraw[block] = raw
        for g in range(2):
            values = raw[:, g * HEAD_SIZE : (g + 1) * HEAD_SIZE]
            values = values * rms_scale(values) * vector(ref.v_kg)
            ref.k[g, block] = turn(values, ref.v_cos[block], -ref.v_sin[block]).astype(jnp.bfloat16)
        low = dot(rows, ref.v_wv[...]).astype(jnp.bfloat16)
        for g in range(2):
            ref.v[g, block] = low[:, g * HEAD_SIZE : (g + 1) * HEAD_SIZE]

    project(me)
    first.wait_sibling()
    project(sibling)
    first.wait_far()
    loads.cot.wait()
    cot.start()
    project(far)
    first.wait_last()
    project(far_sibling)
    store(ref.norm_all, ref.o_norm_all)
    store(ref.q, ref.o_q)
    store(ref.k, ref.o_k)
    store(ref.v, ref.o_v)
    store(ref.qraw, ref.o_qraw)
    store(ref.kraw, ref.o_kraw)

    key_row = lax.broadcasted_iota(jnp.int32, (ROWS, 2 * ROWS), 0)
    query_col = lax.rem(lax.broadcasted_iota(jnp.int32, (ROWS, 2 * ROWS), 1), ROWS)
    allowed = key_row <= query_col
    loads.w_out.wait()
    mixed = Exchange(
        ref.own, ref.p_out, ref.p_near, ref.p_sum, ref.p_arr, ref.p_send, ref.p_recv, me
    )
    back = Exchange(
        ref.own, ref.p_out, ref.b_near, ref.b_sum, ref.b_arr, ref.b_send, ref.b_recv, me
    )

    def attend(block):
        keys = (block + 1) * ROWS
        for g in range(2):
            scores = dot_cols(
                ref.k[g, 0 : block + 1].reshape(keys, HEAD_SIZE), ref.q[g, block]
            )
            probs = jnp.exp2(scores * (SCORE_SCALE * LOG2_E))
            tail = jnp.where(allowed, probs[keys - ROWS :], 0.0)
            probs = jnp.concatenate([probs[: keys - ROWS], tail], axis=0) if block else tail
            total = jnp.sum(probs, axis=0, keepdims=True)
            ref.lse[g, block] = jnp.log(total) * LOG2_E
            values = ref.v[g, 0 : block + 1].reshape(keys, HEAD_SIZE)
            rows = (dot(values.T, probs.astype(jnp.bfloat16)) / total).T.astype(jnp.bfloat16)
            for r in range(2):
                start = (2 * g + r) * HEAD_SIZE
                ref.att[block, :, start : start + HEAD_SIZE] = rows[r * ROWS : (r + 1) * ROWS]
        ref.part[...] = dot(ref.att[block], ref.v_w_out[...])
        mixed.give(block, ref.part)

    attend(3)
    attend(2)
    mixed.cross(3)
    attend(1)
    mixed.cross(2)
    attend(0)
    mixed.cross(1)
    cot.wait_far()
    mixed.cross(0)
    store(ref.att, ref.o_att)
    store(ref.lse, ref.o_lse)
    cot.wait_sibling()
    cot.wait_last()
    for load in (loads.w_down, loads.norm_mid, loads.w_gate, loads.w_up):
        load.wait()

    def mid_norm(block):
        values = ref.tokens_all[block, mixed.mine].astype(jnp.float32) + mixed.total(block)
        ref.hidden[block] = values
        ref.mid_all[block, mixed.mine] = (
            values * rms_scale(values) * vector(ref.v_norm_mid)
        ).astype(jnp.bfloat16)
        mixed.share(block, ref.mid_all).start()

    def feed(block):
        grad = dot_cols(ref.dy_all[block], ref.v_w_down[...])
        mixed.share(block, ref.mid_all).wait()
        gate = dot(ref.mid_all[block], ref.v_w_gate[...])
        up = dot(ref.mid_all[block], ref.v_w_up[...])
        sigmoid = jax.nn.sigmoid(gate)
        silu = gate * sigmoid
        ref.act[block] = (silu * up).astype(jnp.bfloat16)
        ref.dup[block] = (grad * silu).astype(jnp.bfloat16)
        ref.dgate[block] = (grad * up * sigmoid * (1.0 + gate * (1.0 - sigmoid))).astype(jnp.bfloat16)
        value = dot_cols(ref.dgate[block], ref.v_w_gate[...])
        ref.part[...] = value + dot_cols(ref.dup[block], ref.v_w_up[...])
        back.give(block, ref.part)

    for block in (3, 2, 1, 0):
        mid_norm(block)
        feed(block)
        if block < 3:
            back.cross(block + 1)
    back.cross(0)

    streams = []
    table = vars(ref)
    for i, (source, start, size, order) in enumerate(layout.ffn):
        streams.append(
            Stream(
                order,
                table["gw_" + source].at[:, :, :, :, pl.ds(start, size)],
                None,
                [table["early" + str(i)]] + [None] * (STREAM_SCRATCH - 1),
                (ref.f_send.at[i], ref.f_recv.at[i]),
                place,
                where,
            )
        )

    weight_grad(ref.mid_all, ref.dgate, ref.gw_gate)
    for stream in streams[:2]:
        stream.halve(0)
    weight_grad(ref.mid_all, ref.dup, ref.gw_up)
    for stream in streams[2:4]:
        stream.halve(0)
    weight_grad(ref.dy_all, ref.act, ref.gw_down)
    for stream in streams[4:]:
        stream.halve(0)
    store(ref.gw_gate, ref.o_gate)
    store(ref.gw_up, ref.o_up)
    store(ref.gw_down, ref.o_down)
    for block in range(4):
        ref.down_part[block] = dot(ref.act[block], ref.v_w_down[...]).astype(jnp.bfloat16)
    store(ref.down_part, ref.o_down_part)

    own_half = send(
        ref.hidden.at[sibling], ref.hid.at[mixed.mine], ref.h_send, ref.h_recv, mixed.sibling
    )
    own_half.start()
    ref.hid[mixed.mine] = ref.hidden[me]

    ref.gain[...] = jnp.zeros_like(ref.gain)
    for block in (3, 2, 1, 0):
        incoming = back.total(block)
        grad, gain = head_norm_back(incoming, ref.hidden[block], vector(ref.v_norm_mid))
        ref.gh_all[block, back.mine] = (
            ref.dy_all[block, back.mine].astype(jnp.float32) + grad
        ).astype(jnp.bfloat16)
        back.share(block, ref.gh_all).start()
        ref.gain[...] += gain
    ref.gain[...] *= 0.5
    store(ref.gain, ref.o_gain)
    own_half.wait()
    store(ref.hid, ref.o_hidden)
    for block in (3, 2, 1, 0):
        back.share(block, ref.gh_all).wait()
        store(ref.gh_all.at[block], ref.o_gh.at[block])
    for i, stream in enumerate(streams):
        for copy in stream.copies:
            copy.wait()
        store(table["early" + str(i)], table["o_early" + str(i)])
    for copy in stores:
        copy.wait()
    first.drain()
    cot.drain()


def front_part(inputs, ffn):
    low, wide = jnp.bfloat16, jnp.float32
    names = list(inputs)
    outs = dict(
        o_norm_all=((4, ROWS, 1024), low),
        o_q=((2, 4, 2 * ROWS, HEAD_SIZE), low),
        o_k=((2, 4, ROWS, HEAD_SIZE), low),
        o_v=((2, 4, ROWS, HEAD_SIZE), low),
        o_qraw=((4, ROWS, 512), wide),
        o_kraw=((4, ROWS, 256), wide),
        o_att=((4, ROWS, 512), low),
        o_lse=((2, 4, 1, 2 * ROWS), wide),
        o_hidden=((ROWS, 1024), wide),
        o_down=((4, 4, 2, 32, 768), low),
        o_gate=((4, 4, 2, 32, 768), low),
        o_up=((4, 4, 2, 32, 768), low),
        o_down_part=((4, ROWS, 1024), low),
        o_gh=((4, ROWS, 1024), low),
        o_gain=((1, 1024), wide),
    )
    early = {"early" + str(i): ((2, 4, 2, 32, entry[2]), low) for i, entry in enumerate(ffn)}
    outs.update({"o_" + name: spec for name, spec in early.items()})
    whole = ("tokens", COTANGENT)
    scratch = {
        "v_" + name: pltpu.VMEM(inputs[name].shape, inputs[name].dtype)
        for name in names
        if name not in whole
    }
    scratch.update({name: pltpu.VMEM(*spec) for name, spec in early.items()})
    scratch.update(
        load_sems=pltpu.SemaphoreType.DMA((len(names),)),
        store_sems=pltpu.SemaphoreType.DMA((len(outs) + 3,)),
        f_send=pltpu.SemaphoreType.DMA((len(ffn), 2)),
        f_recv=pltpu.SemaphoreType.DMA((len(ffn), 2)),
        h_send=pltpu.SemaphoreType.DMA,
        h_recv=pltpu.SemaphoreType.DMA,
        norm_all=pltpu.VMEM((4, ROWS, 1024), low),
        mid_all=pltpu.VMEM((4, ROWS, 1024), low),
        gh_all=pltpu.VMEM((4, ROWS, 1024), low),
        qraw=pltpu.VMEM((4, ROWS, 512), wide),
        kraw=pltpu.VMEM((4, ROWS, 256), wide),
        q=pltpu.VMEM((2, 4, 2 * ROWS, HEAD_SIZE), low),
        k=pltpu.VMEM((2, 4, ROWS, HEAD_SIZE), low),
        v=pltpu.VMEM((2, 4, ROWS, HEAD_SIZE), low),
        lse=pltpu.VMEM((2, 4, 1, 2 * ROWS), wide),
        att=pltpu.VMEM((4, ROWS, 512), low),
        part=pltpu.VMEM((ROWS, 1024), wide),
        own=pltpu.VMEM((4, HALF, 1024), wide),
        hidden=pltpu.VMEM((4, HALF, 1024), wide),
        hid=pltpu.VMEM((ROWS, 1024), wide),
        p_out=pltpu.VMEM((4, HALF, 1024), low),
        act=pltpu.VMEM((4, ROWS, 768), low),
        dup=pltpu.VMEM((4, ROWS, 768), low),
        dgate=pltpu.VMEM((4, ROWS, 768), low),
        gw_down=pltpu.VMEM((4, 4, 2, 32, 768), low),
        gw_gate=pltpu.VMEM((4, 4, 2, 32, 768), low),
        gw_up=pltpu.VMEM((4, 4, 2, 32, 768), low),
        down_part=pltpu.VMEM((4, ROWS, 1024), low),
        gain=pltpu.VMEM((1, 1024), wide),
    )
    scratch.update(zip(("tokens_all", "n_send", "n_recv"), gather_scratch(ROWS, 1024)))
    scratch.update(zip(("dy_all", "c_send", "c_recv"), gather_scratch(ROWS, 1024)))
    for tag in "pb":
        scratch.update(zip((tag + end for end in SCATTER_PARTS), exchange_scratch()))
    results = pl.pallas_call(
        functools.partial(
            front_kernel,
            names + list(outs) + list(scratch),
            SimpleNamespace(loads=names, ffn=[entry[:4] for entry in ffn]),
        ),
        out_shape=[jax.ShapeDtypeStruct(*spec) for spec in outs.values()],
        in_specs=[pl.BlockSpec(memory_space=pl.ANY)] * len(names),
        out_specs=[pl.BlockSpec(memory_space=pl.ANY)] * len(outs),
        scratch_shapes=list(scratch.values()),
        compiler_params=pltpu.CompilerParams(
            collective_id=4, has_side_effects=True, vmem_limit_bytes=62 << 20
        ),
    )(*inputs.values())
    return SimpleNamespace(**dict(zip(outs, results)))


def rotary_tables():
    position = np.arange(SEQUENCE_TOKENS, dtype=np.float64)
    inverse = 1000000.0 ** (-np.arange(HEAD_SIZE // 2, dtype=np.float64) * 2.0 / HEAD_SIZE)
    angles = position[:, None] * inverse[None, :]
    cosine, sine = np.cos(angles), np.sin(angles)
    return (
        jnp.asarray(
            np.concatenate([table, tail], axis=1).astype(np.float32).reshape(4, ROWS, HEAD_SIZE)
        )
        for table, tail in ((cosine, cosine), (sine, -sine))
    )


def per_device(
    tokens,
    norm_in,
    w_query,
    key_matrix,
    value_matrix,
    query_gain,
    key_gain,
    w_out,
    norm_mid,
    w_gate,
    w_up,
    w_down,
    cotangent,
):
    cosine, sine = rotary_tables()
    ffn = ffn_streams()
    front = front_part(
        dict(
            tokens=tokens,
            norm_in=norm_in,
            wq=w_query,
            wk=key_matrix,
            wv=value_matrix,
            cos=cosine,
            sin=sine,
            qg=query_gain,
            kg=key_gain,
            cot=cotangent,
            w_out=w_out,
            w_down=w_down,
            norm_mid=norm_mid,
            w_gate=w_gate,
            w_up=w_up,
        ),
        ffn,
    )
    outs = back_part(
        dict(
            gh=front.o_gh,
            w_out=w_out,
            att=front.o_att,
            down_part=front.o_down_part,
            gate=front.o_gate,
            up=front.o_up,
            down=front.o_down,
            q=front.o_q,
            k=front.o_k,
            v=front.o_v,
            lse=front.o_lse,
            qraw=front.o_qraw,
            kraw=front.o_kraw,
            cos=cosine,
            sin=sine,
            qg=query_gain,
            kg=key_gain,
            wq=w_query,
            wk=key_matrix,
            wv=value_matrix,
            norm_all=front.o_norm_all,
            hidden=front.o_hidden,
            tokens=tokens,
            norm_in=norm_in,
            gain_mid=front.o_gain,
            **{"early" + str(i): vars(front)["o_early" + str(i)] for i in range(len(ffn))},
        ),
        ffn,
    )
    return (
        outs.result,
        outs.grad_tokens,
        outs.o_norm_in.reshape(1024),
        outs.o_q,
        outs.o_k,
        outs.o_v,
        outs.o_qgain.reshape(HEAD_SIZE),
        outs.o_kgain.reshape(HEAD_SIZE),
        outs.o_out.T,
        outs.o_norm_mid.reshape(1024),
        outs.o_gate,
        outs.o_up,
        outs.o_down.T,
    )


def solution(mesh):
    placed = (
        P(("dp", "tensor"), None),
        P(),
        P(None, "tensor"),
        P(None, "tensor"),
        P(None, "tensor"),
        P(),
        P(),
        P("tensor", None),
        P(),
        P(None, "tensor"),
        P(None, "tensor"),
        P("tensor", None),
        P(("dp", "tensor"), None),
    )
    return jax.shard_map(
        per_device,
        mesh=mesh,
        in_specs=placed,
        out_specs=(
            P(("dp", "tensor"), None),
            P(("dp", "tensor"), None),
            P(),
            P("dp", "tensor"),
            P("dp", "tensor"),
            P("dp", "tensor"),
            P(),
            P(),
            P("tensor", "dp"),
            P(),
            P("dp", "tensor"),
            P("dp", "tensor"),
            P("tensor", "dp"),
        ),
        check_vma=False,
    )
```

```python
import functools
from types import SimpleNamespace

import jax
import jax.numpy as jnp
import numpy as np
from jax import lax
from jax.experimental import pallas as pl
from jax.experimental.pallas import tpu as pltpu
from jax.sharding import PartitionSpec as P

HEAD_SIZE = 128
SEQUENCE_TOKENS = 1024
GROUP = 4
CHUNKS = 4
VMEM_SPACE = pl.BlockSpec(memory_space=pltpu.VMEM)
FLIP, MIRROR = 1, 3
epsilon = 1e-06
contract_cols = (((1,), (1,)), ((), ()))


def partner(index, pairing):
    if pairing == FLIP:
        return index + 1 - 2 * lax.rem(index, 2)
    return 3 - index


def across(index):
    return lax.rem(index + 2, 4)


def send(source, target, send_sem, recv_sem, where):
    return pltpu.make_async_remote_copy(
        src_ref=source,
        dst_ref=target,
        send_sem=send_sem,
        recv_sem=recv_sem,
        device_id=where,
        device_id_type=pl.DeviceIdType.MESH,
    )


def greet(others):
    barrier = pltpu.get_barrier_semaphore()
    for where in others:
        pl.semaphore_signal(barrier, inc=1, device_id=where, device_id_type=pl.DeviceIdType.MESH)
    pl.semaphore_wait(barrier, len(others))


class Stream:
    def __init__(self, order, grad, out, scratch, sems, place, where):
        self.first, self.orders = order[0], order[1:]
        self.grad, self.local, self.out = grad, grad, out
        self.early, self.mid, self.late, self.held, self.low, self.pair, self.last = scratch
        self.send_sems, self.recv_sems = sems
        self.place, self.where = place, where
        self.pending = []
        self.copies = [None, None]

    def axis(self, stage):
        return self.first if stage == 0 else ("z" if self.first == "x" else "x")

    def block(self, stage, index, local=True):
        if stage == 1:
            return self.held.at[index]
        grad = self.local if local else self.grad
        return grad.at[index] if self.first == "x" else grad.at[:, index]

    def launch(self, source, target, slot, where):
        copy = send(source, target, self.send_sems.at[slot], self.recv_sems.at[slot], where)
        copy.start()
        self.pending.append(copy)
        return copy

    def halve(self, stage):
        axis, here = self.axis(stage), self.place[self.axis(stage)]
        other = partner(here, self.orders[stage])
        box = self.early if stage == 0 else self.late
        self.copies = [
            self.launch(
                self.block(stage, index, False), box.at[slot], 4 * stage + slot, self.where(axis, other)
            )
            for slot, index in ((1, across(here)), (0, other))
        ]

    def quarter(self, stage):
        axis, here = self.axis(stage), self.place[self.axis(stage)]
        other = partner(here, FLIP + MIRROR - self.orders[stage])
        box, mid = (self.early, self.mid) if stage == 0 else (self.late, self.low)
        if self.copies[0]:
            self.copies[0].wait_recv()
        mine = self.block(stage, other)

        def add(row, _):
            mid[0, row] = mine[row] + box[1, row]
            return _

        lax.fori_loop(0, mid.shape[1], add, 0)
        self.copies.append(
            self.launch(mid.at[0], mid.at[1], 4 * stage + 2, self.where(axis, other))
        )

    def settle(self, stage):
        here = self.place[self.axis(stage)]
        if self.copies[1]:
            self.copies[1].wait_recv()
        self.copies[2].wait_recv()
        box, mid = (self.early, self.mid) if stage == 0 else (self.late, self.low)
        mine = self.block(stage, here)
        if stage == 0:

            def add(row, _):
                self.held[row] = mine[row] + box[0, row] + mid[1, row]
                return _

            lax.fori_loop(0, mid.shape[1], add, 0)
            return
        keep = self.place["y"]
        give = 1 - keep
        self.pair[0] = (
            mine[give].astype(jnp.float32)
            + box[0, give].astype(jnp.float32)
            + mid[1, give].astype(jnp.float32)
        ).astype(jnp.bfloat16)
        self.copies.append(
            self.launch(self.pair.at[0], self.pair.at[1], 3, self.where("y", give))
        )
        self.last[...] = (
            mine[keep].astype(jnp.float32)
            + box[0, keep].astype(jnp.float32)
            + mid[1, keep].astype(jnp.float32)
        )

    def finish(self):
        self.copies[3].wait_recv()
        self.out[...] = self.last[...] + self.pair[1].astype(jnp.float32)
        for copy in self.pending:
            copy.wait_send()


STREAM_SEMS = 7
STREAM_SCRATCH = 7


def stream_scratch(columns):
    low = jnp.bfloat16
    return [
        pltpu.VMEM((2, 4, 2, 32, columns), low),
        pltpu.VMEM((2, 4, 2, 32, columns), low),
        pltpu.VMEM((2, 2, 32, columns), low),
        pltpu.VMEM((4, 2, 32, columns), low),
        pltpu.VMEM((2, 2, 32, columns), low),
        pltpu.VMEM((2, 32, columns), low),
        pltpu.VMEM((32, columns), jnp.float32),
    ]


def rank_places():
    rank = lax.axis_index("dp")
    return {"x": lax.div(rank, 8), "z": lax.rem(lax.div(rank, 2), 4), "y": lax.rem(rank, 2)}


def rank_where(place):
    def where(axis, index):
        at = dict(place)
        at[axis] = index
        return {"dp": at["x"] * 8 + at["z"] * 2 + at["y"]}

    return where


def rms_scale(values):
    return lax.rsqrt(jnp.mean(values * values, axis=-1, keepdims=True) + epsilon)


class Gather:
    def __init__(self, whole, send_sems, recv_sems, me, shard=None):
        self.shard = shard
        self.whole, self.send_sems, self.recv_sems, self.me = whole, send_sems, recv_sems, me
        self.sibling, self.far = {"tensor": partner(me, FLIP)}, {"tensor": across(me)}
        self.rows = whole.shape[1] // CHUNKS

    def copy(self, lane, chunk, block, where):
        part = pl.ds(chunk * self.rows, self.rows)
        spot = self.whole.at[block, part]
        source = spot if self.shard is None or lane == 2 else self.shard.at[part]
        return send(source, spot, self.send_sems.at[lane, chunk], self.recv_sems.at[lane, chunk], where)

    def start_chunk(self, chunk):
        self.copy(0, chunk, self.me, self.far).start()
        self.copy(1, chunk, self.me, self.sibling).start()

    def start(self):
        for chunk in range(CHUNKS):
            self.copy(0, chunk, self.me, self.far).start()
        for chunk in range(CHUNKS):
            self.copy(1, chunk, self.me, self.sibling).start()

    def wait_sibling(self):
        for chunk in range(CHUNKS):
            self.copy(1, chunk, self.me, self.sibling).wait_recv()

    def wait_far(self):
        for chunk in range(CHUNKS):
            self.copy(0, chunk, self.me, self.far).wait_recv()
            self.copy(2, chunk, across(self.me), self.sibling).start()

    def wait_last(self):
        for chunk in range(CHUNKS):
            self.copy(2, chunk, across(self.me), self.sibling).wait_recv()

    def drain(self):
        for chunk in range(CHUNKS):
            self.copy(0, chunk, self.me, self.far).wait_send()
            self.copy(1, chunk, self.me, self.sibling).wait_send()
            self.copy(2, chunk, across(self.me), self.sibling).wait_send()


class Scatter:
    def __init__(self, partial, near, summed, arrived, send_sems, recv_sems, me):
        self.partial, self.near, self.summed, self.arrived = partial, near, summed, arrived
        self.send_sems, self.recv_sems, self.me = send_sems, recv_sems, me
        self.sibling, self.far = {"tensor": partner(me, FLIP)}, {"tensor": across(me)}
        self.rows = near.shape[1] // CHUNKS

    def part(self, chunk):
        return pl.ds(chunk * self.rows, self.rows)

    def near_copy(self, slot, chunk):
        block = partner(self.me, MIRROR if slot == 0 else FLIP)
        return send(
            self.partial.at[block, self.part(chunk)],
            self.near.at[slot, self.part(chunk)],
            self.send_sems.at[slot, chunk],
            self.recv_sems.at[slot, chunk],
            self.sibling,
        )

    def far_copy(self, chunk):
        return send(
            self.summed.at[self.part(chunk)],
            self.arrived.at[self.part(chunk)],
            self.send_sems.at[2, chunk],
            self.recv_sems.at[2, chunk],
            self.far,
        )

    def start(self, slot):
        for chunk in range(CHUNKS):
            self.near_copy(slot, chunk).start()

    def cross(self, mine):
        for chunk in range(CHUNKS):
            part = self.part(chunk)
            self.near_copy(0, chunk).wait_recv()
            self.summed[part] = (
                mine[part].astype(jnp.float32) + self.near[0, part].astype(jnp.float32)
            ).astype(jnp.bfloat16)
            self.far_copy(chunk).start()

    def total(self, chunk, mine):
        part = self.part(chunk)
        self.near_copy(1, chunk).wait_recv()
        self.far_copy(chunk).wait_recv()
        return (
            mine[part].astype(jnp.float32)
            + self.near[1, part].astype(jnp.float32)
            + self.arrived[part].astype(jnp.float32)
        )

    def drain(self):
        for chunk in range(CHUNKS):
            self.near_copy(0, chunk).wait_send()
            self.near_copy(1, chunk).wait_send()
            self.far_copy(chunk).wait_send()


def scatter_scratch(rows, width):
    return [
        pltpu.VMEM((2, rows, width), jnp.bfloat16),
        pltpu.VMEM((rows, width), jnp.bfloat16),
        pltpu.VMEM((rows, width), jnp.bfloat16),
        pltpu.SemaphoreType.DMA((3, CHUNKS)),
        pltpu.SemaphoreType.DMA((3, CHUNKS)),
    ]


def gather_scratch(rows, width):
    return [
        pltpu.VMEM((GROUP, rows, width), jnp.bfloat16),
        pltpu.SemaphoreType.DMA((3, CHUNKS)),
        pltpu.SemaphoreType.DMA((3, CHUNKS)),
    ]


def vector(ref):
    return ref[...].astype(jnp.float32).reshape(1, ref.shape[0])


def dot(left, right):
    return jnp.dot(left, right, preferred_element_type=jnp.float32)


def dot_cols(left, right):
    return lax.dot_general(left, right, contract_cols, preferred_element_type=jnp.float32)


def turn(values, cosine, sine):
    return values * cosine + pltpu.roll(values, HEAD_SIZE // 2, 1) * sine


def head_norm_back(incoming, values, gain):
    scale = lax.rsqrt(jnp.mean(values * values, axis=-1, keepdims=True) + epsilon)
    scaled = incoming * gain
    grad = scale * scaled - values * (
        scale * scale * scale * jnp.mean(scaled * values, axis=-1, keepdims=True)
    )
    return grad, jnp.sum(incoming * values * scale, axis=0, keepdims=True)


SCORE_SCALE = HEAD_SIZE**-0.5
LOG2_E = 1.4426950408889634
ROWS = 256
HALF = 128
COTANGENT = "cot"
DOWN_PART = "down_part"
MATRICES = ("wq", "wk", "wv")
SCATTER_PARTS = ("_near", "_sum", "_arr", "_send", "_recv")


def start_loads(ref, layout, pairs):
    loads = SimpleNamespace()
    table = vars(ref)
    for slot, name in enumerate(layout.loads):
        source, target = pairs[name] if name in pairs else (table[name], table["v_" + name])
        copy = pltpu.make_async_copy(source, target, ref.load_sems.at[slot])
        copy.start()
        setattr(loads, name, copy)
    return loads


def weight_grad(rows, cols, target):
    width = cols.shape[-1]
    right = cols[...].reshape(SEQUENCE_TOKENS, width)
    for j in range(4):
        left = rows[:, :, j * ROWS : (j + 1) * ROWS].reshape(SEQUENCE_TOKENS, ROWS)
        target[j] = dot(left.T, right).astype(jnp.bfloat16).reshape(4, 2, 32, width)


class RingSum:
    def __init__(self, box, slot, others, send_sems, recv_sems):
        self.box, self.slot, self.others = box, slot, others
        self.send_sems, self.recv_sems = send_sems, recv_sems

    def copy(self, index, slot):
        spot = self.box.at[slot]
        return send(
            spot, spot, self.send_sems.at[index], self.recv_sems.at[slot], self.others[index][1]
        )

    def start(self, value):
        self.box[self.slot] = value
        for index in range(len(self.others)):
            self.copy(index, self.slot).start()

    def end(self):
        for index, (slot, _) in enumerate(self.others):
            self.copy(index, slot).wait_recv()
        total = self.box[0]
        for slot in range(1, self.box.shape[0]):
            total = total + self.box[slot]
        for index in range(len(self.others)):
            self.copy(index, self.slot).wait_send()
        return total


def back_kernel(names, layout, *refs):
    ref = SimpleNamespace(**dict(zip(names, refs)))
    me = lax.axis_index("tensor")
    sibling, far, far_sibling = partner(me, FLIP), across(me), partner(me, MIRROR)
    place = rank_places()
    where = rank_where(place)
    pairs = dict(
        down_part_far=(ref.down_part.at[pl.ds(far, 1)], ref.v_down_part_far),
        down_part_own=(ref.down_part.at[pl.ds(me, 1)], ref.v_down_part_own),
    )
    for g in range(2):
        base = g * 512
        for name, source, start, size in (
            ("wq", ref.wq, 0, 256), ("wk", ref.wk, 256, 128), ("wv", ref.wv, 384, 128)
        ):
            pairs[name + str(g)] = (
                source.at[:, pl.ds(g * size, size)],
                ref.wcat.at[:, pl.ds(base + start, size)],
            )
    for i in range(len(layout.ffn)):
        name = "early" + str(i)
        pairs[name] = (vars(ref)[name], vars(ref)["f" + str(i) + "_0"])
    loads = start_loads(ref, layout, pairs)

    def turns(here):
        return here, partner(here, FLIP), partner(here, MIRROR), across(here)

    y = place["y"]
    eight = [
        (row * 4 + member, dict(where("y", row), tensor=member))
        for row in (y, 1 - y)
        for member in turns(me)
    ]
    rings = []
    for box, members in (
        (ref.box_x, [(x, where("x", x)) for x in turns(place["x"])]),
        (ref.box_z, [(z, where("z", z)) for z in turns(place["z"])]),
        (ref.box_eight, eight),
    ):
        rings.append(
            RingSum(
                box,
                members[0][0],
                members[1:],
                ref.gain_send.at[len(rings)],
                ref.gain_recv.at[len(rings)],
            )
        )
    greet([there for ring in rings for _, there in ring.others])

    down = Scatter(
        ref.down_part, ref.d_near, ref.d_sum, ref.d_arr, ref.d_send, ref.d_recv, me
    )
    down.start(0)
    down.start(1)

    table = vars(ref)

    def streams_of(kind, entries, send_sems, recv_sems):
        out = []
        for i, (source, start, size, order, target, at) in enumerate(entries):
            columns = pl.ds(start, size)
            stream = Stream(
                order,
                table[source].at[:, :, :, :, columns],
                table[target].at[:, pl.ds(at, size)],
                [table[kind + str(i) + "_" + str(j)] for j in range(STREAM_SCRATCH)],
                (send_sems.at[i], recv_sems.at[i]),
                place,
                where,
            )
            if "v_" + source in table:
                stream.local = table["v_" + source].at[:, :, :, :, columns]
            out.append(stream)
        return out

    ffn = streams_of("f", layout.ffn, ref.f_send, ref.f_recv)
    attn = streams_of("a", layout.attn, ref.a_send, ref.a_recv)
    out_streams, group_streams = attn[:4], (attn[4:8], attn[8:])

    def every(streams, *steps):
        for stream in streams:
            for step, *stage in steps:
                step(stream, *stage)

    for load in (loads.w_out, loads.att, loads.gh):
        load.wait()

    def attended_grad(block):
        part = dot_cols(ref.v_gh[block], ref.v_w_out[...]).astype(jnp.bfloat16)
        for head in range(4):
            g, r = head // 2, head % 2
            at = slice(head * HEAD_SIZE, (head + 1) * HEAD_SIZE)
            low = part[:, at]
            ref.do[g, block, r * ROWS : (r + 1) * ROWS, :] = low
            product = low.astype(jnp.float32) * ref.v_att[block, :, at].astype(jnp.float32)
            ref.delta[g, block, :, r * ROWS : (r + 1) * ROWS] = jnp.sum(
                product.T, axis=0, keepdims=True
            )

    attended_grad(3)
    attended_grad(2)

    loads.down_part_far.wait()
    down.cross(ref.v_down_part_far.at[0])
    for load in [loads.gate, loads.up, loads.down] + [
        vars(loads)["early" + str(i)] for i in range(len(ffn))
    ]:
        load.wait()
    every(ffn, (Stream.quarter, 0))
    attended_grad(1)
    attended_grad(0)
    weight_grad(ref.v_gh, ref.v_att, ref.gw_out)
    every(out_streams, (Stream.halve, 0))

    for load in (
        loads.q, loads.k, loads.v, loads.lse, loads.qraw, loads.kraw, loads.cos, loads.sin,
        loads.qg, loads.kg,
    ):
        load.wait()
    ref.qgain[...] = jnp.zeros_like(ref.qgain)
    ref.kgain[...] = jnp.zeros_like(ref.kgain)
    key_row = lax.broadcasted_iota(jnp.int32, (ROWS, 2 * ROWS), 0)
    query_col = lax.rem(lax.broadcasted_iota(jnp.int32, (ROWS, 2 * ROWS), 1), ROWS)
    allowed = key_row <= query_col

    def attend_group(g):
        base = 512 * g
        for qb in (3, 2, 1, 0):
            keys = (qb + 1) * ROWS
            key = ref.v_k[g, 0 : qb + 1].reshape(keys, HEAD_SIZE)
            query, grad_out = ref.v_q[g, qb], ref.do[g, qb]
            probs = jnp.exp2(
                dot_cols(key, query) * (SCORE_SCALE * LOG2_E) - ref.v_lse[g, qb]
            )
            tail = jnp.where(allowed, probs[keys - ROWS :], 0.0)
            probs = jnp.concatenate([probs[: keys - ROWS], tail], axis=0) if qb else tail
            grad_probs = dot_cols(
                ref.v_v[g, 0 : qb + 1].reshape(keys, HEAD_SIZE), grad_out
            )
            grad_scores = (probs * (grad_probs - ref.delta[g, qb])).astype(jnp.bfloat16)
            grad_value = dot(probs.astype(jnp.bfloat16), grad_out).reshape(qb + 1, ROWS, HEAD_SIZE)
            grad_key = dot(grad_scores, query).reshape(qb + 1, ROWS, HEAD_SIZE)
            if qb == 3:
                ref.dv[...] = grad_value
                ref.dk[...] = grad_key
            else:
                ref.dv[0 : qb + 1] += grad_value
                ref.dk[0 : qb + 1] += grad_key
            grads = dot(key.T, grad_scores).T * SCORE_SCALE
            for r in range(2):
                start = (2 * g + r) * HEAD_SIZE
                back = turn(
                    grads[r * ROWS : (r + 1) * ROWS], ref.v_cos[qb], ref.v_sin[qb]
                )
                grad, gain = head_norm_back(
                    back, ref.v_qraw[qb, :, start : start + HEAD_SIZE], vector(ref.v_qg)
                )
                at = base + r * HEAD_SIZE
                ref.dqkv[qb, :, at : at + HEAD_SIZE] = grad.astype(jnp.bfloat16)
                ref.qgain[...] += gain

        for kb in range(4):
            start = g * HEAD_SIZE
            back = turn(ref.dk[kb] * SCORE_SCALE, ref.v_cos[kb], ref.v_sin[kb])
            grad, gain = head_norm_back(
                back, ref.v_kraw[kb, :, start : start + HEAD_SIZE], vector(ref.v_kg)
            )
            ref.dqkv[kb, :, base + 256 : base + 384] = grad.astype(jnp.bfloat16)
            ref.dqkv[kb, :, base + 384 : base + 512] = ref.dv[kb].astype(jnp.bfloat16)
            ref.kgain[...] += gain

    attend_group(0)
    loads.norm_all.wait()
    weight_grad(ref.v_norm_all, ref.dqkv.at[:, :, 0:512], ref.gw_0)
    every(group_streams[0], (Stream.halve, 0))
    every(ffn, (Stream.settle, 0), (Stream.halve, 1))
    every(out_streams, (Stream.quarter, 0))
    attend_group(1)
    every(group_streams[0], (Stream.quarter, 0))
    weight_grad(ref.v_norm_all, ref.dqkv.at[:, :, 512:1024], ref.gw_1)
    every(group_streams[1], (Stream.halve, 0))

    for load in (loads.wq0, loads.wk0, loads.wv0, loads.wq1, loads.wk1, loads.wv1):
        load.wait()
    inward = Scatter(
        ref.x_part, ref.x_near, ref.x_sum, ref.x_arr, ref.x_send, ref.x_recv, me
    )

    loads.norm_in.wait()
    loads.gain_mid.wait()
    ref.gain_in[...] = jnp.zeros_like(ref.gain_in)

    def inward_part(block, target):
        value = dot_cols(ref.dqkv[block], ref.wcat[...])
        target[...] = value.astype(target.dtype)
        ref.gain_in[...] += jnp.sum(
            value * ref.v_norm_all[block].astype(jnp.float32), axis=0, keepdims=True
        )

    inward_part(far_sibling, ref.x_part.at[far_sibling])
    inward.start(0)
    inward_part(far, ref.x_part.at[far])
    inward.cross(ref.x_part.at[far])
    inward_part(sibling, ref.x_part.at[sibling])
    inward.start(1)
    every(group_streams[1], (Stream.quarter, 0))
    every(group_streams[0], (Stream.settle, 0), (Stream.halve, 1))
    inward_part(me, ref.x_own)

    ref.gains[...] = jnp.zeros_like(ref.gains)
    gain_in = ref.gain_in[...] / vector(ref.v_norm_in)
    for row in range(8):
        at = slice(row * HEAD_SIZE, (row + 1) * HEAD_SIZE)
        ref.gains[row : row + 1] = gain_in[:, at]
        ref.gains[8 + row : 9 + row] = ref.v_gain_mid[:, at]
    ref.gains[16:17] = ref.qgain[...]
    ref.gains[17:18] = ref.kgain[...]
    rings[0].start(ref.gains[...])

    every(ffn, (Stream.quarter, 1))
    every(out_streams, (Stream.settle, 0), (Stream.halve, 1))
    rings[1].start(rings[0].end())
    every(group_streams[1], (Stream.settle, 0), (Stream.halve, 1))
    every(group_streams[0], (Stream.quarter, 1))
    every(ffn, (Stream.settle, 1))
    every(out_streams, (Stream.quarter, 1))
    rings[2].start(rings[1].end())
    every(group_streams[1], (Stream.quarter, 1))
    every(group_streams[0], (Stream.settle, 1))
    every(out_streams, (Stream.settle, 1))

    loads.hidden.wait()
    loads.down_part_own.wait()
    for chunk in range(CHUNKS):
        part = down.part(chunk)
        total = down.total(chunk, ref.v_down_part_own.at[0])
        ref.result[part] = (ref.v_hidden[part] + total).astype(jnp.bfloat16)
    every(group_streams[1], (Stream.settle, 1))
    every(ffn, (Stream.finish,))
    total = rings[2].end()
    for row in range(8):
        at = slice(row * HEAD_SIZE, (row + 1) * HEAD_SIZE)
        ref.o_norm_in[:, at] = total[row : row + 1]
        ref.o_norm_mid[:, at] = total[8 + row : 9 + row]
    ref.o_qgain[...] = total[16:17]
    ref.o_kgain[...] = total[17:18]

    loads.tokens.wait()
    for chunk in range(CHUNKS):
        part = inward.part(chunk)
        incoming = inward.total(chunk, ref.x_own)
        values = ref.v_tokens[part].astype(jnp.float32)
        grad, _ = head_norm_back(incoming, values, vector(ref.v_norm_in))
        ref.grad_tokens[part] = (ref.v_gh[me, part].astype(jnp.float32) + grad).astype(
            jnp.bfloat16
        )
    every(out_streams, (Stream.finish,))
    every(group_streams[0] + group_streams[1], (Stream.finish,))
    down.drain()
    inward.drain()


def hand_over_kernel(n, *refs):
    sources, targets, buffers, sems = refs[:n], refs[n : 2 * n], refs[2 * n : 3 * n], refs[3 * n]
    pulls = [pltpu.make_async_copy(sources[i], buffers[i], sems.at[0, i]) for i in range(n)]
    pushes = [pltpu.make_async_copy(buffers[i], targets[i], sems.at[1, i]) for i in range(n)]
    for pull in pulls:
        pull.start()
    for pull, push in zip(pulls, pushes):
        pull.wait()
        push.start()
    for push in pushes:
        push.wait()


def hand_over(arrays):
    n = len(arrays)
    anywhere = [pl.BlockSpec(memory_space=pl.ANY)] * n
    return pl.pallas_call(
        functools.partial(hand_over_kernel, n),
        out_shape=[jax.ShapeDtypeStruct(array.shape, array.dtype) for array in arrays],
        in_specs=anywhere,
        out_specs=anywhere,
        scratch_shapes=[pltpu.VMEM(array.shape, array.dtype) for array in arrays]
        + [pltpu.SemaphoreType.DMA((2, n))],
    )(*arrays)


def ffn_streams():
    xa, xb = ("x", FLIP, FLIP), ("x", MIRROR, MIRROR)
    za, zb = ("z", FLIP, MIRROR), ("z", MIRROR, FLIP)
    return [
        ("gate", 0, 384, xa, "o_gate", 0), ("gate", 384, 384, xb, "o_gate", 384),
        ("up", 0, 384, za, "o_up", 0), ("up", 384, 384, zb, "o_up", 384),
        ("down", 0, 256, xa, "o_down", 0), ("down", 256, 128, xb, "o_down", 256),
        ("down", 384, 256, za, "o_down", 384), ("down", 640, 128, zb, "o_down", 640),
    ]


def back_part(inputs, ffn):
    low, wide = jnp.bfloat16, jnp.float32
    names = list(inputs)
    weights = [name for name in names if name in MATRICES]
    loaded = [name for name in names if name != DOWN_PART and name not in MATRICES]
    loaded += [DOWN_PART + "_far", DOWN_PART + "_own"]
    shapes = {name: (inputs[name].shape, inputs[name].dtype) for name in loaded[:-2]}
    shapes.update({name: ((1, ROWS, 1024), low) for name in loaded[-2:]})
    loaded += [name + str(g) for g in range(2) for name in weights]
    early = [name for name in loaded if name.startswith(("down", "gate", "up", "early"))]
    loaded = loaded[:3] + early + [name for name in loaded[3:] if name not in early]
    outs = dict(
        result=((ROWS, 1024), low),
        grad_tokens=((ROWS, 1024), low),
        o_gate=((32, 768), wide),
        o_up=((32, 768), wide),
        o_down=((32, 768), wide),
        o_q=((32, 512), wide),
        o_k=((32, 256), wide),
        o_v=((32, 256), wide),
        o_out=((32, 512), wide),
        o_norm_in=((1, 1024), wide),
        o_norm_mid=((1, 1024), wide),
        o_qgain=((1, HEAD_SIZE), wide),
        o_kgain=((1, HEAD_SIZE), wide),
    )
    xa, xb = ("x", FLIP, FLIP), ("x", MIRROR, MIRROR)
    za, zb = ("z", FLIP, MIRROR), ("z", MIRROR, FLIP)
    layout = SimpleNamespace(
        loads=loaded,
        ffn=ffn,
        attn=[("gw_out", 128 * i, 128, way, "o_out", 128 * i) for i, way in enumerate((xb, zb, xa, za))]
        + [
            ("gw_" + str(g), 128 * i, 128, way, target, at + step * g)
            for g in range(2)
            for i, (way, target, at, step) in enumerate(
                ((xa, "o_q", 0, 256), (xb, "o_q", 128, 256), (za, "o_k", 0, 128), (zb, "o_v", 0, 128))
            )
        ],
    )
    scratch = {"v_" + name: pltpu.VMEM(*spec) for name, spec in shapes.items()}
    scratch.update(
        load_sems=pltpu.SemaphoreType.DMA((len(loaded),)),
        do=pltpu.VMEM((2, 4, 2 * ROWS, HEAD_SIZE), low),
        delta=pltpu.VMEM((2, 4, 1, 2 * ROWS), wide),
        dk=pltpu.VMEM((4, ROWS, HEAD_SIZE), wide),
        dv=pltpu.VMEM((4, ROWS, HEAD_SIZE), wide),
        dqkv=pltpu.VMEM((4, ROWS, 1024), low),
        wcat=pltpu.VMEM((1024, 1024), low),
        qgain=pltpu.VMEM((1, HEAD_SIZE), wide),
        kgain=pltpu.VMEM((1, HEAD_SIZE), wide),
        x_part=pltpu.VMEM((4, ROWS, 1024), low),
        x_own=pltpu.VMEM((ROWS, 1024), wide),
        gw_out=pltpu.VMEM((4, 4, 2, 32, 512), low),
        gw_0=pltpu.VMEM((4, 4, 2, 32, 512), low),
        gw_1=pltpu.VMEM((4, 4, 2, 32, 512), low),
        gains=pltpu.VMEM((24, HEAD_SIZE), wide),
        gain_in=pltpu.VMEM((1, 1024), wide),
        box_x=pltpu.VMEM((4, 24, HEAD_SIZE), wide),
        box_z=pltpu.VMEM((4, 24, HEAD_SIZE), wide),
        box_eight=pltpu.VMEM((8, 24, HEAD_SIZE), wide),
        gain_send=pltpu.SemaphoreType.DMA((3, 8)),
        gain_recv=pltpu.SemaphoreType.DMA((3, 8)),
    )
    for tag in "dx":
        scratch.update(zip((tag + end for end in SCATTER_PARTS), scatter_scratch(ROWS, 1024)))
    for kind, entries in (("f", layout.ffn), ("a", layout.attn)):
        for way in SCATTER_PARTS[3:]:
            scratch[kind + way] = pltpu.SemaphoreType.DMA((len(entries), STREAM_SEMS))
        for i, entry in enumerate(entries):
            for j, buffer in enumerate(stream_scratch(entry[2])):
                scratch[kind + str(i) + "_" + str(j)] = buffer
    for i in range(len(ffn)):
        scratch["f" + str(i) + "_0"] = scratch.pop("v_early" + str(i))
    results = pl.pallas_call(
        functools.partial(back_kernel, names + list(outs) + list(scratch), layout),
        out_shape=[jax.ShapeDtypeStruct(*spec) for spec in outs.values()],
        in_specs=[pl.BlockSpec(memory_space=pl.ANY)] * len(names),
        out_specs=[VMEM_SPACE] * len(outs),
        scratch_shapes=list(scratch.values()),
        compiler_params=pltpu.CompilerParams(
            collective_id=3, has_side_effects=True, vmem_limit_bytes=61 << 20
        ),
    )(*inputs.values())
    return SimpleNamespace(**dict(zip(outs, hand_over(results))))


class Exchange:
    def __init__(self, own, near_out, near_in, summed, arrived, send_sems, recv_sems, me):
        self.own, self.near_out, self.near_in = own, near_out, near_in
        self.summed, self.arrived = summed, arrived
        self.send_sems, self.recv_sems = send_sems, recv_sems
        self.sibling, self.far = {"tensor": partner(me, FLIP)}, {"tensor": across(me)}
        core = lax.rem(me, 2)
        self.mine = pl.ds(pl.multiple_of(core * HALF, HALF), HALF)
        self.other = pl.ds(pl.multiple_of((1 - core) * HALF, HALF), HALF)

    def near(self, block):
        return send(
            self.near_out.at[block],
            self.near_in.at[block],
            self.send_sems.at[0, block],
            self.recv_sems.at[0, block],
            self.sibling,
        )

    def swap(self, block):
        return send(
            self.summed.at[block],
            self.arrived.at[block],
            self.send_sems.at[1, block],
            self.recv_sems.at[1, block],
            self.far,
        )

    def share(self, block, whole):
        spot = whole.at[block, self.mine]
        return send(
            spot, spot, self.send_sems.at[2, block], self.recv_sems.at[2, block], self.sibling
        )

    def give(self, block, part):
        self.near_out[block] = part[self.other].astype(jnp.bfloat16)
        self.near(block).start()
        self.own[block] = part[self.mine]

    def cross(self, block):
        self.near(block).wait()
        self.summed[block] = (
            self.own[block] + self.near_in[block].astype(jnp.float32)
        ).astype(jnp.bfloat16)
        self.swap(block).start()

    def total(self, block):
        self.swap(block).wait()
        return self.summed[block].astype(jnp.float32) + self.arrived[block].astype(jnp.float32)


def exchange_scratch():
    half = pltpu.VMEM((4, HALF, 1024), jnp.bfloat16)
    sems = pltpu.SemaphoreType.DMA((3, 4))
    return [half, half, half, sems, sems]


def front_kernel(names, layout, *refs):
    ref = SimpleNamespace(**dict(zip(names, refs)))
    me = lax.axis_index("tensor")
    sibling, far, far_sibling = partner(me, FLIP), across(me), partner(me, MIRROR)
    place = rank_places()
    where = rank_where(place)
    loads = start_loads(
        ref,
        layout,
        dict(tokens=(ref.tokens, ref.tokens_all.at[me]), cot=(ref.cot, ref.dy_all.at[me])),
    )
    greet(
        [{"tensor": sibling}, {"tensor": far}]
        + [
            where(axis, partner(place[axis], pairing))
            for axis in ("x", "z")
            for pairing in (FLIP, MIRROR)
        ]
    )
    stores = []

    def store(source, target):
        copy = pltpu.make_async_copy(source, target, ref.store_sems.at[len(stores)])
        copy.start()
        stores.append(copy)

    first = Gather(ref.tokens_all, ref.n_send, ref.n_recv, me, ref.tokens)
    cot = Gather(ref.dy_all, ref.c_send, ref.c_recv, me, ref.cot)
    first.start()
    loads.tokens.wait()
    for load in (
        loads.norm_in, loads.wq, loads.wk, loads.wv, loads.cos, loads.sin, loads.qg, loads.kg
    ):
        load.wait()

    def project(block):
        values = ref.tokens_all[block].astype(jnp.float32)
        rows = (values * rms_scale(values) * vector(ref.v_norm_in)).astype(jnp.bfloat16)
        ref.norm_all[block] = rows
        raw = dot(rows, ref.v_wq[...])
        ref.qraw[block] = raw
        for head in range(4):
            values = raw[:, head * HEAD_SIZE : (head + 1) * HEAD_SIZE]
            values = values * rms_scale(values) * vector(ref.v_qg)
            ref.q[head // 2, block, (head % 2) * ROWS : (head % 2 + 1) * ROWS, :] = turn(
                values, ref.v_cos[block], -ref.v_sin[block]
            ).astype(jnp.bfloat16)
        raw = dot(rows, ref.v_wk[...])
        ref.kraw[block] = raw
        for g in range(2):
            values = raw[:, g * HEAD_SIZE : (g + 1) * HEAD_SIZE]
            values = values * rms_scale(values) * vector(ref.v_kg)
            ref.k[g, block] = turn(values, ref.v_cos[block], -ref.v_sin[block]).astype(jnp.bfloat16)
        low = dot(rows, ref.v_wv[...]).astype(jnp.bfloat16)
        for g in range(2):
            ref.v[g, block] = low[:, g * HEAD_SIZE : (g + 1) * HEAD_SIZE]

    project(me)
    first.wait_sibling()
    project(sibling)
    first.wait_far()
    loads.cot.wait()
    cot.start()
    project(far)
    first.wait_last()
    project(far_sibling)
    store(ref.norm_all, ref.o_norm_all)
    store(ref.q, ref.o_q)
    store(ref.k, ref.o_k)
    store(ref.v, ref.o_v)
    store(ref.qraw, ref.o_qraw)
    store(ref.kraw, ref.o_kraw)

    key_row = lax.broadcasted_iota(jnp.int32, (ROWS, 2 * ROWS), 0)
    query_col = lax.rem(lax.broadcasted_iota(jnp.int32, (ROWS, 2 * ROWS), 1), ROWS)
    allowed = key_row <= query_col
    loads.w_out.wait()
    mixed = Exchange(
        ref.own, ref.p_out, ref.p_near, ref.p_sum, ref.p_arr, ref.p_send, ref.p_recv, me
    )
    back = Exchange(
        ref.own, ref.p_out, ref.b_near, ref.b_sum, ref.b_arr, ref.b_send, ref.b_recv, me
    )

    def attend(block):
        keys = (block + 1) * ROWS
        for g in range(2):
            scores = dot_cols(
                ref.k[g, 0 : block + 1].reshape(keys, HEAD_SIZE), ref.q[g, block]
            )
            probs = jnp.exp2(scores * (SCORE_SCALE * LOG2_E))
            tail = jnp.where(allowed, probs[keys - ROWS :], 0.0)
            probs = jnp.concatenate([probs[: keys - ROWS], tail], axis=0) if block else tail
            total = jnp.sum(probs, axis=0, keepdims=True)
            ref.lse[g, block] = jnp.log(total) * LOG2_E
            values = ref.v[g, 0 : block + 1].reshape(keys, HEAD_SIZE)
            rows = (dot(values.T, probs.astype(jnp.bfloat16)) / total).T.astype(jnp.bfloat16)
            for r in range(2):
                start = (2 * g + r) * HEAD_SIZE
                ref.att[block, :, start : start + HEAD_SIZE] = rows[r * ROWS : (r + 1) * ROWS]
        ref.part[...] = dot(ref.att[block], ref.v_w_out[...])
        mixed.give(block, ref.part)

    attend(3)
    attend(2)
    mixed.cross(3)
    attend(1)
    mixed.cross(2)
    attend(0)
    mixed.cross(1)
    cot.wait_far()
    mixed.cross(0)
    store(ref.att, ref.o_att)
    store(ref.lse, ref.o_lse)
    cot.wait_sibling()
    cot.wait_last()
    for load in (loads.w_down, loads.norm_mid, loads.w_gate, loads.w_up):
        load.wait()

    def mid_norm(block):
        values = ref.tokens_all[block, mixed.mine].astype(jnp.float32) + mixed.total(block)
        ref.hidden[block] = values
        ref.mid_all[block, mixed.mine] = (
            values * rms_scale(values) * vector(ref.v_norm_mid)
        ).astype(jnp.bfloat16)
        mixed.share(block, ref.mid_all).start()

    def feed(block):
        grad = dot_cols(ref.dy_all[block], ref.v_w_down[...])
        mixed.share(block, ref.mid_all).wait()
        gate = dot(ref.mid_all[block], ref.v_w_gate[...])
        up = dot(ref.mid_all[block], ref.v_w_up[...])
        sigmoid = jax.nn.sigmoid(gate)
        silu = gate * sigmoid
        ref.act[block] = (silu * up).astype(jnp.bfloat16)
        ref.dup[block] = (grad * silu).astype(jnp.bfloat16)
        ref.dgate[block] = (grad * up * sigmoid * (1.0 + gate * (1.0 - sigmoid))).astype(jnp.bfloat16)
        value = dot_cols(ref.dgate[block], ref.v_w_gate[...])
        ref.part[...] = value + dot_cols(ref.dup[block], ref.v_w_up[...])
        back.give(block, ref.part)

    for block in (3, 2, 1, 0):
        mid_norm(block)
        feed(block)
        if block < 3:
            back.cross(block + 1)
    back.cross(0)

    streams = []
    table = vars(ref)
    for i, (source, start, size, order) in enumerate(layout.ffn):
        streams.append(
            Stream(
                order,
                table["gw_" + source].at[:, :, :, :, pl.ds(start, size)],
                None,
                [table["early" + str(i)]] + [None] * (STREAM_SCRATCH - 1),
                (ref.f_send.at[i], ref.f_recv.at[i]),
                place,
                where,
            )
        )

    weight_grad(ref.mid_all, ref.dgate, ref.gw_gate)
    for stream in streams[:2]:
        stream.halve(0)
    weight_grad(ref.mid_all, ref.dup, ref.gw_up)
    for stream in streams[2:4]:
        stream.halve(0)
    weight_grad(ref.dy_all, ref.act, ref.gw_down)
    for stream in streams[4:]:
        stream.halve(0)
    store(ref.gw_gate, ref.o_gate)
    store(ref.gw_up, ref.o_up)
    store(ref.gw_down, ref.o_down)
    for block in range(4):
        ref.down_part[block] = dot(ref.act[block], ref.v_w_down[...]).astype(jnp.bfloat16)
    store(ref.down_part, ref.o_down_part)

    own_half = send(
        ref.hidden.at[sibling], ref.hid.at[mixed.mine], ref.h_send, ref.h_recv, mixed.sibling
    )
    own_half.start()
    ref.hid[mixed.mine] = ref.hidden[me]

    ref.gain[...] = jnp.zeros_like(ref.gain)
    for block in (3, 2, 1, 0):
        incoming = back.total(block)
        grad, gain = head_norm_back(incoming, ref.hidden[block], vector(ref.v_norm_mid))
        ref.gh_all[block, back.mine] = (
            ref.dy_all[block, back.mine].astype(jnp.float32) + grad
        ).astype(jnp.bfloat16)
        back.share(block, ref.gh_all).start()
        ref.gain[...] += gain
    ref.gain[...] *= 0.5
    store(ref.gain, ref.o_gain)
    own_half.wait()
    store(ref.hid, ref.o_hidden)
    for block in (3, 2, 1, 0):
        back.share(block, ref.gh_all).wait()
        store(ref.gh_all.at[block], ref.o_gh.at[block])
    for i, stream in enumerate(streams):
        for copy in stream.copies:
            copy.wait()
        store(table["early" + str(i)], table["o_early" + str(i)])
    for copy in stores:
        copy.wait()
    first.drain()
    cot.drain()


def front_part(inputs, ffn):
    low, wide = jnp.bfloat16, jnp.float32
    names = list(inputs)
    outs = dict(
        o_norm_all=((4, ROWS, 1024), low),
        o_q=((2, 4, 2 * ROWS, HEAD_SIZE), low),
        o_k=((2, 4, ROWS, HEAD_SIZE), low),
        o_v=((2, 4, ROWS, HEAD_SIZE), low),
        o_qraw=((4, ROWS, 512), wide),
        o_kraw=((4, ROWS, 256), wide),
        o_att=((4, ROWS, 512), low),
        o_lse=((2, 4, 1, 2 * ROWS), wide),
        o_hidden=((ROWS, 1024), wide),
        o_down=((4, 4, 2, 32, 768), low),
        o_gate=((4, 4, 2, 32, 768), low),
        o_up=((4, 4, 2, 32, 768), low),
        o_down_part=((4, ROWS, 1024), low),
        o_gh=((4, ROWS, 1024), low),
        o_gain=((1, 1024), wide),
    )
    early = {"early" + str(i): ((2, 4, 2, 32, entry[2]), low) for i, entry in enumerate(ffn)}
    outs.update({"o_" + name: spec for name, spec in early.items()})
    whole = ("tokens", COTANGENT)
    scratch = {
        "v_" + name: pltpu.VMEM(inputs[name].shape, inputs[name].dtype)
        for name in names
        if name not in whole
    }
    scratch.update({name: pltpu.VMEM(*spec) for name, spec in early.items()})
    scratch.update(
        load_sems=pltpu.SemaphoreType.DMA((len(names),)),
        store_sems=pltpu.SemaphoreType.DMA((len(outs) + 3,)),
        f_send=pltpu.SemaphoreType.DMA((len(ffn), 2)),
        f_recv=pltpu.SemaphoreType.DMA((len(ffn), 2)),
        h_send=pltpu.SemaphoreType.DMA,
        h_recv=pltpu.SemaphoreType.DMA,
        norm_all=pltpu.VMEM((4, ROWS, 1024), low),
        mid_all=pltpu.VMEM((4, ROWS, 1024), low),
        gh_all=pltpu.VMEM((4, ROWS, 1024), low),
        qraw=pltpu.VMEM((4, ROWS, 512), wide),
        kraw=pltpu.VMEM((4, ROWS, 256), wide),
        q=pltpu.VMEM((2, 4, 2 * ROWS, HEAD_SIZE), low),
        k=pltpu.VMEM((2, 4, ROWS, HEAD_SIZE), low),
        v=pltpu.VMEM((2, 4, ROWS, HEAD_SIZE), low),
        lse=pltpu.VMEM((2, 4, 1, 2 * ROWS), wide),
        att=pltpu.VMEM((4, ROWS, 512), low),
        part=pltpu.VMEM((ROWS, 1024), wide),
        own=pltpu.VMEM((4, HALF, 1024), wide),
        hidden=pltpu.VMEM((4, HALF, 1024), wide),
        hid=pltpu.VMEM((ROWS, 1024), wide),
        p_out=pltpu.VMEM((4, HALF, 1024), low),
        act=pltpu.VMEM((4, ROWS, 768), low),
        dup=pltpu.VMEM((4, ROWS, 768), low),
        dgate=pltpu.VMEM((4, ROWS, 768), low),
        gw_down=pltpu.VMEM((4, 4, 2, 32, 768), low),
        gw_gate=pltpu.VMEM((4, 4, 2, 32, 768), low),
        gw_up=pltpu.VMEM((4, 4, 2, 32, 768), low),
        down_part=pltpu.VMEM((4, ROWS, 1024), low),
        gain=pltpu.VMEM((1, 1024), wide),
    )
    scratch.update(zip(("tokens_all", "n_send", "n_recv"), gather_scratch(ROWS, 1024)))
    scratch.update(zip(("dy_all", "c_send", "c_recv"), gather_scratch(ROWS, 1024)))
    for tag in "pb":
        scratch.update(zip((tag + end for end in SCATTER_PARTS), exchange_scratch()))
    results = pl.pallas_call(
        functools.partial(
            front_kernel,
            names + list(outs) + list(scratch),
            SimpleNamespace(loads=names, ffn=[entry[:4] for entry in ffn]),
        ),
        out_shape=[jax.ShapeDtypeStruct(*spec) for spec in outs.values()],
        in_specs=[pl.BlockSpec(memory_space=pl.ANY)] * len(names),
        out_specs=[pl.BlockSpec(memory_space=pl.ANY)] * len(outs),
        scratch_shapes=list(scratch.values()),
        compiler_params=pltpu.CompilerParams(
            collective_id=4, has_side_effects=True, vmem_limit_bytes=62 << 20
        ),
    )(*inputs.values())
    return SimpleNamespace(**dict(zip(outs, results)))


def rotary_tables():
    position = np.arange(SEQUENCE_TOKENS, dtype=np.float64)
    inverse = 1000000.0 ** (-np.arange(HEAD_SIZE // 2, dtype=np.float64) * 2.0 / HEAD_SIZE)
    angles = position[:, None] * inverse[None, :]
    cosine, sine = np.cos(angles), np.sin(angles)
    return (
        jnp.asarray(
            np.concatenate([table, tail], axis=1).astype(np.float32).reshape(4, ROWS, HEAD_SIZE)
        )
        for table, tail in ((cosine, cosine), (sine, -sine))
    )


def per_device(
    tokens,
    norm_in,
    w_query,
    key_matrix,
    value_matrix,
    query_gain,
    key_gain,
    w_out,
    norm_mid,
    w_gate,
    w_up,
    w_down,
    cotangent,
):
    cosine, sine = rotary_tables()
    ffn = ffn_streams()
    front = front_part(
        dict(
            tokens=tokens,
            norm_in=norm_in,
            wq=w_query,
            wk=key_matrix,
            wv=value_matrix,
            cos=cosine,
            sin=sine,
            qg=query_gain,
            kg=key_gain,
            cot=cotangent,
            w_out=w_out,
            w_down=w_down,
            norm_mid=norm_mid,
            w_gate=w_gate,
            w_up=w_up,
        ),
        ffn,
    )
    outs = back_part(
        dict(
            gh=front.o_gh,
            w_out=w_out,
            att=front.o_att,
            down_part=front.o_down_part,
            gate=front.o_gate,
            up=front.o_up,
            down=front.o_down,
            q=front.o_q,
            k=front.o_k,
            v=front.o_v,
            lse=front.o_lse,
            qraw=front.o_qraw,
            kraw=front.o_kraw,
            cos=cosine,
            sin=sine,
            qg=query_gain,
            kg=key_gain,
            wq=w_query,
            wk=key_matrix,
            wv=value_matrix,
            norm_all=front.o_norm_all,
            hidden=front.o_hidden,
            tokens=tokens,
            norm_in=norm_in,
            gain_mid=front.o_gain,
            **{"early" + str(i): vars(front)["o_early" + str(i)] for i in range(len(ffn))},
        ),
        ffn,
    )
    return (
        outs.result,
        outs.grad_tokens,
        outs.o_norm_in.reshape(1024),
        outs.o_q,
        outs.o_k,
        outs.o_v,
        outs.o_qgain.reshape(HEAD_SIZE),
        outs.o_kgain.reshape(HEAD_SIZE),
        outs.o_out.T,
        outs.o_norm_mid.reshape(1024),
        outs.o_gate,
        outs.o_up,
        outs.o_down.T,
    )


def solution(mesh):
    placed = (
        P(("dp", "tensor"), None),
        P(),
        P(None, "tensor"),
        P(None, "tensor"),
        P(None, "tensor"),
        P(),
        P(),
        P("tensor", None),
        P(),
        P(None, "tensor"),
        P(None, "tensor"),
        P("tensor", None),
        P(("dp", "tensor"), None),
    )
    return jax.shard_map(
        per_device,
        mesh=mesh,
        in_specs=placed,
        out_specs=(
            P(("dp", "tensor"), None),
            P(("dp", "tensor"), None),
            P(),
            P("dp", "tensor"),
            P("dp", "tensor"),
            P("dp", "tensor"),
            P(),
            P(),
            P("tensor", "dp"),
            P(),
            P("dp", "tensor"),
            P("dp", "tensor"),
            P("tensor", "dp"),
        ),
        check_vma=False,
    )
```
